32 devices in a mesh: dp: 8 (over z, y), tp: 4 (over x, core).
Axes of the slice: x: 2, y: 2, z: 4, core: 2. Of those that a mesh axis runs over, the one named last changes fastest.
Arguments:
- tokens: bfloat16 [8192, 1536], P('dp'), may hold values from -6 to 6
- text: bfloat16 [2048, 4096], P('dp'), may hold values from -6 to 6
- cond: bfloat16 [8, 1024], P('dp'), may hold values from -6 to 6
- frames: int32 [8], P('dp'), may hold values from 4 to 16, as said below
- w_query: bfloat16 [1536, 1536], P('dp', 'tp'), may hold values from -0.15625 to 0.15625
- w_key: bfloat16 [1536, 1536], P('dp', 'tp'), may hold values from -0.15625 to 0.15625
- w_value: bfloat16 [1536, 1536], P('dp', 'tp'), may hold values from -0.15625 to 0.15625
- w_out: bfloat16 [1536, 1536], P('tp', 'dp'), may hold values from -2.5 to 2.5
- w_text_key: bfloat16 [4096, 1536], P('dp', 'tp'), may hold values from -0.09375 to 0.09375
- w_text_value: bfloat16 [4096, 1536], P('dp', 'tp'), may hold values from -0.09375 to 0.09375
- w_gate: bfloat16 [1536, 4096], P('dp', 'tp'), may hold values from -0.15625 to 0.15625
- w_up: bfloat16 [1536, 4096], P('dp', 'tp'), may hold values from -0.15625 to 0.15625
- w_down: bfloat16 [4096, 1536], P('tp', 'dp'), may hold values from -0.09375 to 0.09375
- w_ada: bfloat16 [1024, 6144], P('dp'), may hold values from -0.1875 to 0.1875
- ada_bias: bfloat16 [6144], P('dp'), may hold values from -3 to 3
- norm_one: bfloat16 [1536], P('dp'), may hold values from 0.5 to 1.5
- norm_two: bfloat16 [1536], P('dp'), may hold values from 0.5 to 1.5
- query_gain: bfloat16 [1536], P('tp'), may hold values from 0.5 to 1.5
- key_gain: bfloat16 [1536], P('tp'), may hold values from 0.5 to 1.5
- text_key_gain: bfloat16 [1536], P('tp'), may hold values from 0.5 to 1.5
- cross_gate: bfloat16 [24], P('tp'), may hold values from -1.5 to 1.5
- cotangent: bfloat16 [8192, 1536], P('dp'), may hold values from -6 to 6
Outputs:
- block_out: bfloat16 [8192, 1536], P('dp')
- grad_tokens: bfloat16 [8192, 1536], P('dp')
- grad_query: float32 [1536, 1536], P('dp', 'tp')
- grad_key: float32 [1536, 1536], P('dp', 'tp')
- grad_value: float32 [1536, 1536], P('dp', 'tp')
- grad_out: float32 [1536, 1536], P('tp', 'dp')
- grad_text_key: float32 [4096, 1536], P('dp', 'tp')
- grad_text_value: float32 [4096, 1536], P('dp', 'tp')
- grad_gate: float32 [1536, 4096], P('dp', 'tp')
- grad_up: float32 [1536, 4096], P('dp', 'tp')
- grad_down: float32 [4096, 1536], P('tp', 'dp')
- grad_ada: float32 [1024, 6144], P('dp')
- grad_ada_bias: float32 [6144], P('dp')
- grad_norm_one: float32 [1536], P('dp')
- grad_norm_two: float32 [1536], P('dp')
- grad_query_gain: float32 [1536], P('tp')
- grad_key_gain: float32 [1536], P('tp')
- grad_text_key_gain: float32 [1536], P('tp')
- grad_cross_gate: float32 [24], P('tp')
The draws below stay inside these ranges and needn't reach their ends.
Inputs may be any that keep to these rules, and one draw needn't show every extreme that they name: Clip c has frames[c] frames of 64 tokens, the last of each frame being its nextframe token, and occupies the first frames[c] * 64 of its 1024 slots. Every draw has a clip of 16 frames and one of 4 frames.
All inputs are finite; a program needn't handle non-finite values.
Results may differ from the reference program's by a relative error of at most 0.019.
Values may be sent and summed in bfloat16 or wider, within the bound.
A program may use at most 256 MiB of HBM per device.

```python
import jax
import jax.numpy as jnp
from jax import lax

D = 1536
HEADS = 24
HEAD = 64
FF = 4096
CAP = 4096
COND = 1024
TXT = 256
FRAME_TOK = 64
MAXF = 16
MINF = 4
SEQ = 1024
CLIPS = 8
TOKENS = 8192
N_TP = 4


def draw_frames(key, part):
    key = jax.random.fold_in(key, 7)
    keys = jax.random.split(key, 3)
    counts = jax.random.randint(keys[0], (CLIPS,), MINF, MAXF + 1)
    longest = jax.random.randint(keys[1], (), 0, CLIPS)
    shortest = (longest + jax.random.randint(keys[2], (), 1, CLIPS)) % CLIPS
    counts = counts.at[longest].set(MAXF)
    counts = counts.at[shortest].set(MINF)
    return counts.astype(jnp.int32)


def level_of(rng, extent, cuts, smallest, top_value):
    level, own = 1.0, jax.random.fold_in(rng, 6)
    for axis_at, shards_of in cuts:
        draws = jnp.exp(jax.random.uniform(jax.random.fold_in(own, axis_at), (shards_of,), jnp.float32, smallest / len(cuts), top_value / len(cuts)))
        level = level * jnp.repeat(draws, extent[axis_at] // shards_of).reshape([-1 if axis == axis_at else 1 for axis in range(len(extent))])
    return level


def normal_values(own_key, dims, width, most, shards=(), kind=jnp.bfloat16):
    loudness = level_of(own_key, dims, shards, -0.22, 0.18) if shards else 1.0
    values = jax.random.normal(own_key, dims, jnp.float32) * width * loudness
    return jnp.minimum(jnp.maximum(values, -most), most).astype(kind)


def setup_inputs(seed: int = 0) -> dict:
    key_of = jax.random.split(jax.random.key(seed), 23)
    return {
        "tokens": normal_values(key_of[0], (TOKENS, D), 1.0, 6.0, ((0, 8),)),
        "text": normal_values(key_of[1], (CLIPS * TXT, CAP), 1.0, 6.0, ((0, 8),)),
        "cond": normal_values(key_of[2], (CLIPS, COND), 1.0, 6.0, ((0, 8),)),
        "frames": draw_frames(jax.random.fold_in(key_of[22], 71), 0),
        "w_query": normal_values(key_of[4], (D, D), D ** -0.5, 0.15625, ((0, 8), (1, 4))),
        "w_key": normal_values(key_of[5], (D, D), D ** -0.5, 0.15625, ((0, 8), (1, 4))),
        "w_value": normal_values(key_of[6], (D, D), D ** -0.5, 0.15625, ((0, 8), (1, 4))),
        "w_out": normal_values(key_of[7], (D, D), (max(D // 256, 1)) ** -0.5, 2.5, ((0, 4), (1, 8))),
        "w_text_key": normal_values(key_of[8], (CAP, D), CAP ** -0.5, 0.09375, ((0, 8), (1, 4))),
        "w_text_value": normal_values(key_of[9], (CAP, D), CAP ** -0.5, 0.09375, ((0, 8), (1, 4))),
        "w_gate": normal_values(key_of[10], (D, FF), D ** -0.5, 0.15625, ((0, 8), (1, 4))),
        "w_up": normal_values(key_of[11], (D, FF), D ** -0.5, 0.15625, ((0, 8), (1, 4))),
        "w_down": normal_values(key_of[12], (FF, D), FF ** -0.5, 0.09375, ((0, 4), (1, 8))),
        "w_ada": normal_values(key_of[13], (COND, 4 * D), COND ** -0.5, 0.1875, ((0, 8),)),
        "ada_bias": normal_values(key_of[14], (4 * D,), 0.3, 3.0, ((0, 8),)),
        "norm_one": jnp.clip(1.0 + 0.1 * jax.random.normal(key_of[15], (D,), jnp.float32), 0.5, 1.5).astype(jnp.bfloat16),
        "norm_two": jnp.clip(1.0 + 0.1 * jax.random.normal(key_of[16], (D,), jnp.float32), 0.5, 1.5).astype(jnp.bfloat16),
        "query_gain": jnp.clip(1.0 + 0.1 * jax.random.normal(key_of[17], (D,), jnp.float32), 0.5, 1.5).astype(jnp.bfloat16),
        "key_gain": jnp.clip(1.0 + 0.1 * jax.random.normal(key_of[18], (D,), jnp.float32), 0.5, 1.5).astype(jnp.bfloat16),
        "text_key_gain": jnp.clip(1.0 + 0.1 * jax.random.normal(key_of[19], (D,), jnp.float32), 0.5, 1.5).astype(jnp.bfloat16),
        "cross_gate": jnp.clip(jax.random.uniform(key_of[20], (HEADS,), jnp.float32, -1.5, 1.5) * level_of(key_of[20], (HEADS,), ((0, 4),), -0.4, 0.0), -1.5, 1.5).astype(jnp.bfloat16),
        "cotangent": normal_values(key_of[21], (TOKENS, D), 1.0, 6.0, ((0, 8),)),
    }


@jax.custom_vjp
def low(v):
    return lax.optimization_barrier(v.astype(jnp.bfloat16)).astype(jnp.float32)

@jax.custom_vjp
def low_back(v):
    return v

def low_keep(v):
    return (low(v), None)

def low_pass(kept, grad):
    return (grad,)

def back_keep(v):
    return (v, None)

def back_low(kept, grad):
    return (low(grad),)
low.defvjp(low_keep, low_pass)
low_back.defvjp(back_keep, back_low)
EPS = 1e-06
ROPE_BASE = 10000.0
MASKED = -1e+30

def matmul_high(left, right):
    return jnp.dot(left, right, precision=lax.Precision.HIGHEST, preferred_element_type=jnp.float32)

def rms_rows(value, gain):
    return value * lax.rsqrt(lax.optimization_barrier(jnp.mean(value * value, axis=-1, keepdims=True)) + EPS) * gain

def rope_tables(row_count):
    row_index = jnp.arange(row_count, dtype=jnp.int32)
    frame_pos = (row_index // FRAME_TOK).astype(jnp.float32)
    place_pos = (row_index % FRAME_TOK).astype(jnp.float32)
    quarter = HEAD // 4
    freqs = ROPE_BASE ** (-jnp.arange(quarter, dtype=jnp.float32) / quarter)
    first_angle = frame_pos[:, None] * freqs[None, :]
    second_angle = place_pos[:, None] * freqs[None, :]
    angles = jnp.concatenate([first_angle, first_angle, second_angle, second_angle], axis=1)
    return (jnp.cos(angles), jnp.sin(angles))

def rotate(value, cosine_table, sine_table):
    quarter = HEAD // 4
    part_a = value[..., :quarter]
    part_b = value[..., quarter:2 * quarter]
    part_c = value[..., 2 * quarter:3 * quarter]
    part_d = value[..., 3 * quarter:]
    turned = jnp.concatenate([-part_b, part_a, -part_d, part_c], axis=-1)
    return value * cosine_table[:, None, :] + turned * sine_table[:, None, :]

def softmax_rows(scores):
    shifted = scores - lax.optimization_barrier(jnp.max(scores, axis=-1, keepdims=True))
    expo = jnp.exp(shifted)
    return expo / lax.optimization_barrier(jnp.sum(expo, axis=-1, keepdims=True))

def clip_forward(weights, clip_tokens, clip_text, clip_cond, clip_frames):
    w_query, w_key, w_value, w_out, w_text_key, w_text_value, w_gate, w_up, w_down, w_ada, ada_bias, norm_one, norm_two, query_gain, key_gain, text_key_gain, cross_gate = weights
    length = clip_frames * FRAME_TOK
    row_index = jnp.arange(SEQ, dtype=jnp.int32)
    key_valid = row_index < length
    live_rows = key_valid.astype(jnp.float32)[:, None]
    activated = low(jax.nn.silu(clip_cond))
    modulation = matmul_high(activated[None, :], w_ada)[0] + ada_bias
    scale_attn = modulation[:D]
    gate_attn = modulation[D:2 * D]
    scale_ffn = modulation[2 * D:3 * D]
    gate_ffn = modulation[3 * D:]
    h_one = low(rms_rows(clip_tokens, norm_one) * (1.0 + scale_attn))
    queries = low_back(matmul_high(h_one, w_query)).reshape(SEQ, HEADS, HEAD)
    keys = low_back(matmul_high(h_one, w_key)).reshape(SEQ, HEADS, HEAD)
    values = low(low_back(matmul_high(h_one, w_value))).reshape(SEQ, HEADS, HEAD)
    query_norm = rms_rows(queries, query_gain.reshape(HEADS, HEAD))
    key_norm = rms_rows(keys, key_gain.reshape(HEADS, HEAD))
    cosine_table, sine_table = rope_tables(SEQ)
    query_rot = low(rotate(query_norm, cosine_table, sine_table))
    key_rot = low(rotate(key_norm, cosine_table, sine_table))
    query_text = low(query_norm)
    text_keys = low_back(matmul_high(clip_text, w_text_key)).reshape(TXT, HEADS, HEAD)
    text_key_norm = low(rms_rows(text_keys, text_key_gain.reshape(HEADS, HEAD)))
    text_values = low(low_back(matmul_high(clip_text, w_text_value))).reshape(TXT, HEADS, HEAD)
    score_scale = HEAD ** (-0.5)
    self_scores = jnp.einsum('qhd,khd->hqk', query_rot, key_rot, precision=lax.Precision.HIGHEST)
    self_scores = jnp.where(key_valid[None, None, :], low_back(self_scores * score_scale), MASKED)
    self_probs = low(softmax_rows(self_scores))
    self_outs = low_back(jnp.einsum('hqk,khd->qhd', self_probs, values, precision=lax.Precision.HIGHEST))
    text_scores = jnp.einsum('qhd,thd->hqt', query_text, text_key_norm, precision=lax.Precision.HIGHEST)
    text_probs = low(softmax_rows(low_back(text_scores * score_scale)))
    text_outs = low_back(jnp.einsum('hqt,thd->qhd', text_probs, text_values, precision=lax.Precision.HIGHEST))
    gate_tanh = jnp.tanh(cross_gate)
    mixed = low(self_outs + gate_tanh[None, :, None] * text_outs).reshape(SEQ, D)
    local_cols = D // N_TP
    attn_sum = jnp.zeros((SEQ, D), jnp.float32)
    for shard in range(N_TP):
        part_cols = slice(shard * local_cols, (shard + 1) * local_cols)
        attn_sum = attn_sum + low(matmul_high(mixed[:, part_cols], w_out[part_cols, :]))
    attn_sum = low_back(attn_sum)
    hidden_state = clip_tokens + live_rows * jnp.tanh(gate_attn) * attn_sum
    h_two = low(rms_rows(hidden_state, norm_two) * (1.0 + scale_ffn))
    gate_pre = low_back(matmul_high(h_two, w_gate))
    up_pre = low_back(matmul_high(h_two, w_up))
    hidden_units = low(jax.nn.silu(gate_pre) * up_pre)
    local_units = FF // N_TP
    ffn_sum = jnp.zeros((SEQ, D), jnp.float32)
    for shard in range(N_TP):
        part_units = slice(shard * local_units, (shard + 1) * local_units)
        ffn_sum = ffn_sum + low(matmul_high(hidden_units[:, part_units], w_down[part_units, :]))
    ffn_sum = low_back(ffn_sum)
    return hidden_state + live_rows * jnp.tanh(gate_ffn) * ffn_sum

def reference(tokens, text, cond, frames, w_query, w_key, w_value, w_out, w_text_key, w_text_value, w_gate, w_up, w_down, w_ada, ada_bias, norm_one, norm_two, query_gain, key_gain, text_key_gain, cross_gate, cotangent):
    weights = tuple((weight.astype(jnp.float32) for weight in (w_query, w_key, w_value, w_out, w_text_key, w_text_value, w_gate, w_up, w_down, w_ada, ada_bias, norm_one, norm_two, query_gain, key_gain, text_key_gain, cross_gate)))
    clip_text = text.astype(jnp.float32).reshape(CLIPS, TXT, CAP)
    clip_cond = cond.astype(jnp.float32)
    clip_frames = frames.astype(jnp.int32)

    def forward(token_values, weight_values):

        def clip_step(clip_items):
            return clip_forward(weight_values, clip_items[0], clip_items[1], clip_items[2], clip_items[3])
        outputs = lax.map(jax.checkpoint(clip_step), (token_values.reshape(CLIPS, SEQ, D), clip_text, clip_cond, clip_frames))
        return outputs.reshape(TOKENS, D)
    result, pullback = jax.vjp(forward, tokens.astype(jnp.float32), weights)
    grad_input, grad_weights = pullback(cotangent.astype(jnp.float32))
    return (result.astype(jnp.bfloat16), grad_input.astype(jnp.bfloat16), grad_weights[0], grad_weights[1], grad_weights[2], grad_weights[3], grad_weights[4], grad_weights[5], grad_weights[6], grad_weights[7], grad_weights[8], grad_weights[9], grad_weights[10], grad_weights[11], grad_weights[12], grad_weights[13], grad_weights[14], grad_weights[15], grad_weights[16])
```

```python
import functools

import jax
import jax.numpy as jnp
from jax import lax
from jax.experimental import pallas as pl
from jax.experimental.pallas import tpu as pltpu
from jax.sharding import PartitionSpec as P

HEAD = 64
FRAME_TOK = 64


EPS = 1e-06
ROPE_BASE = 10000.0
MASKED = -1e30


def exact_dot(left, right):
    return jnp.dot(left, right, precision=lax.Precision.HIGHEST, preferred_element_type=jnp.float32)


def rope_flat(row_count, width):
    lane = jnp.arange(width, dtype=jnp.int32)
    within = lane % HEAD
    quarter = HEAD // 4
    which = within // quarter
    offset = within % quarter
    freqs = ROPE_BASE ** (-offset.astype(jnp.float32) / quarter)
    row_index = jnp.arange(row_count, dtype=jnp.int32)
    frame_pos = (row_index // FRAME_TOK).astype(jnp.float32)
    place_pos = (row_index % FRAME_TOK).astype(jnp.float32)
    position = jnp.where(which[None, :] < 2, frame_pos[:, None], place_pos[:, None])
    angles = position * freqs[None, :]
    source = lane - within + (which ^ 1) * quarter + offset
    signs = jnp.where(which % 2 == 0, -1.0, 1.0).astype(jnp.float32)
    turner = (lane[:, None] == source[None, :]).astype(jnp.float32) * signs[None, :]
    return (jnp.cos(angles), jnp.sin(angles), turner)


def rotate_flat(value, cosine_table, sine_table, turner):
    return value * cosine_table + exact_dot(value, turner) * sine_table


def rotate_flat_back(grad, cosine_table, sine_table, turner):
    return grad * cosine_table + exact_dot(grad * sine_table, turner.T)


def rms_parts(value):
    inverse = lax.rsqrt(jnp.mean(value * value, axis=-1, keepdims=True) + EPS)
    return (inverse, value * inverse)


def rms_back(inverse, normed, grad):
    return inverse * (grad - normed * jnp.mean(grad * normed, axis=-1, keepdims=True))


def head_norm(value, segment):
    inverse = lax.rsqrt(exact_dot(value * value, segment) / HEAD + EPS)
    inverse_wide = exact_dot(inverse, segment.T)
    return (inverse_wide, value * inverse_wide)


def head_norm_back(inverse_wide, normed, grad, segment):
    average = exact_dot(exact_dot(grad * normed, segment) / HEAD, segment.T)
    return inverse_wide * (grad - normed * average)


def to_heads(value):
    return value.reshape(value.shape[0], -1, HEAD).transpose(1, 0, 2)


def from_heads(value):
    return value.transpose(1, 0, 2).reshape(value.shape[1], -1)


def attend(query_block, keys, values, key_valid, score_scale):
    scores = (
        jnp.einsum("hqd,hkd->hqk", query_block, keys, preferred_element_type=jnp.float32)
        * score_scale
    )
    if key_valid is not None:
        scores = jnp.where(key_valid, scores, MASKED)
    maximum = jnp.max(scores, axis=-1, keepdims=True)
    expo = jnp.exp(scores - maximum)
    denominator = jnp.sum(expo, axis=-1, keepdims=True)
    probability = (expo / denominator).astype(jnp.bfloat16)
    outputs = jnp.einsum("hqk,hkd->hqd", probability, values, preferred_element_type=jnp.float32)
    return (outputs, maximum + jnp.log(denominator))


def attend_back(query_block, keys, values, key_valid, score_scale, log_total, grad_outputs):
    scores = (
        jnp.einsum("hqd,hkd->hqk", query_block, keys, preferred_element_type=jnp.float32)
        * score_scale
    )
    if key_valid is not None:
        scores = jnp.where(key_valid, scores, MASKED)
    probability = jnp.exp(scores - log_total)
    grad_values = jnp.einsum(
        "hqk,hqd->hkd",
        probability.astype(jnp.bfloat16),
        grad_outputs,
        preferred_element_type=jnp.float32,
    )
    grad_probs = jnp.einsum(
        "hqd,hkd->hqk", grad_outputs, values, preferred_element_type=jnp.float32
    )
    grad_scores = probability * (
        grad_probs - jnp.sum(probability * grad_probs, axis=-1, keepdims=True)
    )
    grad_scores = grad_scores.astype(jnp.bfloat16)
    grad_query = (
        jnp.einsum("hqk,hkd->hqd", grad_scores, keys, preferred_element_type=jnp.float32)
        * score_scale
    )
    grad_keys = (
        jnp.einsum("hqk,hqd->hkd", grad_scores, query_block, preferred_element_type=jnp.float32)
        * score_scale
    )
    return (grad_query, grad_keys, grad_values)


MESH = pl.DeviceIdType.MESH
VMEM_LIMIT = 60 * 2**20
GRID = 8
LINE = 4


def remote(src, dst, send, recv, **where):
    return pltpu.make_async_remote_copy(
        src_ref=src, dst_ref=dst, send_sem=send, recv_sem=recv, device_id=where, device_id_type=MESH
    )


def greet(axis, others):
    barrier = pltpu.get_barrier_semaphore()
    for other in others:
        pl.semaphore_signal(barrier, inc=1, device_id={axis: other}, device_id_type=MESH)
    pl.semaphore_wait(barrier, len(others))


def add_rows(out_ref, first, *others):
    rows = out_ref.shape[0]

    def step(i, carry):
        here = pl.ds(pl.multiple_of(i * 16, 16), 16)
        total = first[here, :].astype(jnp.float32)
        for other in others:
            total = total + other[here, :].astype(jnp.float32)
        out_ref[here, :] = total.astype(out_ref.dtype)
        return carry

    lax.fori_loop(0, rows // 16, step, 0)


def gather_kernel(chunks, n_in, n_out, *refs):
    shards, refs = refs[:n_in], refs[n_in:]
    cond_ref, small_ref, ada_ref = refs[:3]
    fulls, refs = refs[3 : 3 + n_out], refs[3 + n_out :]
    mod_ref, smalls_ref, act_ref = refs[:3]
    (conds, part, parts, up_s, up_r, dn_s, dn_r, y_s, y_r, own_sem, c_s, c_r, m_s, m_r, p_s, p_r) = refs[3:]
    me = lax.axis_index("dp")
    z, y = me // 2, lax.rem(me, 2)
    count = len(chunks)
    peers = [lax.rem(me + step, GRID) for step in range(1, GRID)]
    sources = [lax.rem(me + GRID - step, GRID) for step in range(1, GRID)]
    greet("dp", peers)

    def own(c):
        at, row, rows, col, cols = chunks[c][:5]
        return shards[at].at[pl.ds(row, rows), pl.ds(col, cols)]

    def place(c, origin):
        _, row, rows, _, cols, out, depth, out_col = chunks[c]
        start = pl.multiple_of(origin * depth + row, 16)
        return fulls[out].at[pl.ds(start, rows), pl.ds(out_col, cols)]

    def up(c, hop):
        origin = me - 2 * hop
        src = own(c) if hop == 0 else place(c, origin)
        return remote(src, place(c, origin), up_s.at[c, hop], up_r.at[c, hop], dp=me + 2)

    def down(c, hop):
        origin = me + 2 * hop
        src = own(c) if hop == 0 else place(c, origin)
        return remote(src, place(c, origin), dn_s.at[c, hop], dn_r.at[c, hop], dp=me - 2)

    def across(c, line):
        origin = 2 * line + y
        return remote(place(c, origin), place(c, origin), y_s.at[c, line], y_r.at[c, line], dp=me + 1 - 2 * y)

    def across_own(c):
        return remote(own(c), place(c, me), y_s.at[c, z], y_r.at[c, z], dp=me + 1 - 2 * y)

    def came_up(c, hop):
        origin = me - 2 * (hop + 1)
        return remote(place(c, origin), place(c, origin), up_s.at[c, hop], up_r.at[c, hop], dp=me)

    def came_down(c, hop):
        origin = me + 2 * (hop + 1)
        return remote(place(c, origin), place(c, origin), dn_s.at[c, hop], dn_r.at[c, hop], dp=me)

    def came_across(c, line):
        origin = 2 * line + 1 - y
        return remote(place(c, origin), place(c, origin), y_s.at[c, line], y_r.at[c, line], dp=me)

    def local(c):
        return pltpu.make_async_copy(own(c), place(c, me), own_sem.at[c])

    def pump(t):
        if t < count:
            pl.when(z < LINE - 1)(lambda: up(t, 0).start())
            pl.when(z > 0)(lambda: down(t, 0).start())
            across_own(t).start()
            local(t).start()
        for hop in range(LINE - 1):
            c = t - 1 - hop
            if not 0 <= c < count:
                continue

            @pl.when(z - 1 - hop >= 0)
            def _():
                came_up(c, hop).wait_recv()
                if hop < LINE - 2:
                    pl.when(z < LINE - 1)(lambda: up(c, hop + 1).start())
                across(c, z - 1 - hop).start()

            @pl.when(z + 1 + hop <= LINE - 1)
            def _():
                came_down(c, hop).wait_recv()
                if hop < LINE - 2:
                    pl.when(z > 0)(lambda: down(c, hop + 1).start())
                across(c, z + 1 + hop).start()

    pump(0)
    for step in range(1, GRID):
        there = peers[step - 1]
        remote(cond_ref.at[there], conds.at[me], c_s.at[step - 1], c_r.at[step - 1], dp=there).start()
        remote(small_ref, smalls_ref.at[me], m_s.at[step - 1], m_r.at[step - 1], dp=there).start()
    conds[pl.ds(me, 1)] = cond_ref[pl.ds(me, 1)]
    smalls_ref[pl.ds(me, 1)] = small_ref[...][None]
    pump(1)
    for step in range(1, GRID):
        here = sources[step - 1]
        remote(conds.at[here], conds.at[here], c_s.at[step - 1], c_r.at[step - 1], dp=me).wait_recv()
    cond = jnp.concatenate([conds[i] for i in range(GRID)], axis=0)
    act = (cond * (1.0 / (1.0 + jnp.exp(-cond)))).astype(jnp.bfloat16)
    act_ref[...] = act.astype(jnp.float32)
    width = ada_ref.shape[1] // 4
    for i in range(4):
        cols = pl.ds(i * width, width)
        product = jnp.dot(act, ada_ref[:, cols], preferred_element_type=jnp.float32)
        for j in range(GRID):
            part[j, :, cols] = product[j : j + 1, :]
    for step in range(1, GRID):
        there = peers[step - 1]
        remote(part.at[there], parts.at[me], p_s.at[step - 1], p_r.at[step - 1], dp=there).start()
    parts[pl.ds(me, 1)] = part[pl.ds(me, 1)]
    pump(2)
    for step in range(1, GRID):
        here = sources[step - 1]
        remote(parts.at[here], parts.at[here], p_s.at[step - 1], p_r.at[step - 1], dp=me).wait_recv()
    mod_ref[...] = sum(parts[i] for i in range(GRID))
    for t in range(3, count + LINE):
        pump(t)
    for c in range(count):
        for line in range(LINE):
            came_across(c, line).wait_recv()
        local(c).wait()
        for hop in range(LINE - 1):
            pl.when((z < LINE - 1) & (z - hop >= 0))(lambda: up(c, hop).wait_send())
            pl.when((z > 0) & (z + hop <= LINE - 1))(lambda: down(c, hop).wait_send())
        for line in range(LINE):
            across(c, line).wait_send()
    for step in range(1, GRID):
        here, there = sources[step - 1], peers[step - 1]
        remote(small_ref, smalls_ref.at[here], m_s.at[step - 1], m_r.at[step - 1], dp=me).wait_recv()
        remote(cond_ref.at[there], conds.at[me], c_s.at[step - 1], c_r.at[step - 1], dp=there).wait_send()
        remote(small_ref, smalls_ref.at[me], m_s.at[step - 1], m_r.at[step - 1], dp=there).wait_send()
        remote(part.at[there], parts.at[me], p_s.at[step - 1], p_r.at[step - 1], dp=there).wait_send()


def gather_all(shards, groups, cond, small, w_ada):
    chunks, outs = [], []
    for at, group in enumerate(groups):
        col = 0
        depth = shards[group[0]].shape[0]
        for member in group:
            wide = shards[member].shape[1]
            tall = min(256, depth)
            step = 384 if wide % 384 == 0 else 512
            for row in range(0, depth, tall):
                for part in range(0, wide, step):
                    chunks.append((member, row, tall, part, step, at, depth, col + part))
            col += wide
        outs.append(jax.ShapeDtypeStruct((GRID * depth, col), jnp.bfloat16))
    count = len(chunks)
    any_spec = pl.BlockSpec(memory_space=pl.ANY)
    in_vmem = pl.BlockSpec(memory_space=pltpu.VMEM)
    wide = w_ada.shape[1]
    dma = pltpu.SemaphoreType.DMA
    return pl.pallas_call(
        functools.partial(gather_kernel, chunks, len(shards), len(outs)),
        out_shape=outs
        + [
            jax.ShapeDtypeStruct((1, wide), jnp.float32),
            jax.ShapeDtypeStruct((GRID,) + small.shape, jnp.float32),
            jax.ShapeDtypeStruct((GRID, cond.shape[2]), jnp.float32),
        ],
        in_specs=[any_spec] * len(shards) + [in_vmem] * 3,
        out_specs=[any_spec] * len(outs) + [in_vmem] * 3,
        scratch_shapes=[
            pltpu.VMEM((GRID, 1, cond.shape[2]), jnp.float32),
            pltpu.VMEM((GRID, 1, wide), jnp.float32),
            pltpu.VMEM((GRID, 1, wide), jnp.float32),
            dma((count, 3)),
            dma((count, 3)),
            dma((count, 3)),
            dma((count, 3)),
            dma((count, 4)),
            dma((count, 4)),
            dma((count,)),
        ]
        + [dma((GRID - 1,))] * 6,
        compiler_params=pltpu.CompilerParams(
            collective_id=0, has_side_effects=True, vmem_limit_bytes=VMEM_LIMIT
        ),
    )(*shards, cond, small, w_ada)


def scatter_kernel(chunks, n_in, n_out, *refs):
    grads, refs = refs[:n_in], refs[n_in:]
    vec_ref, refs = refs[0], refs[1:]
    outs, refs = refs[:n_out], refs[n_out:]
    vecs_ref, refs = refs[0], refs[1:]
    sets, refs = (refs[:4], refs[4:8], refs[8:12]), refs[12:]
    y_s, y_r, own_sem, up_s, up_r, dn_s, dn_r, v_s, v_r = refs
    me = lax.axis_index("dp")
    z, y = me // 2, lax.rem(me, 2)
    count = len(chunks)
    peers = [lax.rem(me + step, GRID) for step in range(1, GRID)]
    sources = [lax.rem(me + GRID - step, GRID) for step in range(1, GRID)]
    greet("dp", peers)
    for step in range(1, GRID):
        there = peers[step - 1]
        remote(vec_ref, vecs_ref.at[me], v_s.at[step - 1], v_r.at[step - 1], dp=there).start()
    vecs_ref[pl.ds(me, 1)] = vec_ref[...][None]

    def buffers(c):
        which, slot = chunks[c][:2]
        return [ref.at[slot] for ref in sets[which]]

    def mine(c, row_y):
        _, _, at, row, rows, col, cols = chunks[c][:7]
        return grads[at].at[:, row_y, pl.ds(row, rows), pl.ds(col, cols)]

    def across(c):
        return remote(mine(c, 1 - y), buffers(c)[1], y_s.at[c], y_r.at[c], dp=me + 1 - 2 * y)

    def load(c):
        return pltpu.make_async_copy(mine(c, y), buffers(c)[0], own_sem.at[c])

    def up(c, line):
        held, _, above, _ = buffers(c)
        return remote(held.at[line], above.at[line - 1], up_s.at[c, line - 1], up_r.at[c, line - 1], dp=me + 2)

    def down(c, line):
        held, _, _, below = buffers(c)
        return remote(held.at[line], below.at[line], dn_s.at[c, line], dn_r.at[c, line], dp=me - 2)

    def fold(c):
        held, crossed, _, _ = buffers(c)
        across(c).wait_recv()
        load(c).wait()
        for line in range(LINE):
            add_rows(held.at[line], held.at[line], crossed.at[line])

    def send_up(c, here):
        held, _, above, _ = buffers(c)
        for line in range(LINE - 1, here, -1):
            if here > 0:
                up(c, line).wait_recv()
                add_rows(held.at[line], held.at[line], above.at[line - 1])
            up(c, line).start()

    def send_down(c, here):
        held, _, _, below = buffers(c)
        for line in range(here):
            if here < LINE - 1:
                down(c, line).wait_recv()
                add_rows(held.at[line], held.at[line], below.at[line])
            down(c, line).start()

    def finish(c, here):
        held, _, above, below = buffers(c)
        _, _, _, row, rows, _, cols, out, out_col = chunks[c]
        terms = [held.at[here]]
        if here > 0:
            up(c, here).wait_recv()
            terms.append(above.at[here - 1])
        if here < LINE - 1:
            down(c, here).wait_recv()
            terms.append(below.at[here])
        add_rows(outs[out].at[pl.ds(row, rows), pl.ds(out_col, cols)], *terms)

    def pump(t):
        for c in ([0, 1] if t == 0 else [t + 1]):
            if c < count:
                across(c).start()
                load(c).start()
        if 0 <= t - 1 < count:
            fold(t - 1)
        for hop in range(LINE):
            c = t - 1 - hop
            if 0 <= c < count:
                if hop < LINE - 1:
                    pl.when(z == hop)(lambda: send_up(c, hop))
                    pl.when(z == LINE - 1 - hop)(lambda: send_down(c, LINE - 1 - hop))
                else:
                    for here in range(LINE):
                        pl.when(z == here)(lambda: finish(c, here))

    for t in range(count + LINE):
        pump(t)
    for c in range(count):
        across(c).wait_send()
        for here in range(LINE):

            @pl.when(z == here)
            def _():
                for line in range(here + 1, LINE):
                    up(c, line).wait_send()
                for line in range(here):
                    down(c, line).wait_send()

    for step in range(1, GRID):
        here, there = sources[step - 1], peers[step - 1]
        remote(vec_ref, vecs_ref.at[here], v_s.at[step - 1], v_r.at[step - 1], dp=me).wait_recv()
        remote(vec_ref, vecs_ref.at[me], v_s.at[step - 1], v_r.at[step - 1], dp=there).wait_send()


def scatter_all(grads, vec):
    chunks, outs, slots = [], [], [0, 0, 0]
    shapes = [(192, 384), (192, 512), (256, 384)]
    for at, grad in enumerate(grads):
        depth, wide = grad.shape[0] // GRID, grad.shape[1]
        outs.append(jax.ShapeDtypeStruct((depth, wide), jnp.float32))
        which = 2 if depth % 192 else (0 if wide % 384 == 0 else 1)
        tall, step = shapes[which]
        for row in range(0, depth, tall):
            for col in range(0, wide, step):
                chunks.append((which, slots[which], at, row, tall, col, step, at, col))
                slots[which] += 1
    count = len(chunks)
    any_spec = pl.BlockSpec(memory_space=pl.ANY)
    in_vmem = pl.BlockSpec(memory_space=pltpu.VMEM)
    dma = pltpu.SemaphoreType.DMA
    scratch = []
    for which in range(3):
        for lines in (4, 4, 3, 3):
            scratch.append(pltpu.VMEM((slots[which], lines) + shapes[which], jnp.bfloat16))
    views = [g.reshape(LINE, 2, g.shape[0] // GRID, g.shape[1]) for g in grads]
    return pl.pallas_call(
        functools.partial(scatter_kernel, chunks, len(grads), len(outs)),
        out_shape=outs + [jax.ShapeDtypeStruct((GRID,) + vec.shape, jnp.float32)],
        in_specs=[any_spec] * len(grads) + [in_vmem],
        out_specs=[in_vmem] * (len(outs) + 1),
        scratch_shapes=scratch
        + [dma((count,))] * 3
        + [dma((count, 3))] * 4
        + [dma((GRID - 1,))] * 2,
        compiler_params=pltpu.CompilerParams(
            collective_id=1, has_side_effects=True, vmem_limit_bytes=VMEM_LIMIT
        ),
    )(*views, vec)


TP_PARTS = 8


def sum_kernel(p_ref, out_ref, crossed, held, other, c_s, c_r, x_s, x_r, o_s, o_r):
    me = lax.axis_index("tp")
    core = lax.rem(me, 2)
    beside, across = me + 1 - 2 * core, lax.rem(me + 2, 4)
    greet("tp", [beside, across])
    half = p_ref.shape[0] // 2
    rows = half // TP_PARTS

    def spot(k, which):
        return pl.ds(pl.multiple_of(which * half + k * rows, 16), rows)

    def part(k):
        return pl.ds(k * rows, rows)

    def first(k):
        return remote(p_ref.at[spot(k, 1 - core)], crossed.at[part(k)], c_s.at[k], c_r.at[k], tp=beside)

    def second(k):
        return remote(held.at[part(k)], other.at[part(k)], x_s.at[k], x_r.at[k], tp=across)

    def third(k, which):
        return remote(out_ref.at[spot(k, which)], out_ref.at[spot(k, which)], o_s.at[k], o_r.at[k], tp=beside)

    for k in range(TP_PARTS):
        first(k).start()
    for k in range(TP_PARTS):
        first(k).wait_recv()
        add_rows(held.at[part(k)], p_ref.at[spot(k, core)], crossed.at[part(k)])
        second(k).start()
    for k in range(TP_PARTS):
        second(k).wait_recv()
        add_rows(out_ref.at[spot(k, core)], held.at[part(k)], other.at[part(k)])
        third(k, core).start()
    for k in range(TP_PARTS):
        third(k, 1 - core).wait_recv()
        first(k).wait_send()
        second(k).wait_send()
        third(k, core).wait_send()


def sum_tp(partial):
    rows, wide = partial.shape
    dma = pltpu.SemaphoreType.DMA
    in_vmem = pl.BlockSpec(memory_space=pltpu.VMEM)
    return pl.pallas_call(
        sum_kernel,
        out_shape=jax.ShapeDtypeStruct((rows, wide), jnp.bfloat16),
        in_specs=[in_vmem],
        out_specs=in_vmem,
        scratch_shapes=[pltpu.VMEM((rows // 2, wide), jnp.bfloat16)] * 3 + [dma((TP_PARTS,))] * 6,
        compiler_params=pltpu.CompilerParams(
            collective_id=2, has_side_effects=True, vmem_limit_bytes=VMEM_LIMIT
        ),
    )(partial)


def dot_nt(left, right):
    return lax.dot_general(
        left, right, (((1,), (1,)), ((), ())), preferred_element_type=jnp.float32
    )


def dot_tn(left, right):
    return lax.dot_general(
        left, right, (((0,), (0,)), ((), ())), preferred_element_type=jnp.float32
    )


def gather_plain(shards, groups, cond, small, w_ada):
    full = [lax.all_gather(shard, "dp", axis=0, tiled=True) for shard in shards]
    packed = [jnp.concatenate([full[i] for i in group], axis=1) for group in groups]
    act = jax.nn.silu(lax.all_to_all(cond[:, 0], "dp", 0, 0, tiled=True)).astype(jnp.bfloat16)
    parts = jnp.dot(act, w_ada, preferred_element_type=jnp.float32)
    mod = lax.psum_scatter(parts, "dp", scatter_dimension=0, tiled=True)
    smalls = lax.all_gather(small, "dp", axis=0)
    return (*packed, mod, smalls, act.astype(jnp.float32))


def scatter_plain(grads, vec):
    sums = [
        lax.psum_scatter(grad, "dp", scatter_dimension=0, tiled=True).astype(jnp.float32)
        for grad in grads
    ]
    return (*sums, lax.all_gather(vec, "dp", axis=0))


def on_device(
    tokens,
    text,
    cond,
    frames,
    w_query,
    w_key,
    w_value,
    w_out,
    w_text_key,
    w_text_value,
    w_gate,
    w_up,
    w_down,
    w_ada,
    ada_bias,
    norm_one,
    norm_two,
    query_gain,
    key_gain,
    text_key_gain,
    cross_gate,
    cotangent,
):
    row_count = tokens.shape[0]
    text_count = text.shape[0]
    clips = lax.axis_size("dp")
    small = jnp.concatenate([ada_bias, norm_one, norm_two]).astype(jnp.float32)[None, :]
    shards = (w_query, w_key, w_value, w_out.T, w_text_key, w_text_value, w_gate, w_up, w_down.T)
    cond_rows = cond.astype(jnp.float32).reshape(clips, 1, -1)
    if clips == GRID:
        full_attn, full_text, full_ffn, mod_sum, smalls, act_rows = gather_all(
            shards, ((0, 1, 2, 3), (4, 5), (6, 7, 8)), cond_rows, small, w_ada
        )
    else:
        full_attn, full_text, full_ffn, mod_sum, smalls, act_rows = gather_plain(
            shards, ((0, 1, 2, 3), (4, 5), (6, 7, 8)), cond_rows, small, w_ada
        )
    cols, units = w_query.shape[1], w_gate.shape[1]
    full_query, full_key = full_attn[:, :cols], full_attn[:, cols : 2 * cols]
    full_value, out_turned = full_attn[:, 2 * cols : 3 * cols], full_attn[:, 3 * cols :]
    full_text_key, full_text_value = full_text[:, :cols], full_text[:, cols:]
    full_gate, full_up = full_ffn[:, :units], full_ffn[:, units : 2 * units]
    down_turned = full_ffn[:, 2 * units :]
    bias_rows, gain_rows = ada_bias.shape[0], norm_one.shape[0]
    bias_full = smalls[:, 0, :bias_rows].reshape(-1)
    gain_one = smalls[:, 0, bias_rows : bias_rows + gain_rows].reshape(-1)
    gain_two = smalls[:, 0, bias_rows + gain_rows :].reshape(-1)
    local_cols = full_query.shape[1]
    heads_here = local_cols // HEAD
    segment = (
        jnp.arange(local_cols, dtype=jnp.int32)[:, None] // HEAD
        == jnp.arange(heads_here, dtype=jnp.int32)[None, :]
    ).astype(jnp.float32)
    token_values = tokens.astype(jnp.float32)
    modulation = mod_sum[0] + bias_full
    scale_attn, gate_attn, scale_ffn, gate_ffn = jnp.split(modulation, 4)
    row_index = jnp.arange(row_count, dtype=jnp.int32)
    length = frames[0] * FRAME_TOK
    row_valid = row_index < length
    live_rows = row_valid.astype(jnp.float32)[:, None]
    key_valid = row_valid[None, None, :]
    inv_one, hat_one = rms_parts(token_values)
    mult_one = gain_one * (1.0 + scale_attn)
    h_one = (hat_one * mult_one).astype(jnp.bfloat16)
    query_pre = jnp.dot(h_one, full_query, preferred_element_type=jnp.float32)
    key_pre = jnp.dot(h_one, full_key, preferred_element_type=jnp.float32)
    values = to_heads(
        jnp.dot(h_one, full_value, preferred_element_type=jnp.float32).astype(jnp.bfloat16)
    )
    qgain = query_gain.astype(jnp.float32)
    kgain = key_gain.astype(jnp.float32)
    kygain = text_key_gain.astype(jnp.float32)
    inv_query, hat_query = head_norm(query_pre, segment)
    inv_key, hat_key = head_norm(key_pre, segment)
    query_norm = hat_query * qgain
    cosine_table, sine_table, turner = rope_flat(row_count, local_cols)
    query_rot = to_heads(
        rotate_flat(query_norm, cosine_table, sine_table, turner).astype(jnp.bfloat16)
    )
    key_rot = to_heads(
        rotate_flat(hat_key * kgain, cosine_table, sine_table, turner).astype(jnp.bfloat16)
    )
    query_text = to_heads(query_norm.astype(jnp.bfloat16))
    text_pre = jnp.dot(text, full_text_key, preferred_element_type=jnp.float32)
    inv_text, hat_text = head_norm(text_pre, segment)
    text_keys = to_heads((hat_text * kygain).astype(jnp.bfloat16))
    text_values = to_heads(
        jnp.dot(text, full_text_value, preferred_element_type=jnp.float32).astype(jnp.bfloat16)
    )
    score_scale = HEAD ** (-0.5)
    block_rows = min(512, row_count)
    self_parts, self_totals, text_parts, text_totals = ([], [], [], [])
    for start_row in range(0, row_count, block_rows):
        self_block, self_total = attend(
            query_rot[:, start_row : start_row + block_rows],
            key_rot,
            values,
            key_valid,
            score_scale,
        )
        text_block, text_total = attend(
            query_text[:, start_row : start_row + block_rows],
            text_keys,
            text_values,
            None,
            score_scale,
        )
        self_parts.append(self_block)
        self_totals.append(self_total)
        text_parts.append(text_block)
        text_totals.append(text_total)
    self_outs = from_heads(jnp.concatenate(self_parts, axis=1))
    text_outs = from_heads(jnp.concatenate(text_parts, axis=1))
    gate_tanh = jnp.tanh(cross_gate.astype(jnp.float32))
    gate_wide = jnp.repeat(gate_tanh, HEAD)
    mixed = (self_outs + gate_wide[None, :] * text_outs).astype(jnp.bfloat16)
    attn_sum = sum_tp(dot_nt(mixed, out_turned).astype(jnp.bfloat16)).astype(jnp.float32)
    tanh_attn = jnp.tanh(gate_attn)
    hidden_state = token_values + live_rows * tanh_attn * attn_sum
    inv_two, hat_two = rms_parts(hidden_state)
    mult_two = gain_two * (1.0 + scale_ffn)
    h_two = (hat_two * mult_two).astype(jnp.bfloat16)
    gate_pre = jnp.dot(h_two, full_gate, preferred_element_type=jnp.float32)
    up_pre = jnp.dot(h_two, full_up, preferred_element_type=jnp.float32)
    logistic = jax.nn.sigmoid(gate_pre)
    swish = gate_pre * logistic
    hidden_units = (swish * up_pre).astype(jnp.bfloat16)
    ffn_sum = sum_tp(dot_nt(hidden_units, down_turned).astype(jnp.bfloat16)).astype(jnp.float32)
    tanh_ffn = jnp.tanh(gate_ffn)
    result = hidden_state + live_rows * tanh_ffn * ffn_sum
    grad_result = cotangent.astype(jnp.float32)
    grad_ffn = (live_rows * tanh_ffn * grad_result).astype(jnp.bfloat16)
    grad_gate_ffn = jnp.sum(live_rows * ffn_sum * grad_result, axis=0) * (1.0 - tanh_ffn * tanh_ffn)
    grad_hidden = jnp.dot(grad_ffn, down_turned, preferred_element_type=jnp.float32)
    grad_gate_pre = (grad_hidden * up_pre * logistic * (1.0 + gate_pre * (1.0 - logistic))).astype(
        jnp.bfloat16
    )
    grad_up_pre = (grad_hidden * swish).astype(jnp.bfloat16)
    g_down = dot_tn(grad_ffn, hidden_units).astype(jnp.bfloat16)
    g_gate = dot_tn(h_two, grad_gate_pre).astype(jnp.bfloat16)
    g_up = dot_tn(h_two, grad_up_pre).astype(jnp.bfloat16)
    grad_n_two = sum_tp(
        (dot_nt(grad_gate_pre, full_gate) + dot_nt(grad_up_pre, full_up)).astype(jnp.bfloat16)
    ).astype(jnp.float32)
    g_norm_two = jnp.sum(grad_n_two * hat_two * (1.0 + scale_ffn), axis=0)
    grad_scale_ffn = jnp.sum(grad_n_two * hat_two * gain_two, axis=0)
    grad_state = grad_result + rms_back(inv_two, hat_two, grad_n_two * mult_two)
    grad_attn = (live_rows * tanh_attn * grad_state).astype(jnp.bfloat16)
    grad_gate_attn = jnp.sum(live_rows * attn_sum * grad_state, axis=0) * (
        1.0 - tanh_attn * tanh_attn
    )
    grad_mixed = jnp.dot(grad_attn, out_turned, preferred_element_type=jnp.float32)
    g_out = dot_tn(grad_attn, mixed).astype(jnp.bfloat16)
    column_cross = jnp.sum(grad_mixed * text_outs, axis=0)
    g_cross_gate = exact_dot(column_cross[None, :], segment)[0] * (1.0 - gate_tanh * gate_tanh)
    grad_self = to_heads(grad_mixed.astype(jnp.bfloat16))
    grad_text = to_heads((grad_mixed * gate_wide[None, :]).astype(jnp.bfloat16))
    grad_query_rot_parts, grad_query_text_parts = ([], [])
    grad_key_rot = jnp.zeros((heads_here, row_count, HEAD), jnp.float32)
    grad_values = jnp.zeros((heads_here, row_count, HEAD), jnp.float32)
    grad_text_keys = jnp.zeros((heads_here, text_count, HEAD), jnp.float32)
    grad_text_values = jnp.zeros((heads_here, text_count, HEAD), jnp.float32)
    for block_number, start_row in enumerate(range(0, row_count, block_rows)):
        rows_here = slice(start_row, start_row + block_rows)
        query_grad, key_grad, value_grad = attend_back(
            query_rot[:, rows_here],
            key_rot,
            values,
            key_valid,
            score_scale,
            self_totals[block_number],
            grad_self[:, rows_here],
        )
        grad_query_rot_parts.append(query_grad)
        grad_key_rot = grad_key_rot + key_grad
        grad_values = grad_values + value_grad
        query_grad, key_grad, value_grad = attend_back(
            query_text[:, rows_here],
            text_keys,
            text_values,
            None,
            score_scale,
            text_totals[block_number],
            grad_text[:, rows_here],
        )
        grad_query_text_parts.append(query_grad)
        grad_text_keys = grad_text_keys + key_grad
        grad_text_values = grad_text_values + value_grad
    grad_query_norm = rotate_flat_back(
        from_heads(jnp.concatenate(grad_query_rot_parts, axis=1)), cosine_table, sine_table, turner
    ) + from_heads(jnp.concatenate(grad_query_text_parts, axis=1))
    grad_key_norm = rotate_flat_back(from_heads(grad_key_rot), cosine_table, sine_table, turner)
    grad_text_flat = from_heads(grad_text_keys)
    g_query_gain = jnp.sum(grad_query_norm * hat_query, axis=0)
    g_key_gain = jnp.sum(grad_key_norm * hat_key, axis=0)
    g_text_gain = jnp.sum(grad_text_flat * hat_text, axis=0)
    grad_query_pre = head_norm_back(inv_query, hat_query, grad_query_norm * qgain, segment).astype(
        jnp.bfloat16
    )
    grad_key_pre = head_norm_back(inv_key, hat_key, grad_key_norm * kgain, segment).astype(
        jnp.bfloat16
    )
    grad_value_pre = from_heads(grad_values).astype(jnp.bfloat16)
    grad_text_pre = head_norm_back(inv_text, hat_text, grad_text_flat * kygain, segment).astype(
        jnp.bfloat16
    )
    grad_text_vals = from_heads(grad_text_values).astype(jnp.bfloat16)
    g_query = dot_tn(h_one, grad_query_pre).astype(jnp.bfloat16)
    g_key = dot_tn(h_one, grad_key_pre).astype(jnp.bfloat16)
    g_value = dot_tn(h_one, grad_value_pre).astype(jnp.bfloat16)
    g_text_key = dot_tn(text, grad_text_pre).astype(jnp.bfloat16)
    g_text_value = dot_tn(text, grad_text_vals).astype(jnp.bfloat16)
    grad_n_one = sum_tp(
        (
            dot_nt(grad_query_pre, full_query)
            + dot_nt(grad_key_pre, full_key)
            + dot_nt(grad_value_pre, full_value)
        ).astype(jnp.bfloat16)
    ).astype(jnp.float32)
    g_norm_one = jnp.sum(grad_n_one * hat_one * (1.0 + scale_attn), axis=0)
    grad_scale_attn = jnp.sum(grad_n_one * hat_one * gain_one, axis=0)
    grad_input = grad_state + rms_back(inv_one, hat_one, grad_n_one * mult_one)
    gate_pad = jnp.zeros((-heads_here % 128,), jnp.float32)
    vec = jnp.concatenate(
        [
            grad_scale_attn,
            grad_gate_attn,
            grad_scale_ffn,
            grad_gate_ffn,
            g_norm_one,
            g_norm_two,
            g_query_gain,
            g_key_gain,
            g_text_gain,
            g_cross_gate,
            gate_pad,
        ]
    )[None, :]
    grads = (g_down, g_gate, g_up, g_out, g_text_key, g_text_value, g_query, g_key, g_value)
    summed = (scatter_all if clips == GRID else scatter_plain)(grads, vec)
    s_down, s_gate, s_up, s_out, s_text_key, s_text_value, s_query, s_key, s_value, vecs = summed
    vecs = vecs[:, 0, :]
    mod_wide, wide = 4 * tokens.shape[1], tokens.shape[1]
    g_ada = lax.dot_general(
        act_rows,
        vecs[:, :mod_wide],
        (((0,), (0,)), ((), ())),
        precision=lax.Precision.HIGHEST,
        preferred_element_type=jnp.float32,
    )
    sums = jnp.sum(vecs, axis=0)
    me = lax.axis_index("dp")
    g_bias = lax.dynamic_slice(sums, (me * bias_rows,), (bias_rows,))
    g_norm_one = lax.dynamic_slice(sums, (mod_wide + me * gain_rows,), (gain_rows,))
    g_norm_two = lax.dynamic_slice(sums, (mod_wide + wide + me * gain_rows,), (gain_rows,))
    rest = sums[mod_wide + 2 * wide :]
    return (
        result.astype(jnp.bfloat16),
        grad_input.astype(jnp.bfloat16),
        s_query,
        s_key,
        s_value,
        s_out.T,
        s_text_key,
        s_text_value,
        s_gate,
        s_up,
        s_down.T,
        g_ada,
        g_bias,
        g_norm_one,
        g_norm_two,
        rest[:local_cols],
        rest[local_cols : 2 * local_cols],
        rest[2 * local_cols : 3 * local_cols],
        rest[3 * local_cols : 3 * local_cols + heads_here],
    )


def solution(mesh):
    placed = (
        P("dp", None),
        P("dp", None),
        P("dp", None),
        P("dp"),
        P("dp", "tp"),
        P("dp", "tp"),
        P("dp", "tp"),
        P("tp", "dp"),
        P("dp", "tp"),
        P("dp", "tp"),
        P("dp", "tp"),
        P("dp", "tp"),
        P("tp", "dp"),
        P("dp", None),
        P("dp"),
        P("dp"),
        P("dp"),
        P("tp"),
        P("tp"),
        P("tp"),
        P("tp"),
        P("dp", None),
    )
    return jax.shard_map(
        on_device,
        mesh=mesh,
        in_specs=placed,
        out_specs=(
            P("dp", None),
            P("dp", None),
            P("dp", "tp"),
            P("dp", "tp"),
            P("dp", "tp"),
            P("tp", "dp"),
            P("dp", "tp"),
            P("dp", "tp"),
            P("dp", "tp"),
            P("dp", "tp"),
            P("tp", "dp"),
            P("dp", None),
            P("dp"),
            P("dp"),
            P("dp"),
            P("tp"),
            P("tp"),
            P("tp"),
            P("tp"),
        ),
        check_vma=False,
    )
```

```python
import functools

import jax
import jax.numpy as jnp
import numpy as np
from jax import lax
from jax.experimental import pallas as pl
from jax.experimental.pallas import tpu as pltpu
from jax.sharding import PartitionSpec as P

HEAD = 64
FRAME_TOK = 64
EPS = 1e-06
ROPE_BASE = 10000.0
SCALE = HEAD**-0.5
MESH = pl.DeviceIdType.MESH
VMEM_LIMIT = 60 * 2**20
GRID = 8
LINE = 4
PAIR = 2 * HEAD
TP_PARTS = 8
AHEAD = 2
DMA = pltpu.SemaphoreType.DMA
F32 = jnp.float32
BF16 = jnp.bfloat16


def dot_nn(left, right):
    return jnp.dot(left, right, preferred_element_type=F32)


def dot_nt(left, right):
    return lax.dot_general(left, right, (((1,), (1,)), ((), ())), preferred_element_type=F32)


def dot_tn(left, right):
    return lax.dot_general(left, right, (((0,), (0,)), ((), ())), preferred_element_type=F32)


def remote(src, dst, send, recv, **where):
    return pltpu.make_async_remote_copy(
        src_ref=src, dst_ref=dst, send_sem=send, recv_sem=recv, device_id=where, device_id_type=MESH
    )


def greet(dp_peers, tp_peers):
    barrier = pltpu.get_barrier_semaphore()
    for peer in dp_peers:
        pl.semaphore_signal(barrier, inc=1, device_id={"dp": peer}, device_id_type=MESH)
    for peer in tp_peers:
        pl.semaphore_signal(barrier, inc=1, device_id={"tp": peer}, device_id_type=MESH)
    pl.semaphore_wait(barrier, len(dp_peers) + len(tp_peers))


def dp_peers():
    me = lax.axis_index("dp")
    return [lax.rem(me + step, GRID) for step in range(1, GRID)]


def tp_peers():
    me = lax.axis_index("tp")
    return [me + 1 - 2 * lax.rem(me, 2), lax.rem(me + 2, 4)]


def aligned(value, by):
    return value if isinstance(value, int) else pl.multiple_of(value, by)


def loop(count, step):
    def body(i, carry):
        step(i)
        return carry

    lax.fori_loop(0, count, body, 0)


def add_rows(out_ref, first, *others):
    rows = out_ref.shape[0]

    def step(i):
        here = pl.ds(pl.multiple_of(i * 32, 32), 32)
        total = first[here, :].astype(F32)
        for other in others:
            total = total + other[here, :].astype(F32)
        out_ref[here, :] = total.astype(out_ref.dtype)

    loop(rows // 32, step)


class Blocks:
    def __init__(self, depth, wide, rows, cols):
        self.depth, self.wide, self.rows, self.cols = depth, wide, rows, cols
        self.across = wide // cols
        self.count = (depth // rows) * self.across

    def at(self, c):
        if isinstance(c, int):
            return c // self.across * self.rows, c % self.across * self.cols
        row = aligned(lax.div(c, self.across) * self.rows, 16)
        col = aligned(lax.rem(c, self.across) * self.cols, 128)
        return row, col


class Gather:
    def __init__(self, blocks, shard, full, sems):
        self.b, self.shard, self.full = blocks, shard, full
        self.up_s, self.up_r, self.dn_s, self.dn_r, self.y_s, self.y_r, self.own_s = sems
        self.me = lax.axis_index("dp")
        self.z, self.y = self.me // 2, lax.rem(self.me, 2)
        self.ticks = blocks.count + LINE - 2

    @staticmethod
    def scratch(count):
        return [DMA((count, 3))] * 4 + [DMA((count, 4))] * 2 + [DMA((count,))]

    def own(self, c):
        row, col = self.b.at(c)
        return self.shard.at[pl.ds(row, self.b.rows), pl.ds(col, self.b.cols)]

    def place(self, c, origin):
        row, col = self.b.at(c)
        start = pl.multiple_of(origin * self.b.depth + row, 16)
        return self.full.at[pl.ds(start, self.b.rows), pl.ds(col, self.b.cols)]

    def up(self, c, hop):
        origin = self.me - 2 * hop
        src = self.own(c) if hop == 0 else self.place(c, origin)
        return remote(src, self.place(c, origin), self.up_s.at[c, hop], self.up_r.at[c, hop], dp=self.me + 2)

    def down(self, c, hop):
        origin = self.me + 2 * hop
        src = self.own(c) if hop == 0 else self.place(c, origin)
        return remote(src, self.place(c, origin), self.dn_s.at[c, hop], self.dn_r.at[c, hop], dp=self.me - 2)

    def across(self, c, line, mine=False):
        origin = 2 * line + self.y
        src = self.own(c) if mine else self.place(c, origin)
        other = self.me + 1 - 2 * self.y
        return remote(src, self.place(c, origin), self.y_s.at[c, line], self.y_r.at[c, line], dp=other)

    def came(self, c, origin, sems):
        return remote(self.place(c, origin), self.place(c, origin), sems, sems, dp=self.me)

    def local(self, c):
        return pltpu.make_async_copy(self.own(c), self.place(c, self.me), self.own_s.at[c])

    def begin(self, c):
        pl.when(self.z < LINE - 1)(lambda: self.up(c, 0).start())
        pl.when(self.z > 0)(lambda: self.down(c, 0).start())
        self.across(c, self.z, True).start()
        self.local(c).start()

    def start(self):
        for c in range(min(AHEAD, self.b.count)):
            self.begin(c)

    def pump(self, t):
        me, z, count = self.me, self.z, self.b.count
        pl.when(t + AHEAD < count)(lambda: self.begin(t + AHEAD))
        for hop in range(LINE - 1):
            c = t - hop
            valid = (c >= 0) & (c < count)

            @pl.when(valid & (z - 1 - hop >= 0))
            def _():
                self.came(c, me - 2 * (hop + 1), self.up_r.at[c, hop]).wait_recv()
                if hop < LINE - 2:
                    pl.when(z < LINE - 1)(lambda: self.up(c, hop + 1).start())
                self.across(c, z - 1 - hop).start()

            @pl.when(valid & (z + 1 + hop <= LINE - 1))
            def _():
                self.came(c, me + 2 * (hop + 1), self.dn_r.at[c, hop]).wait_recv()
                if hop < LINE - 2:
                    pl.when(z > 0)(lambda: self.down(c, hop + 1).start())
                self.across(c, z + 1 + hop).start()

    def drain(self):
        z = self.z

        def step(c):
            for line in range(LINE):
                self.came(c, 2 * line + 1 - self.y, self.y_r.at[c, line]).wait_recv()
                self.across(c, line).wait_send()
            self.local(c).wait()
            for hop in range(LINE - 1):
                pl.when((z < LINE - 1) & (z - hop >= 0))(lambda: self.up(c, hop).wait_send())
                pl.when((z > 0) & (z + hop <= LINE - 1))(lambda: self.down(c, hop).wait_send())

        loop(self.b.count, step)


class Scatter:
    def __init__(self, blocks, grad, out, bufs, sems):
        self.b, self.grad, self.out = blocks, grad, out
        self.held, self.crossed, self.above, self.below = bufs
        self.y_s, self.y_r, self.own_s, self.up_s, self.up_r, self.dn_s, self.dn_r = sems
        self.me = lax.axis_index("dp")
        self.z, self.y = self.me // 2, lax.rem(self.me, 2)
        self.ticks = blocks.count + LINE - 1

    @staticmethod
    def scratch(blocks):
        shape = (blocks.rows, blocks.cols)
        count = blocks.count
        bufs = [pltpu.VMEM((count, lines) + shape, BF16) for lines in (4, 4, 3, 3)]
        return bufs + [DMA((count,))] * 3 + [DMA((count, 3))] * 4

    def part(self, c, row_y):
        row, col = self.b.at(c)
        return self.grad.at[:, row_y, pl.ds(row, self.b.rows), pl.ds(col, self.b.cols)]

    def across(self, c):
        other = self.me + 1 - 2 * self.y
        return remote(self.part(c, 1 - self.y), self.crossed.at[c], self.y_s.at[c], self.y_r.at[c], dp=other)

    def load(self, c):
        return pltpu.make_async_copy(self.part(c, self.y), self.held.at[c], self.own_s.at[c])

    def up(self, c, line):
        return remote(
            self.held.at[c, line],
            self.above.at[c, line - 1],
            self.up_s.at[c, line - 1],
            self.up_r.at[c, line - 1],
            dp=self.me + 2,
        )

    def down(self, c, line):
        return remote(
            self.held.at[c, line],
            self.below.at[c, line],
            self.dn_s.at[c, line],
            self.dn_r.at[c, line],
            dp=self.me - 2,
        )

    def begin(self, c):
        self.across(c).start()
        self.load(c).start()

    def start(self):
        for c in range(min(AHEAD, self.b.count)):
            self.begin(c)

    def fold(self, c):
        self.across(c).wait_recv()
        self.load(c).wait()
        for line in range(LINE):
            add_rows(self.held.at[c, line], self.held.at[c, line], self.crossed.at[c, line])

    def send_up(self, c, here):
        for line in range(LINE - 1, here, -1):
            if here > 0:
                self.up(c, line).wait_recv()
                add_rows(self.held.at[c, line], self.held.at[c, line], self.above.at[c, line - 1])
            self.up(c, line).start()

    def send_down(self, c, here):
        for line in range(here):
            if here < LINE - 1:
                self.down(c, line).wait_recv()
                add_rows(self.held.at[c, line], self.held.at[c, line], self.below.at[c, line])
            self.down(c, line).start()

    def finish(self, c, here):
        row, col = self.b.at(c)
        terms = [self.held.at[c, here]]
        if here > 0:
            self.up(c, here).wait_recv()
            terms.append(self.above.at[c, here - 1])
        if here < LINE - 1:
            self.down(c, here).wait_recv()
            terms.append(self.below.at[c, here])
        add_rows(self.out.at[pl.ds(row, self.b.rows), pl.ds(col, self.b.cols)], *terms)

    def pump(self, t):
        count, z = self.b.count, self.z
        pl.when(t + AHEAD < count)(lambda: self.begin(t + AHEAD))
        pl.when(t < count)(lambda: self.fold(t))
        for hop in range(LINE):
            c = t - hop
            valid = (c >= 0) & (c < count)
            if hop < LINE - 1:
                pl.when(valid & (z == hop))(lambda: self.send_up(c, hop))
                pl.when(valid & (z == LINE - 1 - hop))(lambda: self.send_down(c, LINE - 1 - hop))
            else:
                for here in range(LINE):
                    pl.when(valid & (z == here))(lambda: self.finish(c, here))

    def drain(self):
        def step(c):
            self.across(c).wait_send()
            for here in range(LINE):

                @pl.when(self.z == here)
                def _():
                    for line in range(here + 1, LINE):
                        self.up(c, line).wait_send()
                    for line in range(here):
                        self.down(c, line).wait_send()

        loop(self.b.count, step)


class Idle:
    ticks = 0

    def start(self):
        pass

    def pump(self, t):
        pass

    def drain(self):
        pass


class TpSum:
    def __init__(self, partial, out, bufs, sems):
        self.p, self.out = partial, out
        self.crossed, self.other = bufs
        self.c_s, self.c_r, self.x_s, self.x_r, self.o_s, self.o_r = sems
        self.core = lax.rem(lax.axis_index("tp"), 2)
        self.beside, self.far = tp_peers()
        self.half = partial.shape[0] // 2
        self.rows = self.half // TP_PARTS

    @staticmethod
    def scratch(rows, wide):
        return [pltpu.VMEM((rows // 2, wide), BF16)] * 2 + [DMA((TP_PARTS,))] * 6

    def spot(self, k, which):
        return pl.ds(pl.multiple_of(which * self.half + k * self.rows, 16), self.rows)

    def part(self, k):
        return pl.ds(aligned(k * self.rows, 16), self.rows)

    def first(self, k):
        return remote(
            self.p.at[self.spot(k, 1 - self.core)],
            self.crossed.at[self.part(k)],
            self.c_s.at[k],
            self.c_r.at[k],
            tp=self.beside,
        )

    def second(self, k):
        here = self.out.at[self.spot(k, self.core)]
        return remote(here, self.other.at[self.part(k)], self.x_s.at[k], self.x_r.at[k], tp=self.far)

    def third(self, k, which):
        here = self.out.at[self.spot(k, which)]
        return remote(here, here, self.o_s.at[k], self.o_r.at[k], tp=self.beside)

    def stage_one(self, k):
        self.first(k).start()

    def stage_two(self, k):
        self.first(k).wait_recv()
        mine = self.spot(k, self.core)
        add_rows(self.out.at[mine], self.p.at[mine], self.crossed.at[self.part(k)])
        self.second(k).start()

    def stage_three(self, k):
        self.second(k).wait()
        mine = self.out.at[self.spot(k, self.core)]
        add_rows(mine, mine, self.other.at[self.part(k)])
        self.third(k, self.core).start()

    def stage_four(self, k):
        self.third(k, 1 - self.core).wait_recv()

    def drain(self):
        def step(k):
            self.first(k).wait_send()
            self.third(k, self.core).wait_send()

        loop(TP_PARTS, step)


def params(number):
    return pltpu.CompilerParams(
        collective_id=number, has_side_effects=True, vmem_limit_bytes=VMEM_LIMIT
    )


ANY = pl.BlockSpec(memory_space=pl.ANY)
IN_VMEM = pl.BlockSpec(memory_space=pltpu.VMEM)
IN_SMEM = pl.BlockSpec(memory_space=pltpu.SMEM)


def shaped(shape, dtype):
    return jax.ShapeDtypeStruct(shape, dtype)


def segment_sum(value, seg):
    high = value.astype(BF16)
    low = (value - high.astype(F32)).astype(BF16)
    return dot_nn(high, seg) + dot_nn(low, seg)


def head_inverse(value, seg):
    return lax.rsqrt(segment_sum(value * value, seg) * (1.0 / HEAD) + EPS)


def thrice(table):
    return jnp.concatenate([table] * 3, axis=1)


def rope(value, cosines, sine_a, sine_b):
    wide = value.shape[1]
    ahead = pltpu.roll(value, wide - HEAD // 4, 1)
    behind = pltpu.roll(value, HEAD // 4, 1)
    return value * cosines + ahead * sine_a + behind * sine_b


def rope_back(grad, cosines, sine_a, sine_b):
    wide = grad.shape[1]
    ahead = pltpu.roll(grad * sine_b, wide - HEAD // 4, 1)
    behind = pltpu.roll(grad * sine_a, HEAD // 4, 1)
    return grad * cosines + ahead + behind


def rope_tables(row_count):
    lane = np.arange(PAIR)
    within = lane % HEAD
    quarter = HEAD // 4
    which = within // quarter
    freqs = (ROPE_BASE ** (-(within % quarter).astype(np.float32) / np.float32(quarter))).astype(np.float32)
    row = np.arange(row_count)
    frame, place = (row // FRAME_TOK).astype(np.float32), (row % FRAME_TOK).astype(np.float32)
    position = np.where(which[None, :] < 2, frame[:, None], place[:, None])
    angles = (position * freqs[None, :]).astype(np.float32)
    cosines, sines = np.cos(angles), np.sin(angles)
    even = (which % 2 == 0)[None, :]
    return (
        jnp.asarray(cosines.astype(np.float32)),
        jnp.asarray(np.where(even, -sines, 0.0).astype(np.float32)),
        jnp.asarray(np.where(even, 0.0, sines).astype(np.float32)),
    )


def segment_ones(wide):
    head = np.arange(wide) // HEAD
    return jnp.asarray((head[:, None] == head[None, :]).astype(np.float32)).astype(BF16)


def live_rows(frames_ref, start, rows, wide):
    row = start + lax.broadcasted_iota(jnp.int32, (rows, wide), 0)
    return (row < frames_ref[0] * FRAME_TOK).astype(F32)


def half_mask(rows, head, dtype):
    lane = lax.broadcasted_iota(jnp.int32, (rows, PAIR), 1)
    return ((lane < HEAD) if head == 0 else (lane >= HEAD)).astype(dtype)


def pair_lanes(pair, wide=PAIR):
    return pl.ds(pl.multiple_of(pair * wide, PAIR), wide)


def block_rows(block, rows):
    return pl.ds(pl.multiple_of(block * rows, rows), rows)


def paced(count, step, pumps, base, engine):
    if pumps == 0 or engine.ticks == 0:
        loop(count, step)
        return base
    if pumps <= count:
        every = count // pumps

        def body(i):
            step(i)
            pl.when(lax.rem(i, every) == every - 1)(lambda: engine.pump(base + lax.div(i, every)))

    else:
        each = pumps // count

        def body(i):
            step(i)
            for j in range(each):
                engine.pump(base + i * each + j)

    loop(count, body)
    return base + pumps


def finish_pumps(base, engine):
    if base < engine.ticks:
        loop(engine.ticks - base, lambda i: engine.pump(base + i))


def first_kernel(blocks, shard, cond_ref, small_ref, ada_ref, full, mod_ref, smalls_ref, act_ref, *refs):
    conds, part, parts, c_s, c_r, m_s, m_r, p_s, p_r = refs[:9]
    engine = Gather(blocks, shard, full, refs[9:])
    me = lax.axis_index("dp")
    peers = dp_peers()
    sources = [lax.rem(me + GRID - step, GRID) for step in range(1, GRID)]
    greet(peers, [])
    engine.start()
    for i, there in enumerate(peers):
        remote(cond_ref.at[there], conds.at[me], c_s.at[i], c_r.at[i], dp=there).start()
        remote(small_ref, smalls_ref.at[me], m_s.at[i], m_r.at[i], dp=there).start()
    conds[pl.ds(me, 1)] = cond_ref[pl.ds(me, 1)]
    smalls_ref[pl.ds(me, 1)] = small_ref[...][None]
    engine.pump(0)
    for i, here in enumerate(sources):
        remote(conds.at[here], conds.at[here], c_s.at[i], c_r.at[i], dp=me).wait_recv()
    cond = jnp.concatenate([conds[i] for i in range(GRID)], axis=0)
    act = (cond * (1.0 / (1.0 + jnp.exp(-cond)))).astype(BF16)
    act_ref[...] = act.astype(F32)
    width = ada_ref.shape[1] // 4
    for i in range(4):
        cols = pl.ds(i * width, width)
        product = dot_nn(act, ada_ref[:, cols])
        for j in range(GRID):
            part[j, :, cols] = product[j : j + 1, :]
    for i, there in enumerate(peers):
        remote(part.at[there], parts.at[me], p_s.at[i], p_r.at[i], dp=there).start()
    parts[pl.ds(me, 1)] = part[pl.ds(me, 1)]
    engine.pump(1)
    engine.pump(2)
    for i, here in enumerate(sources):
        remote(parts.at[here], parts.at[here], p_s.at[i], p_r.at[i], dp=me).wait_recv()
    mod_ref[...] = sum(parts[i] for i in range(GRID))
    finish_pumps(3, engine)
    engine.drain()
    for i, there in enumerate(peers):
        here = sources[i]
        remote(small_ref, smalls_ref.at[here], m_s.at[i], m_r.at[i], dp=me).wait_recv()
        remote(cond_ref.at[there], conds.at[me], c_s.at[i], c_r.at[i], dp=there).wait_send()
        remote(small_ref, smalls_ref.at[me], m_s.at[i], m_r.at[i], dp=there).wait_send()
        remote(part.at[there], parts.at[me], p_s.at[i], p_r.at[i], dp=there).wait_send()


def gather_first(shard, cond, small, w_ada):
    depth, wide = shard.shape
    blocks = Blocks(depth, wide, 96, 384)
    mods = w_ada.shape[1]
    return pl.pallas_call(
        functools.partial(first_kernel, blocks),
        out_shape=[
            shaped((GRID * depth, wide), BF16),
            shaped((1, mods), F32),
            shaped((GRID,) + small.shape, F32),
            shaped((GRID, cond.shape[2]), F32),
        ],
        in_specs=[ANY] + [IN_VMEM] * 3,
        out_specs=[ANY] + [IN_VMEM] * 3,
        scratch_shapes=[
            pltpu.VMEM((GRID, 1, cond.shape[2]), F32),
            pltpu.VMEM((GRID, 1, mods), F32),
            pltpu.VMEM((GRID, 1, mods), F32),
        ]
        + [DMA((GRID - 1,))] * 6
        + Gather.scratch(blocks.count),
        compiler_params=params(0),
    )(shard, cond, small, w_ada)


def self_kernel(blocks, *refs):
    frames, tok, weights, mult, qgain, kgain, cos_ref, sa_ref, sb_ref, seg_ref, shard = refs[:11]
    h_one, q_pre, k_pre, q_rot, k_rot, q_text, v_out, self_o, inv_l, full = refs[11:21]
    vaug, refs = refs[21], refs[22:]
    engine = Idle()
    if blocks is not None:
        engine = Gather(blocks, shard, full, refs)
        greet(dp_peers(), [])
        engine.start()
    cols = q_pre.shape[1]
    rows = tok.shape[0]
    step_rows = 256

    def project(i):
        here = block_rows(i, step_rows)
        x = tok[here, :].astype(F32)
        inverse = lax.rsqrt(jnp.mean(x * x, axis=-1, keepdims=True) + EPS)
        h = (x * inverse * mult[...]).astype(BF16)
        h_one[here, :] = h
        cosines, sine_a, sine_b = thrice(cos_ref[here, :]), thrice(sa_ref[here, :]), thrice(sb_ref[here, :])
        q = dot_nn(h, weights[:, :cols])
        q_pre[here, :] = q
        qn = q * head_inverse(q, seg_ref[...]) * qgain[...]
        q_text[here, :] = (qn * SCALE).astype(BF16)
        q_rot[here, :] = (rope(qn, cosines, sine_a, sine_b) * SCALE).astype(BF16)
        k = dot_nn(h, weights[:, cols : 2 * cols])
        k_pre[here, :] = k
        kn = k * head_inverse(k, seg_ref[...]) * kgain[...]
        k_rot[here, :] = rope(kn, cosines, sine_a, sine_b).astype(BF16)
        v = dot_nn(h, weights[:, 2 * cols : 3 * cols]).astype(BF16)
        v_out[here, :] = v
        live = live_rows(frames, i * step_rows, step_rows, PAIR).astype(BF16)
        for pair in range(cols // PAIR):
            vaug[here, 2 * pair * PAIR : (2 * pair + 1) * PAIR] = v[:, pair * PAIR : (pair + 1) * PAIR] * live
            vaug[here, (2 * pair + 1) * PAIR : (2 * pair + 2) * PAIR] = live

    def attend(i):
        pair, block = lax.div(i, rows // step_rows), lax.rem(i, rows // step_rows)
        here, lanes = block_rows(block, step_rows), pair_lanes(pair)
        q = q_rot[here, lanes]
        keys = k_rot[:, lanes]
        values = vaug[:, pair_lanes(pair, 2 * PAIR)]
        outs = jnp.zeros((step_rows, PAIR), F32)
        sums = jnp.zeros((step_rows, PAIR), F32)
        for head in range(2):
            mask = half_mask(step_rows, head, BF16)
            p = jnp.exp(dot_nt(q * mask, keys)).astype(BF16)
            both = dot_nn(p, values)
            wide_mask = half_mask(step_rows, head, F32)
            outs = outs + both[:, :PAIR] * wide_mask
            sums = sums + both[:, PAIR:] * wide_mask
        inverse = 1.0 / sums
        inv_l[here, lanes] = inverse
        self_o[here, lanes] = outs * inverse

    base = paced(rows // step_rows, project, 4, 0, engine)
    base = paced(cols // PAIR * (rows // step_rows), attend, 6, base, engine)
    finish_pumps(base, engine)
    engine.drain()


def self_forward(clips, frames, tokens, full_attn, mult, qgain, kgain, tables, seg, text_shard):
    rows, wide = tokens.shape
    cols = qgain.shape[1]
    depth, text_wide = text_shard.shape
    blocks = Blocks(depth, text_wide, 64, text_wide) if clips == GRID else None
    f, b = shaped((rows, cols), F32), shaped((rows, cols), BF16)
    return pl.pallas_call(
        functools.partial(self_kernel, blocks),
        out_shape=[shaped((rows, wide), BF16), f, f, b, b, b, b, f, f, shaped((GRID * depth, text_wide), BF16)],
        in_specs=[IN_SMEM] + [IN_VMEM] * 9 + [ANY],
        out_specs=[IN_VMEM] * 9 + [ANY],
        scratch_shapes=[pltpu.VMEM((rows, 2 * cols), BF16)]
        + (Gather.scratch(blocks.count) if blocks is not None else []),
        compiler_params=params(1) if blocks is not None else pltpu.CompilerParams(vmem_limit_bytes=VMEM_LIMIT),
    )(frames, tokens, full_attn, mult, qgain, kgain, *tables, seg, text_shard)


def text_kernel(blocks, *refs):
    frames, text, w_text, kygain, seg_ref, q_text, self_o, gate, weights, tok, tanh_attn, mult, shard = refs[:13]
    ky_pre, kyr, vy_out, text_o, inv_lt, mixed, attn_sum, h_two, full = refs[13:22]
    vaug, partial = refs[22:24]
    sums = TpSum(partial, attn_sum, refs[24:26], refs[26:32])
    engine = Idle()
    if blocks is not None:
        engine = Gather(blocks, shard, full, refs[32:])
        greet(dp_peers(), tp_peers())
        engine.start()
    else:
        greet([], tp_peers())
    cols, rows = self_o.shape[1], tok.shape[0]
    step_rows = 256
    rows_t = text.shape[0]

    ky = dot_nn(text[...], w_text[:, :cols])
    ky_pre[...] = ky
    kyr[...] = (ky * head_inverse(ky, seg_ref[...]) * kygain[...]).astype(BF16)
    engine.pump(0)
    vy = dot_nn(text[...], w_text[:, cols:]).astype(BF16)
    vy_out[...] = vy
    for pair in range(cols // PAIR):
        vaug[:, 2 * pair * PAIR : (2 * pair + 1) * PAIR] = vy[:, pair * PAIR : (pair + 1) * PAIR]
        vaug[:, (2 * pair + 1) * PAIR : (2 * pair + 2) * PAIR] = jnp.ones((rows_t, PAIR), BF16)
    engine.pump(1)

    def attend(i):
        pair, block = lax.div(i, rows // step_rows), lax.rem(i, rows // step_rows)
        here, lanes = block_rows(block, step_rows), pair_lanes(pair)
        q = q_text[here, lanes]
        keys = kyr[:, lanes]
        values = vaug[:, pair_lanes(pair, 2 * PAIR)]
        outs = jnp.zeros((step_rows, PAIR), F32)
        total = jnp.zeros((step_rows, PAIR), F32)
        for head in range(2):
            p = jnp.exp(dot_nt(q * half_mask(step_rows, head, BF16), keys)).astype(BF16)
            both = dot_nn(p, values)
            wide_mask = half_mask(step_rows, head, F32)
            outs = outs + both[:, :PAIR] * wide_mask
            total = total + both[:, PAIR:] * wide_mask
        inverse = 1.0 / total
        inv_lt[here, lanes] = inverse
        out = outs * inverse
        text_o[here, lanes] = out
        mixed[here, lanes] = (self_o[here, lanes] + gate[:, lanes] * out).astype(BF16)

    base = paced(cols // PAIR * (rows // step_rows), attend, 4, 2, engine)

    def project(which):
        def step(i):
            start = which * sums.half + i * step_rows
            here = pl.ds(pl.multiple_of(start, 16), step_rows)
            partial[here, :] = dot_nt(mixed[here, :], weights[...]).astype(BF16)

        return step

    parts_each = TP_PARTS // (sums.half // step_rows)

    def project_send(i):
        project(1 - sums.core)(i)
        loop(parts_each, lambda k: sums.stage_one(i * parts_each + k))

    base = paced(sums.half // step_rows, project_send, 2, base, engine)
    loop(sums.half // step_rows, project(sums.core))
    loop(TP_PARTS, sums.stage_two)

    def update(k, which):
        here = sums.spot(k, which)
        live = live_rows(frames, which * sums.half + k * sums.rows, sums.rows, tok.shape[1])
        state = tok[here, :].astype(F32) + live * tanh_attn[...] * attn_sum[here, :].astype(F32)
        inverse = lax.rsqrt(jnp.mean(state * state, axis=-1, keepdims=True) + EPS)
        h_two[here, :] = (state * inverse * mult[...]).astype(BF16)

    def three(k):
        sums.stage_three(k)
        update(k, sums.core)

    base = paced(TP_PARTS, three, 8, base, engine)

    def four(k):
        sums.stage_four(k)
        update(k, 1 - sums.core)

    base = paced(TP_PARTS, four, 2, base, engine)
    finish_pumps(base, engine)
    sums.drain()
    engine.drain()


def text_forward(
    clips, frames, text, full_text, kygain, seg, q_text, self_o, gate, w_out, tokens, tanh_attn, mult, ffn_shard
):
    rows, wide = tokens.shape
    rows_t = text.shape[0]
    cols = kygain.shape[1]
    depth, ffn_wide = ffn_shard.shape
    blocks = Blocks(depth, ffn_wide, 96, 384) if clips == GRID else None
    f, b = shaped((rows, cols), F32), shaped((rows, cols), BF16)
    return pl.pallas_call(
        functools.partial(text_kernel, blocks),
        out_shape=[
            shaped((rows_t, cols), F32),
            shaped((rows_t, cols), BF16),
            shaped((rows_t, cols), BF16),
            f,
            f,
            b,
            shaped((rows, wide), BF16),
            shaped((rows, wide), BF16),
            shaped((GRID * depth, ffn_wide), BF16),
        ],
        in_specs=[IN_SMEM] + [IN_VMEM] * 11 + [ANY],
        out_specs=[IN_VMEM] * 8 + [ANY],
        scratch_shapes=[pltpu.VMEM((rows_t, 2 * cols), BF16), pltpu.VMEM((rows, wide), BF16)]
        + TpSum.scratch(rows, wide)
        + (Gather.scratch(blocks.count) if blocks is not None else []),
        compiler_params=params(2),
    )(frames, text, full_text, kygain, seg, q_text, self_o, gate, w_out, tokens, tanh_attn, mult, ffn_shard)


def state_kernel(blocks, *refs):
    frames, partial, tok, attn_sum, cot, tanh_attn, mult, grad = refs[:8]
    grad_attn, grad_state, colsums, out = refs[8:12]
    grad_n = refs[12]
    sums = TpSum(partial, grad_n, refs[13:15], refs[15:21])
    engine = Idle()
    if blocks is not None:
        engine = Scatter(blocks, grad, out, refs[21:25], refs[25:])
        greet(dp_peers(), tp_peers())
        engine.start()
    else:
        greet([], tp_peers())
    loop(TP_PARTS, sums.stage_one)
    colsums[...] = jnp.zeros_like(colsums)

    def update(k, which):
        here = sums.spot(k, which)
        live = live_rows(frames, which * sums.half + k * sums.rows, sums.rows, tok.shape[1])
        added = attn_sum[here, :].astype(F32)
        state = tok[here, :].astype(F32) + live * tanh_attn[...] * added
        inverse = lax.rsqrt(jnp.mean(state * state, axis=-1, keepdims=True) + EPS)
        hat = state * inverse
        g = grad_n[here, :].astype(F32)
        scaled = g * mult[...]
        g_hat = g * hat
        back = inverse * (scaled - hat * jnp.mean(scaled * hat, axis=-1, keepdims=True))
        total = cot[here, :].astype(F32) + back
        grad_state[here, :] = total
        live_total = live * total
        grad_attn[here, :] = (tanh_attn[...] * live_total).astype(BF16)
        colsums[0:1, :] += jnp.sum(g_hat, axis=0, keepdims=True)
        colsums[1:2, :] += jnp.sum(live_total * added, axis=0, keepdims=True)

    base = paced(TP_PARTS, sums.stage_two, 2, 0, engine)

    def three(k):
        sums.stage_three(k)
        update(k, sums.core)

    base = paced(TP_PARTS, three, 8, base, engine)

    def four(k):
        sums.stage_four(k)
        update(k, 1 - sums.core)

    base = paced(TP_PARTS, four, 1, base, engine)
    finish_pumps(base, engine)
    sums.drain()
    engine.drain()


def lined(grad):
    return grad.reshape(LINE, 2, grad.shape[0] // GRID, grad.shape[1])


def state_backward(clips, frames, partial, tokens, attn_sum, cotangent, tanh_attn, mult, g_down):
    rows, wide = tokens.shape
    depth, down_wide = g_down.shape[0] // clips, g_down.shape[1]
    blocks = Blocks(depth, down_wide, 96, 256) if clips == GRID else None
    view = lined(g_down) if blocks is not None else g_down
    return pl.pallas_call(
        functools.partial(state_kernel, blocks),
        out_shape=[
            shaped((rows, wide), BF16),
            shaped((rows, wide), F32),
            shaped((8, wide), F32),
            shaped((depth, down_wide), F32),
        ],
        in_specs=[IN_SMEM] + [IN_VMEM] * 6 + [ANY],
        out_specs=[IN_VMEM] * 4,
        scratch_shapes=[pltpu.VMEM((rows, wide), BF16)]
        + TpSum.scratch(rows, wide)
        + (Scatter.scratch(blocks) if blocks is not None else []),
        compiler_params=params(3),
    )(frames, partial, tokens, attn_sum, cotangent, tanh_attn, mult, view)


def attn_back_kernel(blocks, *refs):
    (frames, grad_attn, weights, gate, cos_ref, sa_ref, sb_ref, seg_ref, qgain, kgain, kygain) = refs[:11]
    (q_pre, k_pre, q_rot, k_rot, q_text, v_ref, self_o, inv_l) = refs[11:19]
    (ky_pre, kyr, vy, text_o, inv_lt, partial, grad) = refs[19:26]
    grad_qkv, grad_text, gains, ffn_sum, out = refs[26:31]
    do_self, do_text, d_self, d_text, dq_rot, dq_text, dk, dv, dky, dvy, klive = refs[31:42]
    sums = TpSum(partial, ffn_sum, refs[42:44], refs[44:50])
    engine = Idle()
    if blocks is not None:
        engine = Scatter(blocks, grad, out, refs[50:54], refs[54:])
        greet(dp_peers(), tp_peers())
        engine.start()
    else:
        greet([], tp_peers())
    loop(TP_PARTS, sums.stage_one)
    rows, cols = q_rot.shape
    rows_t = kyr.shape[0]
    step_rows = 256
    blocks_here = rows // step_rows
    pairs = cols // PAIR
    gains[...] = jnp.zeros_like(gains)
    dk[...] = jnp.zeros_like(dk)
    dv[...] = jnp.zeros_like(dv)
    dky[...] = jnp.zeros_like(dky)
    dvy[...] = jnp.zeros_like(dvy)

    def halves(value, first_head):
        lane = lax.broadcasted_iota(jnp.int32, (step_rows, PAIR), 1)
        out = jnp.zeros((step_rows, PAIR), F32)
        for head in range(2):
            total = jnp.sum(value * half_mask(step_rows, head, F32), axis=-1, keepdims=True)
            high = total.astype(BF16).astype(F32)
            spot = 2 * (first_head + head)
            out = out + jnp.where(lane == spot, high, jnp.where(lane == spot + 1, total - high, 0.0))
        return out

    def start_rows(i):
        here = block_rows(i, step_rows)
        g = dot_nn(grad_attn[here, :], weights[...])
        other = text_o[here, :]
        gains[3:4, :] += jnp.sum(g * other, axis=0, keepdims=True)
        first = (g * inv_l[here, :]).astype(BF16)
        do_self[here, :] = first
        second = (g * gate[...] * inv_lt[here, :]).astype(BF16)
        do_text[here, :] = second
        dot_self = first.astype(F32) * self_o[here, :]
        dot_text = second.astype(F32) * other
        each = [slice(pair * PAIR, (pair + 1) * PAIR) for pair in range(pairs)]
        d_self[here, :] = sum(halves(dot_self[:, lanes], 2 * pair) for pair, lanes in enumerate(each)).astype(BF16)
        d_text[here, :] = sum(halves(dot_text[:, lanes], 2 * pair) for pair, lanes in enumerate(each)).astype(BF16)
        klive[here, :] = k_rot[here, :] * live_rows(frames, i * step_rows, step_rows, cols).astype(BF16)

    def back(q_ref, k_ref, k_live, v_in, do_ref, d_ref, dq_ref, dk_ref, dv_ref):
        def step(i):
            pair, block = lax.div(i, blocks_here), lax.rem(i, blocks_here)
            here, lanes = block_rows(block, step_rows), pair_lanes(pair)
            keys = k_ref[:, lanes]
            values = v_in[:, lanes]
            lane = lax.broadcasted_iota(jnp.int32, values.shape, 1)
            dq = jnp.zeros((step_rows, PAIR), F32)
            for head in range(2):
                mask = half_mask(step_rows, head, BF16)
                q = q_ref[here, lanes] * mask
                do = do_ref[here, lanes] * mask
                scores = dot_nt(keys, q)
                p = jnp.exp(scores)
                dv_ref[:, lanes] += dot_nn(p.astype(BF16), do)
                spot = 2 * (2 * pair + head)
                minus = jnp.where((lane == spot) | (lane == spot + 1), -1.0, 0.0).astype(BF16)
                left = jnp.concatenate([values, minus], axis=1)
                right = jnp.concatenate([do, d_ref[here, :]], axis=1)
                ds = (p * dot_nt(left, right)).astype(BF16)
                dk_ref[:, lanes] += dot_nn(ds, q)
                key_mask = half_mask(keys.shape[0], head, BF16)
                dq = dq + dot_tn(ds, k_live[:, lanes] * key_mask)
            dq_ref[here, lanes] = dq * SCALE

        return step

    base = paced(blocks_here, start_rows, 2, 0, engine)
    self_back = back(q_rot, k_rot, klive, v_ref, do_self, d_self, dq_rot, dk, dv)

    def self_step(i):
        self_back(i)
        pl.when(i < TP_PARTS)(lambda: sums.stage_two(i))

    base = paced(pairs * blocks_here, self_step, 6, base, engine)
    text_back = back(q_text, kyr, kyr, vy, do_text, d_text, dq_text, dky, dvy)

    def text_step(i):
        text_back(i)
        pl.when(i < TP_PARTS)(lambda: sums.stage_three(i))

    base = paced(pairs * blocks_here, text_step, 2, base, engine)

    def norm_back(grad_normed, pre, gain, row):
        inverse = head_inverse(pre, seg_ref[...])
        hat = pre * inverse
        gains[row : row + 1, :] += jnp.sum(grad_normed * hat, axis=0, keepdims=True)
        scaled = grad_normed * gain
        average = segment_sum(scaled * hat, seg_ref[...]) * (1.0 / HEAD)
        return (inverse * (scaled - hat * average)).astype(BF16)

    def end_rows(i):
        here = block_rows(i, step_rows)
        cosines, sine_a, sine_b = thrice(cos_ref[here, :]), thrice(sa_ref[here, :]), thrice(sb_ref[here, :])
        live = live_rows(frames, i * step_rows, step_rows, cols)
        dqn = rope_back(dq_rot[here, :], cosines, sine_a, sine_b) + dq_text[here, :]
        grad_qkv[here, :cols] = norm_back(dqn, q_pre[here, :], qgain[...], 0)
        dkn = rope_back(dk[here, :] * live, cosines, sine_a, sine_b)
        grad_qkv[here, cols : 2 * cols] = norm_back(dkn, k_pre[here, :], kgain[...], 1)
        grad_qkv[here, 2 * cols : 3 * cols] = (dv[here, :] * live).astype(BF16)

    base = paced(blocks_here, end_rows, 1, base, engine)
    grad_text[:, :cols] = norm_back(dky[...], ky_pre[...], kygain[...], 2)
    grad_text[:, cols:] = dvy[...].astype(BF16)
    finish_pumps(base, engine)
    loop(TP_PARTS, sums.stage_four)
    sums.drain()
    engine.drain()


def attn_backward(clips, frames, grad_attn, w_out, gate, tables, seg, gain_rows, saved, partial, g_in):
    rows, wide = grad_attn.shape
    cols = gate.shape[1]
    rows_t = saved[8].shape[0]
    depth, in_wide = g_in.shape[0] // clips, g_in.shape[1]
    blocks = Blocks(depth, in_wide, 192, 256) if clips == GRID else None
    view = lined(g_in) if blocks is not None else g_in
    f, b = pltpu.VMEM((rows, cols), F32), pltpu.VMEM((rows, cols), BF16)
    ft = pltpu.VMEM((rows_t, cols), F32)
    slim = pltpu.VMEM((rows, PAIR), BF16)
    return pl.pallas_call(
        functools.partial(attn_back_kernel, blocks),
        out_shape=[
            shaped((rows, 3 * cols), BF16),
            shaped((rows_t, 2 * cols), BF16),
            shaped((8, cols), F32),
            shaped((rows, wide), BF16),
            shaped((depth, in_wide), F32),
        ],
        in_specs=[IN_SMEM] + [IN_VMEM] * 24 + [ANY],
        out_specs=[IN_VMEM] * 5,
        scratch_shapes=[b, b, slim, slim, f, f, f, f, ft, ft, b]
        + TpSum.scratch(rows, wide)
        + (Scatter.scratch(blocks) if blocks is not None else []),
        compiler_params=params(4),
    )(frames, grad_attn, w_out, gate, *tables, seg, *gain_rows, *saved, partial, view)


def last_kernel(blocks_t, blocks_a, *refs):
    partial, tok, grad_state, mult, gain, lift, vec_in, grad_t, grad_a = refs[:9]
    grad_tokens, vecs, out_t, out_a = refs[9:13]
    grad_n, colsum, vec = refs[13:16]
    sums = TpSum(partial, grad_n, refs[16:18], refs[18:24])
    me = lax.axis_index("dp")
    text_engine, attn_engine = Idle(), Idle()
    peers = []
    if blocks_t is not None:
        v_s, v_r = refs[24:26]
        peers = dp_peers()
        text_engine = Scatter(blocks_t, grad_t, out_t, refs[26:30], refs[30:37])
        attn_engine = Scatter(blocks_a, grad_a, out_a, refs[37:41], refs[41:48])
        greet(peers, tp_peers())
        text_engine.start()
    else:
        greet([], tp_peers())
    loop(TP_PARTS, sums.stage_one)
    colsum[...] = jnp.zeros_like(colsum)

    def update(k, which):
        here = sums.spot(k, which)
        x = tok[here, :].astype(F32)
        inverse = lax.rsqrt(jnp.mean(x * x, axis=-1, keepdims=True) + EPS)
        hat = x * inverse
        g = grad_n[here, :].astype(F32)
        scaled = g * mult[...]
        back = inverse * (scaled - hat * jnp.mean(scaled * hat, axis=-1, keepdims=True))
        grad_tokens[here, :] = (grad_state[here, :] + back).astype(BF16)
        colsum[...] += jnp.sum(g * hat, axis=0, keepdims=True)

    base = paced(TP_PARTS, sums.stage_two, 2, 0, text_engine)

    def three(k):
        sums.stage_three(k)
        update(k, sums.core)

    base = paced(TP_PARTS, three, 8, base, text_engine)
    finish_pumps(base, text_engine)
    attn_engine.start()

    def four(k):
        sums.stage_four(k)
        update(k, 1 - sums.core)

    base = paced(TP_PARTS, four, 4, 0, attn_engine)
    vec[...] = vec_in[...]
    wide = tok.shape[1]
    vec[:, :wide] = colsum[...] * gain[...]
    vec[:, 4 * wide : 5 * wide] = colsum[...] * lift[...]
    for i, there in enumerate(peers):
        remote(vec, vecs.at[me], v_s.at[i], v_r.at[i], dp=there).start()
    finish_pumps(base, attn_engine)
    vecs[pl.ds(me if peers else 0, 1)] = vec[...][None]
    for i, there in enumerate(peers):
        here = lax.rem(me + GRID - 1 - i, GRID)
        remote(vec, vecs.at[here], v_s.at[i], v_r.at[i], dp=me).wait_recv()
        remote(vec, vecs.at[me], v_s.at[i], v_r.at[i], dp=there).wait_send()
    sums.drain()
    text_engine.drain()
    attn_engine.drain()


def last_backward(clips, partial, tokens, grad_state, mult, gain, lift, vec, g_text, g_attn):
    rows, wide = tokens.shape
    grid = clips == GRID
    depth_t, wide_t = g_text.shape[0] // clips, g_text.shape[1]
    depth_a, wide_a = g_attn.shape[0] // clips, g_attn.shape[1]
    blocks_t = Blocks(depth_t, wide_t, 64, wide_t) if grid else None
    blocks_a = Blocks(depth_a, wide_a, 96, 384) if grid else None
    views = [lined(g_text), lined(g_attn)] if grid else [g_text, g_attn]
    return pl.pallas_call(
        functools.partial(last_kernel, blocks_t, blocks_a),
        out_shape=[
            shaped((rows, wide), BF16),
            shaped(((GRID if grid else 1),) + vec.shape, F32),
            shaped((depth_t, wide_t), F32),
            shaped((depth_a, wide_a), F32),
        ],
        in_specs=[IN_VMEM] * 7 + [ANY] * 2,
        out_specs=[IN_VMEM] * 4,
        scratch_shapes=[
            pltpu.VMEM((rows, wide), BF16),
            pltpu.VMEM((1, wide), F32),
            pltpu.VMEM(vec.shape, F32),
        ]
        + TpSum.scratch(rows, wide)
        + ([DMA((GRID - 1,))] * 2 + Scatter.scratch(blocks_t) + Scatter.scratch(blocks_a) if grid else []),
        compiler_params=params(5),
    )(partial, tokens, grad_state, mult, gain, lift, vec, *views)


def gather_plain(shard):
    return lax.all_gather(shard, "dp", axis=0, tiled=True)


def scatter_plain(grad):
    return lax.psum_scatter(grad, "dp", scatter_dimension=0, tiled=True).astype(F32)


def first_plain(shard, cond, small, w_ada):
    act = jax.nn.silu(lax.all_to_all(cond[:, 0], "dp", 0, 0, tiled=True)).astype(BF16)
    parts = dot_nn(act, w_ada)
    mod = lax.psum_scatter(parts, "dp", scatter_dimension=0, tiled=True)
    return gather_plain(shard), mod, lax.all_gather(small, "dp", axis=0), act.astype(F32)


def on_device(
    tokens,
    text,
    cond,
    frames,
    w_query,
    w_key,
    w_value,
    w_out,
    w_text_key,
    w_text_value,
    w_gate,
    w_up,
    w_down,
    w_ada,
    ada_bias,
    norm_one,
    norm_two,
    query_gain,
    key_gain,
    text_key_gain,
    cross_gate,
    cotangent,
):
    rows, wide = tokens.shape
    clips = lax.axis_size("dp")
    grid = clips == GRID
    cols, units = w_query.shape[1], w_gate.shape[1]
    heads_here = cols // HEAD
    bias_rows, gain_rows = ada_bias.shape[0], norm_one.shape[0]
    small = jnp.concatenate([ada_bias, norm_one, norm_two]).astype(F32)[None, :]
    cond_rows = cond.astype(F32).reshape(clips, 1, -1)
    attn_shard = jnp.concatenate([w_query, w_key, w_value, w_out.T], axis=1)
    text_shard = jnp.concatenate([w_text_key, w_text_value], axis=1)
    ffn_shard = jnp.concatenate([w_gate, w_up, w_down.T], axis=1)
    first = gather_first if grid else first_plain
    full_attn, mod_sum, smalls, act_rows = first(attn_shard, cond_rows, small, w_ada)
    modulation = mod_sum[0] + smalls[:, 0, :bias_rows].reshape(-1)
    gain_one = smalls[:, 0, bias_rows : bias_rows + gain_rows].reshape(-1)
    gain_two = smalls[:, 0, bias_rows + gain_rows :].reshape(-1)
    scale_attn, gate_attn, scale_ffn, gate_ffn = jnp.split(modulation, 4)
    lift_one, lift_two = 1.0 + scale_attn, 1.0 + scale_ffn
    mult_one, mult_two = (gain_one * lift_one)[None, :], (gain_two * lift_two)[None, :]
    tanh_attn, tanh_ffn = jnp.tanh(gate_attn), jnp.tanh(gate_ffn)
    qgain = query_gain.astype(F32)[None, :]
    kgain = key_gain.astype(F32)[None, :]
    kygain = text_key_gain.astype(F32)[None, :]
    gate_tanh = jnp.tanh(cross_gate.astype(F32))
    gate_wide = jnp.repeat(gate_tanh, HEAD)[None, :]
    tables, seg = rope_tables(rows), segment_ones(cols)
    out_turned = full_attn[:, 3 * cols :]

    h_one, q_pre, k_pre, q_rot, k_rot, q_text, values, self_o, inv_l, full_text = self_forward(
        clips, frames, tokens, full_attn, mult_one, qgain, kgain, tables, seg, text_shard
    )
    if not grid:
        full_text = gather_plain(text_shard)
    ky_pre, kyr, vy, text_o, inv_lt, mixed, attn_sum, h_two, full_ffn = text_forward(
        clips,
        frames,
        text,
        full_text,
        kygain,
        seg,
        q_text,
        self_o,
        gate_wide,
        out_turned,
        tokens,
        tanh_attn[None, :],
        mult_two,
        ffn_shard,
    )
    if not grid:
        full_ffn = gather_plain(ffn_shard)
    live = (jnp.arange(rows, dtype=jnp.int32) < frames[0] * FRAME_TOK).astype(F32)[:, None]

    gate_pre = dot_nn(h_two, full_ffn[:, :units])
    up_pre = dot_nn(h_two, full_ffn[:, units : 2 * units])
    down_turned = full_ffn[:, 2 * units :]
    logistic = jax.nn.sigmoid(gate_pre)
    swish = gate_pre * logistic
    hidden_units = (swish * up_pre).astype(BF16)
    grad_result = cotangent.astype(F32)
    grad_ffn = (live * tanh_ffn * grad_result).astype(BF16)
    grad_hidden = dot_nn(grad_ffn, down_turned)
    g_down = dot_tn(grad_ffn, hidden_units).astype(BF16)
    grad_gate_pre = (grad_hidden * up_pre * logistic * (1.0 + gate_pre * (1.0 - logistic))).astype(BF16)
    grad_up_pre = (grad_hidden * swish).astype(BF16)
    grad_in = jnp.concatenate([grad_gate_pre, grad_up_pre], axis=1)
    partial_two = dot_nt(grad_in, full_ffn[:, : 2 * units]).astype(BF16)
    grad_attn, grad_state, sums_two, s_down = state_backward(
        clips, frames, partial_two, tokens, attn_sum, cotangent, tanh_attn[None, :], mult_two, g_down
    )
    g_in = dot_tn(h_two, grad_in).astype(BF16)
    partial_ffn = dot_nt(hidden_units, down_turned).astype(BF16)
    saved = (q_pre, k_pre, q_rot, k_rot, q_text, values, self_o, inv_l, ky_pre, kyr, vy, text_o, inv_lt)
    grad_qkv, grad_text, gains, ffn_sum, s_in = attn_backward(
        clips, frames, grad_attn, out_turned, gate_wide, tables, seg, (qgain, kgain, kygain), saved, partial_ffn, g_in
    )
    ffn_sum = ffn_sum.astype(F32)
    hidden_state = tokens.astype(F32) + live * tanh_attn * attn_sum.astype(F32)
    result = (hidden_state + live * tanh_ffn * ffn_sum).astype(BF16)
    grad_gate_ffn = jnp.sum(live * ffn_sum * grad_result, axis=0) * (1.0 - tanh_ffn * tanh_ffn)
    g_text = dot_tn(text, grad_text).astype(BF16)
    g_attn = jnp.concatenate(
        [dot_tn(h_one, grad_qkv).astype(BF16), dot_tn(grad_attn, mixed).astype(BF16)], axis=1
    )
    partial_one = dot_nt(grad_qkv, full_attn[:, : 3 * cols]).astype(BF16)
    g_cross_gate = jnp.sum(gains[3].reshape(heads_here, HEAD), axis=1) * (1.0 - gate_tanh * gate_tanh)
    blank = jnp.zeros((wide,), F32)
    vec = jnp.concatenate(
        [
            blank,
            sums_two[1] * (1.0 - tanh_attn * tanh_attn),
            sums_two[0] * gain_two,
            grad_gate_ffn,
            blank,
            sums_two[0] * lift_two,
            gains[0],
            gains[1],
            gains[2],
            g_cross_gate,
            jnp.zeros((-heads_here % 128,), F32),
        ]
    )[None, :]
    grad_tokens, vecs, s_text, s_attn = last_backward(
        clips, partial_one, tokens, grad_state, mult_one, gain_one[None, :], lift_one[None, :], vec, g_text, g_attn
    )
    if not grid:
        s_down, s_in, s_text, s_attn = (scatter_plain(g) for g in (g_down, g_in, g_text, g_attn))
        vecs = lax.all_gather(vecs[0], "dp", axis=0)
    vecs = vecs[:, 0, :]
    mod_wide = 4 * wide
    g_ada = lax.dot_general(
        act_rows,
        vecs[:, :mod_wide],
        (((0,), (0,)), ((), ())),
        precision=lax.Precision.HIGHEST,
        preferred_element_type=F32,
    )
    sums = jnp.sum(vecs, axis=0)
    me = lax.axis_index("dp")
    g_bias = lax.dynamic_slice(sums, (me * bias_rows,), (bias_rows,))
    g_norm_one = lax.dynamic_slice(sums, (mod_wide + me * gain_rows,), (gain_rows,))
    g_norm_two = lax.dynamic_slice(sums, (mod_wide + wide + me * gain_rows,), (gain_rows,))
    rest = sums[mod_wide + 2 * wide :]
    return (
        result,
        grad_tokens,
        s_attn[:, :cols],
        s_attn[:, cols : 2 * cols],
        s_attn[:, 2 * cols : 3 * cols],
        s_attn[:, 3 * cols :].T,
        s_text[:, :cols],
        s_text[:, cols:],
        s_in[:, :units],
        s_in[:, units:],
        s_down.T,
        g_ada,
        g_bias,
        g_norm_one,
        g_norm_two,
        rest[:cols],
        rest[cols : 2 * cols],
        rest[2 * cols : 3 * cols],
        rest[3 * cols : 3 * cols + heads_here],
    )


def solution(mesh):
    placed = (
        P("dp", None),
        P("dp", None),
        P("dp", None),
        P("dp"),
        P("dp", "tp"),
        P("dp", "tp"),
        P("dp", "tp"),
        P("tp", "dp"),
        P("dp", "tp"),
        P("dp", "tp"),
        P("dp", "tp"),
        P("dp", "tp"),
        P("tp", "dp"),
        P("dp", None),
        P("dp"),
        P("dp"),
        P("dp"),
        P("tp"),
        P("tp"),
        P("tp"),
        P("tp"),
        P("dp", None),
    )
    return jax.shard_map(
        on_device,
        mesh=mesh,
        in_specs=placed,
        out_specs=(
            P("dp", None),
            P("dp", None),
            P("dp", "tp"),
            P("dp", "tp"),
            P("dp", "tp"),
            P("tp", "dp"),
            P("dp", "tp"),
            P("dp", "tp"),
            P("dp", "tp"),
            P("dp", "tp"),
            P("tp", "dp"),
            P("dp", None),
            P("dp"),
            P("dp"),
            P("dp"),
            P("tp"),
            P("tp"),
            P("tp"),
            P("tp"),
        ),
        check_vma=False,
    )
```

```python
import functools

import jax
import jax.numpy as jnp
import numpy as np
from jax import lax
from jax.experimental import pallas as pl
from jax.experimental.pallas import tpu as pltpu
from jax.sharding import PartitionSpec as P

HEAD = 64
FRAME_TOK = 64
EPS = 1e-06
ROPE_BASE = 10000.0
SCALE = HEAD**-0.5
MESH = pl.DeviceIdType.MESH
VMEM_LIMIT = 60 * 2**20
GRID = 8
LINE = 4
PAIR = 2 * HEAD
TP_PARTS = 8
AHEAD = 2
DMA = pltpu.SemaphoreType.DMA
F32 = jnp.float32
BF16 = jnp.bfloat16


def dot_nn(left, right):
    return jnp.dot(left, right, preferred_element_type=F32)


def dot_nt(left, right):
    return lax.dot_general(left, right, (((1,), (1,)), ((), ())), preferred_element_type=F32)


def dot_tn(left, right):
    return lax.dot_general(left, right, (((0,), (0,)), ((), ())), preferred_element_type=F32)


def remote(src, dst, send, recv, **where):
    return pltpu.make_async_remote_copy(
        src_ref=src, dst_ref=dst, send_sem=send, recv_sem=recv, device_id=where, device_id_type=MESH
    )


def greet(dp_peers, tp_peers):
    barrier = pltpu.get_barrier_semaphore()
    for peer in dp_peers:
        pl.semaphore_signal(barrier, inc=1, device_id={"dp": peer}, device_id_type=MESH)
    for peer in tp_peers:
        pl.semaphore_signal(barrier, inc=1, device_id={"tp": peer}, device_id_type=MESH)
    pl.semaphore_wait(barrier, len(dp_peers) + len(tp_peers))


def dp_peers():
    me = lax.axis_index("dp")
    return [lax.rem(me + step, GRID) for step in range(1, GRID)]


def tp_peers():
    me = lax.axis_index("tp")
    return [me + 1 - 2 * lax.rem(me, 2), lax.rem(me + 2, 4)]


def aligned(value, by):
    return value if isinstance(value, int) else pl.multiple_of(value, by)


def loop(count, step):
    def body(i, carry):
        step(i)
        return carry

    lax.fori_loop(0, count, body, 0)


def add_rows(out_ref, first, *others):
    rows = out_ref.shape[0]

    def step(i):
        here = pl.ds(pl.multiple_of(i * 32, 32), 32)
        total = first[here, :].astype(F32)
        for other in others:
            total = total + other[here, :].astype(F32)
        out_ref[here, :] = total.astype(out_ref.dtype)

    loop(rows // 32, step)


class Blocks:
    def __init__(self, depth, wide, rows, cols):
        self.depth, self.wide, self.rows, self.cols = depth, wide, rows, cols
        self.across = wide // cols
        self.count = (depth // rows) * self.across

    def at(self, c):
        if isinstance(c, int):
            return c // self.across * self.rows, c % self.across * self.cols
        row = aligned(lax.div(c, self.across) * self.rows, 16)
        col = aligned(lax.rem(c, self.across) * self.cols, 128)
        return row, col


class Gather:
    def __init__(self, blocks, shard, full, sems):
        self.b, self.shard, self.full = blocks, shard, full
        self.up_s, self.up_r, self.dn_s, self.dn_r, self.y_s, self.y_r, self.own_s = sems
        self.me = lax.axis_index("dp")
        self.z, self.y = self.me // 2, lax.rem(self.me, 2)
        self.ticks, self.done = blocks.count + LINE - 2, 0

    @staticmethod
    def scratch(count):
        return [DMA((count, 3))] * 4 + [DMA((count, 4))] * 2 + [DMA((count,))]

    def own(self, c):
        row, col = self.b.at(c)
        return self.shard.at[pl.ds(row, self.b.rows), pl.ds(col, self.b.cols)]

    def place(self, c, origin):
        row, col = self.b.at(c)
        start = pl.multiple_of(origin * self.b.depth + row, 16)
        return self.full.at[pl.ds(start, self.b.rows), pl.ds(col, self.b.cols)]

    def up(self, c, hop):
        origin = self.me - 2 * hop
        src = self.own(c) if hop == 0 else self.place(c, origin)
        return remote(src, self.place(c, origin), self.up_s.at[c, hop], self.up_r.at[c, hop], dp=self.me + 2)

    def down(self, c, hop):
        origin = self.me + 2 * hop
        src = self.own(c) if hop == 0 else self.place(c, origin)
        return remote(src, self.place(c, origin), self.dn_s.at[c, hop], self.dn_r.at[c, hop], dp=self.me - 2)

    def across(self, c, line, mine=False):
        origin = 2 * line + self.y
        src = self.own(c) if mine else self.place(c, origin)
        other = self.me + 1 - 2 * self.y
        return remote(src, self.place(c, origin), self.y_s.at[c, line], self.y_r.at[c, line], dp=other)

    def came(self, c, origin, sems):
        return remote(self.place(c, origin), self.place(c, origin), sems, sems, dp=self.me)

    def local(self, c):
        return pltpu.make_async_copy(self.own(c), self.place(c, self.me), self.own_s.at[c])

    def begin(self, c):
        pl.when(self.z < LINE - 1)(lambda: self.up(c, 0).start())
        pl.when(self.z > 0)(lambda: self.down(c, 0).start())
        self.across(c, self.z, True).start()
        self.local(c).start()

    def start(self):
        for c in range(min(AHEAD, self.b.count)):
            self.begin(c)

    def pump(self, t):
        me, z, count = self.me, self.z, self.b.count
        pl.when(t + AHEAD < count)(lambda: self.begin(t + AHEAD))
        for hop in range(LINE - 1):
            c = t - hop
            valid = (c >= 0) & (c < count)

            @pl.when(valid & (z - 1 - hop >= 0))
            def _():
                self.came(c, me - 2 * (hop + 1), self.up_r.at[c, hop]).wait_recv()
                if hop < LINE - 2:
                    pl.when(z < LINE - 1)(lambda: self.up(c, hop + 1).start())
                self.across(c, z - 1 - hop).start()

            @pl.when(valid & (z + 1 + hop <= LINE - 1))
            def _():
                self.came(c, me + 2 * (hop + 1), self.dn_r.at[c, hop]).wait_recv()
                if hop < LINE - 2:
                    pl.when(z > 0)(lambda: self.down(c, hop + 1).start())
                self.across(c, z + 1 + hop).start()

    def drain(self):
        z = self.z

        def step(c):
            for line in range(LINE):
                self.came(c, 2 * line + 1 - self.y, self.y_r.at[c, line]).wait_recv()
                self.across(c, line).wait_send()
            self.local(c).wait()
            for hop in range(LINE - 1):
                pl.when((z < LINE - 1) & (z - hop >= 0))(lambda: self.up(c, hop).wait_send())
                pl.when((z > 0) & (z + hop <= LINE - 1))(lambda: self.down(c, hop).wait_send())

        loop(self.b.count, step)


class Scatter:
    def __init__(self, blocks, grad, out, bufs, sems):
        self.b, self.grad, self.out = blocks, grad, out
        self.held, self.crossed, self.above, self.below = bufs
        self.y_s, self.y_r, self.own_s, self.up_s, self.up_r, self.dn_s, self.dn_r = sems
        self.me = lax.axis_index("dp")
        self.z, self.y = self.me // 2, lax.rem(self.me, 2)
        self.ticks, self.done = blocks.count + LINE - 1, 0

    @staticmethod
    def scratch(blocks):
        shape = (blocks.rows, blocks.cols)
        count = blocks.count
        bufs = [pltpu.VMEM((count, lines) + shape, BF16) for lines in (4, 4, 3, 3)]
        return bufs + [DMA((count,))] * 3 + [DMA((count, 3))] * 4

    def part(self, c, row_y):
        row, col = self.b.at(c)
        return self.grad.at[:, row_y, pl.ds(row, self.b.rows), pl.ds(col, self.b.cols)]

    def across(self, c):
        other = self.me + 1 - 2 * self.y
        return remote(self.part(c, 1 - self.y), self.crossed.at[c], self.y_s.at[c], self.y_r.at[c], dp=other)

    def load(self, c):
        return pltpu.make_async_copy(self.part(c, self.y), self.held.at[c], self.own_s.at[c])

    def up(self, c, line):
        return remote(
            self.held.at[c, line],
            self.above.at[c, line - 1],
            self.up_s.at[c, line - 1],
            self.up_r.at[c, line - 1],
            dp=self.me + 2,
        )

    def down(self, c, line):
        return remote(
            self.held.at[c, line],
            self.below.at[c, line],
            self.dn_s.at[c, line],
            self.dn_r.at[c, line],
            dp=self.me - 2,
        )

    def begin(self, c):
        self.across(c).start()
        self.load(c).start()

    def start(self):
        for c in range(min(AHEAD, self.b.count)):
            self.begin(c)

    def fold(self, c):
        self.across(c).wait_recv()
        self.load(c).wait()
        for line in range(LINE):
            add_rows(self.held.at[c, line], self.held.at[c, line], self.crossed.at[c, line])

    def send_up(self, c, here):
        for line in range(LINE - 1, here, -1):
            if here > 0:
                self.up(c, line).wait_recv()
                add_rows(self.held.at[c, line], self.held.at[c, line], self.above.at[c, line - 1])
            self.up(c, line).start()

    def send_down(self, c, here):
        for line in range(here):
            if here < LINE - 1:
                self.down(c, line).wait_recv()
                add_rows(self.held.at[c, line], self.held.at[c, line], self.below.at[c, line])
            self.down(c, line).start()

    def finish(self, c, here):
        row, col = self.b.at(c)
        terms = [self.held.at[c, here]]
        if here > 0:
            self.up(c, here).wait_recv()
            terms.append(self.above.at[c, here - 1])
        if here < LINE - 1:
            self.down(c, here).wait_recv()
            terms.append(self.below.at[c, here])
        add_rows(self.out.at[pl.ds(row, self.b.rows), pl.ds(col, self.b.cols)], *terms)

    def pump(self, t):
        count, z = self.b.count, self.z
        pl.when(t + AHEAD < count)(lambda: self.begin(t + AHEAD))
        pl.when(t < count)(lambda: self.fold(t))
        for hop in range(LINE):
            c = t - hop
            valid = (c >= 0) & (c < count)
            if hop < LINE - 1:
                pl.when(valid & (z == hop))(lambda: self.send_up(c, hop))
                pl.when(valid & (z == LINE - 1 - hop))(lambda: self.send_down(c, LINE - 1 - hop))
            else:
                for here in range(LINE):
                    pl.when(valid & (z == here))(lambda: self.finish(c, here))

    def drain(self):
        def step(c):
            self.across(c).wait_send()
            for here in range(LINE):

                @pl.when(self.z == here)
                def _():
                    for line in range(here + 1, LINE):
                        self.up(c, line).wait_send()
                    for line in range(here):
                        self.down(c, line).wait_send()

        loop(self.b.count, step)


class Idle:
    ticks = done = 0

    def start(self):
        pass

    def pump(self, t):
        pass

    def drain(self):
        pass


class TpSum:
    def __init__(self, partial, out, bufs, sems, own_sems=None):
        self.p, self.out = partial, out
        self.crossed, self.other = bufs
        self.c_s, self.c_r, self.x_s, self.x_r, self.o_s, self.o_r = sems
        self.core = lax.rem(lax.axis_index("tp"), 2)
        self.beside, self.far = tp_peers()
        self.half = partial.shape[0] // 2
        self.rows = self.half // TP_PARTS
        self.own_s = own_sems

    @staticmethod
    def scratch(rows, wide):
        return [pltpu.VMEM((rows // 2, wide), BF16)] * 2 + [DMA((TP_PARTS,))] * 6

    def spot(self, k, which):
        return pl.ds(pl.multiple_of(which * self.half + k * self.rows, 16), self.rows)

    def part(self, k):
        return pl.ds(aligned(k * self.rows, 16), self.rows)

    def first(self, k):
        return remote(
            self.p.at[self.spot(k, 1 - self.core)],
            self.crossed.at[self.part(k)],
            self.c_s.at[k],
            self.c_r.at[k],
            tp=self.beside,
        )

    def second(self, k):
        here = self.out.at[self.spot(k, self.core)]
        return remote(here, self.other.at[self.part(k)], self.x_s.at[k], self.x_r.at[k], tp=self.far)

    def third(self, k, which):
        here = self.out.at[self.spot(k, which)]
        return remote(here, here, self.o_s.at[k], self.o_r.at[k], tp=self.beside)

    def load(self, k):
        mine = self.spot(k, self.core)
        return pltpu.make_async_copy(self.p.at[mine], self.out.at[mine], self.own_s.at[k])

    def stage_one(self, k):
        self.first(k).start()
        if self.own_s is not None:
            self.load(k).start()

    def stage_two(self, k):
        self.first(k).wait_recv()
        mine = self.spot(k, self.core)
        held = self.p.at[mine]
        if self.own_s is not None:
            self.load(k).wait()
            held = self.out.at[mine]
        add_rows(self.out.at[mine], held, self.crossed.at[self.part(k)])
        self.second(k).start()

    def stage_three(self, k):
        self.second(k).wait()
        mine = self.out.at[self.spot(k, self.core)]
        add_rows(mine, mine, self.other.at[self.part(k)])
        self.third(k, self.core).start()

    def stage_four(self, k):
        self.third(k, 1 - self.core).wait_recv()

    def drain(self):
        def step(k):
            self.first(k).wait_send()
            self.third(k, self.core).wait_send()

        loop(TP_PARTS, step)


def params(number):
    return pltpu.CompilerParams(
        collective_id=number, has_side_effects=True, vmem_limit_bytes=VMEM_LIMIT
    )


ANY = pl.BlockSpec(memory_space=pl.ANY)
IN_VMEM = pl.BlockSpec(memory_space=pltpu.VMEM)
IN_SMEM = pl.BlockSpec(memory_space=pltpu.SMEM)


def shaped(shape, dtype):
    return jax.ShapeDtypeStruct(shape, dtype)


def segment_sum(value, seg):
    high = value.astype(BF16)
    low = (value - high.astype(F32)).astype(BF16)
    return dot_nn(high, seg) + dot_nn(low, seg)


def head_inverse(value, seg):
    return lax.rsqrt(segment_sum(value * value, seg) * (1.0 / HEAD) + EPS)


def thrice(table):
    return jnp.concatenate([table] * 3, axis=1)


def rope(value, cosines, sine_a, sine_b):
    wide = value.shape[1]
    ahead = pltpu.roll(value, wide - HEAD // 4, 1)
    behind = pltpu.roll(value, HEAD // 4, 1)
    return value * cosines + ahead * sine_a + behind * sine_b


def rope_back(grad, cosines, sine_a, sine_b):
    wide = grad.shape[1]
    ahead = pltpu.roll(grad * sine_b, wide - HEAD // 4, 1)
    behind = pltpu.roll(grad * sine_a, HEAD // 4, 1)
    return grad * cosines + ahead + behind


def rope_tables(row_count):
    lane = np.arange(PAIR)
    within = lane % HEAD
    quarter = HEAD // 4
    which = within // quarter
    freqs = (ROPE_BASE ** (-(within % quarter).astype(np.float32) / np.float32(quarter))).astype(np.float32)
    row = np.arange(row_count)
    frame, place = (row // FRAME_TOK).astype(np.float32), (row % FRAME_TOK).astype(np.float32)
    position = np.where(which[None, :] < 2, frame[:, None], place[:, None])
    angles = (position * freqs[None, :]).astype(np.float32)
    cosines, sines = np.cos(angles), np.sin(angles)
    even = (which % 2 == 0)[None, :]
    return (
        jnp.asarray(cosines.astype(np.float32)),
        jnp.asarray(np.where(even, -sines, 0.0).astype(np.float32)),
        jnp.asarray(np.where(even, 0.0, sines).astype(np.float32)),
    )


def segment_ones(wide):
    head = np.arange(wide) // HEAD
    return jnp.asarray((head[:, None] == head[None, :]).astype(np.float32)).astype(BF16)


def live_rows(frames_ref, start, rows, wide):
    row = start + lax.broadcasted_iota(jnp.int32, (rows, wide), 0)
    return (row < frames_ref[0] * FRAME_TOK).astype(F32)


def half_mask(rows, head, dtype):
    lane = lax.broadcasted_iota(jnp.int32, (rows, PAIR), 1)
    return ((lane < HEAD) if head == 0 else (lane >= HEAD)).astype(dtype)


def pair_lanes(pair, wide=PAIR):
    return pl.ds(pl.multiple_of(pair * wide, PAIR), wide)


def block_rows(block, rows):
    return pl.ds(pl.multiple_of(block * rows, rows), rows)


def paced(count, step, *plans):
    jobs = []
    for engine, pumps in plans:
        pumps = min(pumps, engine.ticks - engine.done)
        if pumps > 0:
            jobs.append((engine, pumps, engine.done))
            engine.done += pumps

    def body(i):
        step(i)
        for engine, pumps, base in jobs:
            if pumps <= count:
                every = count // pumps
                turn = lax.div(i, every)
                now = (lax.rem(i, every) == every - 1) & (turn < pumps)
                pl.when(now)(functools.partial(engine.pump, base + turn))
            else:
                each = -(-pumps // count)
                for j in range(each):
                    pl.when(i * each + j < pumps)(functools.partial(engine.pump, base + i * each + j))

    loop(count, body)


def finish_pumps(engine):
    base = engine.done
    if base < engine.ticks:
        loop(engine.ticks - base, lambda i: engine.pump(base + i))
    engine.done = engine.ticks


def first_kernel(blocks, *refs):
    shard, cond_ref, small_ref, ada_ref, text_ref, w_tk, w_tv = refs[:7]
    full, mod_ref, smalls_ref, act_ref, text_all, products = refs[7:13]
    conds, part, parts, c_s, c_r, m_s, m_r, p_s, p_r, t_s, t_r, q_s, q_r, own_s = refs[13:27]
    engine = Gather(blocks, shard, full, refs[27:])
    me, tp = lax.axis_index("dp"), lax.axis_index("tp")
    peers, (beside, far) = dp_peers(), tp_peers()
    sources = [lax.rem(me + GRID - step, GRID) for step in range(1, GRID)]
    depth = text_all.shape[2]
    share = text_all.shape[1] // 4
    greet(peers, [beside, far])
    engine.start()

    def quarter(which):
        rows = pl.ds(pl.multiple_of(which * share, 16), share)
        return text_all.at[:, rows, :]

    def slab(there, origin):
        rows = pl.ds(pl.multiple_of(tp * share, 16), share)
        return text_ref.at[rows, pl.ds(pl.multiple_of(there * depth, 128), depth)], text_all.at[origin, rows, :]

    for i, there in enumerate(peers):
        remote(cond_ref.at[there], conds.at[me], c_s.at[i], c_r.at[i], dp=there).start()
        remote(small_ref, smalls_ref.at[me], m_s.at[i], m_r.at[i], dp=there).start()
    for i, there in enumerate(peers):
        remote(*slab(there, me), t_s.at[i], t_r.at[i], dp=there).start()
    own = pltpu.make_async_copy(*slab(me, me), own_s)
    own.start()
    conds[pl.ds(me, 1)] = cond_ref[pl.ds(me, 1)]
    smalls_ref[pl.ds(me, 1)] = small_ref[...][None]
    for i, here in enumerate(sources):
        remote(conds.at[here], conds.at[here], c_s.at[i], c_r.at[i], dp=me).wait_recv()
    cond = jnp.concatenate([conds[i] for i in range(GRID)], axis=0)
    act = (cond * (1.0 / (1.0 + jnp.exp(-cond)))).astype(BF16)
    act_ref[...] = act.astype(F32)
    width = ada_ref.shape[1] // 4
    for i in range(4):
        cols = pl.ds(i * width, width)
        product = dot_nn(act, ada_ref[:, cols])
        for j in range(GRID):
            part[j, :, cols] = product[j : j + 1, :]
    for i, there in enumerate(peers):
        remote(part.at[there], parts.at[me], p_s.at[i], p_r.at[i], dp=there).start()
    parts[pl.ds(me, 1)] = part[pl.ds(me, 1)]
    paced(1, lambda i: None, (engine, 1))
    own.wait()
    for i, here in enumerate(sources):
        remote(*slab(here, here), t_s.at[i], t_r.at[i], dp=me).wait_recv()
    mine = quarter(tp)
    to_beside = remote(mine, mine, q_s.at[0], q_r.at[0], tp=beside)
    to_far = remote(mine, mine, q_s.at[1], q_r.at[1], tp=far)
    to_beside.start()
    to_far.start()
    paced(2, lambda i: None, (engine, 2))
    from_far = quarter(lax.rem(tp + 2, 4))
    remote(from_far, from_far, q_s.at[1], q_r.at[1], tp=far).wait_recv()
    passed = remote(from_far, from_far, q_s.at[2], q_r.at[2], tp=beside)
    passed.start()
    for i, here in enumerate(sources):
        remote(parts.at[here], parts.at[here], p_s.at[i], p_r.at[i], dp=me).wait_recv()
    mod_ref[...] = sum(parts[i] for i in range(GRID))
    paced(1, lambda i: None, (engine, 1))
    from_beside = quarter(tp + 1 - 2 * lax.rem(tp, 2))
    remote(from_beside, from_beside, q_s.at[0], q_r.at[0], tp=beside).wait_recv()
    remote(from_beside, from_beside, q_s.at[2], q_r.at[2], tp=beside).wait_recv()
    wide = w_tk.shape[1]

    def multiply(i):
        rows = text_all[i]
        line, y = lax.div(i, 2), lax.rem(i, 2)
        products[line, y, :, :wide] = dot_nn(rows, w_tk[...]).astype(BF16)
        products[line, y, :, wide:] = dot_nn(rows, w_tv[...]).astype(BF16)

    paced(GRID, multiply, (engine, 4))
    finish_pumps(engine)
    engine.drain()
    to_beside.wait_send()
    to_far.wait_send()
    passed.wait_send()
    for i, there in enumerate(peers):
        here = sources[i]
        remote(small_ref, smalls_ref.at[here], m_s.at[i], m_r.at[i], dp=me).wait_recv()
        remote(cond_ref.at[there], conds.at[me], c_s.at[i], c_r.at[i], dp=there).wait_send()
        remote(small_ref, smalls_ref.at[me], m_s.at[i], m_r.at[i], dp=there).wait_send()
        remote(*slab(there, me), t_s.at[i], t_r.at[i], dp=there).wait_send()
        remote(part.at[there], parts.at[me], p_s.at[i], p_r.at[i], dp=there).wait_send()


def gather_first(shard, cond, small, w_ada, text, w_tk, w_tv):
    depth, wide = shard.shape
    blocks = Blocks(depth, wide, 96, 384)
    mods = w_ada.shape[1]
    rows_t, slab, cols = text.shape[0], w_tk.shape[0], w_tk.shape[1]
    return pl.pallas_call(
        functools.partial(first_kernel, blocks),
        out_shape=[
            shaped((GRID * depth, wide), BF16),
            shaped((1, mods), F32),
            shaped((GRID,) + small.shape, F32),
            shaped((GRID, cond.shape[2]), F32),
            shaped((GRID, rows_t, slab), BF16),
            shaped((LINE, 2, rows_t, 2 * cols), BF16),
        ],
        in_specs=[ANY] + [IN_VMEM] * 3 + [ANY] + [IN_VMEM] * 2,
        out_specs=[ANY] + [IN_VMEM] * 5,
        scratch_shapes=[
            pltpu.VMEM((GRID, 1, cond.shape[2]), F32),
            pltpu.VMEM((GRID, 1, mods), F32),
            pltpu.VMEM((GRID, 1, mods), F32),
        ]
        + [DMA((GRID - 1,))] * 8
        + [DMA((3,))] * 2
        + [DMA]
        + Gather.scratch(blocks.count),
        compiler_params=params(0),
    )(shard, cond, small, w_ada, text, w_tk, w_tv)


def forward_kernel(blocks_t, blocks, *refs):
    frames, tok, weights, mult, qgain, kgain, kygain, cos_ref, sa_ref, sb_ref, seg_ref = refs[:11]
    gate, tanh_attn, mult_two, products, shard = refs[11:16]
    h_one, q_pre, k_pre, q_rot, k_rot, q_text, v_out, self_o, inv_l = refs[16:25]
    ky_pre, kyr, vy_out, text_o, inv_lt, mixed, attn_sum, h_two, full = refs[25:34]
    vaug, vyaug, partial, ty = refs[34:38]
    sums = TpSum(partial, attn_sum, refs[38:40], refs[40:46])
    text_engine, engine = Idle(), Idle()
    if blocks is not None:
        text_engine = Scatter(blocks_t, products, ty, refs[46:50], refs[50:57])
        engine = Gather(blocks, shard, full, refs[57:64])
        greet(dp_peers(), tp_peers())
        text_engine.start()
        engine.start()
    else:
        greet([], tp_peers())
        ty = products
    cols = q_pre.shape[1]
    rows = tok.shape[0]
    step_rows = 256
    blocks_here = rows // step_rows
    pairs = cols // PAIR

    def project(i):
        here = block_rows(i, step_rows)
        x = tok[here, :].astype(F32)
        inverse = lax.rsqrt(jnp.mean(x * x, axis=-1, keepdims=True) + EPS)
        h = (x * inverse * mult[...]).astype(BF16)
        h_one[here, :] = h
        cosines, sine_a, sine_b = thrice(cos_ref[here, :]), thrice(sa_ref[here, :]), thrice(sb_ref[here, :])
        q = dot_nn(h, weights[:, :cols])
        q_pre[here, :] = q
        qn = q * head_inverse(q, seg_ref[...]) * qgain[...]
        q_text[here, :] = (qn * SCALE).astype(BF16)
        q_rot[here, :] = (rope(qn, cosines, sine_a, sine_b) * SCALE).astype(BF16)
        k = dot_nn(h, weights[:, cols : 2 * cols])
        k_pre[here, :] = k
        kn = k * head_inverse(k, seg_ref[...]) * kgain[...]
        k_rot[here, :] = rope(kn, cosines, sine_a, sine_b).astype(BF16)
        v = dot_nn(h, weights[:, 2 * cols : 3 * cols]).astype(BF16)
        v_out[here, :] = v
        live = live_rows(frames, i * step_rows, step_rows, PAIR).astype(BF16)
        for pair in range(pairs):
            vaug[here, 2 * pair * PAIR : (2 * pair + 1) * PAIR] = v[:, pair * PAIR : (pair + 1) * PAIR] * live
            vaug[here, (2 * pair + 1) * PAIR : (2 * pair + 2) * PAIR] = live

    def attention(q_ref, k_ref, v_ref, inv_ref):
        def step(i):
            pair, block = lax.div(i, blocks_here), lax.rem(i, blocks_here)
            here, lanes = block_rows(block, step_rows), pair_lanes(pair)
            q = q_ref[here, lanes]
            keys = k_ref[:, lanes]
            values = v_ref[:, pair_lanes(pair, 2 * PAIR)]
            outs = jnp.zeros((step_rows, PAIR), F32)
            total = jnp.zeros((step_rows, PAIR), F32)
            for head in range(2):
                p = jnp.exp(dot_nt(q * half_mask(step_rows, head, BF16), keys)).astype(BF16)
                both = dot_nn(p, values)
                wide_mask = half_mask(step_rows, head, F32)
                outs = outs + both[:, :PAIR] * wide_mask
                total = total + both[:, PAIR:] * wide_mask
            inverse = 1.0 / total
            inv_ref[here, lanes] = inverse
            return here, lanes, outs * inverse

        return step

    self_attention = attention(q_rot, k_rot, vaug, inv_l)
    text_attention = attention(q_text, kyr, vyaug, inv_lt)

    def attend(i):
        here, lanes, out = self_attention(i)
        mixed_self[here, lanes] = out
        self_o[here, lanes] = out.astype(BF16)

    def attend_text(i):
        here, lanes, out = text_attention(i)
        text_o[here, lanes] = out.astype(BF16)
        mixed[here, lanes] = (mixed_self[here, lanes] + gate[:, lanes] * out).astype(BF16)

    mixed_self = refs[-1]
    paced(blocks_here, project, (text_engine, 6))
    paced(pairs * blocks_here, attend, (text_engine, 12), (engine, 2))
    finish_pumps(text_engine)

    ky = ty[:, :cols]
    ky_pre[...] = ky
    kyr[...] = (ky * head_inverse(ky, seg_ref[...]) * kygain[...]).astype(BF16)
    vy = ty[:, cols:].astype(BF16)
    vy_out[...] = vy
    for pair in range(pairs):
        vyaug[:, 2 * pair * PAIR : (2 * pair + 1) * PAIR] = vy[:, pair * PAIR : (pair + 1) * PAIR]
        vyaug[:, (2 * pair + 1) * PAIR : (2 * pair + 2) * PAIR] = jnp.ones((vy.shape[0], PAIR), BF16)
    paced(pairs * blocks_here, attend_text, (engine, 2))

    def output(which):
        def step(i):
            here = pl.ds(pl.multiple_of(which * sums.half + i * step_rows, 16), step_rows)
            partial[here, :] = dot_nt(mixed[here, :], weights[:, 3 * cols :]).astype(BF16)

        return step

    parts_each = TP_PARTS // (sums.half // step_rows)

    def output_send(i):
        output(1 - sums.core)(i)
        loop(parts_each, lambda k: sums.stage_one(i * parts_each + k))

    paced(sums.half // step_rows, output_send)
    paced(sums.half // step_rows, output(sums.core), (engine, 2))
    paced(TP_PARTS, sums.stage_two, (engine, 2))

    def update(k, which):
        here = sums.spot(k, which)
        live = live_rows(frames, which * sums.half + k * sums.rows, sums.rows, tok.shape[1])
        state = tok[here, :].astype(F32) + live * tanh_attn[...] * attn_sum[here, :].astype(F32)
        inverse = lax.rsqrt(jnp.mean(state * state, axis=-1, keepdims=True) + EPS)
        h_two[here, :] = (state * inverse * mult_two[...]).astype(BF16)

    def three(k):
        sums.stage_three(k)
        update(k, sums.core)

    paced(TP_PARTS, three, (engine, 8))

    def four(k):
        sums.stage_four(k)
        update(k, 1 - sums.core)

    paced(TP_PARTS, four, (engine, 2))
    finish_pumps(engine)
    sums.drain()
    text_engine.drain()
    engine.drain()


def forward(clips, frames, tokens, full_attn, mult, gain_rows, tables, seg, gate, tanh_attn, mult_two, products, ffn_shard):
    rows, wide = tokens.shape
    cols = gate.shape[1]
    rows_t = products.shape[-2]
    depth, ffn_wide = ffn_shard.shape
    grid = clips == GRID
    blocks_t = Blocks(rows_t, 2 * cols, 32, 2 * cols) if grid else None
    blocks = Blocks(depth, ffn_wide, 96, 384) if grid else None
    f, b = shaped((rows, cols), F32), shaped((rows, cols), BF16)
    bt = shaped((rows_t, cols), BF16)
    return pl.pallas_call(
        functools.partial(forward_kernel, blocks_t, blocks),
        out_shape=[
            shaped((rows, wide), BF16),
            f,
            f,
            b,
            b,
            b,
            b,
            b,
            f,
            shaped((rows_t, cols), F32),
            bt,
            bt,
            b,
            f,
            b,
            shaped((rows, wide), BF16),
            shaped((rows, wide), BF16),
            shaped((GRID * depth, ffn_wide), BF16),
        ],
        in_specs=[IN_SMEM] + [IN_VMEM] * 13 + [ANY if grid else IN_VMEM, ANY],
        out_specs=[IN_VMEM] * 17 + [ANY],
        scratch_shapes=[
            pltpu.VMEM((rows, 2 * cols), BF16),
            pltpu.VMEM((rows_t, 2 * cols), BF16),
            pltpu.VMEM((rows, wide), BF16),
            pltpu.VMEM((rows_t, 2 * cols), F32),
        ]
        + TpSum.scratch(rows, wide)
        + (Scatter.scratch(blocks_t) + Gather.scratch(blocks.count) if grid else [])
        + [pltpu.VMEM((rows, cols), F32)],
        compiler_params=params(1),
    )(frames, tokens, full_attn, mult, *gain_rows, *tables, seg, gate, tanh_attn, mult_two, products, ffn_shard)


def state_kernel(blocks, *refs):
    frames, partial, tok, attn_sum, cot, tanh_attn, mult, h_two, grad_ffn, hid, grad_in, down = refs[:12]
    grad_attn, grad_state, colsums, out, g_in, p_ffn = refs[12:18]
    grad_n, g_down, staged, stage_s, p_staged, p_s = refs[18:24]
    sums = TpSum(partial, grad_n, refs[24:26], refs[26:32])
    engine = Idle()
    if blocks is not None:
        engine = Scatter(blocks, g_down, out, refs[32:36], refs[36:])
        greet(dp_peers(), tp_peers())
    else:
        greet([], tp_peers())
    loop(TP_PARTS, sums.stage_one)
    colsums[...] = jnp.zeros_like(colsums)
    wide = tok.shape[1]
    units = hid.shape[1]
    step_rows = 256
    tall = wide // LINE

    def down_block(m):
        lanes = pl.ds(pl.multiple_of(m * tall, 128), tall)
        product = dot_tn(grad_ffn[:, lanes], hid[...]).astype(BF16)
        g_down[m, 0] = product[: tall // 2]
        g_down[m, 1] = product[tall // 2 :]

    def in_copy(m):
        return pltpu.make_async_copy(staged.at[lax.rem(m, 2)], g_in.at[m], stage_s.at[lax.rem(m, 2)])

    def in_block(m):
        lanes = pl.ds(pl.multiple_of(m * tall, 128), tall)
        pl.when(m >= 2)(lambda: in_copy(m - 2).wait())
        for half in range(2):
            cols = slice(half * units, (half + 1) * units)
            product = dot_tn(h_two[:, lanes], grad_in[:, cols]).astype(BF16)
            staged[lax.rem(m, 2), 0, :, cols] = product[: tall // 2]
            staged[lax.rem(m, 2), 1, :, cols] = product[tall // 2 :]
        in_copy(m).start()

    def p_copy(i):
        return pltpu.make_async_copy(
            p_staged.at[lax.rem(i, 2)], p_ffn.at[block_rows(i, step_rows)], p_s.at[lax.rem(i, 2)]
        )

    def p_block(i):
        pl.when(i >= 2)(lambda: p_copy(i - 2).wait())
        p_staged[lax.rem(i, 2)] = dot_nt(hid[block_rows(i, step_rows), :], down[...]).astype(BF16)
        p_copy(i).start()

    def update(k, which):
        here = sums.spot(k, which)
        live = live_rows(frames, which * sums.half + k * sums.rows, sums.rows, wide)
        added = attn_sum[here, :].astype(F32)
        state = tok[here, :].astype(F32) + live * tanh_attn[...] * added
        inverse = lax.rsqrt(jnp.mean(state * state, axis=-1, keepdims=True) + EPS)
        hat = state * inverse
        g = grad_n[here, :].astype(F32)
        scaled = g * mult[...]
        g_hat = g * hat
        back = inverse * (scaled - hat * jnp.mean(scaled * hat, axis=-1, keepdims=True))
        total = cot[here, :].astype(F32) + back
        grad_state[here, :] = total.astype(BF16)
        live_total = live * total
        grad_attn[here, :] = (tanh_attn[...] * live_total).astype(BF16)
        colsums[0:1, :] += jnp.sum(g_hat, axis=0, keepdims=True)
        colsums[1:2, :] += jnp.sum(live_total * added, axis=0, keepdims=True)

    loop(2, down_block)
    loop(TP_PARTS, sums.stage_two)
    loop(2, lambda m: down_block(m + 2))
    if blocks is None:
        out[...] = g_down[...]
    engine.start()
    paced(LINE, in_block, (engine, 2))
    paced(p_ffn.shape[0] // step_rows, p_block, (engine, 1))

    def three(k):
        sums.stage_three(k)
        update(k, sums.core)

    paced(TP_PARTS, three, (engine, 8))

    def four(k):
        sums.stage_four(k)
        update(k, 1 - sums.core)

    paced(TP_PARTS, four, (engine, 1))
    finish_pumps(engine)
    last_p = p_ffn.shape[0] // step_rows
    for i in (1, 2):
        in_copy(LINE - i).wait()
        p_copy(last_p - i).wait()
    sums.drain()
    engine.drain()


def state_backward(clips, frames, partial, tokens, attn_sum, cotangent, tanh_attn, mult, h_two, grad_ffn, hid, grad_in, down):
    rows, wide = tokens.shape
    units = hid.shape[1]
    depth = wide // GRID
    blocks = Blocks(depth, units, 96, 256) if clips == GRID else None
    return pl.pallas_call(
        functools.partial(state_kernel, blocks),
        out_shape=[
            shaped((rows, wide), BF16),
            shaped((rows, wide), BF16),
            shaped((8, wide), F32),
            shaped((depth, units), F32) if clips == GRID else shaped((LINE, 2, depth, units), BF16),
            shaped((LINE, 2, depth, 2 * units), BF16),
            shaped((rows, wide), BF16),
        ],
        in_specs=[IN_SMEM] + [IN_VMEM] * 11,
        out_specs=[IN_VMEM] * 4 + [ANY] * 2,
        scratch_shapes=[
            pltpu.VMEM((rows, wide), BF16),
            pltpu.VMEM((LINE, 2, depth, units), BF16),
            pltpu.VMEM((2, 2, depth, 2 * units), BF16),
            DMA((2,)),
            pltpu.VMEM((2, 256, wide), BF16),
            DMA((2,)),
        ]
        + TpSum.scratch(rows, wide)
        + (Scatter.scratch(blocks) if blocks is not None else []),
        compiler_params=params(2),
    )(frames, partial, tokens, attn_sum, cotangent, tanh_attn, mult, h_two, grad_ffn, hid, grad_in, down)


def attn_back_kernel(blocks, *refs):
    (frames, grad_attn, weights, gate, cos_ref, sa_ref, sb_ref, seg_ref, qgain, kgain, kygain) = refs[:11]
    (q_pre, k_pre, q_rot, k_rot, q_text, v_ref, self_o, inv_l) = refs[11:19]
    (ky_pre, kyr, vy, text_o, inv_lt, h_one, mixed, partial, grad) = refs[19:28]
    grad_qkv, grad_text, gains, ffn_sum, out, g_attn = refs[28:34]
    do_self, do_text, d_self, d_text, dqn, dk, dv, dky, dvy, klive, staged, stage_s = refs[34:46]
    sums = TpSum(partial, ffn_sum, refs[46:48], refs[48:54], refs[54])
    engine = Idle()
    if blocks is not None:
        engine = Scatter(blocks, grad, out, refs[55:59], refs[59:])
        greet(dp_peers(), tp_peers())
        engine.start()
    else:
        greet([], tp_peers())
    loop(TP_PARTS, sums.stage_one)
    rows, cols = q_rot.shape
    wide = grad_attn.shape[1]
    step_rows = 256
    blocks_here = rows // step_rows
    pairs = cols // PAIR
    gains[...] = jnp.zeros_like(gains)
    dk[...] = jnp.zeros_like(dk)
    dv[...] = jnp.zeros_like(dv)
    dky[...] = jnp.zeros_like(dky)
    dvy[...] = jnp.zeros_like(dvy)

    def halves(value, first_head):
        lane = lax.broadcasted_iota(jnp.int32, (step_rows, PAIR), 1)
        out = jnp.zeros((step_rows, PAIR), F32)
        for head in range(2):
            total = jnp.sum(value * half_mask(step_rows, head, F32), axis=-1, keepdims=True)
            high = total.astype(BF16).astype(F32)
            spot = 2 * (first_head + head)
            out = out + jnp.where(lane == spot, high, jnp.where(lane == spot + 1, total - high, 0.0))
        return out

    def start_rows(i):
        here = block_rows(i, step_rows)
        g = dot_nn(grad_attn[here, :], weights[...])
        other = text_o[here, :].astype(F32)
        gains[3:4, :] += jnp.sum(g * other, axis=0, keepdims=True)
        first = (g * inv_l[here, :]).astype(BF16)
        do_self[here, :] = first
        second = (g * gate[...] * inv_lt[here, :]).astype(BF16)
        do_text[here, :] = second
        dot_self = first.astype(F32) * self_o[here, :].astype(F32)
        dot_text = second.astype(F32) * other
        each = [slice(pair * PAIR, (pair + 1) * PAIR) for pair in range(pairs)]
        d_self[here, :] = sum(halves(dot_self[:, lanes], 2 * pair) for pair, lanes in enumerate(each)).astype(BF16)
        d_text[here, :] = sum(halves(dot_text[:, lanes], 2 * pair) for pair, lanes in enumerate(each)).astype(BF16)
        klive[here, :] = k_rot[here, :] * live_rows(frames, i * step_rows, step_rows, cols).astype(BF16)

    def back(q_ref, k_ref, k_live, v_in, do_ref, d_ref, dk_ref, dv_ref, turned):
        def step(i):
            pair, block = lax.div(i, blocks_here), lax.rem(i, blocks_here)
            here, lanes = block_rows(block, step_rows), pair_lanes(pair)
            keys = k_ref[:, lanes]
            values = v_in[:, lanes]
            lane = lax.broadcasted_iota(jnp.int32, values.shape, 1)
            dq = jnp.zeros((step_rows, PAIR), F32)
            for head in range(2):
                mask = half_mask(step_rows, head, BF16)
                q = q_ref[here, lanes] * mask
                do = do_ref[here, lanes] * mask
                scores = dot_nt(keys, q)
                p = jnp.exp(scores)
                dv_ref[:, lanes] += dot_nn(p.astype(BF16), do)
                spot = 2 * (2 * pair + head)
                minus = jnp.where((lane == spot) | (lane == spot + 1), -1.0, 0.0).astype(BF16)
                left = jnp.concatenate([values, minus], axis=1)
                right = jnp.concatenate([do, d_ref[here, :]], axis=1)
                ds = (p * dot_nt(left, right)).astype(BF16)
                dk_ref[:, lanes] += dot_nn(ds, q)
                key_mask = half_mask(keys.shape[0], head, BF16)
                dq = dq + dot_tn(ds, k_live[:, lanes] * key_mask)
            dq = dq * SCALE
            if turned:
                dqn[here, lanes] = rope_back(dq, cos_ref[here, :], sa_ref[here, :], sb_ref[here, :])
            else:
                dqn[here, lanes] += dq

        return step

    paced(blocks_here, start_rows, (engine, 2))
    self_back = back(q_rot, k_rot, klive, v_ref, do_self, d_self, dk, dv, True)

    def self_step(i):
        self_back(i)
        pl.when(i < TP_PARTS)(lambda: sums.stage_two(i))

    paced(pairs * blocks_here, self_step, (engine, 4))
    text_back = back(q_text, kyr, kyr, vy, do_text, d_text, dky, dvy, False)

    def text_step(i):
        text_back(i)
        pl.when(i < TP_PARTS)(lambda: sums.stage_three(i))

    paced(pairs * blocks_here, text_step, (engine, 2))

    def norm_back(grad_normed, pre, gain, row):
        inverse = head_inverse(pre, seg_ref[...])
        hat = pre * inverse
        gains[row : row + 1, :] += jnp.sum(grad_normed * hat, axis=0, keepdims=True)
        scaled = grad_normed * gain
        average = segment_sum(scaled * hat, seg_ref[...]) * (1.0 / HEAD)
        return (inverse * (scaled - hat * average)).astype(BF16)

    def end_rows(i):
        here = block_rows(i, step_rows)
        cosines, sine_a, sine_b = thrice(cos_ref[here, :]), thrice(sa_ref[here, :]), thrice(sb_ref[here, :])
        live = live_rows(frames, i * step_rows, step_rows, cols)
        grad_qkv[here, :cols] = norm_back(dqn[here, :], q_pre[here, :], qgain[...], 0)
        dkn = rope_back(dk[here, :] * live, cosines, sine_a, sine_b)
        grad_qkv[here, cols : 2 * cols] = norm_back(dkn, k_pre[here, :], kgain[...], 1)
        grad_qkv[here, 2 * cols : 3 * cols] = (dv[here, :] * live).astype(BF16)

    paced(blocks_here, end_rows, (engine, 1))
    grad_text[:, :cols] = norm_back(dky[...], ky_pre[...], kygain[...], 2)
    grad_text[:, cols:] = dvy[...].astype(BF16)
    tall = wide // LINE

    def copy(m):
        return pltpu.make_async_copy(staged.at[lax.rem(m, 2)], g_attn.at[m], stage_s.at[lax.rem(m, 2)])

    def products(m):
        lanes = pl.ds(pl.multiple_of(m * tall, 128), tall)
        pl.when(m >= 2)(lambda: copy(m - 2).wait())
        first = dot_tn(h_one[:, lanes], grad_qkv[...]).astype(BF16)
        second = dot_tn(grad_attn[:, lanes], mixed[...]).astype(BF16)
        for y in range(2):
            part = slice(y * tall // 2, (y + 1) * tall // 2)
            staged[lax.rem(m, 2), y, :, : 3 * cols] = first[part]
            staged[lax.rem(m, 2), y, :, 3 * cols :] = second[part]
        copy(m).start()

    paced(LINE, products, (engine, 2))
    finish_pumps(engine)
    loop(TP_PARTS, sums.stage_four)
    copy(LINE - 2).wait()
    copy(LINE - 1).wait()
    sums.drain()
    engine.drain()


def attn_backward(clips, frames, grad_attn, w_out, gate, tables, seg, gain_rows, saved, partial, g_in):
    rows, wide = grad_attn.shape
    cols = gate.shape[1]
    rows_t = saved[8].shape[0]
    depth, in_wide = wide // GRID, g_in.shape[-1]
    blocks = Blocks(depth, in_wide, 192, 256) if clips == GRID else None
    f, b = pltpu.VMEM((rows, cols), F32), pltpu.VMEM((rows, cols), BF16)
    ft = pltpu.VMEM((rows_t, cols), F32)
    slim = pltpu.VMEM((rows, PAIR), BF16)
    return pl.pallas_call(
        functools.partial(attn_back_kernel, blocks),
        out_shape=[
            shaped((rows, 3 * cols), BF16),
            shaped((rows_t, 2 * cols), BF16),
            shaped((8, cols), F32),
            shaped((rows, wide), BF16),
            shaped((depth, in_wide), F32),
            shaped((LINE, 2, depth, 4 * cols), BF16),
        ],
        in_specs=[IN_SMEM] + [IN_VMEM] * 25 + [ANY] * 2,
        out_specs=[IN_VMEM] * 5 + [ANY],
        scratch_shapes=[b, b, slim, slim, f, f, f, ft, ft, b]
        + [pltpu.VMEM((2, 2, depth, 4 * cols), BF16), DMA((2,))]
        + TpSum.scratch(rows, wide)
        + [DMA((TP_PARTS,))]
        + (Scatter.scratch(blocks) if blocks is not None else []),
        compiler_params=params(3),
    )(frames, grad_attn, w_out, gate, *tables, seg, *gain_rows, *saved, partial, g_in)


def last_kernel(blocks_t, blocks_a, *refs):
    grad_qkv, weights, tok, grad_state, mult, gain, lift, vec_in, text_all, grad_text, grad_a = refs[:11]
    grad_tokens, vecs, g_tk, g_tv, out_a = refs[11:16]
    partial, grad_n, colsum, vec = refs[16:20]
    sums = TpSum(partial, grad_n, refs[20:22], refs[22:28])
    me = lax.axis_index("dp")
    text_engine, attn_engine = Idle(), Idle()
    peers = []
    if blocks_t is not None:
        v_s, v_r, all_text = refs[28:31]
        peers = dp_peers()
        text_engine = Gather(blocks_t, grad_text, all_text, refs[31:38])
        attn_engine = Scatter(blocks_a, grad_a, out_a, refs[38:42], refs[42:49])
        greet(peers, tp_peers())
        attn_engine.start()
        text_engine.start()
    else:
        greet([], tp_peers())
    colsum[...] = jnp.zeros_like(colsum)
    wide = tok.shape[1]
    cols = grad_qkv.shape[1] // 3
    step_rows = 256

    def project(which):
        def step(i):
            here = pl.ds(pl.multiple_of(which * sums.half + i * step_rows, 16), step_rows)
            partial[here, :] = dot_nt(grad_qkv[here, :], weights[:, : 3 * cols]).astype(BF16)

        return step

    parts_each = TP_PARTS // (sums.half // step_rows)

    def project_send(i):
        project(1 - sums.core)(i)
        loop(parts_each, lambda k: sums.stage_one(i * parts_each + k))

    paced(sums.half // step_rows, project_send)
    paced(sums.half // step_rows, project(sums.core), (attn_engine, 1))

    def update(k, which):
        here = sums.spot(k, which)
        x = tok[here, :].astype(F32)
        inverse = lax.rsqrt(jnp.mean(x * x, axis=-1, keepdims=True) + EPS)
        hat = x * inverse
        g = grad_n[here, :].astype(F32)
        scaled = g * mult[...]
        back = inverse * (scaled - hat * jnp.mean(scaled * hat, axis=-1, keepdims=True))
        grad_tokens[here, :] = (grad_state[here, :].astype(F32) + back).astype(BF16)
        colsum[...] += jnp.sum(g * hat, axis=0, keepdims=True)

    paced(TP_PARTS, sums.stage_two, (attn_engine, 2))

    def three(k):
        sums.stage_three(k)
        update(k, sums.core)

    paced(TP_PARTS, three, (attn_engine, 4), (text_engine, 4))

    def four(k):
        sums.stage_four(k)
        update(k, 1 - sums.core)

    paced(TP_PARTS, four, (attn_engine, 2), (text_engine, 2))
    vec[...] = vec_in[...]
    vec[:, :wide] = colsum[...] * gain[...]
    vec[:, 4 * wide : 5 * wide] = colsum[...] * lift[...]
    for i, there in enumerate(peers):
        remote(vec, vecs.at[me], v_s.at[i], v_r.at[i], dp=there).start()
    finish_pumps(text_engine)
    finish_pumps(attn_engine)
    text_engine.drain()
    if blocks_t is not None:
        rows_t = grad_text.shape[0]
        total_k = jnp.zeros(g_tk.shape, F32)
        total_v = jnp.zeros(g_tv.shape, F32)
        for clip in range(GRID):
            here = slice(clip * rows_t, (clip + 1) * rows_t)
            total_k = total_k + dot_tn(text_all[clip], all_text[here, :cols])
            total_v = total_v + dot_tn(text_all[clip], all_text[here, cols:])
        g_tk[...] = total_k
        g_tv[...] = total_v
    vecs[pl.ds(me if peers else 0, 1)] = vec[...][None]
    for i, there in enumerate(peers):
        here = lax.rem(me + GRID - 1 - i, GRID)
        remote(vec, vecs.at[here], v_s.at[i], v_r.at[i], dp=me).wait_recv()
        remote(vec, vecs.at[me], v_s.at[i], v_r.at[i], dp=there).wait_send()
    sums.drain()
    attn_engine.drain()


def last_backward(clips, grad_qkv, full_attn, tokens, grad_state, mult, gain, lift, vec, text_all, grad_text, g_attn):
    rows, wide = tokens.shape
    grid = clips == GRID
    rows_t, cols2 = grad_text.shape
    depth_a, wide_a = g_attn.shape[-2:]
    slab = text_all.shape[-1]
    blocks_t = Blocks(rows_t, cols2, 64, cols2) if grid else None
    blocks_a = Blocks(depth_a, wide_a, 96, 384) if grid else None
    return pl.pallas_call(
        functools.partial(last_kernel, blocks_t, blocks_a),
        out_shape=[
            shaped((rows, wide), BF16),
            shaped(((GRID if grid else 1),) + vec.shape, F32),
            shaped((slab, cols2 // 2), F32),
            shaped((slab, cols2 // 2), F32),
            shaped((depth_a, wide_a), F32),
        ],
        in_specs=[IN_VMEM] * 10 + [ANY],
        out_specs=[IN_VMEM] * 5,
        scratch_shapes=[
            pltpu.VMEM((rows, wide), BF16),
            pltpu.VMEM((rows, wide), BF16),
            pltpu.VMEM((1, wide), F32),
            pltpu.VMEM(vec.shape, F32),
        ]
        + TpSum.scratch(rows, wide)
        + (
            [DMA((GRID - 1,))] * 2
            + [pltpu.VMEM((GRID * rows_t, cols2), BF16)]
            + Gather.scratch(blocks_t.count)
            + Scatter.scratch(blocks_a)
            if grid
            else []
        ),
        compiler_params=params(4),
    )(grad_qkv, full_attn, tokens, grad_state, mult, gain, lift, vec, text_all, grad_text, g_attn)


def gather_plain(shard):
    return lax.all_gather(shard, "dp", axis=0, tiled=True)


def scatter_plain(grad):
    return lax.psum_scatter(grad, "dp", scatter_dimension=0, tiled=True).astype(F32)


def first_plain(shard, cond, small, w_ada, text, w_tk, w_tv):
    act = jax.nn.silu(lax.all_to_all(cond[:, 0], "dp", 0, 0, tiled=True)).astype(BF16)
    parts = dot_nn(act, w_ada)
    mod = lax.psum_scatter(parts, "dp", scatter_dimension=0, tiled=True)
    full_text = gather_plain(jnp.concatenate([w_tk, w_tv], axis=1))
    smalls = lax.all_gather(small, "dp", axis=0)
    return gather_plain(shard), mod, smalls, act.astype(F32), text[:1, :128], dot_nn(text, full_text)


def on_device(
    tokens,
    text,
    cond,
    frames,
    w_query,
    w_key,
    w_value,
    w_out,
    w_text_key,
    w_text_value,
    w_gate,
    w_up,
    w_down,
    w_ada,
    ada_bias,
    norm_one,
    norm_two,
    query_gain,
    key_gain,
    text_key_gain,
    cross_gate,
    cotangent,
):
    rows, wide = tokens.shape
    clips = lax.axis_size("dp")
    grid = clips == GRID
    cols, units = w_query.shape[1], w_gate.shape[1]
    heads_here = cols // HEAD
    bias_rows, gain_rows = ada_bias.shape[0], norm_one.shape[0]
    small = jnp.concatenate([ada_bias, norm_one, norm_two]).astype(F32)[None, :]
    cond_rows = cond.astype(F32).reshape(clips, 1, -1)
    attn_shard = jnp.concatenate([w_query, w_key, w_value, w_out.T], axis=1)
    ffn_shard = jnp.concatenate([w_gate, w_up, w_down.T], axis=1)
    first = gather_first if grid else first_plain
    full_attn, mod_sum, smalls, act_rows, text_all, products = first(
        attn_shard, cond_rows, small, w_ada, text, w_text_key, w_text_value
    )
    modulation = mod_sum[0] + smalls[:, 0, :bias_rows].reshape(-1)
    gain_one = smalls[:, 0, bias_rows : bias_rows + gain_rows].reshape(-1)
    gain_two = smalls[:, 0, bias_rows + gain_rows :].reshape(-1)
    scale_attn, gate_attn, scale_ffn, gate_ffn = jnp.split(modulation, 4)
    lift_one, lift_two = 1.0 + scale_attn, 1.0 + scale_ffn
    mult_one, mult_two = (gain_one * lift_one)[None, :], (gain_two * lift_two)[None, :]
    tanh_attn, tanh_ffn = jnp.tanh(gate_attn), jnp.tanh(gate_ffn)
    qgain = query_gain.astype(F32)[None, :]
    kgain = key_gain.astype(F32)[None, :]
    kygain = text_key_gain.astype(F32)[None, :]
    gate_tanh = jnp.tanh(cross_gate.astype(F32))
    gate_wide = jnp.repeat(gate_tanh, HEAD)[None, :]
    tables, seg = rope_tables(rows), segment_ones(cols)
    out_turned = full_attn[:, 3 * cols :]

    gain_set = (qgain, kgain, kygain)
    (h_one, *saved, mixed, attn_sum, h_two, full_ffn) = forward(
        clips,
        frames,
        tokens,
        full_attn,
        mult_one,
        gain_set,
        tables,
        seg,
        gate_wide,
        tanh_attn[None, :],
        mult_two,
        products,
        ffn_shard,
    )
    if not grid:
        full_ffn = gather_plain(ffn_shard)
    live = (jnp.arange(rows, dtype=jnp.int32) < frames[0] * FRAME_TOK).astype(F32)[:, None]

    gate_pre = dot_nn(h_two, full_ffn[:, :units])
    up_pre = dot_nn(h_two, full_ffn[:, units : 2 * units])
    down_turned = full_ffn[:, 2 * units :]
    logistic = jax.nn.sigmoid(gate_pre)
    swish = gate_pre * logistic
    hidden_units = (swish * up_pre).astype(BF16)
    grad_result = cotangent.astype(F32)
    grad_ffn = (live * tanh_ffn * grad_result).astype(BF16)
    grad_hidden = dot_nn(grad_ffn, down_turned)
    grad_gate_pre = (grad_hidden * up_pre * logistic * (1.0 + gate_pre * (1.0 - logistic))).astype(BF16)
    grad_up_pre = (grad_hidden * swish).astype(BF16)
    grad_in = jnp.concatenate([grad_gate_pre, grad_up_pre], axis=1)
    partial_two = dot_nt(grad_in, full_ffn[:, : 2 * units]).astype(BF16)
    grad_attn, grad_state, sums_two, s_down, g_in, partial_ffn = state_backward(
        clips,
        frames,
        partial_two,
        tokens,
        attn_sum,
        cotangent,
        tanh_attn[None, :],
        mult_two,
        h_two,
        grad_ffn,
        hidden_units,
        grad_in,
        down_turned,
    )
    grad_qkv, grad_text, gains, ffn_sum, s_in, g_attn = attn_backward(
        clips,
        frames,
        grad_attn,
        out_turned,
        gate_wide,
        tables,
        seg,
        gain_set,
        (*saved, h_one, mixed),
        partial_ffn,
        g_in,
    )
    ffn_sum = ffn_sum.astype(F32)
    hidden_state = tokens.astype(F32) + live * tanh_attn * attn_sum.astype(F32)
    result = (hidden_state + live * tanh_ffn * ffn_sum).astype(BF16)
    grad_gate_ffn = jnp.sum(live * ffn_sum * grad_result, axis=0) * (1.0 - tanh_ffn * tanh_ffn)
    g_cross_gate = jnp.sum(gains[3].reshape(heads_here, HEAD), axis=1) * (1.0 - gate_tanh * gate_tanh)
    blank = jnp.zeros((wide,), F32)
    vec = jnp.concatenate(
        [
            blank,
            sums_two[1] * (1.0 - tanh_attn * tanh_attn),
            sums_two[0] * gain_two,
            grad_gate_ffn,
            blank,
            sums_two[0] * lift_two,
            gains[0],
            gains[1],
            gains[2],
            g_cross_gate,
            jnp.zeros((-heads_here % 128,), F32),
        ]
    )[None, :]
    grad_tokens, vecs, s_text_key, s_text_value, s_attn = last_backward(
        clips,
        grad_qkv,
        full_attn,
        tokens,
        grad_state,
        mult_one,
        gain_one[None, :],
        lift_one[None, :],
        vec,
        text_all,
        grad_text,
        g_attn,
    )
    if not grid:
        s_down, s_in, s_attn = (scatter_plain(g.reshape(wide, -1)) for g in (s_down, g_in, g_attn))
        s_text = scatter_plain(dot_tn(text, grad_text).astype(BF16))
        s_text_key, s_text_value = s_text[:, :cols], s_text[:, cols:]
        vecs = lax.all_gather(vecs[0], "dp", axis=0)
    vecs = vecs[:, 0, :]
    mod_wide = 4 * wide
    g_ada = lax.dot_general(
        act_rows,
        vecs[:, :mod_wide],
        (((0,), (0,)), ((), ())),
        precision=lax.Precision.HIGHEST,
        preferred_element_type=F32,
    )
    sums = jnp.sum(vecs, axis=0)
    me = lax.axis_index("dp")
    g_bias = lax.dynamic_slice(sums, (me * bias_rows,), (bias_rows,))
    g_norm_one = lax.dynamic_slice(sums, (mod_wide + me * gain_rows,), (gain_rows,))
    g_norm_two = lax.dynamic_slice(sums, (mod_wide + wide + me * gain_rows,), (gain_rows,))
    rest = sums[mod_wide + 2 * wide :]
    return (
        result,
        grad_tokens,
        s_attn[:, :cols],
        s_attn[:, cols : 2 * cols],
        s_attn[:, 2 * cols : 3 * cols],
        s_attn[:, 3 * cols :].T,
        s_text_key,
        s_text_value,
        s_in[:, :units],
        s_in[:, units:],
        s_down.T,
        g_ada,
        g_bias,
        g_norm_one,
        g_norm_two,
        rest[:cols],
        rest[cols : 2 * cols],
        rest[2 * cols : 3 * cols],
        rest[3 * cols : 3 * cols + heads_here],
    )


def solution(mesh):
    placed = (
        P("dp", None),
        P("dp", None),
        P("dp", None),
        P("dp"),
        P("dp", "tp"),
        P("dp", "tp"),
        P("dp", "tp"),
        P("tp", "dp"),
        P("dp", "tp"),
        P("dp", "tp"),
        P("dp", "tp"),
        P("dp", "tp"),
        P("tp", "dp"),
        P("dp", None),
        P("dp"),
        P("dp"),
        P("dp"),
        P("tp"),
        P("tp"),
        P("tp"),
        P("tp"),
        P("dp", None),
    )
    return jax.shard_map(
        on_device,
        mesh=mesh,
        in_specs=placed,
        out_specs=(
            P("dp", None),
            P("dp", None),
            P("dp", "tp"),
            P("dp", "tp"),
            P("dp", "tp"),
            P("tp", "dp"),
            P("dp", "tp"),
            P("dp", "tp"),
            P("dp", "tp"),
            P("dp", "tp"),
            P("tp", "dp"),
            P("dp", None),
            P("dp"),
            P("dp"),
            P("dp"),
            P("tp"),
            P("tp"),
            P("tp"),
            P("tp"),
        ),
        check_vma=False,
    )
```

```python
import functools
import types

import jax
import jax.numpy as jnp
import numpy as np
from jax import lax
from jax.experimental import pallas as pl
from jax.experimental.pallas import tpu as pltpu
from jax.sharding import PartitionSpec as P

HEAD = 64
FRAME_TOK = 64
EPS = 1e-06
ROPE_BASE = 10000.0
SCALE = HEAD**-0.5
MESH = pl.DeviceIdType.MESH
VMEM_LIMIT = 60 * 2**20
GRID = 8
LINE = 4
PAIR = 2 * HEAD
TP_PARTS = 8
AHEAD = 2
LAG = 3
P_1 = 1
P_2 = 0
P_3 = 4
P_4 = 4
O_1 = 2
O_2 = 2
O_3 = 1
O_4 = 1
A_A = 3
A_T = 2
A_S1 = 2
A_S0 = 2
A_S2 = 3
A_P = 2
DMA = pltpu.SemaphoreType.DMA
F32 = jnp.float32
BF16 = jnp.bfloat16


def dot_nn(left, right):
    return jnp.dot(left, right, preferred_element_type=F32)


def dot_nt(left, right):
    return lax.dot_general(left, right, (((1,), (1,)), ((), ())), preferred_element_type=F32)


def dot_tn(left, right):
    return lax.dot_general(left, right, (((0,), (0,)), ((), ())), preferred_element_type=F32)


def remote(src, dst, send, recv, **where):
    return pltpu.make_async_remote_copy(
        src_ref=src, dst_ref=dst, send_sem=send, recv_sem=recv, device_id=where, device_id_type=MESH
    )


def greet(dp_peers, tp_peers):
    barrier = pltpu.get_barrier_semaphore()
    for peer in dp_peers:
        pl.semaphore_signal(barrier, inc=1, device_id={"dp": peer}, device_id_type=MESH)
    for peer in tp_peers:
        pl.semaphore_signal(barrier, inc=1, device_id={"tp": peer}, device_id_type=MESH)
    pl.semaphore_wait(barrier, len(dp_peers) + len(tp_peers))


def dp_peers():
    me = lax.axis_index("dp")
    return [lax.rem(me + step, GRID) for step in range(1, GRID)]


def tp_peers():
    me = lax.axis_index("tp")
    return [me + 1 - 2 * lax.rem(me, 2), lax.rem(me + 2, 4)]


def aligned(value, by):
    return value if isinstance(value, int) else pl.multiple_of(value, by)


def loop(count, step):
    def body(i, carry):
        step(i)
        return carry

    lax.fori_loop(0, count, body, 0)


def add_rows(out_ref, first, *others):
    rows, wide = out_ref.shape
    tall = min(rows, 96 if wide <= 384 else 32)
    plain = len(others) == 1 and out_ref.dtype == BF16

    def step(i):
        here = pl.ds(aligned(i * tall, 16), tall)
        total = first[here, :] if plain else first[here, :].astype(F32)
        for other in others:
            total = total + (other[here, :] if plain else other[here, :].astype(F32))
        out_ref[here, :] = total.astype(out_ref.dtype)

    if rows == tall:
        step(0)
    else:
        loop(rows // tall, step)


class Blocks:
    def __init__(self, depth, wide, rows, cols, first=0):
        self.depth, self.wide, self.rows, self.cols, self.first = depth, wide, rows, cols, first
        self.down = depth // rows
        self.count = self.down * (wide // cols)

    def at(self, c):
        if isinstance(c, int):
            return c % self.down * self.rows, self.first + c // self.down * self.cols
        row = aligned(lax.rem(c, self.down) * self.rows, 16)
        col = aligned(self.first + lax.div(c, self.down) * self.cols, 128)
        return row, col

class Gather:
    def __init__(self, blocks, shard, full, sems, ahead=AHEAD):
        self.b, self.shard, self.full, self.ahead = blocks, shard, full, min(ahead, blocks.count)
        self.z_s, self.z_r, self.y_s, self.y_r, self.own_s = sems
        self.me = lax.axis_index("dp")
        self.z, self.y = self.me // 2, lax.rem(self.me, 2)
        self.lines = [lax.rem(self.z + step, LINE) for step in range(1, LINE)]
        self.ticks, self.done = blocks.count, 0

    @staticmethod
    def scratch(count):
        return [DMA((count, 3))] * 2 + [DMA((count, 4))] * 2 + [DMA((count,))]

    def own(self, c):
        row, col = self.b.at(c)
        return self.shard.at[pl.ds(row, self.b.rows), pl.ds(col, self.b.cols)]

    def place(self, c, origin):
        row, col = self.b.at(c)
        start = pl.multiple_of(origin * self.b.depth + row, 16)
        return self.full.at[pl.ds(start, self.b.rows), pl.ds(col, self.b.cols)]

    def along(self, c, i):
        there = 2 * self.lines[i] + self.y
        return remote(self.own(c), self.place(c, self.me), self.z_s.at[c, i], self.z_r.at[c, i], dp=there)

    def came_along(self, c, i):
        line = lax.rem(self.z + LINE - 1 - i, LINE)
        place = self.place(c, 2 * line + self.y)
        return line, remote(place, place, self.z_s.at[c, i], self.z_r.at[c, i], dp=self.me)

    def across(self, c, line, mine=False):
        origin = 2 * line + self.y
        src = self.own(c) if mine else self.place(c, origin)
        other = self.me + 1 - 2 * self.y
        return remote(src, self.place(c, origin), self.y_s.at[c, line], self.y_r.at[c, line], dp=other)

    def came_across(self, c, line):
        place = self.place(c, 2 * line + 1 - self.y)
        return remote(place, place, self.y_s.at[c, line], self.y_r.at[c, line], dp=self.me)

    def local(self, c):
        return pltpu.make_async_copy(self.own(c), self.place(c, self.me), self.own_s.at[c])

    def begin(self, c):
        for i in range(LINE - 1):
            self.along(c, i).start()
        self.across(c, self.z, True).start()
        self.local(c).start()

    def start(self):
        for c in range(self.ahead):
            self.begin(c)

    def pump(self, t):
        pl.when(t + self.ahead < self.b.count)(lambda: self.begin(t + self.ahead))
        for i in range(LINE - 1):
            line, came = self.came_along(t, i)
            came.wait_recv()
            self.across(t, line).start()

    def arrive(self, first=0, count=None):
        def step(i):
            c = first + i
            for line in range(LINE):
                self.came_across(c, line).wait_recv()
            self.local(c).wait()

        loop(self.b.count if count is None else count, step)

    def drain(self):
        def step(c):
            for line in range(LINE):
                self.across(c, line).wait_send()
            for i in range(LINE - 1):
                self.along(c, i).wait_send()

        loop(self.b.count, step)


class GatherChain:
    def __init__(self, blocks, shard, full, sems, ahead=AHEAD):
        self.b, self.shard, self.full, self.ahead = blocks, shard, full, min(ahead, blocks.count)
        self.up_s, self.up_r, self.dn_s, self.dn_r, self.y_s, self.y_r, self.own_s = sems
        self.me = lax.axis_index("dp")
        self.z, self.y = self.me // 2, lax.rem(self.me, 2)
        self.ticks, self.done = blocks.count + LINE - 2, 0

    @staticmethod
    def scratch(count):
        return [DMA((count, 3))] * 4 + [DMA((count, 4))] * 2 + [DMA((count,))]

    def own(self, c):
        row, col = self.b.at(c)
        return self.shard.at[pl.ds(row, self.b.rows), pl.ds(col, self.b.cols)]

    def place(self, c, origin):
        row, col = self.b.at(c)
        start = pl.multiple_of(origin * self.b.depth + row, 16)
        return self.full.at[pl.ds(start, self.b.rows), pl.ds(col, self.b.cols)]

    def up(self, c, hop):
        origin = self.me - 2 * hop
        src = self.own(c) if hop == 0 else self.place(c, origin)
        return remote(src, self.place(c, origin), self.up_s.at[c, hop], self.up_r.at[c, hop], dp=self.me + 2)

    def down(self, c, hop):
        origin = self.me + 2 * hop
        src = self.own(c) if hop == 0 else self.place(c, origin)
        return remote(src, self.place(c, origin), self.dn_s.at[c, hop], self.dn_r.at[c, hop], dp=self.me - 2)

    def across(self, c, line, mine=False):
        origin = 2 * line + self.y
        src = self.own(c) if mine else self.place(c, origin)
        other = self.me + 1 - 2 * self.y
        return remote(src, self.place(c, origin), self.y_s.at[c, line], self.y_r.at[c, line], dp=other)

    def came(self, c, origin, sems):
        return remote(self.place(c, origin), self.place(c, origin), sems, sems, dp=self.me)

    def local(self, c):
        return pltpu.make_async_copy(self.own(c), self.place(c, self.me), self.own_s.at[c])

    def begin(self, c):
        pl.when(self.z < LINE - 1)(lambda: self.up(c, 0).start())
        pl.when(self.z > 0)(lambda: self.down(c, 0).start())
        self.across(c, self.z, True).start()
        self.local(c).start()

    def start(self):
        for c in range(self.ahead):
            self.begin(c)

    def pump(self, t):
        me, z, count = self.me, self.z, self.b.count
        pl.when(t + self.ahead < count)(lambda: self.begin(t + self.ahead))
        for hop in range(LINE - 1):
            c = t - hop
            valid = (c >= 0) & (c < count)

            @pl.when(valid & (z - 1 - hop >= 0))
            def _():
                self.came(c, me - 2 * (hop + 1), self.up_r.at[c, hop]).wait_recv()
                if hop < LINE - 2:
                    pl.when(z < LINE - 1)(lambda: self.up(c, hop + 1).start())
                self.across(c, z - 1 - hop).start()

            @pl.when(valid & (z + 1 + hop <= LINE - 1))
            def _():
                self.came(c, me + 2 * (hop + 1), self.dn_r.at[c, hop]).wait_recv()
                if hop < LINE - 2:
                    pl.when(z > 0)(lambda: self.down(c, hop + 1).start())
                self.across(c, z + 1 + hop).start()

    def arrive(self, first=0, count=None):
        def step(i):
            c = first + i
            for line in range(LINE):
                self.came(c, 2 * line + 1 - self.y, self.y_r.at[c, line]).wait_recv()
            self.local(c).wait()

        loop(self.b.count if count is None else count, step)

    def drain(self):
        z = self.z

        def step(c):
            for line in range(LINE):
                self.across(c, line).wait_send()
            for hop in range(LINE - 1):
                pl.when((z < LINE - 1) & (z - hop >= 0))(lambda: self.up(c, hop).wait_send())
                pl.when((z > 0) & (z + hop <= LINE - 1))(lambda: self.down(c, hop).wait_send())

        loop(self.b.count, step)


class Scatter:
    def __init__(self, blocks, grad, out, refs, inplace=False, ahead=AHEAD):
        self.b, self.grad, self.out, self.inplace = blocks, grad, out, inplace
        self.ahead = min(ahead, blocks.count)
        self.crossed, self.landed = refs[:2]
        self.y_s, self.y_r, self.own_s, self.z_s, self.z_r = refs[2:7]
        self.held = None if inplace else refs[7]
        self.me = lax.axis_index("dp")
        self.z, self.y = self.me // 2, lax.rem(self.me, 2)
        self.lines = [lax.rem(self.z + step, LINE) for step in range(1, LINE)]
        self.ticks, self.done = blocks.count + LAG, 0

    @staticmethod
    def scratch(blocks, inplace=False):
        shape = (blocks.rows, blocks.cols)
        count = blocks.count
        bufs = [pltpu.VMEM((count, lines) + shape, BF16) for lines in (4, 3)]
        held = [] if inplace else [pltpu.VMEM((count, 4) + shape, BF16)]
        return bufs + [DMA((count,))] * 3 + [DMA((count, 3))] * 2 + held

    def part(self, c, row_y):
        row, col = self.b.at(c)
        return self.grad.at[:, row_y, pl.ds(row, self.b.rows), pl.ds(col, self.b.cols)]

    def hold(self, c, line):
        if not self.inplace:
            return self.held.at[c, line]
        row, col = self.b.at(c)
        return self.grad.at[line, self.y, pl.ds(row, self.b.rows), pl.ds(col, self.b.cols)]

    def across(self, c):
        other = self.me + 1 - 2 * self.y
        return remote(self.part(c, 1 - self.y), self.crossed.at[c], self.y_s.at[c], self.y_r.at[c], dp=other)

    def load(self, c):
        return pltpu.make_async_copy(self.part(c, self.y), self.held.at[c], self.own_s.at[c])

    def along(self, c, i):
        line = self.lines[i]
        return remote(
            self.hold(c, line), self.landed.at[c, i], self.z_s.at[c, i], self.z_r.at[c, i], dp=2 * line + self.y
        )

    def begin(self, c):
        self.across(c).start()
        if not self.inplace:
            self.load(c).start()

    def start(self):
        for c in range(self.ahead):
            self.begin(c)

    def fold(self, c):
        self.across(c).wait_recv()
        if not self.inplace:
            self.load(c).wait()
        for i in (1, 0, 2):
            line = self.lines[i]
            add_rows(self.hold(c, line), self.hold(c, line), self.crossed.at[c, line])
            self.along(c, i).start()

    def finish(self, c):
        row, col = self.b.at(c)
        for i in range(LINE - 1):
            self.along(c, i).wait_recv()
        out_col = aligned(col - self.b.first, 128)
        out = self.out.at[pl.ds(row, self.b.rows), pl.ds(out_col, self.b.cols)]
        landed = [self.landed.at[c, i] for i in range(LINE - 1)]
        add_rows(out, self.hold(c, self.z), self.crossed.at[c, self.z], *landed)

    def pump(self, t):
        pl.when(t + self.ahead < self.b.count)(lambda: self.begin(t + self.ahead))
        pl.when(t < self.b.count)(lambda: self.fold(t))
        pl.when(t >= LAG)(lambda: self.finish(t - LAG))

    def drain(self):
        def step(c):
            self.across(c).wait_send()
            for i in range(LINE - 1):
                self.along(c, i).wait_send()

        loop(self.b.count, step)


class Idle:
    ticks = done = 0

    def start(self):
        pass

    def pump(self, t):
        pass

    def arrive(self):
        pass

    def drain(self):
        pass


class TpSum:
    def __init__(self, partial, out, bufs, sems, own_sems=None):
        self.p, self.out = partial, out
        self.crossed, self.other = bufs
        self.c_s, self.c_r, self.x_s, self.x_r, self.o_s, self.o_r = sems
        self.core = lax.rem(lax.axis_index("tp"), 2)
        self.beside, self.far = tp_peers()
        self.half = partial.shape[0] // 2
        self.rows = self.half // TP_PARTS
        self.own_s = own_sems

    @staticmethod
    def scratch(rows, wide):
        return [pltpu.VMEM((rows // 2, wide), BF16)] * 2 + [DMA((TP_PARTS,))] * 6

    def spot(self, k, which):
        return pl.ds(pl.multiple_of(which * self.half + k * self.rows, 16), self.rows)

    def part(self, k):
        return pl.ds(aligned(k * self.rows, 16), self.rows)

    def first(self, k):
        return remote(
            self.p.at[self.spot(k, 1 - self.core)],
            self.crossed.at[self.part(k)],
            self.c_s.at[k],
            self.c_r.at[k],
            tp=self.beside,
        )

    def second(self, k):
        here = self.out.at[self.spot(k, self.core)]
        return remote(here, self.other.at[self.part(k)], self.x_s.at[k], self.x_r.at[k], tp=self.far)

    def third(self, k, which):
        here = self.out.at[self.spot(k, which)]
        return remote(here, here, self.o_s.at[k], self.o_r.at[k], tp=self.beside)

    def load(self, k):
        mine = self.spot(k, self.core)
        return pltpu.make_async_copy(self.p.at[mine], self.out.at[mine], self.own_s.at[k])

    def stage_one(self, k):
        self.first(k).start()
        if self.own_s is not None:
            self.load(k).start()

    def stage_two(self, k):
        self.first(k).wait_recv()
        mine = self.spot(k, self.core)
        held = self.p.at[mine]
        if self.own_s is not None:
            self.load(k).wait()
            held = self.out.at[mine]
        add_rows(self.out.at[mine], held, self.crossed.at[self.part(k)])
        self.second(k).start()

    def stage_three(self, k):
        self.second(k).wait()
        mine = self.out.at[self.spot(k, self.core)]
        add_rows(mine, mine, self.other.at[self.part(k)])
        self.third(k, self.core).start()

    def stage_four(self, k):
        self.third(k, 1 - self.core).wait_recv()

    def sent(self, k):
        self.third(k, self.core).wait_send()

    def drain(self, sent=False):
        def step(k):
            self.first(k).wait_send()
            if not sent:
                self.sent(k)

        loop(TP_PARTS, step)


def params(number):
    return pltpu.CompilerParams(
        collective_id=number, has_side_effects=True, vmem_limit_bytes=VMEM_LIMIT
    )


def plain_params():
    return pltpu.CompilerParams(vmem_limit_bytes=VMEM_LIMIT)


ANY = pl.BlockSpec(memory_space=pl.ANY)
IN_VMEM = pl.BlockSpec(memory_space=pltpu.VMEM)
IN_SMEM = pl.BlockSpec(memory_space=pltpu.SMEM)


def shaped(shape, dtype):
    return jax.ShapeDtypeStruct(shape, dtype)


def segment_sum(value, seg):
    high = value.astype(BF16)
    low = (value - high.astype(F32)).astype(BF16)
    return dot_nn(high, seg) + dot_nn(low, seg)


def head_inverse(value, seg):
    return lax.rsqrt(segment_sum(value * value, seg) * (1.0 / HEAD) + EPS)


def thrice(table):
    return jnp.concatenate([table] * 3, axis=1)


def rope(value, cosines, sine_a, sine_b):
    wide = value.shape[1]
    ahead = pltpu.roll(value, wide - HEAD // 4, 1)
    behind = pltpu.roll(value, HEAD // 4, 1)
    return value * cosines + ahead * sine_a + behind * sine_b


def rope_back(grad, cosines, sine_a, sine_b):
    wide = grad.shape[1]
    ahead = pltpu.roll(grad * sine_b, wide - HEAD // 4, 1)
    behind = pltpu.roll(grad * sine_a, HEAD // 4, 1)
    return grad * cosines + ahead + behind


def rope_tables(row_count):
    lane = np.arange(PAIR)
    within = lane % HEAD
    quarter = HEAD // 4
    which = within // quarter
    freqs = (ROPE_BASE ** (-(within % quarter).astype(np.float32) / np.float32(quarter))).astype(np.float32)
    row = np.arange(row_count)
    frame, place = (row // FRAME_TOK).astype(np.float32), (row % FRAME_TOK).astype(np.float32)
    position = np.where(which[None, :] < 2, frame[:, None], place[:, None])
    angles = (position * freqs[None, :]).astype(np.float32)
    cosines, sines = np.cos(angles), np.sin(angles)
    even = (which % 2 == 0)[None, :]
    return (
        jnp.asarray(cosines.astype(np.float32)),
        jnp.asarray(np.where(even, -sines, 0.0).astype(np.float32)),
        jnp.asarray(np.where(even, 0.0, sines).astype(np.float32)),
    )


def segment_ones(wide):
    head = np.arange(wide) // HEAD
    return jnp.asarray((head[:, None] == head[None, :]).astype(np.float32)).astype(BF16)


def live_rows(frames_ref, start, rows, wide):
    row = start + lax.broadcasted_iota(jnp.int32, (rows, wide), 0)
    return (row < frames_ref[0] * FRAME_TOK).astype(F32)


def half_mask(rows, head, dtype):
    lane = lax.broadcasted_iota(jnp.int32, (rows, PAIR), 1)
    return ((lane < HEAD) if head == 0 else (lane >= HEAD)).astype(dtype)


def pair_lanes(pair, wide=PAIR):
    return pl.ds(pl.multiple_of(pair * wide, PAIR), wide)


def block_rows(block, rows):
    return pl.ds(pl.multiple_of(block * rows, rows), rows)


def paced(count, step, *plans):
    jobs = []
    for engine, pumps in plans:
        pumps = min(pumps, engine.ticks - engine.done)
        if pumps > 0:
            jobs.append((engine, pumps, engine.done))
            engine.done += pumps

    def body(i):
        step(i)
        for engine, pumps, base in jobs:
            if pumps <= count:
                every = count // pumps
                turn = lax.div(i, every)
                now = (lax.rem(i, every) == every - 1) & (turn < pumps)
                pl.when(now)(functools.partial(engine.pump, base + turn))
            else:
                each = -(-pumps // count)
                for j in range(each):
                    pl.when(i * each + j < pumps)(functools.partial(engine.pump, base + i * each + j))

    loop(count, body)


def finish_pumps(engine):
    base = engine.done
    if base < engine.ticks:
        loop(engine.ticks - base, lambda i: engine.pump(base + i))
    engine.done = engine.ticks


class Named:
    def __init__(self):
        self.ins, self.outs, self.scratch = {}, {}, {}

    def take(self, refs):
        found, at = {}, 0
        for name in (*self.ins, *self.outs):
            found[name] = refs[at]
            at += 1
        for name, item in self.scratch.items():
            many = isinstance(item, list)
            found[name] = refs[at : at + len(item)] if many else refs[at]
            at += len(item) if many else 1
        return types.SimpleNamespace(**found)

    def call(self, kernel, compiler_params):
        flat = []
        for item in self.scratch.values():
            flat += item if isinstance(item, list) else [item]
        results = pl.pallas_call(
            kernel,
            out_shape=[shape for shape, _ in self.outs.values()],
            in_specs=[spec for _, spec in self.ins.values()],
            out_specs=[spec for _, spec in self.outs.values()],
            scratch_shapes=flat,
            compiler_params=compiler_params,
        )(*[value for value, _ in self.ins.values()])
        return types.SimpleNamespace(**dict(zip(self.outs, results)))


class Opening:
    def __init__(self, r):
        self.r = r
        self.me, self.tp = lax.axis_index("dp"), lax.axis_index("tp")
        self.peers, (self.beside, self.far) = dp_peers(), tp_peers()
        self.sources = [lax.rem(self.me + GRID - step, GRID) for step in range(1, GRID)]
        self.share = r.text_all.shape[1] // 4
        self.cond, self.small, self.parts, self.slabs, self.quarters = (r.sems_set[2 * i : 2 * i + 2] for i in range(5))
        self.own_s = r.sems_set[10]

    def send(self, sems, i, src, dst, **where):
        return remote(src, dst, sems[0].at[i], sems[1].at[i], **where)

    def quarter(self, which):
        rows = pl.ds(pl.multiple_of(which * self.share, 16), self.share)
        return self.r.text_all.at[:, rows, :]

    def slab(self, there, origin):
        depth = self.r.text_all.shape[2]
        rows = pl.ds(pl.multiple_of(self.tp * self.share, 16), self.share)
        src = self.r.text.at[rows, pl.ds(pl.multiple_of(there * depth, 128), depth)]
        return src, self.r.text_all.at[origin, rows, :]

    def cond_out(self, i):
        there = self.peers[i]
        return self.send(self.cond, i, self.r.cond.at[there], self.r.conds.at[self.me], dp=there)

    def small_out(self, i):
        return self.send(self.small, i, self.r.small, self.r.smalls.at[self.me], dp=self.peers[i])

    def slab_out(self, i):
        return self.send(self.slabs, i, *self.slab(self.peers[i], self.me), dp=self.peers[i])

    def part_out(self, i):
        there = self.peers[i]
        return self.send(self.parts, i, self.r.part.at[there], self.r.parts.at[self.me], dp=there)

    def came(self, sems, i, ref):
        self.send(sems, i, ref, ref, dp=self.me).wait_recv()

    def begin(self):
        r, me = self.r, self.me
        for i in range(GRID - 1):
            self.cond_out(i).start()
            self.small_out(i).start()
        for i in range(GRID - 1):
            self.slab_out(i).start()
        pltpu.make_async_copy(*self.slab(me, me), self.own_s).start()
        r.conds[pl.ds(me, 1)] = r.cond[pl.ds(me, 1)]
        r.smalls[pl.ds(me, 1)] = r.small[...][None]

    def partial_rows(self):
        r, me = self.r, self.me
        for i, here in enumerate(self.sources):
            self.came(self.cond, i, r.conds.at[here])
        cond = jnp.concatenate([r.conds[i] for i in range(GRID)], axis=0)
        act = (cond * (1.0 / (1.0 + jnp.exp(-cond)))).astype(BF16)
        r.act[...] = act.astype(F32)
        width = r.w_ada.shape[1] // 4
        for i in range(4):
            cols = pl.ds(i * width, width)
            product = dot_nn(act, r.w_ada[:, cols])
            for j in range(GRID):
                r.part[j, :, cols] = product[j : j + 1, :]
        for i in range(GRID - 1):
            self.part_out(i).start()
        r.parts[pl.ds(me, 1)] = r.part[pl.ds(me, 1)]

    def spread(self):
        pltpu.make_async_copy(*self.slab(self.me, self.me), self.own_s).wait()
        for i, here in enumerate(self.sources):
            self.came(self.slabs, i, self.slab(here, here)[1])
        mine = self.quarter(self.tp)
        self.send(self.quarters, 0, mine, mine, tp=self.beside).start()
        self.send(self.quarters, 1, mine, mine, tp=self.far).start()

    def modulate(self):
        r = self.r
        for i, here in enumerate(self.sources):
            self.came(self.parts, i, r.parts.at[here])
            self.came(self.small, i, r.smalls.at[here])
        wide = r.rows.shape[1]
        bias = r.small.shape[1] - 2 * (wide // GRID)
        ends = r.small.shape[1]
        smalls = [r.smalls[i] for i in range(GRID)]
        mods = sum(r.parts[i] for i in range(GRID)) + jnp.concatenate([v[:, :bias] for v in smalls], axis=1)
        gain_one = jnp.concatenate([v[:, bias : bias + wide // GRID] for v in smalls], axis=1)
        gain_two = jnp.concatenate([v[:, bias + wide // GRID : ends] for v in smalls], axis=1)
        lift_one, lift_two = 1.0 + mods[:, :wide], 1.0 + mods[:, 2 * wide : 3 * wide]
        tanh_one, tanh_two = jnp.tanh(mods[:, wide : 2 * wide]), jnp.tanh(mods[:, 3 * wide :])
        values = (gain_one * lift_one, tanh_one, gain_two * lift_two, tanh_two, gain_one, lift_one, gain_two, lift_two)
        for i, value in enumerate(values):
            r.rows[i : i + 1, :] = value

    def pass_on(self):
        from_far = self.quarter(lax.rem(self.tp + 2, 4))
        self.send(self.quarters, 1, from_far, from_far, tp=self.far).wait_recv()
        self.send(self.quarters, 2, from_far, from_far, tp=self.beside).start()

    def collect(self):
        near = self.quarter(self.tp + 1 - 2 * lax.rem(self.tp, 2))
        self.send(self.quarters, 0, near, near, tp=self.beside).wait_recv()
        self.send(self.quarters, 2, near, near, tp=self.beside).wait_recv()

    def multiply(self, i):
        r = self.r
        cols = r.w_tk.shape[1]
        rows = r.text_all[i]
        line, y = lax.div(i, 2), lax.rem(i, 2)
        r.products[line, y, :, :cols] = dot_nn(rows, r.w_tk[...]).astype(BF16)
        r.products[line, y, :, cols:] = dot_nn(rows, r.w_tv[...]).astype(BF16)

    def drain(self):
        mine = self.quarter(self.tp)
        self.send(self.quarters, 0, mine, mine, tp=self.beside).wait_send()
        self.send(self.quarters, 1, mine, mine, tp=self.far).wait_send()
        self.send(self.quarters, 2, mine, mine, tp=self.beside).wait_send()
        for i in range(GRID - 1):
            self.cond_out(i).wait_send()
            self.small_out(i).wait_send()
            self.slab_out(i).wait_send()
            self.part_out(i).wait_send()


def forward_kernel(named, grid, cuts, *refs):
    r = named.take(refs)
    tok, weights, rows_ref, heads_ref = r.tok, r.weights, r.rows, r.heads
    cos_ref, sa_ref, sb_ref, seg_ref = r.cos, r.sa, r.sb, r.seg
    attn_sum, partial, mixed, ty = r.attn_sum, r.partial, r.mixed, r.ty
    sums = TpSum(partial, attn_sum, r.tp_set[:2], r.tp_set[2:8])
    mult, tanh_attn, mult_two = rows_ref.at[0:1], rows_ref.at[1:2], rows_ref.at[2:3]
    qgain, kgain, kygain, gate = (heads_ref.at[i : i + 1] for i in range(4))
    rows, cols = r.q_rot.shape
    step_rows = 256
    blocks_here = rows // step_rows
    pairs = cols // PAIR
    attn_engine = text_engine = engine = Idle()
    if grid:
        opening = Opening(r)
        attn_engine = GatherChain(cuts[0], r.attn_shard, weights, r.attn_set, A_A)
        text_engine = Scatter(cuts[1], r.products, ty, r.text_set, True, ahead=A_P)
        engine = GatherChain(cuts[2], r.ffn_shard, r.full_ffn, r.ffn_set)
        greet(dp_peers(), tp_peers())
        opening.begin()
        attn_engine.start()
        opening.partial_rows()
        paced(1, lambda i: None, (attn_engine, O_1))
        opening.spread()
        paced(1, lambda i: None, (attn_engine, O_2))
        opening.modulate()
        paced(1, lambda i: None, (attn_engine, O_3))
        opening.pass_on()
        paced(1, lambda i: None, (attn_engine, O_4))
        opening.collect()
        paced(GRID, opening.multiply, (attn_engine, 2))
        text_engine.start()
        engine.start()
        finish_pumps(attn_engine)
        attn_engine.arrive()
    else:
        greet([], tp_peers())

    def project(i):
        here = block_rows(i, step_rows)
        x = tok[here, :].astype(F32)
        inverse = lax.rsqrt(jnp.mean(x * x, axis=-1, keepdims=True) + EPS)
        h = (x * inverse * mult[...]).astype(BF16)
        r.h_one[here, :] = h
        cosines, sine_a, sine_b = thrice(cos_ref[here, :]), thrice(sa_ref[here, :]), thrice(sb_ref[here, :])
        q = dot_nn(h, weights[:, :cols])
        r.q_pre[here, :] = q
        qn = q * head_inverse(q, seg_ref[...]) * qgain[...]
        r.q_text[here, :] = (qn * SCALE).astype(BF16)
        r.q_rot[here, :] = (rope(qn, cosines, sine_a, sine_b) * SCALE).astype(BF16)
        k = dot_nn(h, weights[:, cols : 2 * cols])
        r.k_pre[here, :] = k
        kn = k * head_inverse(k, seg_ref[...]) * kgain[...]
        r.k_rot[here, :] = rope(kn, cosines, sine_a, sine_b).astype(BF16)
        v = dot_nn(h, weights[:, 2 * cols : 3 * cols]).astype(BF16)
        r.values[here, :] = v
        live = live_rows(r.frames, i * step_rows, step_rows, PAIR).astype(BF16)
        for pair in range(pairs):
            r.vaug[here, 2 * pair * PAIR : (2 * pair + 1) * PAIR] = v[:, pair * PAIR : (pair + 1) * PAIR] * live
            r.vaug[here, (2 * pair + 1) * PAIR : (2 * pair + 2) * PAIR] = live

    def attention(q_ref, k_ref, v_ref, inv_ref):
        def step(i):
            pair, block = lax.div(i, blocks_here), lax.rem(i, blocks_here)
            here, lanes = block_rows(block, step_rows), pair_lanes(pair)
            q = q_ref[here, lanes]
            keys = k_ref[:, lanes]
            values = v_ref[:, pair_lanes(pair, 2 * PAIR)]
            outs = jnp.zeros((step_rows, PAIR), F32)
            total = jnp.zeros((step_rows, PAIR), F32)
            for head in range(2):
                p = jnp.exp(dot_nt(q * half_mask(step_rows, head, BF16), keys)).astype(BF16)
                both = dot_nn(p, values)
                wide_mask = half_mask(step_rows, head, F32)
                outs = outs + both[:, :PAIR] * wide_mask
                total = total + both[:, PAIR:] * wide_mask
            inverse = 1.0 / total
            inv_ref[here, lanes] = inverse
            return here, lanes, outs * inverse

        return step

    self_attention = attention(r.q_rot, r.k_rot, r.vaug, r.inv_l)
    text_attention = attention(r.q_text, r.kyr, r.vyaug, r.inv_lt)

    def attend(i):
        here, lanes, out = self_attention(i)
        r.mixed_self[here, lanes] = out
        r.self_o[here, lanes] = out.astype(BF16)

    def attend_text(i):
        here, lanes, out = text_attention(i)
        r.text_o[here, lanes] = out.astype(BF16)
        mixed[here, lanes] = (r.mixed_self[here, lanes] + gate[:, lanes] * out).astype(BF16)

    half_blocks = blocks_here // 2
    parts_each = TP_PARTS // half_blocks

    def output(which):
        def step(i):
            block = which * half_blocks + i
            for pair in range(pairs):
                attend_text(pair * blocks_here + block)
            here = block_rows(block, step_rows)
            partial[here, :] = dot_nt(mixed[here, :], weights[:, 3 * cols :]).astype(BF16)

        return step

    def output_send(i):
        output(1 - sums.core)(i)
        loop(parts_each, lambda k: sums.stage_one(i * parts_each + k))

    def output_add(i):
        output(sums.core)(i)
        loop(parts_each, lambda k: sums.stage_two(i * parts_each + k))

    paced(blocks_here, project, (text_engine, 4), (engine, 2))
    paced(pairs * blocks_here, attend, (text_engine, 4), (engine, 3))
    finish_pumps(text_engine)

    ky = ty[:, :cols]
    r.ky_pre[...] = ky
    r.kyr[...] = (ky * head_inverse(ky, seg_ref[...]) * kygain[...]).astype(BF16)
    vy = ty[:, cols:].astype(BF16)
    r.vy[...] = vy
    for pair in range(pairs):
        r.vyaug[:, 2 * pair * PAIR : (2 * pair + 1) * PAIR] = vy[:, pair * PAIR : (pair + 1) * PAIR]
        r.vyaug[:, (2 * pair + 1) * PAIR : (2 * pair + 2) * PAIR] = jnp.ones((vy.shape[0], PAIR), BF16)
    paced(half_blocks, output_send, (engine, 2))
    paced(half_blocks, output_add, (engine, 2))

    def update(k, which):
        here = sums.spot(k, which)
        live = live_rows(r.frames, which * sums.half + k * sums.rows, sums.rows, tok.shape[1])
        state = tok[here, :].astype(F32) + live * tanh_attn[...] * attn_sum[here, :].astype(F32)
        inverse = lax.rsqrt(jnp.mean(state * state, axis=-1, keepdims=True) + EPS)
        r.h_two[here, :] = (state * inverse * mult_two[...]).astype(BF16)

    def three(k):
        sums.stage_three(k)
        update(k, sums.core)

    paced(TP_PARTS, three, (engine, 4))

    def four(k):
        sums.stage_four(k)
        update(k, 1 - sums.core)

    paced(TP_PARTS, four, (engine, 1))
    finish_pumps(engine)
    engine.arrive()
    sums.drain()
    if grid:
        opening.drain()
    attn_engine.drain()
    text_engine.drain()
    engine.drain()


def forward(clips, frames, tokens, heads_table, tables, seg, ffn_shard, start):
    rows, wide = tokens.shape
    cols = heads_table.shape[1]
    grid = clips == GRID
    depth, ffn_wide = ffn_shard.shape
    n = Named()
    n.ins.update(frames=(frames, IN_SMEM), tok=(tokens, IN_VMEM), heads=(heads_table, IN_VMEM))
    n.ins.update(cos=(tables[0], IN_VMEM), sa=(tables[1], IN_VMEM), sb=(tables[2], IN_VMEM), seg=(seg, IN_VMEM))
    cuts = None
    if grid:
        attn_shard, cond, small, w_ada, text, w_tk, w_tv = start
        rows_t, slab = text.shape[0], w_tk.shape[0]
        mods = w_ada.shape[1]
        n.ins.update(attn_shard=(attn_shard, ANY), cond=(cond, IN_VMEM), small=(small, IN_VMEM))
        n.ins.update(w_ada=(w_ada, IN_VMEM), text=(text, ANY), w_tk=(w_tk, IN_VMEM), w_tv=(w_tv, IN_VMEM))
        n.ins.update(ffn_shard=(ffn_shard, ANY))
        cuts = (
            Blocks(*attn_shard.shape, 96, 384),
            Blocks(rows_t, 2 * cols, 32, 2 * cols),
            Blocks(depth, ffn_wide, 96, 384),
        )
    else:
        weights, rows_table, ty = start
        rows_t = ty.shape[0]
        n.ins.update(weights=(weights, IN_VMEM), rows=(rows_table, IN_VMEM), ty=(ty, IN_VMEM))
    f, b = (shaped((rows, cols), F32), IN_VMEM), (shaped((rows, cols), BF16), IN_VMEM)
    ft, bt = (shaped((rows_t, cols), F32), IN_VMEM), (shaped((rows_t, cols), BF16), IN_VMEM)
    whole = (shaped((rows, wide), BF16), IN_VMEM)
    n.outs.update(q_pre=f, k_pre=f, q_rot=b, k_rot=b, q_text=b, values=b, self_o=b, inv_l=f, ky_pre=ft, kyr=bt, vy=bt)
    n.outs.update(text_o=b, inv_lt=f, h_one=whole, mixed=b, attn_sum=whole, h_two=whole)
    n.scratch.update(
        vaug=pltpu.VMEM((rows, 2 * cols), BF16),
        vyaug=pltpu.VMEM((rows_t, 2 * cols), BF16),
        partial=pltpu.VMEM((rows, wide), BF16),
        mixed_self=pltpu.VMEM((rows, cols), F32),
        tp_set=TpSum.scratch(rows, wide),
    )
    if grid:
        n.outs.update(
            weights=(shaped((GRID * attn_shard.shape[0], attn_shard.shape[1]), BF16), IN_VMEM),
            rows=(shaped((8, wide), F32), IN_VMEM),
            act=(shaped((GRID, cond.shape[2]), F32), IN_VMEM),
            text_all=(shaped((GRID, rows_t, slab), BF16), IN_VMEM),
            full_ffn=(shaped((GRID * depth, ffn_wide), BF16), ANY),
        )
        n.scratch.update(
            ty=pltpu.VMEM((rows_t, 2 * cols), F32),
            products=pltpu.VMEM((LINE, 2, rows_t, 2 * cols), BF16),
            smalls=pltpu.VMEM((GRID,) + small.shape, F32),
            conds=pltpu.VMEM((GRID, 1, cond.shape[2]), F32),
            part=pltpu.VMEM((GRID, 1, mods), F32),
            parts=pltpu.VMEM((GRID, 1, mods), F32),
            sems_set=[DMA((GRID - 1,))] * 8 + [DMA((3,))] * 2 + [DMA],
            attn_set=GatherChain.scratch(cuts[0].count),
            text_set=Scatter.scratch(cuts[1], True),
            ffn_set=GatherChain.scratch(cuts[2].count),
        )
    out = n.call(functools.partial(forward_kernel, n, grid, cuts), params(1))
    if not grid:
        out.weights, out.rows, out.text_all = weights, rows_table, jnp.zeros((1, 16, 128), BF16)
    return out


UNITS = 256
ONES = 3


def ffn_kernel(named, cut, cut_back, *refs):
    r = named.take(refs)
    engine, scatter = Idle(), Idle()
    if cut is not None:
        engine = GatherChain(cut, r.shard, r.w_two, r.gather_set)
        scatter = Scatter(cut_back, r.grads, r.out, r.scatter_set)
        greet(dp_peers(), [])
        engine.start()
    rows, wide = r.h_two.shape
    step_rows = 256
    count = rows // step_rows
    tall = wide // LINE
    tanh_two = r.rows[3:4, :]
    ones, twos = r.w_one.shape[1] // (3 * UNITS), r.w_two.shape[1] // (3 * UNITS)

    def start_rows(i):
        here = block_rows(i, step_rows)
        live = live_rows(r.frames, i * step_rows, step_rows, wide)
        r.grad_ffn[here, :] = (live * tanh_two * r.cot[here, :].astype(F32)).astype(BF16)

    def copy(b):
        place = r.grads.at[:, :, :, pl.ds(b * 3 * UNITS, 3 * UNITS)]
        return pltpu.make_async_copy(r.staged.at[b % 2], place, r.stage_s.at[b % 2])

    def block(b):
        w = r.w_one if b < ones else r.w_two
        first = (b if b < ones else b - ones) * 3 * UNITS
        last = b == ones + twos - 1
        dgu = r.dgu_last if last else r.dgu

        def units(i):
            here = block_rows(i, step_rows)
            both = dot_nn(r.h_two[here, :], w[:, first : first + 2 * UNITS])
            gate, up = both[:, :UNITS], both[:, UNITS:]
            back = dot_nn(r.grad_ffn[here, :], w[:, first + 2 * UNITS : first + 3 * UNITS])
            logistic = 1.0 / (1.0 + jnp.exp(-gate))
            swish = gate * logistic
            r.hid[here, b * UNITS : (b + 1) * UNITS] = (swish * up).astype(BF16)
            d_gate = (back * up * logistic * (1.0 + gate * (1.0 - logistic))).astype(BF16)
            d_both = jnp.concatenate([d_gate, (back * swish).astype(BF16)], axis=1)
            dgu[here, :] = d_both
            added = dot_nt(d_both, w[:, first : first + 2 * UNITS])
            if b == 0:
                r.total[here, :] = added
            elif not last:
                r.total[here, :] += added
            else:
                r.partial[here, :] = (r.total[here, :] + added).astype(BF16)

        def products(m):
            lanes = pl.ds(pl.multiple_of(m * tall, 128), tall)
            downs = dot_tn(r.grad_ffn[:, lanes], r.hid[:, b * UNITS : (b + 1) * UNITS]).astype(BF16)
            ins = dot_tn(r.h_two[:, lanes], dgu[...]).astype(BF16)
            for y in range(2):
                part = slice(y * tall // 2, (y + 1) * tall // 2)
                r.staged[b % 2, m, y, :, : 2 * UNITS] = ins[part]
                r.staged[b % 2, m, y, :, 2 * UNITS :] = downs[part]

        pumps = 1 if b < ones else 2
        paced(count, units, (engine, pumps), (scatter, 2 if b > 0 else 0))
        if not last:
            if b >= 2 and (b > 2 or cut is None):
                copy(b - 2).wait()
            paced(LINE, products, (engine, pumps), (scatter, 2 if b > 0 else 0))
            copy(b).start()
        if b == 0 and cut is not None:
            copy(0).wait()
            scatter.start()

    paced(count, start_rows, (engine, 1))
    each = cut.count // twos if cut is not None else 0
    for b in range(ones):
        block(b)
    for b in range(ones, ones + twos):
        if cut is not None:
            need = min(engine.ticks, (b - ones + 1) * each + 2)
            while engine.done < need:
                paced(1, lambda i: None, (engine, 1))
            engine.arrive((b - ones) * each, each)
        block(b)
    copy(ones + twos - 3).wait()
    copy(ones + twos - 2).wait()
    finish_pumps(scatter)
    scatter.drain()
    engine.drain()


def ffn(clips, frames, h_two, cotangent, rows_table, w_one, second):
    rows, wide = h_two.shape
    half_wide = second.shape[1]
    blocks = (w_one.shape[1] + half_wide) // (3 * UNITS)
    grid = clips == GRID
    depth = wide // GRID
    n = Named()
    n.ins.update(frames=(frames, IN_SMEM), h_two=(h_two, IN_VMEM), cot=(cotangent, IN_VMEM), rows=(rows_table, IN_VMEM))
    n.ins.update(w_one=(w_one, IN_VMEM))
    whole = (shaped((rows, wide), BF16), IN_VMEM)
    cut = Blocks(depth, half_wide, 96, 384) if grid else None
    cut_back = None
    if grid:
        n.ins.update(shard=(second, ANY))
        cut_back = Blocks(depth, 3 * UNITS, 96, 256)
        n.outs.update(w_two=(shaped((wide, half_wide), BF16), IN_VMEM), out=(shaped((depth, 3 * UNITS), F32), IN_VMEM))
        n.scratch.update(gather_set=GatherChain.scratch(cut.count), scatter_set=Scatter.scratch(cut_back))
    else:
        n.ins.update(w_two=(second, IN_VMEM))
    n.outs.update(partial=whole, grad_ffn=whole, hid=(shaped((rows, blocks * UNITS), BF16), IN_VMEM))
    n.outs.update(dgu_last=(shaped((rows, 2 * UNITS), BF16), IN_VMEM))
    n.outs.update(grads=(shaped((LINE, 2, depth, (blocks - 1) * 3 * UNITS), BF16), ANY))
    n.scratch.update(
        dgu=pltpu.VMEM((rows, 2 * UNITS), BF16),
        total=pltpu.VMEM((rows, wide), F32),
        staged=pltpu.VMEM((2, LINE, 2, depth, 3 * UNITS), BF16),
        stage_s=DMA((2,)),
    )
    out = n.call(functools.partial(ffn_kernel, n, cut, cut_back), params(5) if grid else plain_params())
    if not grid:
        out.w_two = second
    return out


def state_kernel(named, cut, *refs):
    r = named.take(refs)
    sums = TpSum(r.partial, r.grad_attn, r.tp_set[:2], r.tp_set[2:8], r.tp_set[8])
    tanh_attn, mult = r.rows.at[1:2], r.rows.at[2:3]
    engine = Idle()
    if cut is not None:
        engine = Scatter(cut, r.grads, r.out, r.scatter_set, ahead=A_S0)
        greet(dp_peers(), tp_peers())
        engine.start()
    else:
        greet([], tp_peers())
    loop(TP_PARTS, sums.stage_one)
    rows, wide = r.tok.shape
    step_rows = 256
    tall = wide // LINE
    blocks = r.hid.shape[1] // UNITS
    ones = r.w_one.shape[1] // (3 * UNITS)

    def down_copy(b):
        w = r.w_one if b < ones else r.w_two
        first = (b if b < ones else b - ones) * 3 * UNITS + 2 * UNITS
        place = r.down.at[:, pl.ds(b * UNITS, UNITS)]
        return pltpu.make_async_copy(w.at[:, pl.ds(first, UNITS)], place, r.down_s.at[b])

    for b in range(blocks):
        down_copy(b).start()
    r.colsums[...] = jnp.zeros_like(r.colsums)

    def products(m):
        lanes = pl.ds(pl.multiple_of(m * tall, 128), tall)
        downs = dot_tn(r.grad_ffn[:, lanes], r.hid[:, (blocks - 1) * UNITS :]).astype(BF16)
        ins = dot_tn(r.h_two[:, lanes], r.dgu[...]).astype(BF16)
        for y in range(2):
            part = slice(y * tall // 2, (y + 1) * tall // 2)
            r.g_last[m, y, :, : 2 * UNITS] = ins[part]
            r.g_last[m, y, :, 2 * UNITS :] = downs[part]

    def p_copy(i):
        place = r.p_ffn.at[block_rows(i, step_rows)]
        return pltpu.make_async_copy(r.p_staged.at[lax.rem(i, 2)], place, r.p_s.at[lax.rem(i, 2)])

    def p_block(i):
        pl.when(i >= 2)(lambda: p_copy(i - 2).wait())
        r.p_staged[lax.rem(i, 2)] = dot_nt(r.hid[block_rows(i, step_rows), :], r.down[...]).astype(BF16)
        p_copy(i).start()

    def update(k, which):
        here = sums.spot(k, which)
        live = live_rows(r.frames, which * sums.half + k * sums.rows, sums.rows, wide)
        added = r.attn_sum[here, :].astype(F32)
        state = r.tok[here, :].astype(F32) + live * tanh_attn[...] * added
        inverse = lax.rsqrt(jnp.mean(state * state, axis=-1, keepdims=True) + EPS)
        hat = state * inverse
        g = r.grad_attn[here, :].astype(F32)
        scaled = g * mult[...]
        g_hat = g * hat
        back = inverse * (scaled - hat * jnp.mean(scaled * hat, axis=-1, keepdims=True))
        total = r.cot[here, :].astype(F32) + back
        r.grad_state[here, :] = total.astype(BF16)
        live_total = live * total
        r.grad_attn[here, :] = (tanh_attn[...] * live_total).astype(BF16)
        r.colsums[0:1, :] += jnp.sum(g_hat, axis=0, keepdims=True)
        r.colsums[1:2, :] += jnp.sum(live_total * added, axis=0, keepdims=True)

    paced(TP_PARTS, sums.stage_two, (engine, 2))
    paced(LINE, products, (engine, 2))
    for b in range(blocks):
        down_copy(b).wait()
    paced(rows // step_rows, p_block, (engine, 2))

    def three(k):
        sums.stage_three(k)

        @pl.when(k > 0)
        def _():
            sums.sent(k - 1)
            update(k - 1, sums.core)

    paced(TP_PARTS, three, (engine, 8))
    sums.sent(TP_PARTS - 1)
    update(TP_PARTS - 1, sums.core)

    def four(k):
        sums.stage_four(k)
        update(k, 1 - sums.core)

    paced(TP_PARTS, four, (engine, 2))
    finish_pumps(engine)
    for i in (1, 2):
        p_copy(rows // step_rows - i).wait()
    sums.drain(True)
    engine.drain()


def state_backward(clips, frames, tokens, attn_sum, cotangent, rows_table, h_two, w_one, fed):
    rows, wide = tokens.shape
    grid = clips == GRID
    depth = wide // GRID
    units, scattered = fed.hid.shape[1], fed.grads.shape[-1]
    cut = Blocks(depth, scattered - 3 * UNITS, 96, 256, 3 * UNITS) if grid else None
    n = Named()
    n.ins.update(frames=(frames, IN_SMEM), tok=(tokens, IN_VMEM), attn_sum=(attn_sum, IN_VMEM), cot=(cotangent, IN_VMEM))
    n.ins.update(rows=(rows_table, IN_VMEM), h_two=(h_two, IN_VMEM), grad_ffn=(fed.grad_ffn, IN_VMEM))
    n.ins.update(hid=(fed.hid, IN_VMEM), dgu=(fed.dgu_last, IN_VMEM), w_one=(w_one, ANY), w_two=(fed.w_two, ANY))
    n.ins.update(partial=(fed.partial, ANY))
    whole = shaped((rows, wide), BF16)
    n.outs.update(grad_attn=(whole, IN_VMEM), grad_state=(whole, IN_VMEM), colsums=(shaped((8, wide), F32), IN_VMEM))
    n.outs.update(g_last=(shaped((LINE, 2, depth, 3 * UNITS), BF16), IN_VMEM), p_ffn=(whole, ANY))
    n.scratch.update(
        down=pltpu.VMEM((wide, units), BF16),
        down_s=DMA((units // UNITS,)),
        p_staged=pltpu.VMEM((2, 256, wide), BF16),
        p_s=DMA((2,)),
        tp_set=TpSum.scratch(rows, wide) + [DMA((TP_PARTS,))],
    )
    if grid:
        n.ins.update(grads=(fed.grads, ANY))
        n.outs.update(out=(shaped((depth, scattered - 3 * UNITS), F32), IN_VMEM))
        n.scratch.update(scatter_set=Scatter.scratch(cut))
    return n.call(functools.partial(state_kernel, n, cut), params(2))


def attn_back_kernel(blocks, blocks_t, *refs):
    frames, grad_attn, weights, heads_ref, cos_ref, sa_ref, sb_ref, seg_ref = refs[:8]
    (q_pre, k_pre, q_rot, k_rot, q_text, v_ref, self_o, inv_l) = refs[8:16]
    (ky_pre, kyr, vy, text_o, inv_lt, h_one, mixed, partial, grad) = refs[16:25]
    grad_qkv, grad_text, gains, ffn_sum, out, g_attn, all_text = refs[25:32]
    do_self, do_text, d_self, d_text, dqn, dk, dv, dky, dvy, klive, staged, stage_s = refs[32:44]
    sums = TpSum(partial, ffn_sum, refs[44:46], refs[46:52], refs[52])
    qgain, kgain, kygain, gate = (heads_ref.at[i : i + 1] for i in range(4))
    engine, text_engine = Idle(), Idle()
    if blocks is not None:
        engine = Scatter(blocks, grad, out, refs[53:61], ahead=A_S1)
        text_engine = GatherChain(blocks_t, grad_text, all_text, refs[61:], A_T)
        greet(dp_peers(), tp_peers())
        engine.start()
    else:
        greet([], tp_peers())
    loop(TP_PARTS, sums.stage_one)
    rows, cols = q_rot.shape
    wide = grad_attn.shape[1]
    step_rows = 256
    blocks_here = rows // step_rows
    pairs = cols // PAIR
    gains[...] = jnp.zeros_like(gains)
    dk[...] = jnp.zeros_like(dk)
    dv[...] = jnp.zeros_like(dv)
    dky[...] = jnp.zeros_like(dky)
    dvy[...] = jnp.zeros_like(dvy)

    def halves(value, first_head):
        lane = lax.broadcasted_iota(jnp.int32, (step_rows, PAIR), 1)
        out = jnp.zeros((step_rows, PAIR), F32)
        for head in range(2):
            total = jnp.sum(value * half_mask(step_rows, head, F32), axis=-1, keepdims=True)
            high = total.astype(BF16).astype(F32)
            spot = 2 * (first_head + head)
            out = out + jnp.where(lane == spot, high, jnp.where(lane == spot + 1, total - high, 0.0))
        return out

    def start_rows(i):
        here = block_rows(i, step_rows)
        g = dot_nn(grad_attn[here, :], weights[...])
        other = text_o[here, :].astype(F32)
        gains[3:4, :] += jnp.sum(g * other, axis=0, keepdims=True)
        first = (g * inv_l[here, :]).astype(BF16)
        do_self[here, :] = first
        second = (g * gate[...] * inv_lt[here, :]).astype(BF16)
        do_text[here, :] = second
        dot_self = first.astype(F32) * self_o[here, :].astype(F32)
        dot_text = second.astype(F32) * other
        each = [slice(pair * PAIR, (pair + 1) * PAIR) for pair in range(pairs)]
        d_self[here, :] = sum(halves(dot_self[:, lanes], 2 * pair) for pair, lanes in enumerate(each)).astype(BF16)
        d_text[here, :] = sum(halves(dot_text[:, lanes], 2 * pair) for pair, lanes in enumerate(each)).astype(BF16)
        klive[here, :] = k_rot[here, :] * live_rows(frames, i * step_rows, step_rows, cols).astype(BF16)

    def back(q_ref, k_ref, k_live, v_in, do_ref, d_ref, dk_ref, dv_ref, turned):
        def step(i):
            pair, block = lax.div(i, blocks_here), lax.rem(i, blocks_here)
            here, lanes = block_rows(block, step_rows), pair_lanes(pair)
            keys = k_ref[:, lanes]
            values = v_in[:, lanes]
            lane = lax.broadcasted_iota(jnp.int32, values.shape, 1)
            dq = jnp.zeros((step_rows, PAIR), F32)
            for head in range(2):
                mask = half_mask(step_rows, head, BF16)
                q = q_ref[here, lanes] * mask
                do = do_ref[here, lanes] * mask
                scores = dot_nt(keys, q)
                p = jnp.exp(scores)
                dv_ref[:, lanes] += dot_nn(p.astype(BF16), do)
                spot = 2 * (2 * pair + head)
                minus = jnp.where((lane == spot) | (lane == spot + 1), -1.0, 0.0).astype(BF16)
                left = jnp.concatenate([values, minus], axis=1)
                right = jnp.concatenate([do, d_ref[here, :]], axis=1)
                ds = (p * dot_nt(left, right)).astype(BF16)
                dk_ref[:, lanes] += dot_nn(ds, q)
                key_mask = half_mask(keys.shape[0], head, BF16)
                dq = dq + dot_tn(ds, k_live[:, lanes] * key_mask)
            dq = dq * SCALE
            if turned:
                dqn[here, lanes] += rope_back(dq, cos_ref[here, :], sa_ref[here, :], sb_ref[here, :])
            else:
                dqn[here, lanes] = dq

        return step

    paced(blocks_here, start_rows, (engine, 2))
    def norm_back(grad_normed, pre, gain, row):
        inverse = head_inverse(pre, seg_ref[...])
        hat = pre * inverse
        gains[row : row + 1, :] += jnp.sum(grad_normed * hat, axis=0, keepdims=True)
        scaled = grad_normed * gain
        average = segment_sum(scaled * hat, seg_ref[...]) * (1.0 / HEAD)
        return (inverse * (scaled - hat * average)).astype(BF16)

    def end_rows(i):
        here = block_rows(i, step_rows)
        cosines, sine_a, sine_b = thrice(cos_ref[here, :]), thrice(sa_ref[here, :]), thrice(sb_ref[here, :])
        live = live_rows(frames, i * step_rows, step_rows, cols)
        grad_qkv[here, :cols] = norm_back(dqn[here, :], q_pre[here, :], qgain[...], 0)
        dkn = rope_back(dk[here, :] * live, cosines, sine_a, sine_b)
        grad_qkv[here, cols : 2 * cols] = norm_back(dkn, k_pre[here, :], kgain[...], 1)
        grad_qkv[here, 2 * cols : 3 * cols] = (dv[here, :] * live).astype(BF16)
        for k in range(TP_PARTS // blocks_here):
            sums.stage_three(i * (TP_PARTS // blocks_here) + k)

    text_back = back(q_text, kyr, kyr, vy, do_text, d_text, dky, dvy, False)

    def text_step(i):
        text_back(i)
        pl.when(i < TP_PARTS)(lambda: sums.stage_two(i))

    paced(pairs * blocks_here, text_step, (engine, 3))
    grad_text[:, :cols] = norm_back(dky[...], ky_pre[...], kygain[...], 2)
    grad_text[:, cols:] = dvy[...].astype(BF16)
    text_engine.start()
    self_back = back(q_rot, k_rot, klive, v_ref, do_self, d_self, dk, dv, True)

    half = pairs * blocks_here // 2
    paced(half, self_back, (engine, 6), (text_engine, 2))
    paced(half, lambda i: self_back(i + half), (text_engine, 3))
    paced(blocks_here, end_rows, (text_engine, 2))
    tall = wide // LINE

    def copy(m):
        return pltpu.make_async_copy(staged.at[lax.rem(m, 2)], g_attn.at[m], stage_s.at[lax.rem(m, 2)])

    def products(m):
        lanes = pl.ds(pl.multiple_of(m * tall, 128), tall)
        pl.when(m >= 2)(lambda: copy(m - 2).wait())
        first = dot_tn(h_one[:, lanes], grad_qkv[...]).astype(BF16)
        second = dot_tn(grad_attn[:, lanes], mixed[...]).astype(BF16)
        for y in range(2):
            part = slice(y * tall // 2, (y + 1) * tall // 2)
            staged[lax.rem(m, 2), y, :, : 3 * cols] = first[part]
            staged[lax.rem(m, 2), y, :, 3 * cols :] = second[part]
        copy(m).start()

    paced(LINE, products, (text_engine, 4))
    finish_pumps(engine)
    finish_pumps(text_engine)
    text_engine.arrive()
    loop(TP_PARTS, sums.stage_four)
    copy(LINE - 2).wait()
    copy(LINE - 1).wait()
    sums.drain()
    engine.drain()
    text_engine.drain()


def attn_backward(clips, frames, grad_attn, w_out, heads_table, tables, seg, saved, partial, g_up):
    rows, wide = grad_attn.shape
    cols = heads_table.shape[1]
    rows_t = saved[8].shape[0]
    depth, units = wide // GRID, g_up.shape[-1]
    grid = clips == GRID
    parts = Blocks(depth, units, 96, 256) if grid else None
    blocks_t = Blocks(rows_t, 2 * cols, 32, 2 * cols) if grid else None
    f, b = pltpu.VMEM((rows, cols), F32), pltpu.VMEM((rows, cols), BF16)
    ft = pltpu.VMEM((rows_t, cols), F32)
    slim = pltpu.VMEM((rows, PAIR), BF16)
    return pl.pallas_call(
        functools.partial(attn_back_kernel, parts, blocks_t),
        out_shape=[
            shaped((rows, 3 * cols), BF16),
            shaped((rows_t, 2 * cols), BF16),
            shaped((8, cols), F32),
            shaped((rows, wide), BF16),
            shaped((depth, units), F32),
            shaped((LINE, 2, depth, 4 * cols), BF16),
            shaped((GRID * rows_t, 2 * cols), BF16),
        ],
        in_specs=[IN_SMEM] + [IN_VMEM] * 22 + [ANY] * 2,
        out_specs=[IN_VMEM] * 5 + [ANY] * 2,
        scratch_shapes=[b, b, slim, slim, f, f, f, ft, ft, b]
        + [pltpu.VMEM((2, 2, depth, 4 * cols), BF16), DMA((2,))]
        + TpSum.scratch(rows, wide)
        + [DMA((TP_PARTS,))]
        + (Scatter.scratch(parts) + GatherChain.scratch(blocks_t.count) if grid else []),
        compiler_params=params(3),
    )(frames, grad_attn, w_out, heads_table, *tables, seg, *saved, partial, g_up)


def last_kernel(parts, *refs):
    frames, grad_qkv, weights, tok, grad_state, rows_ref, sums_two, gains = refs[:8]
    ffn_sum, attn_sum, cot, text_all, all_text, grad_a = refs[8:14]
    result, grad_tokens, vecs, g_tk, g_tv, out_a = refs[14:20]
    partial, grad_n, colsum, outsum, vec = refs[20:25]
    sums = TpSum(partial, grad_n, refs[25:27], refs[27:33])
    me = lax.axis_index("dp")
    engine = Idle()
    peers = []
    if parts is not None:
        v_s, v_r = refs[33:35]
        peers = dp_peers()
        engine = Scatter(parts, grad_a, out_a, refs[35:], ahead=A_S2)
        greet(peers, tp_peers())
        engine.start()
    else:
        greet([], tp_peers())
    mult_one, tanh_one, _, tanh_two, gain_one, lift_one, gain_two, lift_two = (rows_ref[i : i + 1, :] for i in range(8))
    colsum[...] = jnp.zeros_like(colsum)
    outsum[...] = jnp.zeros_like(outsum)
    wide = tok.shape[1]
    cols = grad_qkv.shape[1] // 3
    step_rows = 256

    def project(which):
        def step(i):
            here = pl.ds(pl.multiple_of(which * sums.half + i * step_rows, 16), step_rows)
            partial[here, :] = dot_nt(grad_qkv[here, :], weights[:, : 3 * cols]).astype(BF16)

        return step

    parts_each = TP_PARTS // (sums.half // step_rows)

    def project_send(i):
        project(1 - sums.core)(i)
        loop(parts_each, lambda k: sums.stage_one(i * parts_each + k))

    paced(sums.half // step_rows, project_send)
    paced(sums.half // step_rows, project(sums.core), (engine, P_1))
    paced(TP_PARTS, sums.stage_two, (engine, P_2))

    def output(i):
        here = block_rows(i, 64)
        live = live_rows(frames, i * 64, 64, wide)
        added = live * ffn_sum[here, :].astype(F32)
        state = tok[here, :].astype(F32) + live * tanh_one * attn_sum[here, :].astype(F32)
        result[here, :] = (state + tanh_two * added).astype(BF16)
        outsum[...] += jnp.sum(added * cot[here, :].astype(F32), axis=0, keepdims=True)

    paced(tok.shape[0] // 64, output, (engine, P_3))
    if parts is not None:
        rows_t = text_all.shape[1]

        def text_products(i):
            here = block_rows(i, rows_t)
            g_tk[...] += dot_tn(text_all[i], all_text[here, :cols])
            g_tv[...] += dot_tn(text_all[i], all_text[here, cols:])

        g_tk[...] = jnp.zeros_like(g_tk)
        g_tv[...] = jnp.zeros_like(g_tv)
        paced(GRID, text_products, (engine, P_4))

    def update(k, which):
        here = sums.spot(k, which)
        x = tok[here, :].astype(F32)
        inverse = lax.rsqrt(jnp.mean(x * x, axis=-1, keepdims=True) + EPS)
        hat = x * inverse
        g = grad_n[here, :].astype(F32)
        scaled = g * mult_one
        back = inverse * (scaled - hat * jnp.mean(scaled * hat, axis=-1, keepdims=True))
        grad_tokens[here, :] = (grad_state[here, :].astype(F32) + back).astype(BF16)
        colsum[...] += jnp.sum(g * hat, axis=0, keepdims=True)

    def three(k):
        sums.stage_three(k)
        update(k, sums.core)

    paced(TP_PARTS, three, (engine, 4))

    def four(k):
        sums.stage_four(k)
        update(k, 1 - sums.core)

    paced(TP_PARTS, four, (engine, 2))
    pieces = (
        colsum[...] * gain_one,
        sums_two[1:2, :] * (1.0 - tanh_one * tanh_one),
        sums_two[0:1, :] * gain_two,
        outsum[...] * (1.0 - tanh_two * tanh_two),
        colsum[...] * lift_one,
        sums_two[0:1, :] * lift_two,
    )
    for i, piece in enumerate(pieces):
        vec[:, i * wide : (i + 1) * wide] = piece
    for i in range(4):
        vec[:, 6 * wide + i * cols : 6 * wide + (i + 1) * cols] = gains[i : i + 1, :]
    for i, there in enumerate(peers):
        remote(vec, vecs.at[me], v_s.at[i], v_r.at[i], dp=there).start()
    finish_pumps(engine)
    vecs[pl.ds(me if peers else 0, 1)] = vec[...][None]
    for i, there in enumerate(peers):
        here = lax.rem(me + GRID - 1 - i, GRID)
        remote(vec, vecs.at[here], v_s.at[i], v_r.at[i], dp=me).wait_recv()
        remote(vec, vecs.at[me], v_s.at[i], v_r.at[i], dp=there).wait_send()
    sums.drain()
    engine.drain()


def last_backward(
    clips, frames, grad_qkv, full_attn, tokens, grad_state, rows_table, sums_two, gains, ffn_sum, attn_sum, cotangent,
    text_all, all_text, g_attn
):
    rows, wide = tokens.shape
    grid = clips == GRID
    cols = gains.shape[1]
    depth, wide_a = g_attn.shape[-2:]
    slab = text_all.shape[-1]
    parts = Blocks(depth, wide_a, 96, 256) if grid else None
    whole = shaped((rows, wide), BF16)
    vec = (1, 6 * wide + 4 * cols)
    return pl.pallas_call(
        functools.partial(last_kernel, parts),
        out_shape=[
            whole,
            whole,
            shaped(((GRID if grid else 1),) + vec, F32),
            shaped((slab, cols), F32),
            shaped((slab, cols), F32),
            shaped((depth, wide_a), F32),
        ],
        in_specs=[IN_SMEM] + [IN_VMEM] * 12 + [ANY],
        out_specs=[IN_VMEM] * 6,
        scratch_shapes=[
            pltpu.VMEM((rows, wide), BF16),
            pltpu.VMEM((rows, wide), BF16),
            pltpu.VMEM((1, wide), F32),
            pltpu.VMEM((1, wide), F32),
            pltpu.VMEM(vec, F32),
        ]
        + TpSum.scratch(rows, wide)
        + ([DMA((GRID - 1,))] * 2 + Scatter.scratch(parts) if grid else []),
        compiler_params=params(4),
    )(
        frames, grad_qkv, full_attn, tokens, grad_state, rows_table, sums_two, gains, ffn_sum, attn_sum, cotangent,
        text_all, all_text, g_attn
    )


def gather_plain(shard):
    return lax.all_gather(shard, "dp", axis=0, tiled=True)


def scatter_plain(grad):
    return lax.psum_scatter(grad, "dp", scatter_dimension=0, tiled=True).astype(F32)


def first_plain(shard, cond, small, w_ada, text, w_tk, w_tv):
    act = jax.nn.silu(lax.all_to_all(cond[:, 0], "dp", 0, 0, tiled=True)).astype(BF16)
    parts = dot_nn(act, w_ada)
    mods = lax.psum_scatter(parts, "dp", scatter_dimension=0, tiled=True)[0]
    full_text = gather_plain(jnp.concatenate([w_tk, w_tv], axis=1))
    smalls = lax.all_gather(small, "dp", axis=0)[:, 0, :]
    wide = w_ada.shape[1] // 4
    bias, gain = 4 * wide // smalls.shape[0], wide // smalls.shape[0]
    scale_one, gate_one, scale_two, gate_two = jnp.split(mods + smalls[:, :bias].reshape(-1), 4)
    gain_one, gain_two = smalls[:, bias : bias + gain].reshape(-1), smalls[:, bias + gain :].reshape(-1)
    lift_one, lift_two = 1.0 + scale_one, 1.0 + scale_two
    values = (
        gain_one * lift_one,
        jnp.tanh(gate_one),
        gain_two * lift_two,
        jnp.tanh(gate_two),
        gain_one,
        lift_one,
        gain_two,
        lift_two,
    )
    return gather_plain(shard), jnp.stack(values), act.astype(F32), dot_nn(text, full_text)


def on_device(
    tokens,
    text,
    cond,
    frames,
    w_query,
    w_key,
    w_value,
    w_out,
    w_text_key,
    w_text_value,
    w_gate,
    w_up,
    w_down,
    w_ada,
    ada_bias,
    norm_one,
    norm_two,
    query_gain,
    key_gain,
    text_key_gain,
    cross_gate,
    cotangent,
):
    rows, wide = tokens.shape
    clips = lax.axis_size("dp")
    grid = clips == GRID
    cols, units = w_query.shape[1], w_gate.shape[1]
    heads_here = cols // HEAD
    bias_rows, gain_rows = ada_bias.shape[0], norm_one.shape[0]
    small = jnp.concatenate([ada_bias, norm_one, norm_two]).astype(F32)[None, :]
    cond_rows = cond.astype(F32).reshape(clips, 1, -1)
    attn_shard = jnp.concatenate([w_query, w_key, w_value, w_out.T], axis=1)
    turned = w_down.T
    pieces = [
        jnp.concatenate(
            [w[:, b * UNITS : (b + 1) * UNITS] for b in range(*ends) for w in (w_gate, w_up, turned)],
            axis=1,
        )
        for ends in ((0, ONES), (ONES, units // UNITS))
    ]
    opening = (attn_shard, cond_rows, small, w_ada, text, w_text_key, w_text_value)
    if not grid:
        full_attn, rows_table, act_rows, ty = first_plain(*opening)
        opening = (full_attn, rows_table, ty)
    gate_tanh = jnp.tanh(cross_gate.astype(F32))
    blank = jnp.zeros((cols,), F32)
    heads_table = jnp.stack(
        [query_gain.astype(F32), key_gain.astype(F32), text_key_gain.astype(F32), jnp.repeat(gate_tanh, HEAD)]
        + [blank] * 4
    )
    tables, seg = rope_tables(rows), segment_ones(cols)
    passed = forward(clips, frames, tokens, heads_table, tables, seg, pieces[0], opening)
    full_attn, rows_table = passed.weights, passed.rows
    if grid:
        act_rows, half_one, second = passed.act, passed.full_ffn, pieces[1]
    else:
        half_one, second = gather_plain(pieces[0]), gather_plain(pieces[1])
    p = passed
    saved = (p.q_pre, p.k_pre, p.q_rot, p.k_rot, p.q_text, p.values, p.self_o, p.inv_l)
    saved += (p.ky_pre, p.kyr, p.vy, p.text_o, p.inv_lt, p.h_one, p.mixed)
    fed = ffn(clips, frames, p.h_two, cotangent, rows_table, half_one, second)
    state = state_backward(clips, frames, tokens, p.attn_sum, cotangent, rows_table, p.h_two, half_one, fed)
    out_turned = full_attn[:, 3 * cols :]
    grad_qkv, grad_text, gains, ffn_sum, s_last, g_attn, all_text = attn_backward(
        clips, frames, state.grad_attn, out_turned, heads_table, tables, seg, saved, state.p_ffn, state.g_last
    )
    result, grad_tokens, vecs, s_text_key, s_text_value, s_attn = last_backward(
        clips,
        frames,
        grad_qkv,
        full_attn,
        tokens,
        state.grad_state,
        rows_table,
        state.colsums,
        gains,
        ffn_sum,
        p.attn_sum,
        cotangent,
        p.text_all,
        all_text if grid else grad_text,
        g_attn,
    )
    s_blocks = [fed.out, state.out] if grid else [scatter_plain(fed.grads.reshape(wide, -1))]
    if not grid:
        s_last, s_attn = (scatter_plain(g.reshape(wide, -1)) for g in (state.g_last, g_attn))
        s_text = scatter_plain(dot_tn(text, grad_text).astype(BF16))
        s_text_key, s_text_value = s_text[:, :cols], s_text[:, cols:]
        vecs = lax.all_gather(vecs[0], "dp", axis=0)
    s_ffn = [
        jnp.concatenate(
            [
                s[:, at + i * UNITS : at + (i + 1) * UNITS]
                for s in (*s_blocks, s_last)
                for at in range(0, s.shape[1], 3 * UNITS)
            ],
            axis=1,
        )
        for i in range(3)
    ]
    vecs = vecs[:, 0, :]
    mod_wide = 4 * wide
    g_ada = lax.dot_general(
        act_rows,
        vecs[:, :mod_wide],
        (((0,), (0,)), ((), ())),
        precision=lax.Precision.HIGHEST,
        preferred_element_type=F32,
    )
    sums = jnp.sum(vecs, axis=0)
    me = lax.axis_index("dp")
    g_bias = lax.dynamic_slice(sums, (me * bias_rows,), (bias_rows,))
    g_norm_one = lax.dynamic_slice(sums, (mod_wide + me * gain_rows,), (gain_rows,))
    g_norm_two = lax.dynamic_slice(sums, (mod_wide + wide + me * gain_rows,), (gain_rows,))
    rest = sums[mod_wide + 2 * wide :]
    g_cross_gate = jnp.sum(rest[3 * cols :].reshape(heads_here, HEAD), axis=1) * (1.0 - gate_tanh * gate_tanh)
    return (
        result,
        grad_tokens,
        s_attn[:, :cols],
        s_attn[:, cols : 2 * cols],
        s_attn[:, 2 * cols : 3 * cols],
        s_attn[:, 3 * cols :].T,
        s_text_key,
        s_text_value,
        s_ffn[0],
        s_ffn[1],
        s_ffn[2].T,
        g_ada,
        g_bias,
        g_norm_one,
        g_norm_two,
        rest[:cols],
        rest[cols : 2 * cols],
        rest[2 * cols : 3 * cols],
        g_cross_gate,
    )


def solution(mesh):
    placed = (
        P("dp", None),
        P("dp", None),
        P("dp", None),
        P("dp"),
        P("dp", "tp"),
        P("dp", "tp"),
        P("dp", "tp"),
        P("tp", "dp"),
        P("dp", "tp"),
        P("dp", "tp"),
        P("dp", "tp"),
        P("dp", "tp"),
        P("tp", "dp"),
        P("dp", None),
        P("dp"),
        P("dp"),
        P("dp"),
        P("tp"),
        P("tp"),
        P("tp"),
        P("tp"),
        P("dp", None),
    )
    return jax.shard_map(
        on_device,
        mesh=mesh,
        in_specs=placed,
        out_specs=(
            P("dp", None),
            P("dp", None),
            P("dp", "tp"),
            P("dp", "tp"),
            P("dp", "tp"),
            P("tp", "dp"),
            P("dp", "tp"),
            P("dp", "tp"),
            P("dp", "tp"),
            P("dp", "tp"),
            P("tp", "dp"),
            P("dp", None),
            P("dp"),
            P("dp"),
            P("dp"),
            P("tp"),
            P("tp"),
            P("tp"),
            P("tp"),
        ),
        check_vma=False,
    )
```

```python
import functools
import types

import jax
import jax.numpy as jnp
import numpy as np
from jax import lax
from jax.experimental import pallas as pl
from jax.experimental.pallas import tpu as pltpu
from jax.sharding import PartitionSpec as P

HEAD = 64
FRAME_TOK = 64
EPS = 1e-06
ROPE_BASE = 10000.0
SCALE = HEAD**-0.5
MESH = pl.DeviceIdType.MESH
VMEM_LIMIT = 60 * 2**20
GRID = 8
LINE = 4
PAIR = 2 * HEAD
TP_PARTS = 8
AHEAD = 2
LAG = 3
P_1 = 1
P_2 = 0
P_3 = 4
P_4 = 4
O_1 = 2
O_2 = 2
O_3 = 1
O_4 = 1
A_A = 3
A_T = 2
A_S1 = 2
A_S0 = 2
A_S2 = 3
A_P = 2
DMA = pltpu.SemaphoreType.DMA
F32 = jnp.float32
BF16 = jnp.bfloat16


def dot_nn(left, right):
    return jnp.dot(left, right, preferred_element_type=F32)


def dot_nt(left, right):
    return lax.dot_general(left, right, (((1,), (1,)), ((), ())), preferred_element_type=F32)


def dot_tn(left, right):
    return lax.dot_general(left, right, (((0,), (0,)), ((), ())), preferred_element_type=F32)


def remote(src, dst, send, recv, **where):
    return pltpu.make_async_remote_copy(
        src_ref=src, dst_ref=dst, send_sem=send, recv_sem=recv, device_id=where, device_id_type=MESH
    )


def greet(dp_peers, tp_peers):
    barrier = pltpu.get_barrier_semaphore()
    for peer in dp_peers:
        pl.semaphore_signal(barrier, inc=1, device_id={"dp": peer}, device_id_type=MESH)
    for peer in tp_peers:
        pl.semaphore_signal(barrier, inc=1, device_id={"tp": peer}, device_id_type=MESH)
    pl.semaphore_wait(barrier, len(dp_peers) + len(tp_peers))


def dp_peers():
    me = lax.axis_index("dp")
    return [lax.rem(me + step, GRID) for step in range(1, GRID)]


def tp_peers():
    me = lax.axis_index("tp")
    return [me + 1 - 2 * lax.rem(me, 2), lax.rem(me + 2, 4)]


def aligned(value, by):
    return value if isinstance(value, int) else pl.multiple_of(value, by)


def loop(count, step):
    def body(i, carry):
        step(i)
        return carry

    lax.fori_loop(0, count, body, 0)


def add_rows(out_ref, first, *others):
    rows, wide = out_ref.shape
    tall = min(rows, 96 if wide <= 384 else 32)
    plain = len(others) == 1 and out_ref.dtype == BF16

    def step(i):
        here = pl.ds(aligned(i * tall, 16), tall)
        total = first[here, :] if plain else first[here, :].astype(F32)
        for other in others:
            total = total + (other[here, :] if plain else other[here, :].astype(F32))
        out_ref[here, :] = total.astype(out_ref.dtype)

    if rows == tall:
        step(0)
    else:
        loop(rows // tall, step)


class Blocks:
    def __init__(self, depth, wide, rows, cols, first=0):
        self.depth, self.wide, self.rows, self.cols, self.first = depth, wide, rows, cols, first
        self.down = depth // rows
        self.count = self.down * (wide // cols)

    def at(self, c):
        if isinstance(c, int):
            return c % self.down * self.rows, self.first + c // self.down * self.cols
        row = aligned(lax.rem(c, self.down) * self.rows, 16)
        col = aligned(self.first + lax.div(c, self.down) * self.cols, 128)
        return row, col

class Gather:
    def __init__(self, blocks, shard, full, sems, ahead=AHEAD):
        self.b, self.shard, self.full, self.ahead = blocks, shard, full, min(ahead, blocks.count)
        self.z_s, self.z_r, self.y_s, self.y_r, self.own_s = sems
        self.me = lax.axis_index("dp")
        self.z, self.y = self.me // 2, lax.rem(self.me, 2)
        self.lines = [lax.rem(self.z + step, LINE) for step in range(1, LINE)]
        self.ticks, self.done = blocks.count, 0

    @staticmethod
    def scratch(count):
        return [DMA((count, 3))] * 2 + [DMA((count, 4))] * 2 + [DMA((count,))]

    def own(self, c):
        row, col = self.b.at(c)
        return self.shard.at[pl.ds(row, self.b.rows), pl.ds(col, self.b.cols)]

    def place(self, c, origin):
        row, col = self.b.at(c)
        start = pl.multiple_of(origin * self.b.depth + row, 16)
        return self.full.at[pl.ds(start, self.b.rows), pl.ds(col, self.b.cols)]

    def along(self, c, i):
        there = 2 * self.lines[i] + self.y
        return remote(self.own(c), self.place(c, self.me), self.z_s.at[c, i], self.z_r.at[c, i], dp=there)

    def came_along(self, c, i):
        line = lax.rem(self.z + LINE - 1 - i, LINE)
        place = self.place(c, 2 * line + self.y)
        return line, remote(place, place, self.z_s.at[c, i], self.z_r.at[c, i], dp=self.me)

    def across(self, c, line, mine=False):
        origin = 2 * line + self.y
        src = self.own(c) if mine else self.place(c, origin)
        other = self.me + 1 - 2 * self.y
        return remote(src, self.place(c, origin), self.y_s.at[c, line], self.y_r.at[c, line], dp=other)

    def came_across(self, c, line):
        place = self.place(c, 2 * line + 1 - self.y)
        return remote(place, place, self.y_s.at[c, line], self.y_r.at[c, line], dp=self.me)

    def local(self, c):
        return pltpu.make_async_copy(self.own(c), self.place(c, self.me), self.own_s.at[c])

    def begin(self, c):
        for i in range(LINE - 1):
            self.along(c, i).start()
        self.across(c, self.z, True).start()
        self.local(c).start()

    def start(self):
        for c in range(self.ahead):
            self.begin(c)

    def pump(self, t):
        pl.when(t + self.ahead < self.b.count)(lambda: self.begin(t + self.ahead))
        for i in range(LINE - 1):
            line, came = self.came_along(t, i)
            came.wait_recv()
            self.across(t, line).start()

    def arrive(self, first=0, count=None):
        def step(i):
            c = first + i
            for line in range(LINE):
                self.came_across(c, line).wait_recv()
            self.local(c).wait()

        loop(self.b.count if count is None else count, step)

    def drain(self):
        def step(c):
            for line in range(LINE):
                self.across(c, line).wait_send()
            for i in range(LINE - 1):
                self.along(c, i).wait_send()

        loop(self.b.count, step)


class GatherChain:
    def __init__(self, blocks, shard, full, sems, ahead=AHEAD):
        self.b, self.shard, self.full, self.ahead = blocks, shard, full, min(ahead, blocks.count)
        self.up_s, self.up_r, self.dn_s, self.dn_r, self.y_s, self.y_r, self.own_s = sems
        self.me = lax.axis_index("dp")
        self.z, self.y = self.me // 2, lax.rem(self.me, 2)
        self.ticks, self.done = blocks.count + LINE - 2, 0

    @staticmethod
    def scratch(count):
        return [DMA((count, 3))] * 4 + [DMA((count, 4))] * 2 + [DMA((count,))]

    def own(self, c):
        row, col = self.b.at(c)
        return self.shard.at[pl.ds(row, self.b.rows), pl.ds(col, self.b.cols)]

    def place(self, c, origin):
        row, col = self.b.at(c)
        start = pl.multiple_of(origin * self.b.depth + row, 16)
        return self.full.at[pl.ds(start, self.b.rows), pl.ds(col, self.b.cols)]

    def up(self, c, hop):
        origin = self.me - 2 * hop
        src = self.own(c) if hop == 0 else self.place(c, origin)
        return remote(src, self.place(c, origin), self.up_s.at[c, hop], self.up_r.at[c, hop], dp=self.me + 2)

    def down(self, c, hop):
        origin = self.me + 2 * hop
        src = self.own(c) if hop == 0 else self.place(c, origin)
        return remote(src, self.place(c, origin), self.dn_s.at[c, hop], self.dn_r.at[c, hop], dp=self.me - 2)

    def across(self, c, line, mine=False):
        origin = 2 * line + self.y
        src = self.own(c) if mine else self.place(c, origin)
        other = self.me + 1 - 2 * self.y
        return remote(src, self.place(c, origin), self.y_s.at[c, line], self.y_r.at[c, line], dp=other)

    def came(self, c, origin, sems):
        return remote(self.place(c, origin), self.place(c, origin), sems, sems, dp=self.me)

    def local(self, c):
        return pltpu.make_async_copy(self.own(c), self.place(c, self.me), self.own_s.at[c])

    def begin(self, c):
        pl.when(self.z < LINE - 1)(lambda: self.up(c, 0).start())
        pl.when(self.z > 0)(lambda: self.down(c, 0).start())
        self.across(c, self.z, True).start()
        self.local(c).start()

    def start(self):
        for c in range(self.ahead):
            self.begin(c)

    def pump(self, t):
        me, z, count = self.me, self.z, self.b.count
        pl.when(t + self.ahead < count)(lambda: self.begin(t + self.ahead))
        for hop in range(LINE - 1):
            c = t - hop
            valid = (c >= 0) & (c < count)

            @pl.when(valid & (z - 1 - hop >= 0))
            def _():
                self.came(c, me - 2 * (hop + 1), self.up_r.at[c, hop]).wait_recv()
                if hop < LINE - 2:
                    pl.when(z < LINE - 1)(lambda: self.up(c, hop + 1).start())
                self.across(c, z - 1 - hop).start()

            @pl.when(valid & (z + 1 + hop <= LINE - 1))
            def _():
                self.came(c, me + 2 * (hop + 1), self.dn_r.at[c, hop]).wait_recv()
                if hop < LINE - 2:
                    pl.when(z > 0)(lambda: self.down(c, hop + 1).start())
                self.across(c, z + 1 + hop).start()

    def arrive(self, first=0, count=None):
        def step(i):
            c = first + i
            for line in range(LINE):
                self.came(c, 2 * line + 1 - self.y, self.y_r.at[c, line]).wait_recv()
            self.local(c).wait()

        loop(self.b.count if count is None else count, step)

    def drain(self):
        z = self.z

        def step(c):
            for line in range(LINE):
                self.across(c, line).wait_send()
            for hop in range(LINE - 1):
                pl.when((z < LINE - 1) & (z - hop >= 0))(lambda: self.up(c, hop).wait_send())
                pl.when((z > 0) & (z + hop <= LINE - 1))(lambda: self.down(c, hop).wait_send())

        loop(self.b.count, step)


class Scatter:
    def __init__(self, blocks, grad, out, refs, inplace=False, ahead=AHEAD):
        self.b, self.grad, self.out, self.inplace = blocks, grad, out, inplace
        self.ahead = min(ahead, blocks.count)
        self.crossed, self.landed = refs[:2]
        self.y_s, self.y_r, self.own_s, self.z_s, self.z_r = refs[2:7]
        self.held = None if inplace else refs[7]
        self.me = lax.axis_index("dp")
        self.z, self.y = self.me // 2, lax.rem(self.me, 2)
        self.lines = [lax.rem(self.z + step, LINE) for step in range(1, LINE)]
        self.ticks, self.done = blocks.count + LAG, 0

    @staticmethod
    def scratch(blocks, inplace=False):
        shape = (blocks.rows, blocks.cols)
        count = blocks.count
        bufs = [pltpu.VMEM((count, lines) + shape, BF16) for lines in (4, 3)]
        held = [] if inplace else [pltpu.VMEM((count, 4) + shape, BF16)]
        return bufs + [DMA((count,))] * 3 + [DMA((count, 3))] * 2 + held

    def part(self, c, row_y):
        row, col = self.b.at(c)
        return self.grad.at[:, row_y, pl.ds(row, self.b.rows), pl.ds(col, self.b.cols)]

    def hold(self, c, line):
        if not self.inplace:
            return self.held.at[c, line]
        row, col = self.b.at(c)
        return self.grad.at[line, self.y, pl.ds(row, self.b.rows), pl.ds(col, self.b.cols)]

    def across(self, c):
        other = self.me + 1 - 2 * self.y
        return remote(self.part(c, 1 - self.y), self.crossed.at[c], self.y_s.at[c], self.y_r.at[c], dp=other)

    def load(self, c):
        return pltpu.make_async_copy(self.part(c, self.y), self.held.at[c], self.own_s.at[c])

    def along(self, c, i):
        line = self.lines[i]
        return remote(
            self.hold(c, line), self.landed.at[c, i], self.z_s.at[c, i], self.z_r.at[c, i], dp=2 * line + self.y
        )

    def begin(self, c):
        self.across(c).start()
        if not self.inplace:
            self.load(c).start()

    def start(self):
        for c in range(self.ahead):
            self.begin(c)

    def fold(self, c):
        self.across(c).wait_recv()
        if not self.inplace:
            self.load(c).wait()
        for i in (1, 0, 2):
            line = self.lines[i]
            add_rows(self.hold(c, line), self.hold(c, line), self.crossed.at[c, line])
            self.along(c, i).start()

    def finish(self, c):
        row, col = self.b.at(c)
        for i in range(LINE - 1):
            self.along(c, i).wait_recv()
        out_col = aligned(col - self.b.first, 128)
        out = self.out.at[pl.ds(row, self.b.rows), pl.ds(out_col, self.b.cols)]
        landed = [self.landed.at[c, i] for i in range(LINE - 1)]
        add_rows(out, self.hold(c, self.z), self.crossed.at[c, self.z], *landed)

    def pump(self, t):
        pl.when(t + self.ahead < self.b.count)(lambda: self.begin(t + self.ahead))
        pl.when(t < self.b.count)(lambda: self.fold(t))
        pl.when(t >= LAG)(lambda: self.finish(t - LAG))

    def drain(self):
        def step(c):
            self.across(c).wait_send()
            for i in range(LINE - 1):
                self.along(c, i).wait_send()

        loop(self.b.count, step)


class Idle:
    ticks = done = 0

    def start(self):
        pass

    def pump(self, t):
        pass

    def arrive(self):
        pass

    def drain(self):
        pass


class TpSum:
    def __init__(self, partial, out, bufs, sems, own_sems=None):
        self.p, self.out = partial, out
        self.crossed, self.other = bufs
        self.c_s, self.c_r, self.x_s, self.x_r, self.o_s, self.o_r = sems
        self.core = lax.rem(lax.axis_index("tp"), 2)
        self.beside, self.far = tp_peers()
        self.half = partial.shape[0] // 2
        self.rows = self.half // TP_PARTS
        self.own_s = own_sems

    @staticmethod
    def scratch(rows, wide):
        return [pltpu.VMEM((rows // 2, wide), BF16)] * 2 + [DMA((TP_PARTS,))] * 6

    def spot(self, k, which):
        return pl.ds(pl.multiple_of(which * self.half + k * self.rows, 16), self.rows)

    def part(self, k):
        return pl.ds(aligned(k * self.rows, 16), self.rows)

    def first(self, k):
        return remote(
            self.p.at[self.spot(k, 1 - self.core)],
            self.crossed.at[self.part(k)],
            self.c_s.at[k],
            self.c_r.at[k],
            tp=self.beside,
        )

    def second(self, k):
        here = self.out.at[self.spot(k, self.core)]
        return remote(here, self.other.at[self.part(k)], self.x_s.at[k], self.x_r.at[k], tp=self.far)

    def third(self, k, which):
        here = self.out.at[self.spot(k, which)]
        return remote(here, here, self.o_s.at[k], self.o_r.at[k], tp=self.beside)

    def load(self, k):
        mine = self.spot(k, self.core)
        return pltpu.make_async_copy(self.p.at[mine], self.out.at[mine], self.own_s.at[k])

    def stage_one(self, k):
        self.first(k).start()
        if self.own_s is not None:
            self.load(k).start()

    def stage_two(self, k):
        self.first(k).wait_recv()
        mine = self.spot(k, self.core)
        held = self.p.at[mine]
        if self.own_s is not None:
            self.load(k).wait()
            held = self.out.at[mine]
        add_rows(self.out.at[mine], held, self.crossed.at[self.part(k)])
        self.second(k).start()

    def stage_three(self, k):
        self.second(k).wait()
        mine = self.out.at[self.spot(k, self.core)]
        add_rows(mine, mine, self.other.at[self.part(k)])
        self.third(k, self.core).start()

    def stage_four(self, k):
        self.third(k, 1 - self.core).wait_recv()

    def sent(self, k):
        self.third(k, self.core).wait_send()

    def drain(self, sent=False):
        def step(k):
            self.first(k).wait_send()
            if not sent:
                self.sent(k)

        loop(TP_PARTS, step)


def params(number):
    return pltpu.CompilerParams(
        collective_id=number, has_side_effects=True, vmem_limit_bytes=VMEM_LIMIT
    )


def plain_params():
    return pltpu.CompilerParams(vmem_limit_bytes=VMEM_LIMIT)


ANY = pl.BlockSpec(memory_space=pl.ANY)
IN_VMEM = pl.BlockSpec(memory_space=pltpu.VMEM)
IN_SMEM = pl.BlockSpec(memory_space=pltpu.SMEM)


def shaped(shape, dtype):
    return jax.ShapeDtypeStruct(shape, dtype)


def segment_sum(value, seg):
    high = value.astype(BF16)
    low = (value - high.astype(F32)).astype(BF16)
    return dot_nn(high, seg) + dot_nn(low, seg)


def head_inverse(value, seg):
    return lax.rsqrt(segment_sum(value * value, seg) * (1.0 / HEAD) + EPS)


def thrice(table):
    return jnp.concatenate([table] * 3, axis=1)


def rope(value, cosines, sine_a, sine_b):
    wide = value.shape[1]
    ahead = pltpu.roll(value, wide - HEAD // 4, 1)
    behind = pltpu.roll(value, HEAD // 4, 1)
    return value * cosines + ahead * sine_a + behind * sine_b


def rope_back(grad, cosines, sine_a, sine_b):
    wide = grad.shape[1]
    ahead = pltpu.roll(grad * sine_b, wide - HEAD // 4, 1)
    behind = pltpu.roll(grad * sine_a, HEAD // 4, 1)
    return grad * cosines + ahead + behind


def rope_tables(row_count):
    lane = np.arange(PAIR)
    within = lane % HEAD
    quarter = HEAD // 4
    which = within // quarter
    freqs = (ROPE_BASE ** (-(within % quarter).astype(np.float32) / np.float32(quarter))).astype(np.float32)
    row = np.arange(row_count)
    frame, place = (row // FRAME_TOK).astype(np.float32), (row % FRAME_TOK).astype(np.float32)
    position = np.where(which[None, :] < 2, frame[:, None], place[:, None])
    angles = (position * freqs[None, :]).astype(np.float32)
    cosines, sines = np.cos(angles), np.sin(angles)
    even = (which % 2 == 0)[None, :]
    return (
        jnp.asarray(cosines.astype(np.float32)),
        jnp.asarray(np.where(even, -sines, 0.0).astype(np.float32)),
        jnp.asarray(np.where(even, 0.0, sines).astype(np.float32)),
    )


def segment_ones(wide):
    head = np.arange(wide) // HEAD
    return jnp.asarray((head[:, None] == head[None, :]).astype(np.float32)).astype(BF16)


def live_rows(frames_ref, start, rows, wide):
    row = start + lax.broadcasted_iota(jnp.int32, (rows, wide), 0)
    return (row < frames_ref[0] * FRAME_TOK).astype(F32)


def half_mask(rows, head, dtype):
    lane = lax.broadcasted_iota(jnp.int32, (rows, PAIR), 1)
    return ((lane < HEAD) if head == 0 else (lane >= HEAD)).astype(dtype)


def pair_lanes(pair, wide=PAIR):
    return pl.ds(pl.multiple_of(pair * wide, PAIR), wide)


def block_rows(block, rows):
    return pl.ds(pl.multiple_of(block * rows, rows), rows)


def paced(count, step, *plans):
    jobs = []
    for engine, pumps in plans:
        pumps = min(pumps, engine.ticks - engine.done)
        if pumps > 0:
            jobs.append((engine, pumps, engine.done))
            engine.done += pumps

    def body(i):
        step(i)
        for engine, pumps, base in jobs:
            if pumps <= count:
                every = count // pumps
                turn = lax.div(i, every)
                now = (lax.rem(i, every) == every - 1) & (turn < pumps)
                pl.when(now)(functools.partial(engine.pump, base + turn))
            else:
                each = -(-pumps // count)
                for j in range(each):
                    pl.when(i * each + j < pumps)(functools.partial(engine.pump, base + i * each + j))

    loop(count, body)


def finish_pumps(engine):
    base = engine.done
    if base < engine.ticks:
        loop(engine.ticks - base, lambda i: engine.pump(base + i))
    engine.done = engine.ticks


class Named:
    def __init__(self):
        self.ins, self.outs, self.scratch, self.late = {}, {}, {}, {}

    def take(self, refs):
        found, at = {}, 0
        for name in (*self.ins, *self.outs):
            found[name] = refs[at]
            at += 1
        for name, item in self.scratch.items():
            many = isinstance(item, list)
            found[name] = refs[at : at + len(item)] if many else refs[at]
            at += len(item) if many else 1
        count = len(self.late)
        copies = []
        for i, name in enumerate(self.late):
            found[name] = refs[at + count + i]
            copies.append(pltpu.make_async_copy(refs[at + i], found[name], refs[at + 2 * count + i]))
        r = types.SimpleNamespace(**found)
        r.fetch = types.SimpleNamespace(**dict(zip(self.late, copies)))
        r.fetches = copies
        return r

    def call(self, kernel, compiler_params):
        flat = []
        for item in self.scratch.values():
            flat += item if isinstance(item, list) else [item]
        late = list(self.late.values())
        flat += [pltpu.VMEM(value.shape, value.dtype) for value in late] + [DMA] * len(late)
        ins, outs = list(self.ins.values()), list(self.outs.values())
        first, many = len(ins) + len(outs), len(late)

        def body(*refs):
            own = refs[: len(ins)] + refs[len(ins) + many : first + many]
            scratch = refs[first + many : len(refs) - 2 * many]
            kernel(*own, *scratch, *refs[len(ins) : len(ins) + many], *refs[len(refs) - 2 * many :])

        results = pl.pallas_call(
            body,
            out_shape=[shape for shape, _ in outs],
            in_specs=[spec for _, spec in ins] + [ANY] * many,
            out_specs=[spec for _, spec in outs],
            scratch_shapes=flat,
            compiler_params=compiler_params,
        )(*[value for value, _ in ins], *late)
        return types.SimpleNamespace(**dict(zip(self.outs, results)))


class Opening:
    def __init__(self, r):
        self.r = r
        self.me, self.tp = lax.axis_index("dp"), lax.axis_index("tp")
        self.peers, (self.beside, self.far) = dp_peers(), tp_peers()
        self.sources = [lax.rem(self.me + GRID - step, GRID) for step in range(1, GRID)]
        self.share = r.text_all.shape[1] // 4
        self.cond, self.small, self.parts, self.slabs, self.quarters = (r.sems_set[2 * i : 2 * i + 2] for i in range(5))
        self.own_s = r.sems_set[10]

    def send(self, sems, i, src, dst, **where):
        return remote(src, dst, sems[0].at[i], sems[1].at[i], **where)

    def quarter(self, which):
        rows = pl.ds(pl.multiple_of(which * self.share, 16), self.share)
        return self.r.text_all.at[:, rows, :]

    def slab(self, there, origin):
        depth = self.r.text_all.shape[2]
        rows = pl.ds(pl.multiple_of(self.tp * self.share, 16), self.share)
        src = self.r.text.at[rows, pl.ds(pl.multiple_of(there * depth, 128), depth)]
        return src, self.r.text_all.at[origin, rows, :]

    def cond_out(self, i):
        there = self.peers[i]
        return self.send(self.cond, i, self.r.cond.at[there], self.r.conds.at[self.me], dp=there)

    def small_out(self, i):
        return self.send(self.small, i, self.r.small, self.r.smalls.at[self.me], dp=self.peers[i])

    def slab_out(self, i):
        return self.send(self.slabs, i, *self.slab(self.peers[i], self.me), dp=self.peers[i])

    def part_out(self, i):
        there = self.peers[i]
        return self.send(self.parts, i, self.r.part.at[there], self.r.parts.at[self.me], dp=there)

    def came(self, sems, i, ref):
        self.send(sems, i, ref, ref, dp=self.me).wait_recv()

    def begin(self):
        r, me = self.r, self.me
        for i in range(GRID - 1):
            self.cond_out(i).start()
            self.small_out(i).start()
        for i in range(GRID - 1):
            self.slab_out(i).start()
        pltpu.make_async_copy(*self.slab(me, me), self.own_s).start()
        r.conds[pl.ds(me, 1)] = r.cond[pl.ds(me, 1)]
        r.smalls[pl.ds(me, 1)] = r.small[...][None]

    def partial_rows(self):
        r, me = self.r, self.me
        for i, here in enumerate(self.sources):
            self.came(self.cond, i, r.conds.at[here])
        cond = jnp.concatenate([r.conds[i] for i in range(GRID)], axis=0)
        act = (cond * (1.0 / (1.0 + jnp.exp(-cond)))).astype(BF16)
        r.act[...] = act.astype(F32)
        width = r.w_ada.shape[1] // 4
        for i in range(4):
            cols = pl.ds(i * width, width)
            product = dot_nn(act, r.w_ada[:, cols])
            for j in range(GRID):
                r.part[j, :, cols] = product[j : j + 1, :]
        for i in range(GRID - 1):
            self.part_out(i).start()
        r.parts[pl.ds(me, 1)] = r.part[pl.ds(me, 1)]

    def spread(self):
        pltpu.make_async_copy(*self.slab(self.me, self.me), self.own_s).wait()
        for i, here in enumerate(self.sources):
            self.came(self.slabs, i, self.slab(here, here)[1])
        mine = self.quarter(self.tp)
        self.send(self.quarters, 0, mine, mine, tp=self.beside).start()
        self.send(self.quarters, 1, mine, mine, tp=self.far).start()

    def modulate(self):
        r = self.r
        for i, here in enumerate(self.sources):
            self.came(self.parts, i, r.parts.at[here])
            self.came(self.small, i, r.smalls.at[here])
        wide = r.rows.shape[1]
        bias = r.small.shape[1] - 2 * (wide // GRID)
        ends = r.small.shape[1]
        smalls = [r.smalls[i] for i in range(GRID)]
        mods = sum(r.parts[i] for i in range(GRID)) + jnp.concatenate([v[:, :bias] for v in smalls], axis=1)
        gain_one = jnp.concatenate([v[:, bias : bias + wide // GRID] for v in smalls], axis=1)
        gain_two = jnp.concatenate([v[:, bias + wide // GRID : ends] for v in smalls], axis=1)
        lift_one, lift_two = 1.0 + mods[:, :wide], 1.0 + mods[:, 2 * wide : 3 * wide]
        tanh_one, tanh_two = jnp.tanh(mods[:, wide : 2 * wide]), jnp.tanh(mods[:, 3 * wide :])
        values = (gain_one * lift_one, tanh_one, gain_two * lift_two, tanh_two, gain_one, lift_one, gain_two, lift_two)
        for i, value in enumerate(values):
            r.rows[i : i + 1, :] = value

    def pass_on(self):
        from_far = self.quarter(lax.rem(self.tp + 2, 4))
        self.send(self.quarters, 1, from_far, from_far, tp=self.far).wait_recv()
        self.send(self.quarters, 2, from_far, from_far, tp=self.beside).start()

    def collect(self):
        near = self.quarter(self.tp + 1 - 2 * lax.rem(self.tp, 2))
        self.send(self.quarters, 0, near, near, tp=self.beside).wait_recv()
        self.send(self.quarters, 2, near, near, tp=self.beside).wait_recv()

    def multiply(self, i):
        r = self.r
        cols = r.w_tk.shape[1]
        rows = r.text_all[i]
        line, y = lax.div(i, 2), lax.rem(i, 2)
        r.products[line, y, :, :cols] = dot_nn(rows, r.w_tk[...]).astype(BF16)
        r.products[line, y, :, cols:] = dot_nn(rows, r.w_tv[...]).astype(BF16)

    def drain(self):
        mine = self.quarter(self.tp)
        self.send(self.quarters, 0, mine, mine, tp=self.beside).wait_send()
        self.send(self.quarters, 1, mine, mine, tp=self.far).wait_send()
        self.send(self.quarters, 2, mine, mine, tp=self.beside).wait_send()
        for i in range(GRID - 1):
            self.cond_out(i).wait_send()
            self.small_out(i).wait_send()
            self.slab_out(i).wait_send()
            self.part_out(i).wait_send()


def pack_kernel(q, k, v, out, gate, up, down, attn_ref, one_ref, two_ref):
    cols = q.shape[1]
    for i, w in enumerate((q, k, v)):
        attn_ref[:, i * cols : (i + 1) * cols] = w[...]
    attn_ref[:, 3 * cols :] = out[...]
    for b in range(gate.shape[1] // UNITS):
        ref, at = (one_ref, b) if b < ONES else (two_ref, b - ONES)
        here = slice(b * UNITS, (b + 1) * UNITS)
        for i, value in enumerate((gate[:, here], up[:, here], down[:, here])):
            ref[:, (3 * at + i) * UNITS : (3 * at + i + 1) * UNITS] = value


def pack(q, k, v, out, gate, up, down):
    depth, cols = q.shape
    blocks = gate.shape[1] // UNITS
    widths = (4 * cols, 3 * UNITS * ONES, 3 * UNITS * (blocks - ONES))
    return pl.pallas_call(
        pack_kernel,
        out_shape=[shaped((depth, wide), BF16) for wide in widths],
        in_specs=[IN_VMEM] * 7,
        out_specs=[IN_VMEM] * 3,
        compiler_params=plain_params(),
    )(q, k, v, out, gate, up, down)


def forward_kernel(named, grid, cuts, *refs):
    r = named.take(refs)
    tok, weights, rows_ref, heads_ref = r.tok, r.weights, r.rows, r.heads
    cos_ref, sa_ref, sb_ref, seg_ref = r.cos, r.sa, r.sb, r.seg
    attn_sum, partial, mixed, ty = r.attn_sum, r.partial, r.mixed, r.ty
    sums = TpSum(partial, attn_sum, r.tp_set[:2], r.tp_set[2:8])
    mult, tanh_attn, mult_two = rows_ref.at[0:1], rows_ref.at[1:2], rows_ref.at[2:3]
    qgain, kgain, kygain, gate = (heads_ref.at[i : i + 1] for i in range(4))
    rows, cols = r.q_rot.shape
    step_rows = 256
    blocks_here = rows // step_rows
    pairs = cols // PAIR
    attn_engine = text_engine = engine = Idle()
    for fetch in r.fetches:
        fetch.start()
    if grid:
        opening = Opening(r)
        attn_engine = GatherChain(cuts[0], r.attn_shard, weights, r.attn_set, A_A)
        text_engine = Scatter(cuts[1], r.products, ty, r.text_set, True, ahead=A_P)
        engine = GatherChain(cuts[2], r.ffn_shard, r.full_ffn, r.ffn_set)
        greet(dp_peers(), tp_peers())
        opening.begin()
        attn_engine.start()
        opening.partial_rows()
        paced(1, lambda i: None, (attn_engine, O_1))
        opening.spread()
        paced(1, lambda i: None, (attn_engine, O_2))
        opening.modulate()
        paced(1, lambda i: None, (attn_engine, O_3))
        opening.pass_on()
        paced(1, lambda i: None, (attn_engine, O_4))
        opening.collect()
        r.fetch.w_tk.wait()
        r.fetch.w_tv.wait()
        paced(GRID, opening.multiply, (attn_engine, 2))
        text_engine.start()
        engine.start()
        finish_pumps(attn_engine)
        attn_engine.arrive()
    else:
        greet([], tp_peers())

    def project(i):
        here = block_rows(i, step_rows)
        x = tok[here, :].astype(F32)
        inverse = lax.rsqrt(jnp.mean(x * x, axis=-1, keepdims=True) + EPS)
        h = (x * inverse * mult[...]).astype(BF16)
        r.h_one[here, :] = h
        cosines, sine_a, sine_b = thrice(cos_ref[here, :]), thrice(sa_ref[here, :]), thrice(sb_ref[here, :])
        q = dot_nn(h, weights[:, :cols])
        r.q_pre[here, :] = q
        qn = q * head_inverse(q, seg_ref[...]) * qgain[...]
        r.q_text[here, :] = (qn * SCALE).astype(BF16)
        r.q_rot[here, :] = (rope(qn, cosines, sine_a, sine_b) * SCALE).astype(BF16)
        k = dot_nn(h, weights[:, cols : 2 * cols])
        r.k_pre[here, :] = k
        kn = k * head_inverse(k, seg_ref[...]) * kgain[...]
        r.k_rot[here, :] = rope(kn, cosines, sine_a, sine_b).astype(BF16)
        v = dot_nn(h, weights[:, 2 * cols : 3 * cols]).astype(BF16)
        r.values[here, :] = v
        live = live_rows(r.frames, i * step_rows, step_rows, PAIR).astype(BF16)
        for pair in range(pairs):
            r.vaug[here, 2 * pair * PAIR : (2 * pair + 1) * PAIR] = v[:, pair * PAIR : (pair + 1) * PAIR] * live
            r.vaug[here, (2 * pair + 1) * PAIR : (2 * pair + 2) * PAIR] = live

    def attention(q_ref, k_ref, v_ref, inv_ref):
        def step(i):
            pair, block = lax.div(i, blocks_here), lax.rem(i, blocks_here)
            here, lanes = block_rows(block, step_rows), pair_lanes(pair)
            q = q_ref[here, lanes]
            keys = k_ref[:, lanes]
            values = v_ref[:, pair_lanes(pair, 2 * PAIR)]
            outs = jnp.zeros((step_rows, PAIR), F32)
            total = jnp.zeros((step_rows, PAIR), F32)
            for head in range(2):
                p = jnp.exp(dot_nt(q * half_mask(step_rows, head, BF16), keys)).astype(BF16)
                both = dot_nn(p, values)
                wide_mask = half_mask(step_rows, head, F32)
                outs = outs + both[:, :PAIR] * wide_mask
                total = total + both[:, PAIR:] * wide_mask
            inverse = 1.0 / total
            inv_ref[here, lanes] = inverse
            return here, lanes, outs * inverse

        return step

    self_attention = attention(r.q_rot, r.k_rot, r.vaug, r.inv_l)
    text_attention = attention(r.q_text, r.kyr, r.vyaug, r.inv_lt)

    def attend(i):
        here, lanes, out = self_attention(i)
        r.mixed_self[here, lanes] = out
        r.self_o[here, lanes] = out.astype(BF16)

    def attend_text(i):
        here, lanes, out = text_attention(i)
        r.text_o[here, lanes] = out.astype(BF16)
        mixed[here, lanes] = (r.mixed_self[here, lanes] + gate[:, lanes] * out).astype(BF16)

    half_blocks = blocks_here // 2
    parts_each = TP_PARTS // half_blocks

    def output(which):
        def step(i):
            block = which * half_blocks + i
            for pair in range(pairs):
                attend_text(pair * blocks_here + block)
            here = block_rows(block, step_rows)
            partial[here, :] = dot_nt(mixed[here, :], weights[:, 3 * cols :]).astype(BF16)

        return step

    def output_send(i):
        output(1 - sums.core)(i)
        loop(parts_each, lambda k: sums.stage_one(i * parts_each + k))

    def output_add(i):
        output(sums.core)(i)
        loop(parts_each, lambda k: sums.stage_two(i * parts_each + k))

    for fetch in (r.fetch.tok, r.fetch.cos, r.fetch.sa, r.fetch.sb, r.fetch.seg):
        fetch.wait()
    paced(blocks_here, project, (text_engine, 4), (engine, 2))
    paced(pairs * blocks_here, attend, (text_engine, 4), (engine, 3))
    finish_pumps(text_engine)

    ky = ty[:, :cols]
    r.ky_pre[...] = ky
    r.kyr[...] = (ky * head_inverse(ky, seg_ref[...]) * kygain[...]).astype(BF16)
    vy = ty[:, cols:].astype(BF16)
    r.vy[...] = vy
    for pair in range(pairs):
        r.vyaug[:, 2 * pair * PAIR : (2 * pair + 1) * PAIR] = vy[:, pair * PAIR : (pair + 1) * PAIR]
        r.vyaug[:, (2 * pair + 1) * PAIR : (2 * pair + 2) * PAIR] = jnp.ones((vy.shape[0], PAIR), BF16)
    paced(half_blocks, output_send, (engine, 2))
    paced(half_blocks, output_add, (engine, 2))

    def update(k, which):
        here = sums.spot(k, which)
        live = live_rows(r.frames, which * sums.half + k * sums.rows, sums.rows, tok.shape[1])
        state = tok[here, :].astype(F32) + live * tanh_attn[...] * attn_sum[here, :].astype(F32)
        inverse = lax.rsqrt(jnp.mean(state * state, axis=-1, keepdims=True) + EPS)
        r.h_two[here, :] = (state * inverse * mult_two[...]).astype(BF16)

    def three(k):
        sums.stage_three(k)
        update(k, sums.core)

    paced(TP_PARTS, three, (engine, 4))

    def four(k):
        sums.stage_four(k)
        update(k, 1 - sums.core)

    paced(TP_PARTS, four, (engine, 1))
    finish_pumps(engine)
    engine.arrive()
    sums.drain()
    if grid:
        opening.drain()
    attn_engine.drain()
    text_engine.drain()
    engine.drain()


def forward(clips, frames, tokens, heads_table, tables, seg, ffn_shard, start):
    rows, wide = tokens.shape
    cols = heads_table.shape[1]
    grid = clips == GRID
    depth, ffn_wide = ffn_shard.shape
    n = Named()
    n.ins.update(frames=(frames, IN_SMEM), heads=(heads_table, IN_VMEM))
    cuts = None
    if grid:
        attn_shard, cond, small, w_ada, text, w_tk, w_tv = start
        rows_t, slab = text.shape[0], w_tk.shape[0]
        mods = w_ada.shape[1]
        n.ins.update(attn_shard=(attn_shard, ANY), cond=(cond, IN_VMEM), small=(small, IN_VMEM))
        n.ins.update(w_ada=(w_ada, IN_VMEM), text=(text, ANY))
        n.late.update(w_tk=w_tk, w_tv=w_tv)
        n.ins.update(ffn_shard=(ffn_shard, ANY))
        cuts = (
            Blocks(*attn_shard.shape, 96, 384),
            Blocks(rows_t, 2 * cols, 32, 2 * cols),
            Blocks(depth, ffn_wide, 96, 384),
        )
    else:
        weights, rows_table, ty = start
        rows_t = ty.shape[0]
        n.ins.update(weights=(weights, IN_VMEM), rows=(rows_table, IN_VMEM), ty=(ty, IN_VMEM))
    f, b = (shaped((rows, cols), F32), IN_VMEM), (shaped((rows, cols), BF16), IN_VMEM)
    ft, bt = (shaped((rows_t, cols), F32), IN_VMEM), (shaped((rows_t, cols), BF16), IN_VMEM)
    whole = (shaped((rows, wide), BF16), IN_VMEM)
    n.outs.update(q_pre=f, k_pre=f, q_rot=b, k_rot=b, q_text=b, values=b, self_o=b, inv_l=f, ky_pre=ft, kyr=bt, vy=bt)
    n.outs.update(text_o=b, inv_lt=f, h_one=whole, mixed=b, attn_sum=whole, h_two=whole)
    n.scratch.update(
        vaug=pltpu.VMEM((rows, 2 * cols), BF16),
        vyaug=pltpu.VMEM((rows_t, 2 * cols), BF16),
        partial=pltpu.VMEM((rows, wide), BF16),
        mixed_self=pltpu.VMEM((rows, cols), F32),
        tp_set=TpSum.scratch(rows, wide),
    )
    if grid:
        n.outs.update(
            weights=(shaped((GRID * attn_shard.shape[0], attn_shard.shape[1]), BF16), IN_VMEM),
            rows=(shaped((8, wide), F32), IN_VMEM),
            act=(shaped((GRID, cond.shape[2]), F32), IN_VMEM),
            text_all=(shaped((GRID, rows_t, slab), BF16), IN_VMEM),
            full_ffn=(shaped((GRID * depth, ffn_wide), BF16), ANY),
        )
        n.scratch.update(
            ty=pltpu.VMEM((rows_t, 2 * cols), F32),
            products=pltpu.VMEM((LINE, 2, rows_t, 2 * cols), BF16),
            smalls=pltpu.VMEM((GRID,) + small.shape, F32),
            conds=pltpu.VMEM((GRID, 1, cond.shape[2]), F32),
            part=pltpu.VMEM((GRID, 1, mods), F32),
            parts=pltpu.VMEM((GRID, 1, mods), F32),
            sems_set=[DMA((GRID - 1,))] * 8 + [DMA((3,))] * 2 + [DMA],
            attn_set=GatherChain.scratch(cuts[0].count),
            text_set=Scatter.scratch(cuts[1], True),
            ffn_set=GatherChain.scratch(cuts[2].count),
        )
    n.late.update(tok=tokens, cos=tables[0], sa=tables[1], sb=tables[2], seg=seg)
    out = n.call(functools.partial(forward_kernel, n, grid, cuts), params(1))
    if not grid:
        out.weights, out.rows, out.text_all = weights, rows_table, jnp.zeros((1, 16, 128), BF16)
    return out


UNITS = 256
ONES = 3
SP = ((0, 0), (2, 2), (2, 2), (2, 0))


def ffn_kernel(named, cut, cut_back, *refs):
    r = named.take(refs)
    engine, scatter = Idle(), Idle()
    for fetch in r.fetches:
        fetch.start()
    if cut is not None:
        engine = GatherChain(cut, r.shard, r.w_two, r.gather_set)
        scatter = Scatter(cut_back, r.grads, r.out, r.scatter_set)
        greet(dp_peers(), [])
        engine.start()
    rows, wide = r.h_two.shape
    step_rows = 256
    count = rows // step_rows
    tall = wide // LINE
    tanh_two = r.rows[3:4, :]
    ones, twos = r.w_one.shape[1] // (3 * UNITS), r.w_two.shape[1] // (3 * UNITS)

    def start_rows(i):
        here = block_rows(i, step_rows)
        live = live_rows(r.frames, i * step_rows, step_rows, wide)
        r.grad_ffn[here, :] = (live * tanh_two * r.cot[here, :].astype(F32)).astype(BF16)

    def copy(b):
        place = r.grads.at[:, :, :, pl.ds(b * 3 * UNITS, 3 * UNITS)]
        return pltpu.make_async_copy(r.staged.at[b % 2], place, r.stage_s.at[b % 2])

    def block(b):
        w = r.w_one if b < ones else r.w_two
        first = (b if b < ones else b - ones) * 3 * UNITS
        last = b == ones + twos - 1
        dgu = r.dgu_last if last else r.dgu

        def units(i):
            here = block_rows(i, step_rows)
            both = dot_nn(r.h_two[here, :], w[:, first : first + 2 * UNITS])
            gate, up = both[:, :UNITS], both[:, UNITS:]
            back = dot_nn(r.grad_ffn[here, :], w[:, first + 2 * UNITS : first + 3 * UNITS])
            logistic = 1.0 / (1.0 + jnp.exp(-gate))
            swish = gate * logistic
            r.hid[here, b * UNITS : (b + 1) * UNITS] = (swish * up).astype(BF16)
            d_gate = (back * up * logistic * (1.0 + gate * (1.0 - logistic))).astype(BF16)
            d_both = jnp.concatenate([d_gate, (back * swish).astype(BF16)], axis=1)
            dgu[here, :] = d_both
            added = dot_nt(d_both, w[:, first : first + 2 * UNITS])
            if b == 0:
                r.total[here, :] = added
            elif not last:
                r.total[here, :] += added
            else:
                r.partial[here, :] = (r.total[here, :] + added).astype(BF16)

        def products(m):
            lanes = pl.ds(pl.multiple_of(m * tall, 128), tall)
            downs = dot_tn(r.grad_ffn[:, lanes], r.hid[:, b * UNITS : (b + 1) * UNITS]).astype(BF16)
            ins = dot_tn(r.h_two[:, lanes], dgu[...]).astype(BF16)
            for y in range(2):
                part = slice(y * tall // 2, (y + 1) * tall // 2)
                r.staged[b % 2, m, y, :, : 2 * UNITS] = ins[part]
                r.staged[b % 2, m, y, :, 2 * UNITS :] = downs[part]

        pumps = 1 if b < ones else 2
        paced(count, units, (engine, pumps), (scatter, SP[b][0]))
        if not last:
            if b >= 2 and (b > 2 or cut is None):
                copy(b - 2).wait()
            paced(LINE, products, (engine, pumps), (scatter, SP[b][1]))
            copy(b).start()
        if b == 0 and cut is not None:
            copy(0).wait()
            scatter.start()

    paced(count, start_rows, (engine, 1))
    r.fetch.h_two.wait()
    r.fetch.w_one.wait()
    each = cut.count // twos if cut is not None else 0
    for b in range(ones):
        block(b)
    for b in range(ones, ones + twos):
        if cut is not None:
            need = min(engine.ticks, (b - ones + 1) * each + 2)
            while engine.done < need:
                paced(1, lambda i: None, (engine, 1))
            engine.arrive((b - ones) * each, each)
        block(b)
    copy(ones + twos - 3).wait()
    copy(ones + twos - 2).wait()
    finish_pumps(scatter)
    scatter.drain()
    engine.drain()


def ffn(clips, frames, h_two, cotangent, rows_table, w_one, second):
    rows, wide = h_two.shape
    half_wide = second.shape[1]
    blocks = (w_one.shape[1] + half_wide) // (3 * UNITS)
    grid = clips == GRID
    depth = wide // GRID
    n = Named()
    n.ins.update(frames=(frames, IN_SMEM), cot=(cotangent, IN_VMEM), rows=(rows_table, IN_VMEM))
    n.late.update(h_two=h_two, w_one=w_one)
    whole = (shaped((rows, wide), BF16), IN_VMEM)
    cut = Blocks(depth, half_wide, 96, 384) if grid else None
    cut_back = None
    if grid:
        n.ins.update(shard=(second, ANY))
        cut_back = Blocks(depth, 3 * UNITS, 96, 256)
        n.outs.update(w_two=(shaped((wide, half_wide), BF16), IN_VMEM), out=(shaped((depth, 3 * UNITS), F32), IN_VMEM))
        n.scratch.update(gather_set=GatherChain.scratch(cut.count), scatter_set=Scatter.scratch(cut_back))
    else:
        n.ins.update(w_two=(second, IN_VMEM))
    n.outs.update(partial=whole, grad_ffn=whole, hid=(shaped((rows, blocks * UNITS), BF16), IN_VMEM))
    n.outs.update(dgu_last=(shaped((rows, 2 * UNITS), BF16), IN_VMEM))
    n.outs.update(grads=(shaped((LINE, 2, depth, (blocks - 1) * 3 * UNITS), BF16), ANY))
    n.scratch.update(
        dgu=pltpu.VMEM((rows, 2 * UNITS), BF16),
        total=pltpu.VMEM((rows, wide), F32),
        staged=pltpu.VMEM((2, LINE, 2, depth, 3 * UNITS), BF16),
        stage_s=DMA((2,)),
    )
    out = n.call(functools.partial(ffn_kernel, n, cut, cut_back), params(5) if grid else plain_params())
    if not grid:
        out.w_two = second
    return out


def state_kernel(named, cut, *refs):
    r = named.take(refs)
    sums = TpSum(r.partial, r.grad_attn, r.tp_set[:2], r.tp_set[2:8], r.tp_set[8])
    tanh_attn, mult = r.rows.at[1:2], r.rows.at[2:3]
    engine = Idle()
    if cut is not None:
        engine = Scatter(cut, r.grads, r.out, r.scatter_set, ahead=A_S0)
        greet(dp_peers(), tp_peers())
        engine.start()
    else:
        greet([], tp_peers())
    loop(TP_PARTS, sums.stage_one)
    rows, wide = r.tok.shape
    step_rows = 256
    tall = wide // LINE
    blocks = r.hid.shape[1] // UNITS
    ones = r.w_one.shape[1] // (3 * UNITS)

    def down_copy(b):
        w = r.w_one if b < ones else r.w_two
        first = (b if b < ones else b - ones) * 3 * UNITS + 2 * UNITS
        place = r.down.at[:, pl.ds(b * UNITS, UNITS)]
        return pltpu.make_async_copy(w.at[:, pl.ds(first, UNITS)], place, r.down_s.at[b])

    for fetch in r.fetches:
        fetch.start()
    for b in range(blocks):
        down_copy(b).start()
    r.colsums[...] = jnp.zeros_like(r.colsums)

    def products(m):
        lanes = pl.ds(pl.multiple_of(m * tall, 128), tall)
        downs = dot_tn(r.grad_ffn[:, lanes], r.hid[:, (blocks - 1) * UNITS :]).astype(BF16)
        ins = dot_tn(r.h_two[:, lanes], r.dgu[...]).astype(BF16)
        for y in range(2):
            part = slice(y * tall // 2, (y + 1) * tall // 2)
            r.g_last[m, y, :, : 2 * UNITS] = ins[part]
            r.g_last[m, y, :, 2 * UNITS :] = downs[part]

    def p_copy(i):
        place = r.p_ffn.at[block_rows(i, step_rows)]
        return pltpu.make_async_copy(r.p_staged.at[lax.rem(i, 2)], place, r.p_s.at[lax.rem(i, 2)])

    def p_block(i):
        pl.when(i >= 2)(lambda: p_copy(i - 2).wait())
        r.p_staged[lax.rem(i, 2)] = dot_nt(r.hid[block_rows(i, step_rows), :], r.down[...]).astype(BF16)
        p_copy(i).start()

    def update(k, which):
        here = sums.spot(k, which)
        live = live_rows(r.frames, which * sums.half + k * sums.rows, sums.rows, wide)
        added = r.attn_sum[here, :].astype(F32)
        state = r.tok[here, :].astype(F32) + live * tanh_attn[...] * added
        inverse = lax.rsqrt(jnp.mean(state * state, axis=-1, keepdims=True) + EPS)
        hat = state * inverse
        g = r.grad_attn[here, :].astype(F32)
        scaled = g * mult[...]
        g_hat = g * hat
        back = inverse * (scaled - hat * jnp.mean(scaled * hat, axis=-1, keepdims=True))
        total = r.cot[here, :].astype(F32) + back
        r.grad_state[here, :] = total.astype(BF16)
        live_total = live * total
        r.grad_attn[here, :] = (tanh_attn[...] * live_total).astype(BF16)
        r.colsums[0:1, :] += jnp.sum(g_hat, axis=0, keepdims=True)
        r.colsums[1:2, :] += jnp.sum(live_total * added, axis=0, keepdims=True)

    paced(TP_PARTS, sums.stage_two, (engine, 2))
    for fetch in (r.fetch.h_two, r.fetch.grad_ffn, r.fetch.hid, r.fetch.dgu):
        fetch.wait()
    paced(LINE, products, (engine, 2))
    for b in range(blocks):
        down_copy(b).wait()
    paced(rows // step_rows, p_block, (engine, 2))

    for fetch in (r.fetch.tok, r.fetch.attn_sum, r.fetch.cot):
        fetch.wait()

    def three(k):
        sums.stage_three(k)

        @pl.when(k > 0)
        def _():
            sums.sent(k - 1)
            update(k - 1, sums.core)

    paced(TP_PARTS, three, (engine, 8))
    sums.sent(TP_PARTS - 1)
    update(TP_PARTS - 1, sums.core)

    def four(k):
        sums.stage_four(k)
        update(k, 1 - sums.core)

    paced(TP_PARTS, four, (engine, 2))
    finish_pumps(engine)
    for i in (1, 2):
        p_copy(rows // step_rows - i).wait()
    sums.drain(True)
    engine.drain()


def state_backward(clips, frames, tokens, attn_sum, cotangent, rows_table, h_two, w_one, fed):
    rows, wide = tokens.shape
    grid = clips == GRID
    depth = wide // GRID
    units, scattered = fed.hid.shape[1], fed.grads.shape[-1]
    cut = Blocks(depth, scattered - 3 * UNITS, 96, 256, 3 * UNITS) if grid else None
    n = Named()
    n.ins.update(frames=(frames, IN_SMEM), rows=(rows_table, IN_VMEM), w_one=(w_one, ANY), w_two=(fed.w_two, ANY))
    n.ins.update(partial=(fed.partial, ANY))
    n.late.update(h_two=h_two, grad_ffn=fed.grad_ffn, hid=fed.hid, dgu=fed.dgu_last)
    n.late.update(tok=tokens, attn_sum=attn_sum, cot=cotangent)
    whole = shaped((rows, wide), BF16)
    n.outs.update(grad_attn=(whole, IN_VMEM), grad_state=(whole, IN_VMEM), colsums=(shaped((8, wide), F32), IN_VMEM))
    n.outs.update(g_last=(shaped((LINE, 2, depth, 3 * UNITS), BF16), IN_VMEM), p_ffn=(whole, ANY))
    n.scratch.update(
        down=pltpu.VMEM((wide, units), BF16),
        down_s=DMA((units // UNITS,)),
        p_staged=pltpu.VMEM((2, 256, wide), BF16),
        p_s=DMA((2,)),
        tp_set=TpSum.scratch(rows, wide) + [DMA((TP_PARTS,))],
    )
    if grid:
        n.ins.update(grads=(fed.grads, ANY))
        n.outs.update(out=(shaped((depth, scattered - 3 * UNITS), F32), IN_VMEM))
        n.scratch.update(scatter_set=Scatter.scratch(cut))
    return n.call(functools.partial(state_kernel, n, cut), params(2))


def attn_back_kernel(named, blocks, blocks_t, *refs):
    r = named.take(refs)
    out_cols = r.full.shape[1] * 3 // 4
    out_fetch = pltpu.make_async_copy(r.full.at[:, out_cols:], r.weights, r.weights_s)
    out_fetch.start()
    frames, grad_attn, weights, heads_ref, seg_ref = r.frames, r.grad_attn, r.weights, r.heads, r.seg
    cos_ref, sa_ref, sb_ref = r.cos, r.sa, r.sb
    q_pre, k_pre, q_rot, k_rot, q_text, v_ref, self_o, inv_l = (
        r.q_pre, r.k_pre, r.q_rot, r.k_rot, r.q_text, r.values, r.self_o, r.inv_l
    )
    ky_pre, kyr, vy, text_o, inv_lt, h_one, mixed = r.ky_pre, r.kyr, r.vy, r.text_o, r.inv_lt, r.h_one, r.mixed
    grad_qkv, grad_text, gains, g_attn = r.grad_qkv, r.grad_text, r.gains, r.g_attn
    do_self, do_text, d_self, d_text, dqn, dk, dv, dky, dvy, klive, staged, stage_s = r.work_set
    sums = TpSum(r.partial, r.ffn_sum, r.tp_set[:2], r.tp_set[2:8], r.tp_set[8])
    for fetch in r.fetches:
        fetch.start()
    qgain, kgain, kygain, gate = (heads_ref.at[i : i + 1] for i in range(4))
    engine, text_engine = Idle(), Idle()
    if blocks is not None:
        engine = Scatter(blocks, r.grad, r.out, r.scatter_set, ahead=A_S1)
        text_engine = GatherChain(blocks_t, grad_text, r.all_text, r.gather_set, A_T)
        greet(dp_peers(), tp_peers())
        engine.start()
    else:
        greet([], tp_peers())
    loop(TP_PARTS, sums.stage_one)
    rows, cols = q_rot.shape
    wide = grad_attn.shape[1]
    step_rows = 256
    blocks_here = rows // step_rows
    pairs = cols // PAIR
    gains[...] = jnp.zeros_like(gains)
    dk[...] = jnp.zeros_like(dk)
    dv[...] = jnp.zeros_like(dv)
    dky[...] = jnp.zeros_like(dky)
    dvy[...] = jnp.zeros_like(dvy)

    def halves(value, first_head):
        lane = lax.broadcasted_iota(jnp.int32, (step_rows, PAIR), 1)
        out = jnp.zeros((step_rows, PAIR), F32)
        for head in range(2):
            total = jnp.sum(value * half_mask(step_rows, head, F32), axis=-1, keepdims=True)
            high = total.astype(BF16).astype(F32)
            spot = 2 * (first_head + head)
            out = out + jnp.where(lane == spot, high, jnp.where(lane == spot + 1, total - high, 0.0))
        return out

    def start_rows(i):
        here = block_rows(i, step_rows)
        g = dot_nn(grad_attn[here, :], weights[...])
        other = text_o[here, :].astype(F32)
        gains[3:4, :] += jnp.sum(g * other, axis=0, keepdims=True)
        first = (g * inv_l[here, :]).astype(BF16)
        do_self[here, :] = first
        second = (g * gate[...] * inv_lt[here, :]).astype(BF16)
        do_text[here, :] = second
        dot_self = first.astype(F32) * self_o[here, :].astype(F32)
        dot_text = second.astype(F32) * other
        each = [slice(pair * PAIR, (pair + 1) * PAIR) for pair in range(pairs)]
        d_self[here, :] = sum(halves(dot_self[:, lanes], 2 * pair) for pair, lanes in enumerate(each)).astype(BF16)
        d_text[here, :] = sum(halves(dot_text[:, lanes], 2 * pair) for pair, lanes in enumerate(each)).astype(BF16)
        klive[here, :] = k_rot[here, :] * live_rows(frames, i * step_rows, step_rows, cols).astype(BF16)

    def back(q_ref, k_ref, k_live, v_in, do_ref, d_ref, dk_ref, dv_ref, turned):
        def step(i):
            pair, block = lax.div(i, blocks_here), lax.rem(i, blocks_here)
            here, lanes = block_rows(block, step_rows), pair_lanes(pair)
            keys = k_ref[:, lanes]
            values = v_in[:, lanes]
            lane = lax.broadcasted_iota(jnp.int32, values.shape, 1)
            dq = jnp.zeros((step_rows, PAIR), F32)
            for head in range(2):
                mask = half_mask(step_rows, head, BF16)
                q = q_ref[here, lanes] * mask
                do = do_ref[here, lanes] * mask
                scores = dot_nt(keys, q)
                p = jnp.exp(scores)
                dv_ref[:, lanes] += dot_nn(p.astype(BF16), do)
                spot = 2 * (2 * pair + head)
                minus = jnp.where((lane == spot) | (lane == spot + 1), -1.0, 0.0).astype(BF16)
                left = jnp.concatenate([values, minus], axis=1)
                right = jnp.concatenate([do, d_ref[here, :]], axis=1)
                ds = (p * dot_nt(left, right)).astype(BF16)
                dk_ref[:, lanes] += dot_nn(ds, q)
                key_mask = half_mask(keys.shape[0], head, BF16)
                dq = dq + dot_tn(ds, k_live[:, lanes] * key_mask)
            dq = dq * SCALE
            if turned:
                dqn[here, lanes] += rope_back(dq, cos_ref[here, :], sa_ref[here, :], sb_ref[here, :])
            else:
                dqn[here, lanes] = dq

        return step

    out_fetch.wait()
    paced(blocks_here, start_rows, (engine, 2))
    def norm_back(grad_normed, pre, gain, row):
        inverse = head_inverse(pre, seg_ref[...])
        hat = pre * inverse
        gains[row : row + 1, :] += jnp.sum(grad_normed * hat, axis=0, keepdims=True)
        scaled = grad_normed * gain
        average = segment_sum(scaled * hat, seg_ref[...]) * (1.0 / HEAD)
        return (inverse * (scaled - hat * average)).astype(BF16)

    def end_rows(i):
        here = block_rows(i, step_rows)
        cosines, sine_a, sine_b = thrice(cos_ref[here, :]), thrice(sa_ref[here, :]), thrice(sb_ref[here, :])
        live = live_rows(frames, i * step_rows, step_rows, cols)
        grad_qkv[here, :cols] = norm_back(dqn[here, :], q_pre[here, :], qgain[...], 0)
        dkn = rope_back(dk[here, :] * live, cosines, sine_a, sine_b)
        grad_qkv[here, cols : 2 * cols] = norm_back(dkn, k_pre[here, :], kgain[...], 1)
        grad_qkv[here, 2 * cols : 3 * cols] = (dv[here, :] * live).astype(BF16)
        for k in range(TP_PARTS // blocks_here):
            sums.stage_three(i * (TP_PARTS // blocks_here) + k)

    for fetch in (r.fetch.q_text, r.fetch.kyr, r.fetch.vy):
        fetch.wait()
    text_back = back(q_text, kyr, kyr, vy, do_text, d_text, dky, dvy, False)

    def text_step(i):
        text_back(i)
        pl.when(i < TP_PARTS)(lambda: sums.stage_two(i))

    paced(pairs * blocks_here, text_step, (engine, 3))
    for fetch in (r.fetch.seg, r.fetch.ky_pre, r.fetch.q_rot, r.fetch.values, r.fetch.cos, r.fetch.sa, r.fetch.sb):
        fetch.wait()
    grad_text[:, :cols] = norm_back(dky[...], ky_pre[...], kygain[...], 2)
    grad_text[:, cols:] = dvy[...].astype(BF16)
    text_engine.start()
    self_back = back(q_rot, k_rot, klive, v_ref, do_self, d_self, dk, dv, True)

    half = pairs * blocks_here // 2
    paced(half, self_back, (engine, 6), (text_engine, 2))
    paced(half, lambda i: self_back(i + half), (text_engine, 3))
    for fetch in (r.fetch.q_pre, r.fetch.k_pre, r.fetch.h_one, r.fetch.mixed):
        fetch.wait()
    paced(blocks_here, end_rows, (text_engine, 2))
    tall = wide // LINE

    def copy(m):
        return pltpu.make_async_copy(staged.at[lax.rem(m, 2)], g_attn.at[m], stage_s.at[lax.rem(m, 2)])

    def products(m):
        lanes = pl.ds(pl.multiple_of(m * tall, 128), tall)
        pl.when(m >= 2)(lambda: copy(m - 2).wait())
        first = dot_tn(h_one[:, lanes], grad_qkv[...]).astype(BF16)
        second = dot_tn(grad_attn[:, lanes], mixed[...]).astype(BF16)
        for y in range(2):
            part = slice(y * tall // 2, (y + 1) * tall // 2)
            staged[lax.rem(m, 2), y, :, : 3 * cols] = first[part]
            staged[lax.rem(m, 2), y, :, 3 * cols :] = second[part]
        copy(m).start()

    paced(LINE, products, (text_engine, 4))
    finish_pumps(engine)
    finish_pumps(text_engine)
    text_engine.arrive()
    loop(TP_PARTS, sums.stage_four)
    copy(LINE - 2).wait()
    copy(LINE - 1).wait()
    sums.drain()
    engine.drain()
    text_engine.drain()


def attn_backward(clips, frames, grad_attn, full_attn, heads_table, tables, seg, p, partial, g_last):
    rows, wide = grad_attn.shape
    cols = heads_table.shape[1]
    rows_t = p.kyr.shape[0]
    depth, last_wide = wide // GRID, g_last.shape[-1]
    grid = clips == GRID
    f, b = pltpu.VMEM((rows, cols), F32), pltpu.VMEM((rows, cols), BF16)
    ft = pltpu.VMEM((rows_t, cols), F32)
    slim = pltpu.VMEM((rows, PAIR), BF16)
    n = Named()
    n.ins.update(frames=(frames, IN_SMEM), grad_attn=(grad_attn, IN_VMEM), full=(full_attn, ANY))
    n.ins.update(heads=(heads_table, IN_VMEM), k_rot=(p.k_rot, IN_VMEM), self_o=(p.self_o, IN_VMEM))
    n.ins.update(inv_l=(p.inv_l, IN_VMEM), text_o=(p.text_o, IN_VMEM), inv_lt=(p.inv_lt, IN_VMEM), partial=(partial, ANY))
    n.late.update(q_text=p.q_text, kyr=p.kyr, vy=p.vy, seg=seg, ky_pre=p.ky_pre, q_rot=p.q_rot, values=p.values)
    n.late.update(cos=tables[0], sa=tables[1], sb=tables[2], q_pre=p.q_pre, k_pre=p.k_pre, h_one=p.h_one, mixed=p.mixed)
    n.outs.update(
        grad_qkv=(shaped((rows, 3 * cols), BF16), IN_VMEM),
        grad_text=(shaped((rows_t, 2 * cols), BF16), IN_VMEM),
        gains=(shaped((8, cols), F32), IN_VMEM),
        ffn_sum=(shaped((rows, wide), BF16), IN_VMEM),
        g_attn=(shaped((LINE, 2, depth, 4 * cols), BF16), ANY),
    )
    n.scratch.update(
        work_set=[b, b, slim, slim, f, f, f, ft, ft, b, pltpu.VMEM((2, 2, depth, 4 * cols), BF16), DMA((2,))],
        tp_set=TpSum.scratch(rows, wide) + [DMA((TP_PARTS,))],
        weights=pltpu.VMEM((wide, cols), BF16),
        weights_s=DMA,
    )
    parts = blocks_t = None
    if grid:
        parts = Blocks(depth, last_wide, 96, 256)
        blocks_t = Blocks(rows_t, 2 * cols, 32, 2 * cols)
        n.ins.update(grad=(g_last, ANY))
        n.outs.update(
            out=(shaped((depth, last_wide), F32), IN_VMEM), all_text=(shaped((GRID * rows_t, 2 * cols), BF16), ANY)
        )
        n.scratch.update(scatter_set=Scatter.scratch(parts), gather_set=GatherChain.scratch(blocks_t.count))
    return n.call(functools.partial(attn_back_kernel, n, parts, blocks_t), params(3))


def last_kernel(named, parts, *refs):
    r = named.take(refs)
    frames, grad_qkv, weights, tok, grad_state = r.frames, r.grad_qkv, r.weights, r.tok, r.grad_state
    rows_ref, sums_two, gains, ffn_sum, attn_sum, cot = r.rows, r.sums_two, r.gains, r.ffn_sum, r.attn_sum, r.cot
    result, grad_tokens, vecs = r.result, r.grad_tokens, r.vecs
    partial, grad_n, colsum, outsum, vec = r.work_set
    sums = TpSum(partial, grad_n, r.tp_set[:2], r.tp_set[2:8])
    me = lax.axis_index("dp")
    engine = Idle()
    peers = []
    for fetch in r.fetches:
        fetch.start()
    if parts is not None:
        v_s, v_r = r.sems_set
        text_all, all_text, g_tk, g_tv = r.text_all, r.all_text, r.g_tk, r.g_tv
        peers = dp_peers()
        engine = Scatter(parts, r.grad_a, r.out_a, r.scatter_set, ahead=A_S2)
        greet(peers, tp_peers())
        engine.start()
    else:
        greet([], tp_peers())
    mult_one, tanh_one, _, tanh_two, gain_one, lift_one, gain_two, lift_two = (rows_ref[i : i + 1, :] for i in range(8))
    colsum[...] = jnp.zeros_like(colsum)
    outsum[...] = jnp.zeros_like(outsum)
    wide = tok.shape[1]
    cols = grad_qkv.shape[1] // 3
    step_rows = 256

    def project(which):
        def step(i):
            here = pl.ds(pl.multiple_of(which * sums.half + i * step_rows, 16), step_rows)
            partial[here, :] = dot_nt(grad_qkv[here, :], weights[:, : 3 * cols]).astype(BF16)

        return step

    parts_each = TP_PARTS // (sums.half // step_rows)

    def project_send(i):
        project(1 - sums.core)(i)
        loop(parts_each, lambda k: sums.stage_one(i * parts_each + k))

    paced(sums.half // step_rows, project_send)
    paced(sums.half // step_rows, project(sums.core), (engine, P_1))
    paced(TP_PARTS, sums.stage_two, (engine, P_2))

    def output(i):
        here = block_rows(i, 64)
        live = live_rows(frames, i * 64, 64, wide)
        added = live * ffn_sum[here, :].astype(F32)
        state = tok[here, :].astype(F32) + live * tanh_one * attn_sum[here, :].astype(F32)
        result[here, :] = (state + tanh_two * added).astype(BF16)
        outsum[...] += jnp.sum(added * cot[here, :].astype(F32), axis=0, keepdims=True)

    for fetch in (r.fetch.tok, r.fetch.ffn_sum, r.fetch.attn_sum, r.fetch.cot):
        fetch.wait()
    paced(tok.shape[0] // 64, output, (engine, P_3))
    if parts is not None:
        rows_t = text_all.shape[1]

        def text_products(i):
            here = block_rows(i, rows_t)
            g_tk[...] += dot_tn(text_all[i], all_text[here, :cols])
            g_tv[...] += dot_tn(text_all[i], all_text[here, cols:])

        g_tk[...] = jnp.zeros_like(g_tk)
        g_tv[...] = jnp.zeros_like(g_tv)
        r.fetch.text_all.wait()
        r.fetch.all_text.wait()
        paced(GRID, text_products, (engine, P_4))

    def update(k, which):
        here = sums.spot(k, which)
        x = tok[here, :].astype(F32)
        inverse = lax.rsqrt(jnp.mean(x * x, axis=-1, keepdims=True) + EPS)
        hat = x * inverse
        g = grad_n[here, :].astype(F32)
        scaled = g * mult_one
        back = inverse * (scaled - hat * jnp.mean(scaled * hat, axis=-1, keepdims=True))
        grad_tokens[here, :] = (grad_state[here, :].astype(F32) + back).astype(BF16)
        colsum[...] += jnp.sum(g * hat, axis=0, keepdims=True)

    def three(k):
        sums.stage_three(k)
        update(k, sums.core)

    r.fetch.grad_state.wait()
    paced(TP_PARTS, three, (engine, 4))

    def four(k):
        sums.stage_four(k)
        update(k, 1 - sums.core)

    paced(TP_PARTS, four, (engine, 2))
    pieces = (
        colsum[...] * gain_one,
        sums_two[1:2, :] * (1.0 - tanh_one * tanh_one),
        sums_two[0:1, :] * gain_two,
        outsum[...] * (1.0 - tanh_two * tanh_two),
        colsum[...] * lift_one,
        sums_two[0:1, :] * lift_two,
    )
    for i, piece in enumerate(pieces):
        vec[:, i * wide : (i + 1) * wide] = piece
    for i in range(4):
        vec[:, 6 * wide + i * cols : 6 * wide + (i + 1) * cols] = gains[i : i + 1, :]
    for i, there in enumerate(peers):
        remote(vec, vecs.at[me], v_s.at[i], v_r.at[i], dp=there).start()
    finish_pumps(engine)
    vecs[pl.ds(me if peers else 0, 1)] = vec[...][None]
    for i, there in enumerate(peers):
        here = lax.rem(me + GRID - 1 - i, GRID)
        remote(vec, vecs.at[here], v_s.at[i], v_r.at[i], dp=me).wait_recv()
        remote(vec, vecs.at[me], v_s.at[i], v_r.at[i], dp=there).wait_send()
    sums.drain()
    engine.drain()


def last_backward(clips, frames, tokens, cotangent, p, state, back, qkv_weights):
    rows, wide = tokens.shape
    grid = clips == GRID
    cols = back.gains.shape[1]
    depth, wide_a = back.g_attn.shape[-2:]
    whole = (shaped((rows, wide), BF16), IN_VMEM)
    vec = (1, 6 * wide + 4 * cols)
    n = Named()
    n.ins.update(frames=(frames, IN_SMEM), grad_qkv=(back.grad_qkv, IN_VMEM), weights=(qkv_weights, IN_VMEM))
    n.ins.update(rows=(p.rows, IN_VMEM), sums_two=(state.colsums, IN_VMEM), gains=(back.gains, IN_VMEM))
    n.late.update(tok=tokens, ffn_sum=back.ffn_sum, attn_sum=p.attn_sum, cot=cotangent)
    n.outs.update(result=whole, grad_tokens=whole, vecs=(shaped(((GRID if grid else 1),) + vec, F32), IN_VMEM))
    n.scratch.update(
        work_set=[
            pltpu.VMEM((rows, wide), BF16),
            pltpu.VMEM((rows, wide), BF16),
            pltpu.VMEM((1, wide), F32),
            pltpu.VMEM((1, wide), F32),
            pltpu.VMEM(vec, F32),
        ],
        tp_set=TpSum.scratch(rows, wide),
    )
    parts = None
    if grid:
        parts = Blocks(depth, wide_a, 96, 256)
        g_text = (shaped((p.text_all.shape[-1], cols), F32), IN_VMEM)
        n.ins.update(grad_a=(back.g_attn, ANY))
        n.late.update(text_all=p.text_all, all_text=back.all_text)
        n.outs.update(g_tk=g_text, g_tv=g_text, out_a=(shaped((depth, wide_a), F32), IN_VMEM))
        n.scratch.update(sems_set=[DMA((GRID - 1,))] * 2, scatter_set=Scatter.scratch(parts))
    n.late.update(grad_state=state.grad_state)
    return n.call(functools.partial(last_kernel, n, parts), params(4))


def gather_plain(shard):
    return lax.all_gather(shard, "dp", axis=0, tiled=True)


def scatter_plain(grad):
    return lax.psum_scatter(grad, "dp", scatter_dimension=0, tiled=True).astype(F32)


def first_plain(shard, cond, small, w_ada, text, w_tk, w_tv):
    act = jax.nn.silu(lax.all_to_all(cond[:, 0], "dp", 0, 0, tiled=True)).astype(BF16)
    parts = dot_nn(act, w_ada)
    mods = lax.psum_scatter(parts, "dp", scatter_dimension=0, tiled=True)[0]
    full_text = gather_plain(jnp.concatenate([w_tk, w_tv], axis=1))
    smalls = lax.all_gather(small, "dp", axis=0)[:, 0, :]
    wide = w_ada.shape[1] // 4
    bias, gain = 4 * wide // smalls.shape[0], wide // smalls.shape[0]
    scale_one, gate_one, scale_two, gate_two = jnp.split(mods + smalls[:, :bias].reshape(-1), 4)
    gain_one, gain_two = smalls[:, bias : bias + gain].reshape(-1), smalls[:, bias + gain :].reshape(-1)
    lift_one, lift_two = 1.0 + scale_one, 1.0 + scale_two
    values = (
        gain_one * lift_one,
        jnp.tanh(gate_one),
        gain_two * lift_two,
        jnp.tanh(gate_two),
        gain_one,
        lift_one,
        gain_two,
        lift_two,
    )
    return gather_plain(shard), jnp.stack(values), act.astype(F32), dot_nn(text, full_text)


def unpack_kernel(count, *refs):
    blocks, (attn, vecs, act) = refs[:count], refs[count : count + 3]
    q, k, v, out, gate, up, down, g_ada, bias, g_one, g_two, rest = refs[count + 3 :]
    cols = q.shape[1]
    for i, ref in enumerate((q, k, v, out)):
        ref[...] = attn[:, i * cols : (i + 1) * cols]
    b = 0
    for ref in blocks:
        for at in range(0, ref.shape[1], 3 * UNITS):
            for i, place in enumerate((gate, up, down)):
                place[:, b * UNITS : (b + 1) * UNITS] = ref[:, at + i * UNITS : at + (i + 1) * UNITS]
            b += 1
    total = vecs[0]
    for i in range(1, vecs.shape[0]):
        total = total + vecs[i]
    wide = g_ada.shape[1] // 4
    rest[...] = total[:, 6 * wide :]
    me = lax.axis_index("dp")
    for i in range(vecs.shape[0]):

        @pl.when(me == i)
        def _():
            bias[...] = total[:, i * bias.shape[1] : (i + 1) * bias.shape[1]]
            gain = g_one.shape[1]
            g_one[...] = total[:, 4 * wide + i * gain : 4 * wide + (i + 1) * gain]
            g_two[...] = total[:, 5 * wide + i * gain : 5 * wide + (i + 1) * gain]

    clips = jnp.concatenate([vecs[i][:, : 4 * wide] for i in range(vecs.shape[0])], axis=0)
    turned = act[...].T
    for at in range(0, 4 * wide, 512):
        part = turned[:, 0:1] * clips[0:1, at : at + 512]
        for i in range(1, clips.shape[0]):
            part = part + turned[:, i : i + 1] * clips[i : i + 1, at : at + 512]
        g_ada[:, at : at + 512] = part


def unpack(blocks, attn, vecs, act, units, bias_rows, gain_rows):
    depth, cols = attn.shape[0], attn.shape[1] // 4
    wide = (vecs.shape[2] - 4 * cols) // 6
    shapes = [(depth, cols)] * 4 + [(depth, units)] * 3
    shapes += [(act.shape[1], 4 * wide), (1, bias_rows), (1, gain_rows), (1, gain_rows), (1, 4 * cols)]
    return pl.pallas_call(
        functools.partial(unpack_kernel, len(blocks)),
        out_shape=[shaped(shape, F32) for shape in shapes],
        in_specs=[IN_VMEM] * (len(blocks) + 3),
        out_specs=[IN_VMEM] * len(shapes),
        compiler_params=plain_params(),
    )(*blocks, attn, vecs, act)


def on_device(
    tokens,
    text,
    cond,
    frames,
    w_query,
    w_key,
    w_value,
    w_out,
    w_text_key,
    w_text_value,
    w_gate,
    w_up,
    w_down,
    w_ada,
    ada_bias,
    norm_one,
    norm_two,
    query_gain,
    key_gain,
    text_key_gain,
    cross_gate,
    cotangent,
):
    rows, wide = tokens.shape
    clips = lax.axis_size("dp")
    grid = clips == GRID
    cols, units = w_query.shape[1], w_gate.shape[1]
    heads_here = cols // HEAD
    bias_rows, gain_rows = ada_bias.shape[0], norm_one.shape[0]
    small = jnp.concatenate([ada_bias, norm_one, norm_two]).astype(F32)[None, :]
    cond_rows = cond.astype(F32).reshape(clips, 1, -1)
    attn_shard, *pieces = pack(w_query, w_key, w_value, w_out.T, w_gate, w_up, w_down.T)
    opening = (attn_shard, cond_rows, small, w_ada, text, w_text_key, w_text_value)
    if not grid:
        full_attn, rows_table, act_rows, ty = first_plain(*opening)
        opening = (full_attn, rows_table, ty)
    gate_tanh = jnp.tanh(cross_gate.astype(F32))
    blank = jnp.zeros((cols,), F32)
    heads_table = jnp.stack(
        [query_gain.astype(F32), key_gain.astype(F32), text_key_gain.astype(F32), jnp.repeat(gate_tanh, HEAD)]
        + [blank] * 4
    )
    tables, seg = rope_tables(rows), segment_ones(cols)
    passed = forward(clips, frames, tokens, heads_table, tables, seg, pieces[0], opening)
    full_attn, rows_table = passed.weights, passed.rows
    if grid:
        act_rows, half_one, second = passed.act, passed.full_ffn, pieces[1]
    else:
        half_one, second = gather_plain(pieces[0]), gather_plain(pieces[1])
    p = passed
    fed = ffn(clips, frames, p.h_two, cotangent, p.rows, half_one, second)
    state = state_backward(clips, frames, tokens, p.attn_sum, cotangent, p.rows, p.h_two, half_one, fed)
    back = attn_backward(
        clips, frames, state.grad_attn, full_attn, heads_table, tables, seg, p, state.p_ffn, state.g_last
    )
    last = last_backward(clips, frames, tokens, cotangent, p, state, back, full_attn)
    vecs = last.vecs
    s_blocks = [fed.out, state.out] if grid else [scatter_plain(fed.grads.reshape(wide, -1))]
    if grid:
        s_last, s_attn, s_text_key, s_text_value = back.out, last.out_a, last.g_tk, last.g_tv
    if not grid:
        s_last, s_attn = (scatter_plain(g.reshape(wide, -1)) for g in (state.g_last, back.g_attn))
        s_text = scatter_plain(dot_tn(text, back.grad_text).astype(BF16))
        s_text_key, s_text_value = s_text[:, :cols], s_text[:, cols:]
        vecs = lax.all_gather(vecs[0], "dp", axis=0)
    g_query, g_key, g_value, g_out, g_gate, g_up, g_down, g_ada, g_bias, g_one, g_two, rest = unpack(
        (*s_blocks, s_last), s_attn, vecs, act_rows, units, bias_rows, gain_rows
    )
    rest = rest[0]
    g_cross_gate = jnp.sum(rest[3 * cols :].reshape(heads_here, HEAD), axis=1) * (1.0 - gate_tanh * gate_tanh)
    return (
        last.result,
        last.grad_tokens,
        g_query,
        g_key,
        g_value,
        g_out.T,
        s_text_key,
        s_text_value,
        g_gate,
        g_up,
        g_down.T,
        g_ada,
        g_bias[0],
        g_one[0],
        g_two[0],
        rest[:cols],
        rest[cols : 2 * cols],
        rest[2 * cols : 3 * cols],
        g_cross_gate,
    )


def solution(mesh):
    placed = (
        P("dp", None),
        P("dp", None),
        P("dp", None),
        P("dp"),
        P("dp", "tp"),
        P("dp", "tp"),
        P("dp", "tp"),
        P("tp", "dp"),
        P("dp", "tp"),
        P("dp", "tp"),
        P("dp", "tp"),
        P("dp", "tp"),
        P("tp", "dp"),
        P("dp", None),
        P("dp"),
        P("dp"),
        P("dp"),
        P("tp"),
        P("tp"),
        P("tp"),
        P("tp"),
        P("dp", None),
    )
    return jax.shard_map(
        on_device,
        mesh=mesh,
        in_specs=placed,
        out_specs=(
            P("dp", None),
            P("dp", None),
            P("dp", "tp"),
            P("dp", "tp"),
            P("dp", "tp"),
            P("tp", "dp"),
            P("dp", "tp"),
            P("dp", "tp"),
            P("dp", "tp"),
            P("dp", "tp"),
            P("tp", "dp"),
            P("dp", None),
            P("dp"),
            P("dp"),
            P("dp"),
            P("tp"),
            P("tp"),
            P("tp"),
            P("tp"),
        ),
        check_vma=False,
    )
```

```python
import functools
import types

import jax
import jax.numpy as jnp
import numpy as np
from jax import lax
from jax.experimental import pallas as pl
from jax.experimental.pallas import tpu as pltpu
from jax.sharding import PartitionSpec as P

HEAD = 64
FRAME_TOK = 64
EPS = 1e-06
ROPE_BASE = 10000.0
SCALE = HEAD**-0.5
MESH = pl.DeviceIdType.MESH
VMEM_LIMIT = 60 * 2**20
GRID = 8
LINE = 4
PAIR = 2 * HEAD
TP_PARTS = 8
AHEAD = 2
LAG = 3
P_1 = 1
P_2 = 0
P_3 = 4
P_4 = 4
O_1 = 2
O_2 = 2
O_3 = 1
O_4 = 1
A_A = 3
A_T = 2
A_S1 = 2
A_S0 = 2
A_S2 = 3
A_P = 2
DMA = pltpu.SemaphoreType.DMA
F32 = jnp.float32
BF16 = jnp.bfloat16


def dot_nn(left, right):
    return jnp.dot(left, right, preferred_element_type=F32)


def dot_nt(left, right):
    return lax.dot_general(left, right, (((1,), (1,)), ((), ())), preferred_element_type=F32)


def dot_tn(left, right):
    return lax.dot_general(left, right, (((0,), (0,)), ((), ())), preferred_element_type=F32)


def remote(src, dst, send, recv, **where):
    return pltpu.make_async_remote_copy(
        src_ref=src, dst_ref=dst, send_sem=send, recv_sem=recv, device_id=where, device_id_type=MESH
    )


def greet(dp_peers, tp_peers):
    barrier = pltpu.get_barrier_semaphore()
    for peer in dp_peers:
        pl.semaphore_signal(barrier, inc=1, device_id={"dp": peer}, device_id_type=MESH)
    for peer in tp_peers:
        pl.semaphore_signal(barrier, inc=1, device_id={"tp": peer}, device_id_type=MESH)
    pl.semaphore_wait(barrier, len(dp_peers) + len(tp_peers))


def dp_peers():
    me = lax.axis_index("dp")
    return [lax.rem(me + step, GRID) for step in range(1, GRID)]


def tp_peers():
    me = lax.axis_index("tp")
    return [me + 1 - 2 * lax.rem(me, 2), lax.rem(me + 2, 4)]


def aligned(value, by):
    return value if isinstance(value, int) else pl.multiple_of(value, by)


def loop(count, step):
    def body(i, carry):
        step(i)
        return carry

    lax.fori_loop(0, count, body, 0)


def add_rows(out_ref, first, *others):
    rows, wide = out_ref.shape
    tall = min(rows, 96 if wide <= 384 else 32)
    plain = len(others) == 1 and out_ref.dtype == BF16

    def step(i):
        here = pl.ds(aligned(i * tall, 16), tall)
        total = first[here, :] if plain else first[here, :].astype(F32)
        for other in others:
            total = total + (other[here, :] if plain else other[here, :].astype(F32))
        out_ref[here, :] = total.astype(out_ref.dtype)

    if rows == tall:
        step(0)
    else:
        loop(rows // tall, step)


class Blocks:
    def __init__(self, depth, wide, rows, cols, first=0):
        self.depth, self.wide, self.rows, self.cols, self.first = depth, wide, rows, cols, first
        self.down = depth // rows
        self.count = self.down * (wide // cols)

    def at(self, c):
        if isinstance(c, int):
            return c % self.down * self.rows, self.first + c // self.down * self.cols
        row = aligned(lax.rem(c, self.down) * self.rows, 16)
        col = aligned(self.first + lax.div(c, self.down) * self.cols, 128)
        return row, col

class Gather:
    def __init__(self, blocks, shard, full, sems, ahead=AHEAD):
        self.b, self.shard, self.full, self.ahead = blocks, shard, full, min(ahead, blocks.count)
        self.z_s, self.z_r, self.y_s, self.y_r, self.own_s = sems
        self.me = lax.axis_index("dp")
        self.z, self.y = self.me // 2, lax.rem(self.me, 2)
        self.lines = [lax.rem(self.z + step, LINE) for step in range(1, LINE)]
        self.ticks, self.done = blocks.count, 0

    @staticmethod
    def scratch(count):
        return [DMA((count, 3))] * 2 + [DMA((count, 4))] * 2 + [DMA((count,))]

    def own(self, c):
        row, col = self.b.at(c)
        return self.shard.at[pl.ds(row, self.b.rows), pl.ds(col, self.b.cols)]

    def place(self, c, origin):
        row, col = self.b.at(c)
        start = pl.multiple_of(origin * self.b.depth + row, 16)
        return self.full.at[pl.ds(start, self.b.rows), pl.ds(col, self.b.cols)]

    def along(self, c, i):
        there = 2 * self.lines[i] + self.y
        return remote(self.own(c), self.place(c, self.me), self.z_s.at[c, i], self.z_r.at[c, i], dp=there)

    def came_along(self, c, i):
        line = lax.rem(self.z + LINE - 1 - i, LINE)
        place = self.place(c, 2 * line + self.y)
        return line, remote(place, place, self.z_s.at[c, i], self.z_r.at[c, i], dp=self.me)

    def across(self, c, line, mine=False):
        origin = 2 * line + self.y
        src = self.own(c) if mine else self.place(c, origin)
        other = self.me + 1 - 2 * self.y
        return remote(src, self.place(c, origin), self.y_s.at[c, line], self.y_r.at[c, line], dp=other)

    def came_across(self, c, line):
        place = self.place(c, 2 * line + 1 - self.y)
        return remote(place, place, self.y_s.at[c, line], self.y_r.at[c, line], dp=self.me)

    def local(self, c):
        return pltpu.make_async_copy(self.own(c), self.place(c, self.me), self.own_s.at[c])

    def begin(self, c):
        for i in range(LINE - 1):
            self.along(c, i).start()
        self.across(c, self.z, True).start()
        self.local(c).start()

    def start(self):
        for c in range(self.ahead):
            self.begin(c)

    def pump(self, t):
        pl.when(t + self.ahead < self.b.count)(lambda: self.begin(t + self.ahead))
        for i in range(LINE - 1):
            line, came = self.came_along(t, i)
            came.wait_recv()
            self.across(t, line).start()

    def arrive(self, first=0, count=None):
        def step(i):
            c = first + i
            for line in range(LINE):
                self.came_across(c, line).wait_recv()
            self.local(c).wait()

        loop(self.b.count if count is None else count, step)

    def drain(self):
        def step(c):
            for line in range(LINE):
                self.across(c, line).wait_send()
            for i in range(LINE - 1):
                self.along(c, i).wait_send()

        loop(self.b.count, step)


class GatherChain:
    def __init__(self, blocks, shard, full, sems, ahead=AHEAD):
        self.b, self.shard, self.full, self.ahead = blocks, shard, full, min(ahead, blocks.count)
        self.up_s, self.up_r, self.dn_s, self.dn_r, self.y_s, self.y_r, self.own_s = sems
        self.me = lax.axis_index("dp")
        self.z, self.y = self.me // 2, lax.rem(self.me, 2)
        self.ticks, self.done = blocks.count + LINE - 2, 0

    @staticmethod
    def scratch(count):
        return [DMA((count, 3))] * 4 + [DMA((count, 4))] * 2 + [DMA((count,))]

    def own(self, c):
        row, col = self.b.at(c)
        return self.shard.at[pl.ds(row, self.b.rows), pl.ds(col, self.b.cols)]

    def place(self, c, origin):
        row, col = self.b.at(c)
        start = pl.multiple_of(origin * self.b.depth + row, 16)
        return self.full.at[pl.ds(start, self.b.rows), pl.ds(col, self.b.cols)]

    def up(self, c, hop):
        origin = self.me - 2 * hop
        src = self.own(c) if hop == 0 else self.place(c, origin)
        return remote(src, self.place(c, origin), self.up_s.at[c, hop], self.up_r.at[c, hop], dp=self.me + 2)

    def down(self, c, hop):
        origin = self.me + 2 * hop
        src = self.own(c) if hop == 0 else self.place(c, origin)
        return remote(src, self.place(c, origin), self.dn_s.at[c, hop], self.dn_r.at[c, hop], dp=self.me - 2)

    def across(self, c, line, mine=False):
        origin = 2 * line + self.y
        src = self.own(c) if mine else self.place(c, origin)
        other = self.me + 1 - 2 * self.y
        return remote(src, self.place(c, origin), self.y_s.at[c, line], self.y_r.at[c, line], dp=other)

    def came(self, c, origin, sems):
        return remote(self.place(c, origin), self.place(c, origin), sems, sems, dp=self.me)

    def local(self, c):
        return pltpu.make_async_copy(self.own(c), self.place(c, self.me), self.own_s.at[c])

    def begin(self, c):
        pl.when(self.z < LINE - 1)(lambda: self.up(c, 0).start())
        pl.when(self.z > 0)(lambda: self.down(c, 0).start())
        self.across(c, self.z, True).start()
        self.local(c).start()

    def start(self):
        for c in range(self.ahead):
            self.begin(c)

    def pump(self, t):
        me, z, count = self.me, self.z, self.b.count
        pl.when(t + self.ahead < count)(lambda: self.begin(t + self.ahead))
        for hop in range(LINE - 1):
            c = t - hop
            valid = (c >= 0) & (c < count)

            @pl.when(valid & (z - 1 - hop >= 0))
            def _():
                self.came(c, me - 2 * (hop + 1), self.up_r.at[c, hop]).wait_recv()
                if hop < LINE - 2:
                    pl.when(z < LINE - 1)(lambda: self.up(c, hop + 1).start())
                self.across(c, z - 1 - hop).start()

            @pl.when(valid & (z + 1 + hop <= LINE - 1))
            def _():
                self.came(c, me + 2 * (hop + 1), self.dn_r.at[c, hop]).wait_recv()
                if hop < LINE - 2:
                    pl.when(z > 0)(lambda: self.down(c, hop + 1).start())
                self.across(c, z + 1 + hop).start()

    def arrive(self, first=0, count=None):
        def step(i):
            c = first + i
            for line in range(LINE):
                self.came(c, 2 * line + 1 - self.y, self.y_r.at[c, line]).wait_recv()
            self.local(c).wait()

        loop(self.b.count if count is None else count, step)

    def drain(self):
        z = self.z

        def step(c):
            for line in range(LINE):
                self.across(c, line).wait_send()
            for hop in range(LINE - 1):
                pl.when((z < LINE - 1) & (z - hop >= 0))(lambda: self.up(c, hop).wait_send())
                pl.when((z > 0) & (z + hop <= LINE - 1))(lambda: self.down(c, hop).wait_send())

        loop(self.b.count, step)


class Scatter:
    def __init__(self, blocks, grad, out, refs, inplace=False, ahead=AHEAD):
        self.b, self.grad, self.out, self.inplace = blocks, grad, out, inplace
        self.ahead = min(ahead, blocks.count)
        self.crossed, self.landed = refs[:2]
        self.y_s, self.y_r, self.own_s, self.z_s, self.z_r = refs[2:7]
        self.held = None if inplace else refs[7]
        self.me = lax.axis_index("dp")
        self.z, self.y = self.me // 2, lax.rem(self.me, 2)
        self.lines = [lax.rem(self.z + step, LINE) for step in range(1, LINE)]
        self.ticks, self.done = blocks.count + LAG, 0

    @staticmethod
    def scratch(blocks, inplace=False):
        shape = (blocks.rows, blocks.cols)
        count = blocks.count
        bufs = [pltpu.VMEM((count, lines) + shape, BF16) for lines in (4, 3)]
        held = [] if inplace else [pltpu.VMEM((count, 4) + shape, BF16)]
        return bufs + [DMA((count,))] * 3 + [DMA((count, 3))] * 2 + held

    def part(self, c, row_y):
        row, col = self.b.at(c)
        return self.grad.at[:, row_y, pl.ds(row, self.b.rows), pl.ds(col, self.b.cols)]

    def hold(self, c, line):
        if not self.inplace:
            return self.held.at[c, line]
        row, col = self.b.at(c)
        return self.grad.at[line, self.y, pl.ds(row, self.b.rows), pl.ds(col, self.b.cols)]

    def across(self, c):
        other = self.me + 1 - 2 * self.y
        return remote(self.part(c, 1 - self.y), self.crossed.at[c], self.y_s.at[c], self.y_r.at[c], dp=other)

    def load(self, c):
        return pltpu.make_async_copy(self.part(c, self.y), self.held.at[c], self.own_s.at[c])

    def along(self, c, i):
        line = self.lines[i]
        return remote(
            self.hold(c, line), self.landed.at[c, i], self.z_s.at[c, i], self.z_r.at[c, i], dp=2 * line + self.y
        )

    def begin(self, c):
        self.across(c).start()
        if not self.inplace:
            self.load(c).start()

    def start(self):
        for c in range(self.ahead):
            self.begin(c)

    def fold(self, c):
        self.across(c).wait_recv()
        if not self.inplace:
            self.load(c).wait()
        for i in (1, 0, 2):
            line = self.lines[i]
            add_rows(self.hold(c, line), self.hold(c, line), self.crossed.at[c, line])
            self.along(c, i).start()

    def finish(self, c):
        row, col = self.b.at(c)
        for i in range(LINE - 1):
            self.along(c, i).wait_recv()
        out_col = aligned(col - self.b.first, 128)
        out = self.out.at[pl.ds(row, self.b.rows), pl.ds(out_col, self.b.cols)]
        landed = [self.landed.at[c, i] for i in range(LINE - 1)]
        add_rows(out, self.hold(c, self.z), self.crossed.at[c, self.z], *landed)

    def pump(self, t):
        pl.when(t + self.ahead < self.b.count)(lambda: self.begin(t + self.ahead))
        pl.when(t < self.b.count)(lambda: self.fold(t))
        pl.when(t >= LAG)(lambda: self.finish(t - LAG))

    def drain(self):
        def step(c):
            self.across(c).wait_send()
            for i in range(LINE - 1):
                self.along(c, i).wait_send()

        loop(self.b.count, step)


class Idle:
    ticks = done = 0

    def start(self):
        pass

    def pump(self, t):
        pass

    def arrive(self):
        pass

    def drain(self):
        pass


class TpSum:
    def __init__(self, partial, out, bufs, sems, own_sems=None):
        self.p, self.out = partial, out
        self.crossed, self.other = bufs
        self.c_s, self.c_r, self.x_s, self.x_r, self.o_s, self.o_r = sems
        self.core = lax.rem(lax.axis_index("tp"), 2)
        self.beside, self.far = tp_peers()
        self.half = partial.shape[0] // 2
        self.rows = self.half // TP_PARTS
        self.own_s = own_sems

    @staticmethod
    def scratch(rows, wide):
        return [pltpu.VMEM((rows // 2, wide), BF16)] * 2 + [DMA((TP_PARTS,))] * 6

    def spot(self, k, which):
        return pl.ds(pl.multiple_of(which * self.half + k * self.rows, 16), self.rows)

    def part(self, k):
        return pl.ds(aligned(k * self.rows, 16), self.rows)

    def first(self, k):
        return remote(
            self.p.at[self.spot(k, 1 - self.core)],
            self.crossed.at[self.part(k)],
            self.c_s.at[k],
            self.c_r.at[k],
            tp=self.beside,
        )

    def second(self, k):
        here = self.out.at[self.spot(k, self.core)]
        return remote(here, self.other.at[self.part(k)], self.x_s.at[k], self.x_r.at[k], tp=self.far)

    def third(self, k, which):
        here = self.out.at[self.spot(k, which)]
        return remote(here, here, self.o_s.at[k], self.o_r.at[k], tp=self.beside)

    def load(self, k):
        mine = self.spot(k, self.core)
        return pltpu.make_async_copy(self.p.at[mine], self.out.at[mine], self.own_s.at[k])

    def stage_one(self, k):
        self.first(k).start()
        if self.own_s is not None:
            self.load(k).start()

    def stage_two(self, k):
        self.first(k).wait_recv()
        mine = self.spot(k, self.core)
        held = self.p.at[mine]
        if self.own_s is not None:
            self.load(k).wait()
            held = self.out.at[mine]
        add_rows(self.out.at[mine], held, self.crossed.at[self.part(k)])
        self.second(k).start()

    def stage_three(self, k):
        self.second(k).wait()
        mine = self.out.at[self.spot(k, self.core)]
        add_rows(mine, mine, self.other.at[self.part(k)])
        self.third(k, self.core).start()

    def stage_four(self, k):
        self.third(k, 1 - self.core).wait_recv()

    def sent(self, k):
        self.third(k, self.core).wait_send()

    def drain(self, sent=False):
        def step(k):
            self.first(k).wait_send()
            if not sent:
                self.sent(k)

        loop(TP_PARTS, step)


def params(number):
    return pltpu.CompilerParams(
        collective_id=number, has_side_effects=True, vmem_limit_bytes=VMEM_LIMIT
    )


def plain_params():
    return pltpu.CompilerParams(vmem_limit_bytes=VMEM_LIMIT)


ANY = pl.BlockSpec(memory_space=pl.ANY)
IN_VMEM = pl.BlockSpec(memory_space=pltpu.VMEM)
IN_SMEM = pl.BlockSpec(memory_space=pltpu.SMEM)


def shaped(shape, dtype):
    return jax.ShapeDtypeStruct(shape, dtype)


def segment_sum(value, seg):
    high = value.astype(BF16)
    low = (value - high.astype(F32)).astype(BF16)
    return dot_nn(high, seg) + dot_nn(low, seg)


def head_inverse(value, seg):
    return lax.rsqrt(segment_sum(value * value, seg) * (1.0 / HEAD) + EPS)


def thrice(table):
    return jnp.concatenate([table] * 3, axis=1)


def rope(value, cosines, sine_a, sine_b):
    wide = value.shape[1]
    ahead = pltpu.roll(value, wide - HEAD // 4, 1)
    behind = pltpu.roll(value, HEAD // 4, 1)
    return value * cosines + ahead * sine_a + behind * sine_b


def rope_back(grad, cosines, sine_a, sine_b):
    wide = grad.shape[1]
    ahead = pltpu.roll(grad * sine_b, wide - HEAD // 4, 1)
    behind = pltpu.roll(grad * sine_a, HEAD // 4, 1)
    return grad * cosines + ahead + behind


def rope_tables(row_count):
    lane = np.arange(PAIR)
    within = lane % HEAD
    quarter = HEAD // 4
    which = within // quarter
    freqs = (ROPE_BASE ** (-(within % quarter).astype(np.float32) / np.float32(quarter))).astype(np.float32)
    row = np.arange(row_count)
    frame, place = (row // FRAME_TOK).astype(np.float32), (row % FRAME_TOK).astype(np.float32)
    position = np.where(which[None, :] < 2, frame[:, None], place[:, None])
    angles = (position * freqs[None, :]).astype(np.float32)
    cosines, sines = np.cos(angles), np.sin(angles)
    even = (which % 2 == 0)[None, :]
    return (
        jnp.asarray(cosines.astype(np.float32)),
        jnp.asarray(np.where(even, -sines, 0.0).astype(np.float32)),
        jnp.asarray(np.where(even, 0.0, sines).astype(np.float32)),
    )


def segment_ones(wide):
    head = np.arange(wide) // HEAD
    return jnp.asarray((head[:, None] == head[None, :]).astype(np.float32)).astype(BF16)


def live_rows(frames_ref, start, rows, wide):
    row = start + lax.broadcasted_iota(jnp.int32, (rows, wide), 0)
    return (row < frames_ref[0] * FRAME_TOK).astype(F32)


def half_mask(rows, head, dtype):
    lane = lax.broadcasted_iota(jnp.int32, (rows, PAIR), 1)
    return ((lane < HEAD) if head == 0 else (lane >= HEAD)).astype(dtype)


def pair_lanes(pair, wide=PAIR):
    return pl.ds(pl.multiple_of(pair * wide, PAIR), wide)


def block_rows(block, rows):
    return pl.ds(pl.multiple_of(block * rows, rows), rows)


def paced(count, step, *plans):
    jobs = []
    for engine, pumps in plans:
        pumps = min(pumps, engine.ticks - engine.done)
        if pumps > 0:
            jobs.append((engine, pumps, engine.done))
            engine.done += pumps

    def body(i):
        step(i)
        for engine, pumps, base in jobs:
            if pumps <= count:
                every = count // pumps
                turn = lax.div(i, every)
                now = (lax.rem(i, every) == every - 1) & (turn < pumps)
                pl.when(now)(functools.partial(engine.pump, base + turn))
            else:
                each = -(-pumps // count)
                for j in range(each):
                    pl.when(i * each + j < pumps)(functools.partial(engine.pump, base + i * each + j))

    loop(count, body)


def finish_pumps(engine):
    base = engine.done
    if base < engine.ticks:
        loop(engine.ticks - base, lambda i: engine.pump(base + i))
    engine.done = engine.ticks


class Named:
    def __init__(self):
        self.ins, self.outs, self.scratch, self.late = {}, {}, {}, {}

    def take(self, refs):
        found, at = {}, 0
        for name in (*self.ins, *self.outs):
            found[name] = refs[at]
            at += 1
        for name, item in self.scratch.items():
            many = isinstance(item, list)
            found[name] = refs[at : at + len(item)] if many else refs[at]
            at += len(item) if many else 1
        count = len(self.late)
        copies = []
        for i, name in enumerate(self.late):
            found[name] = refs[at + count + i]
            copies.append(pltpu.make_async_copy(refs[at + i], found[name], refs[at + 2 * count + i]))
        r = types.SimpleNamespace(**found)
        r.fetch = types.SimpleNamespace(**dict(zip(self.late, copies)))
        r.fetches = copies
        return r

    def call(self, kernel, compiler_params):
        flat = []
        for item in self.scratch.values():
            flat += item if isinstance(item, list) else [item]
        late = list(self.late.values())
        flat += [pltpu.VMEM(value.shape, value.dtype) for value in late] + [DMA] * len(late)
        ins, outs = list(self.ins.values()), list(self.outs.values())
        first, many = len(ins) + len(outs), len(late)

        def body(*refs):
            own = refs[: len(ins)] + refs[len(ins) + many : first + many]
            scratch = refs[first + many : len(refs) - 2 * many]
            kernel(*own, *scratch, *refs[len(ins) : len(ins) + many], *refs[len(refs) - 2 * many :])

        results = pl.pallas_call(
            body,
            out_shape=[shape for shape, _ in outs],
            in_specs=[spec for _, spec in ins] + [ANY] * many,
            out_specs=[spec for _, spec in outs],
            scratch_shapes=flat,
            compiler_params=compiler_params,
        )(*[value for value, _ in ins], *late)
        return types.SimpleNamespace(**dict(zip(self.outs, results)))


class Opening:
    def __init__(self, r):
        self.r = r
        self.me, self.tp = lax.axis_index("dp"), lax.axis_index("tp")
        self.peers, (self.beside, self.far) = dp_peers(), tp_peers()
        self.sources = [lax.rem(self.me + GRID - step, GRID) for step in range(1, GRID)]
        self.share = r.text_all.shape[1] // 4
        self.cond, self.small, self.parts, self.slabs, self.quarters = (r.sems_set[2 * i : 2 * i + 2] for i in range(5))
        self.own_s = r.sems_set[10]

    def send(self, sems, i, src, dst, **where):
        return remote(src, dst, sems[0].at[i], sems[1].at[i], **where)

    def quarter(self, which):
        rows = pl.ds(pl.multiple_of(which * self.share, 16), self.share)
        return self.r.text_all.at[:, rows, :]

    def slab(self, there, origin):
        depth = self.r.text_all.shape[2]
        rows = pl.ds(pl.multiple_of(self.tp * self.share, 16), self.share)
        src = self.r.text.at[rows, pl.ds(pl.multiple_of(there * depth, 128), depth)]
        return src, self.r.text_all.at[origin, rows, :]

    def cond_out(self, i):
        there = self.peers[i]
        return self.send(self.cond, i, self.r.cond.at[there], self.r.conds.at[self.me], dp=there)

    def small_out(self, i):
        return self.send(self.small, i, self.r.small, self.r.smalls.at[self.me], dp=self.peers[i])

    def slab_out(self, i):
        return self.send(self.slabs, i, *self.slab(self.peers[i], self.me), dp=self.peers[i])

    def part_out(self, i):
        there = self.peers[i]
        return self.send(self.parts, i, self.r.part.at[there], self.r.parts.at[self.me], dp=there)

    def came(self, sems, i, ref):
        self.send(sems, i, ref, ref, dp=self.me).wait_recv()

    def begin(self):
        r, me = self.r, self.me
        for i in range(GRID - 1):
            self.cond_out(i).start()
            self.small_out(i).start()
        for i in range(GRID - 1):
            self.slab_out(i).start()
        pltpu.make_async_copy(*self.slab(me, me), self.own_s).start()
        r.conds[pl.ds(me, 1)] = r.cond[pl.ds(me, 1)]
        r.smalls[pl.ds(me, 1)] = r.small[...][None]

    def partial_rows(self):
        r, me = self.r, self.me
        for i, here in enumerate(self.sources):
            self.came(self.cond, i, r.conds.at[here])
        cond = jnp.concatenate([r.conds[i] for i in range(GRID)], axis=0)
        act = (cond * (1.0 / (1.0 + jnp.exp(-cond)))).astype(BF16)
        r.act[...] = act.astype(F32)
        width = r.w_ada.shape[1] // 4
        for i in range(4):
            cols = pl.ds(i * width, width)
            product = dot_nn(act, r.w_ada[:, cols])
            for j in range(GRID):
                r.part[j, :, cols] = product[j : j + 1, :]
        for i in range(GRID - 1):
            self.part_out(i).start()
        r.parts[pl.ds(me, 1)] = r.part[pl.ds(me, 1)]

    def spread(self):
        pltpu.make_async_copy(*self.slab(self.me, self.me), self.own_s).wait()
        for i, here in enumerate(self.sources):
            self.came(self.slabs, i, self.slab(here, here)[1])
        mine = self.quarter(self.tp)
        self.send(self.quarters, 0, mine, mine, tp=self.beside).start()
        self.send(self.quarters, 1, mine, mine, tp=self.far).start()

    def modulate(self):
        r = self.r
        for i, here in enumerate(self.sources):
            self.came(self.parts, i, r.parts.at[here])
            self.came(self.small, i, r.smalls.at[here])
        wide = r.rows.shape[1]
        bias = r.small.shape[1] - 2 * (wide // GRID)
        ends = r.small.shape[1]
        smalls = [r.smalls[i] for i in range(GRID)]
        mods = sum(r.parts[i] for i in range(GRID)) + jnp.concatenate([v[:, :bias] for v in smalls], axis=1)
        gain_one = jnp.concatenate([v[:, bias : bias + wide // GRID] for v in smalls], axis=1)
        gain_two = jnp.concatenate([v[:, bias + wide // GRID : ends] for v in smalls], axis=1)
        lift_one, lift_two = 1.0 + mods[:, :wide], 1.0 + mods[:, 2 * wide : 3 * wide]
        tanh_one, tanh_two = jnp.tanh(mods[:, wide : 2 * wide]), jnp.tanh(mods[:, 3 * wide :])
        values = (gain_one * lift_one, tanh_one, gain_two * lift_two, tanh_two, gain_one, lift_one, gain_two, lift_two)
        for i, value in enumerate(values):
            r.rows[i : i + 1, :] = value

    def pass_on(self):
        from_far = self.quarter(lax.rem(self.tp + 2, 4))
        self.send(self.quarters, 1, from_far, from_far, tp=self.far).wait_recv()
        self.send(self.quarters, 2, from_far, from_far, tp=self.beside).start()

    def collect(self):
        near = self.quarter(self.tp + 1 - 2 * lax.rem(self.tp, 2))
        self.send(self.quarters, 0, near, near, tp=self.beside).wait_recv()
        self.send(self.quarters, 2, near, near, tp=self.beside).wait_recv()

    def multiply(self, i):
        r = self.r
        cols = r.w_tk.shape[1]
        rows = r.text_all[i]
        line, y = lax.div(i, 2), lax.rem(i, 2)
        r.products[line, y, :, :cols] = dot_nn(rows, r.w_tk[...]).astype(BF16)
        r.products[line, y, :, cols:] = dot_nn(rows, r.w_tv[...]).astype(BF16)

    def drain(self):
        mine = self.quarter(self.tp)
        self.send(self.quarters, 0, mine, mine, tp=self.beside).wait_send()
        self.send(self.quarters, 1, mine, mine, tp=self.far).wait_send()
        self.send(self.quarters, 2, mine, mine, tp=self.beside).wait_send()
        for i in range(GRID - 1):
            self.cond_out(i).wait_send()
            self.small_out(i).wait_send()
            self.slab_out(i).wait_send()
            self.part_out(i).wait_send()


def pack_kernel(q, k, v, out, gate, up, down, *refs):
    vectors, (attn_ref, one_ref, two_ref, small_ref, heads_ref) = refs[:7], refs[7:]
    cols = q.shape[1]
    at = 0
    for vector in vectors[:3]:
        count = vector.shape[0]
        small_ref[:, at : at + count] = vector[...].astype(F32).reshape(1, count)
        at += count
    heads_ref[...] = jnp.zeros_like(heads_ref)
    for i, vector in enumerate(vectors[3:]):
        heads_ref[i : i + 1, :] = vector[...].astype(F32).reshape(1, cols)
    for i, w in enumerate((q, k, v)):
        attn_ref[:, i * cols : (i + 1) * cols] = w[...]
    attn_ref[:, 3 * cols :] = out[...]
    for b in range(gate.shape[1] // UNITS):
        ref, at = (one_ref, b) if b < ONES else (two_ref, b - ONES)
        here = slice(b * UNITS, (b + 1) * UNITS)
        for i, value in enumerate((gate[:, here], up[:, here], down[:, here])):
            ref[:, (3 * at + i) * UNITS : (3 * at + i + 1) * UNITS] = value


def pack(q, k, v, out, gate, up, down, vectors):
    depth, cols = q.shape
    blocks = gate.shape[1] // UNITS
    widths = (4 * cols, 3 * UNITS * ONES, 3 * UNITS * (blocks - ONES))
    return pl.pallas_call(
        pack_kernel,
        out_shape=[shaped((depth, wide), BF16) for wide in widths]
        + [shaped((1, sum(vector.shape[0] for vector in vectors[:3])), F32), shaped((8, cols), F32)],
        in_specs=[IN_VMEM] * 14,
        out_specs=[IN_VMEM] * 5,
        compiler_params=plain_params(),
    )(q, k, v, out, gate, up, down, *vectors)


def forward_kernel(named, grid, cuts, *refs):
    r = named.take(refs)
    tok, weights, rows_ref, heads_ref = r.tok, r.weights, r.rows, r.heads
    cos_ref, sa_ref, sb_ref, seg_ref = r.cos, r.sa, r.sb, r.seg
    attn_sum, partial, mixed, ty = r.attn_sum, r.partial, r.mixed, r.ty
    sums = TpSum(partial, attn_sum, r.tp_set[:2], r.tp_set[2:8])
    mult, tanh_attn, mult_two = rows_ref.at[0:1], rows_ref.at[1:2], rows_ref.at[2:3]
    qgain, kgain, kygain, gate = (heads_ref.at[i : i + 1] for i in range(4))
    rows, cols = r.q_rot.shape
    step_rows = 256
    blocks_here = rows // step_rows
    pairs = cols // PAIR
    attn_engine = text_engine = engine = Idle()
    for fetch in r.fetches:
        fetch.start()
    if grid:
        opening = Opening(r)
        attn_engine = GatherChain(cuts[0], r.attn_shard, weights, r.attn_set, A_A)
        text_engine = Scatter(cuts[1], r.products, ty, r.text_set, True, ahead=A_P)
        engine = GatherChain(cuts[2], r.ffn_shard, r.full_ffn, r.ffn_set)
        greet(dp_peers(), tp_peers())
        opening.begin()
        attn_engine.start()
        opening.partial_rows()
        paced(1, lambda i: None, (attn_engine, O_1))
        opening.spread()
        paced(1, lambda i: None, (attn_engine, O_2))
        opening.modulate()
        paced(1, lambda i: None, (attn_engine, O_3))
        opening.pass_on()
        paced(1, lambda i: None, (attn_engine, O_4))
        opening.collect()
        r.fetch.w_tk.wait()
        r.fetch.w_tv.wait()
        paced(GRID, opening.multiply, (attn_engine, 2))
        text_engine.start()
        engine.start()
        finish_pumps(attn_engine)
        attn_engine.arrive()
    else:
        greet([], tp_peers())

    def project(i):
        here = block_rows(i, step_rows)
        x = tok[here, :].astype(F32)
        inverse = lax.rsqrt(jnp.mean(x * x, axis=-1, keepdims=True) + EPS)
        h = (x * inverse * mult[...]).astype(BF16)
        r.h_one[here, :] = h
        cosines, sine_a, sine_b = thrice(cos_ref[here, :]), thrice(sa_ref[here, :]), thrice(sb_ref[here, :])
        q = dot_nn(h, weights[:, :cols])
        r.q_pre[here, :] = q
        qn = q * head_inverse(q, seg_ref[...]) * qgain[...]
        r.q_text[here, :] = (qn * SCALE).astype(BF16)
        r.q_rot[here, :] = (rope(qn, cosines, sine_a, sine_b) * SCALE).astype(BF16)
        k = dot_nn(h, weights[:, cols : 2 * cols])
        r.k_pre[here, :] = k
        kn = k * head_inverse(k, seg_ref[...]) * kgain[...]
        r.k_rot[here, :] = rope(kn, cosines, sine_a, sine_b).astype(BF16)
        v = dot_nn(h, weights[:, 2 * cols : 3 * cols]).astype(BF16)
        r.values[here, :] = v
        live = live_rows(r.frames, i * step_rows, step_rows, PAIR).astype(BF16)
        for pair in range(pairs):
            r.vaug[here, 2 * pair * PAIR : (2 * pair + 1) * PAIR] = v[:, pair * PAIR : (pair + 1) * PAIR] * live
            r.vaug[here, (2 * pair + 1) * PAIR : (2 * pair + 2) * PAIR] = live

    def attention(q_ref, k_ref, v_ref, inv_ref):
        def step(i):
            pair, block = lax.div(i, blocks_here), lax.rem(i, blocks_here)
            here, lanes = block_rows(block, step_rows), pair_lanes(pair)
            q = q_ref[here, lanes]
            keys = k_ref[:, lanes]
            values = v_ref[:, pair_lanes(pair, 2 * PAIR)]
            outs = jnp.zeros((step_rows, PAIR), F32)
            total = jnp.zeros((step_rows, PAIR), F32)
            for head in range(2):
                p = jnp.exp(dot_nt(q * half_mask(step_rows, head, BF16), keys)).astype(BF16)
                both = dot_nn(p, values)
                wide_mask = half_mask(step_rows, head, F32)
                outs = outs + both[:, :PAIR] * wide_mask
                total = total + both[:, PAIR:] * wide_mask
            inverse = 1.0 / total
            inv_ref[here, lanes] = inverse
            return here, lanes, outs * inverse

        return step

    self_attention = attention(r.q_rot, r.k_rot, r.vaug, r.inv_l)
    text_attention = attention(r.q_text, r.kyr, r.vyaug, r.inv_lt)

    def attend(i):
        here, lanes, out = self_attention(i)
        r.mixed_self[here, lanes] = out
        r.self_o[here, lanes] = out.astype(BF16)

    def attend_text(i):
        here, lanes, out = text_attention(i)
        r.text_o[here, lanes] = out.astype(BF16)
        mixed[here, lanes] = (r.mixed_self[here, lanes] + gate[:, lanes] * out).astype(BF16)

    half_blocks = blocks_here // 2
    parts_each = TP_PARTS // half_blocks

    def output(which):
        def step(i):
            block = which * half_blocks + i
            for pair in range(pairs):
                attend_text(pair * blocks_here + block)
            here = block_rows(block, step_rows)
            partial[here, :] = dot_nt(mixed[here, :], weights[:, 3 * cols :]).astype(BF16)

        return step

    def output_send(i):
        output(1 - sums.core)(i)
        loop(parts_each, lambda k: sums.stage_one(i * parts_each + k))

    def output_add(i):
        output(sums.core)(i)
        loop(parts_each, lambda k: sums.stage_two(i * parts_each + k))

    for fetch in (r.fetch.tok, r.fetch.cos, r.fetch.sa, r.fetch.sb, r.fetch.seg):
        fetch.wait()
    paced(blocks_here, project, (text_engine, 4), (engine, 2))
    paced(pairs * blocks_here, attend, (text_engine, 4), (engine, 3))
    finish_pumps(text_engine)

    ky = ty[:, :cols]
    r.ky_pre[...] = ky
    r.kyr[...] = (ky * head_inverse(ky, seg_ref[...]) * kygain[...]).astype(BF16)
    vy = ty[:, cols:].astype(BF16)
    r.vy[...] = vy
    for pair in range(pairs):
        r.vyaug[:, 2 * pair * PAIR : (2 * pair + 1) * PAIR] = vy[:, pair * PAIR : (pair + 1) * PAIR]
        r.vyaug[:, (2 * pair + 1) * PAIR : (2 * pair + 2) * PAIR] = jnp.ones((vy.shape[0], PAIR), BF16)
    paced(half_blocks, output_send, (engine, 2))
    paced(half_blocks, output_add, (engine, 2))

    def update(k, which):
        here = sums.spot(k, which)
        live = live_rows(r.frames, which * sums.half + k * sums.rows, sums.rows, tok.shape[1])
        state = tok[here, :].astype(F32) + live * tanh_attn[...] * attn_sum[here, :].astype(F32)
        inverse = lax.rsqrt(jnp.mean(state * state, axis=-1, keepdims=True) + EPS)
        r.h_two[here, :] = (state * inverse * mult_two[...]).astype(BF16)

    def three(k):
        sums.stage_three(k)
        update(k, sums.core)

    paced(TP_PARTS, three, (engine, 4))

    def four(k):
        sums.stage_four(k)
        update(k, 1 - sums.core)

    paced(TP_PARTS, four, (engine, 1))
    finish_pumps(engine)
    engine.arrive()
    sums.drain()
    if grid:
        opening.drain()
    attn_engine.drain()
    text_engine.drain()
    engine.drain()


def forward(clips, frames, tokens, heads_table, tables, seg, ffn_shard, start):
    rows, wide = tokens.shape
    cols = heads_table.shape[1]
    grid = clips == GRID
    depth, ffn_wide = ffn_shard.shape
    n = Named()
    n.ins.update(frames=(frames, IN_SMEM), heads=(heads_table, IN_VMEM))
    cuts = None
    if grid:
        attn_shard, cond, small, w_ada, text, w_tk, w_tv = start
        rows_t, slab = text.shape[0], w_tk.shape[0]
        mods = w_ada.shape[1]
        n.ins.update(attn_shard=(attn_shard, ANY), cond=(cond, IN_VMEM), small=(small, IN_VMEM))
        n.ins.update(w_ada=(w_ada, IN_VMEM), text=(text, ANY))
        n.late.update(w_tk=w_tk, w_tv=w_tv)
        n.ins.update(ffn_shard=(ffn_shard, ANY))
        cuts = (
            Blocks(*attn_shard.shape, 96, 384),
            Blocks(rows_t, 2 * cols, 32, 2 * cols),
            Blocks(depth, ffn_wide, 96, 384),
        )
    else:
        weights, rows_table, ty = start
        rows_t = ty.shape[0]
        n.ins.update(weights=(weights, IN_VMEM), rows=(rows_table, IN_VMEM), ty=(ty, IN_VMEM))
    f, b = (shaped((rows, cols), F32), IN_VMEM), (shaped((rows, cols), BF16), IN_VMEM)
    ft, bt = (shaped((rows_t, cols), F32), IN_VMEM), (shaped((rows_t, cols), BF16), IN_VMEM)
    whole = (shaped((rows, wide), BF16), IN_VMEM)
    n.outs.update(q_pre=f, k_pre=f, q_rot=b, k_rot=b, q_text=b, values=b, self_o=b, inv_l=f, ky_pre=ft, kyr=bt, vy=bt)
    n.outs.update(text_o=b, inv_lt=f, h_one=whole, mixed=b, attn_sum=whole, h_two=whole)
    n.scratch.update(
        vaug=pltpu.VMEM((rows, 2 * cols), BF16),
        vyaug=pltpu.VMEM((rows_t, 2 * cols), BF16),
        partial=pltpu.VMEM((rows, wide), BF16),
        mixed_self=pltpu.VMEM((rows, cols), F32),
        tp_set=TpSum.scratch(rows, wide),
    )
    if grid:
        n.outs.update(
            weights=(shaped((GRID * attn_shard.shape[0], attn_shard.shape[1]), BF16), IN_VMEM),
            rows=(shaped((8, wide), F32), IN_VMEM),
            act=(shaped((GRID, cond.shape[2]), F32), IN_VMEM),
            text_all=(shaped((GRID, rows_t, slab), BF16), IN_VMEM),
            full_ffn=(shaped((GRID * depth, ffn_wide), BF16), ANY),
        )
        n.scratch.update(
            ty=pltpu.VMEM((rows_t, 2 * cols), F32),
            products=pltpu.VMEM((LINE, 2, rows_t, 2 * cols), BF16),
            smalls=pltpu.VMEM((GRID,) + small.shape, F32),
            conds=pltpu.VMEM((GRID, 1, cond.shape[2]), F32),
            part=pltpu.VMEM((GRID, 1, mods), F32),
            parts=pltpu.VMEM((GRID, 1, mods), F32),
            sems_set=[DMA((GRID - 1,))] * 8 + [DMA((3,))] * 2 + [DMA],
            attn_set=GatherChain.scratch(cuts[0].count),
            text_set=Scatter.scratch(cuts[1], True),
            ffn_set=GatherChain.scratch(cuts[2].count),
        )
    n.late.update(tok=tokens, cos=tables[0], sa=tables[1], sb=tables[2], seg=seg)
    out = n.call(functools.partial(forward_kernel, n, grid, cuts), params(1))
    if not grid:
        out.weights, out.rows, out.text_all = weights, rows_table, jnp.zeros((1, 16, 128), BF16)
    return out


UNITS = 256
ONES = 3
SP = ((0, 0), (2, 2), (2, 2), (2, 0))


def ffn_kernel(named, cut, cut_back, *refs):
    r = named.take(refs)
    engine, scatter = Idle(), Idle()
    for fetch in r.fetches:
        fetch.start()
    if cut is not None:
        engine = GatherChain(cut, r.shard, r.w_two, r.gather_set)
        scatter = Scatter(cut_back, r.grads, r.out, r.scatter_set)
        greet(dp_peers(), [])
        engine.start()
    rows, wide = r.h_two.shape
    step_rows = 256
    count = rows // step_rows
    tall = wide // LINE
    tanh_two = r.rows[3:4, :]
    ones, twos = r.w_one.shape[1] // (3 * UNITS), r.w_two.shape[1] // (3 * UNITS)

    def start_rows(i):
        here = block_rows(i, step_rows)
        live = live_rows(r.frames, i * step_rows, step_rows, wide)
        r.grad_ffn[here, :] = (live * tanh_two * r.cot[here, :].astype(F32)).astype(BF16)

    def copy(b):
        place = r.grads.at[:, :, :, pl.ds(b * 3 * UNITS, 3 * UNITS)]
        return pltpu.make_async_copy(r.staged.at[b % 2], place, r.stage_s.at[b % 2])

    def block(b):
        w = r.w_one if b < ones else r.w_two
        first = (b if b < ones else b - ones) * 3 * UNITS
        last = b == ones + twos - 1
        dgu = r.dgu_last if last else r.dgu

        def units(i):
            here = block_rows(i, step_rows)
            both = dot_nn(r.h_two[here, :], w[:, first : first + 2 * UNITS])
            gate, up = both[:, :UNITS], both[:, UNITS:]
            back = dot_nn(r.grad_ffn[here, :], w[:, first + 2 * UNITS : first + 3 * UNITS])
            logistic = 1.0 / (1.0 + jnp.exp(-gate))
            swish = gate * logistic
            r.hid[here, b * UNITS : (b + 1) * UNITS] = (swish * up).astype(BF16)
            d_gate = (back * up * logistic * (1.0 + gate * (1.0 - logistic))).astype(BF16)
            d_both = jnp.concatenate([d_gate, (back * swish).astype(BF16)], axis=1)
            dgu[here, :] = d_both
            added = dot_nt(d_both, w[:, first : first + 2 * UNITS])
            if b == 0:
                r.total[here, :] = added
            elif not last:
                r.total[here, :] += added
            else:
                r.partial[here, :] = (r.total[here, :] + added).astype(BF16)

        def products(m):
            lanes = pl.ds(pl.multiple_of(m * tall, 128), tall)
            downs = dot_tn(r.grad_ffn[:, lanes], r.hid[:, b * UNITS : (b + 1) * UNITS]).astype(BF16)
            ins = dot_tn(r.h_two[:, lanes], dgu[...]).astype(BF16)
            for y in range(2):
                part = slice(y * tall // 2, (y + 1) * tall // 2)
                r.staged[b % 2, m, y, :, : 2 * UNITS] = ins[part]
                r.staged[b % 2, m, y, :, 2 * UNITS :] = downs[part]

        pumps = 1 if b < ones else 2
        paced(count, units, (engine, pumps), (scatter, SP[b][0]))
        if not last:
            if b >= 2 and (b > 2 or cut is None):
                copy(b - 2).wait()
            paced(LINE, products, (engine, pumps), (scatter, SP[b][1]))
            copy(b).start()
        if b == 0 and cut is not None:
            copy(0).wait()
            scatter.start()

    paced(count, start_rows, (engine, 1))
    r.fetch.h_two.wait()
    r.fetch.w_one.wait()
    each = cut.count // twos if cut is not None else 0
    for b in range(ones):
        block(b)
    for b in range(ones, ones + twos):
        if cut is not None:
            need = min(engine.ticks, (b - ones + 1) * each + 2)
            while engine.done < need:
                paced(1, lambda i: None, (engine, 1))
            engine.arrive((b - ones) * each, each)
        block(b)
    copy(ones + twos - 3).wait()
    copy(ones + twos - 2).wait()
    finish_pumps(scatter)
    scatter.drain()
    engine.drain()


def ffn(clips, frames, h_two, cotangent, rows_table, w_one, second):
    rows, wide = h_two.shape
    half_wide = second.shape[1]
    blocks = (w_one.shape[1] + half_wide) // (3 * UNITS)
    grid = clips == GRID
    depth = wide // GRID
    n = Named()
    n.ins.update(frames=(frames, IN_SMEM), cot=(cotangent, IN_VMEM), rows=(rows_table, IN_VMEM))
    n.late.update(h_two=h_two, w_one=w_one)
    whole = (shaped((rows, wide), BF16), IN_VMEM)
    cut = Blocks(depth, half_wide, 96, 384) if grid else None
    cut_back = None
    if grid:
        n.ins.update(shard=(second, ANY))
        cut_back = Blocks(depth, 3 * UNITS, 96, 256)
        n.outs.update(w_two=(shaped((wide, half_wide), BF16), IN_VMEM), out=(shaped((depth, 3 * UNITS), F32), IN_VMEM))
        n.scratch.update(gather_set=GatherChain.scratch(cut.count), scatter_set=Scatter.scratch(cut_back))
    else:
        n.ins.update(w_two=(second, IN_VMEM))
    n.outs.update(partial=whole, grad_ffn=whole, hid=(shaped((rows, blocks * UNITS), BF16), IN_VMEM))
    n.outs.update(dgu_last=(shaped((rows, 2 * UNITS), BF16), IN_VMEM))
    n.outs.update(grads=(shaped((LINE, 2, depth, (blocks - 1) * 3 * UNITS), BF16), ANY))
    n.scratch.update(
        dgu=pltpu.VMEM((rows, 2 * UNITS), BF16),
        total=pltpu.VMEM((rows, wide), F32),
        staged=pltpu.VMEM((2, LINE, 2, depth, 3 * UNITS), BF16),
        stage_s=DMA((2,)),
    )
    out = n.call(functools.partial(ffn_kernel, n, cut, cut_back), params(5) if grid else plain_params())
    if not grid:
        out.w_two = second
    return out


def state_kernel(named, cut, *refs):
    r = named.take(refs)
    sums = TpSum(r.partial, r.grad_attn, r.tp_set[:2], r.tp_set[2:8], r.tp_set[8])
    tanh_attn, mult = r.rows.at[1:2], r.rows.at[2:3]
    engine = Idle()
    if cut is not None:
        engine = Scatter(cut, r.grads, r.out, r.scatter_set, ahead=A_S0)
        greet(dp_peers(), tp_peers())
        engine.start()
    else:
        greet([], tp_peers())
    loop(TP_PARTS, sums.stage_one)
    rows, wide = r.tok.shape
    step_rows = 256
    tall = wide // LINE
    blocks = r.hid.shape[1] // UNITS
    ones = r.w_one.shape[1] // (3 * UNITS)

    def down_copy(b):
        w = r.w_one if b < ones else r.w_two
        first = (b if b < ones else b - ones) * 3 * UNITS + 2 * UNITS
        place = r.down.at[:, pl.ds(b * UNITS, UNITS)]
        return pltpu.make_async_copy(w.at[:, pl.ds(first, UNITS)], place, r.down_s.at[b])

    for fetch in r.fetches:
        fetch.start()
    for b in range(blocks):
        down_copy(b).start()
    r.colsums[...] = jnp.zeros_like(r.colsums)

    def products(m):
        lanes = pl.ds(pl.multiple_of(m * tall, 128), tall)
        downs = dot_tn(r.grad_ffn[:, lanes], r.hid[:, (blocks - 1) * UNITS :]).astype(BF16)
        ins = dot_tn(r.h_two[:, lanes], r.dgu[...]).astype(BF16)
        for y in range(2):
            part = slice(y * tall // 2, (y + 1) * tall // 2)
            r.g_last[m, y, :, : 2 * UNITS] = ins[part]
            r.g_last[m, y, :, 2 * UNITS :] = downs[part]

    def p_copy(i):
        place = r.p_ffn.at[block_rows(i, step_rows)]
        return pltpu.make_async_copy(r.p_staged.at[lax.rem(i, 2)], place, r.p_s.at[lax.rem(i, 2)])

    def p_block(i):
        pl.when(i >= 2)(lambda: p_copy(i - 2).wait())
        r.p_staged[lax.rem(i, 2)] = dot_nt(r.hid[block_rows(i, step_rows), :], r.down[...]).astype(BF16)
        p_copy(i).start()

    def update(k, which):
        here = sums.spot(k, which)
        live = live_rows(r.frames, which * sums.half + k * sums.rows, sums.rows, wide)
        added = r.attn_sum[here, :].astype(F32)
        state = r.tok[here, :].astype(F32) + live * tanh_attn[...] * added
        inverse = lax.rsqrt(jnp.mean(state * state, axis=-1, keepdims=True) + EPS)
        hat = state * inverse
        g = r.grad_attn[here, :].astype(F32)
        scaled = g * mult[...]
        g_hat = g * hat
        back = inverse * (scaled - hat * jnp.mean(scaled * hat, axis=-1, keepdims=True))
        total = r.cot[here, :].astype(F32) + back
        r.grad_state[here, :] = total.astype(BF16)
        live_total = live * total
        r.grad_attn[here, :] = (tanh_attn[...] * live_total).astype(BF16)
        r.colsums[0:1, :] += jnp.sum(g_hat, axis=0, keepdims=True)
        r.colsums[1:2, :] += jnp.sum(live_total * added, axis=0, keepdims=True)

    paced(TP_PARTS, sums.stage_two, (engine, 2))
    for fetch in (r.fetch.h_two, r.fetch.grad_ffn, r.fetch.hid, r.fetch.dgu):
        fetch.wait()
    paced(LINE, products, (engine, 2))
    for b in range(blocks):
        down_copy(b).wait()
    paced(rows // step_rows, p_block, (engine, 2))

    for fetch in (r.fetch.tok, r.fetch.attn_sum, r.fetch.cot):
        fetch.wait()

    def three(k):
        sums.stage_three(k)

        @pl.when(k > 0)
        def _():
            sums.sent(k - 1)
            update(k - 1, sums.core)

    paced(TP_PARTS, three, (engine, 8))
    sums.sent(TP_PARTS - 1)
    update(TP_PARTS - 1, sums.core)

    def four(k):
        sums.stage_four(k)
        update(k, 1 - sums.core)

    paced(TP_PARTS, four, (engine, 2))
    finish_pumps(engine)
    for i in (1, 2):
        p_copy(rows // step_rows - i).wait()
    sums.drain(True)
    engine.drain()


def state_backward(clips, frames, tokens, attn_sum, cotangent, rows_table, h_two, w_one, fed):
    rows, wide = tokens.shape
    grid = clips == GRID
    depth = wide // GRID
    units, scattered = fed.hid.shape[1], fed.grads.shape[-1]
    cut = Blocks(depth, scattered - 3 * UNITS, 96, 256, 3 * UNITS) if grid else None
    n = Named()
    n.ins.update(frames=(frames, IN_SMEM), rows=(rows_table, IN_VMEM), w_one=(w_one, ANY), w_two=(fed.w_two, ANY))
    n.ins.update(partial=(fed.partial, ANY))
    n.late.update(h_two=h_two, grad_ffn=fed.grad_ffn, hid=fed.hid, dgu=fed.dgu_last)
    n.late.update(tok=tokens, attn_sum=attn_sum, cot=cotangent)
    whole = shaped((rows, wide), BF16)
    n.outs.update(grad_attn=(whole, IN_VMEM), grad_state=(whole, IN_VMEM), colsums=(shaped((8, wide), F32), IN_VMEM))
    n.outs.update(g_last=(shaped((LINE, 2, depth, 3 * UNITS), BF16), IN_VMEM), p_ffn=(whole, ANY))
    n.scratch.update(
        down=pltpu.VMEM((wide, units), BF16),
        down_s=DMA((units // UNITS,)),
        p_staged=pltpu.VMEM((2, 256, wide), BF16),
        p_s=DMA((2,)),
        tp_set=TpSum.scratch(rows, wide) + [DMA((TP_PARTS,))],
    )
    if grid:
        n.ins.update(grads=(fed.grads, ANY))
        n.outs.update(out=(shaped((depth, scattered - 3 * UNITS), F32), IN_VMEM))
        n.scratch.update(scatter_set=Scatter.scratch(cut))
    return n.call(functools.partial(state_kernel, n, cut), params(2))


def attn_back_kernel(named, blocks, blocks_t, *refs):
    r = named.take(refs)
    out_cols = r.full.shape[1] * 3 // 4
    out_fetch = pltpu.make_async_copy(r.full.at[:, out_cols:], r.weights, r.weights_s)
    out_fetch.start()
    frames, grad_attn, weights, heads_ref, seg_ref = r.frames, r.grad_attn, r.weights, r.heads, r.seg
    cos_ref, sa_ref, sb_ref = r.cos, r.sa, r.sb
    q_pre, k_pre, q_rot, k_rot, q_text, v_ref, self_o, inv_l = (
        r.q_pre, r.k_pre, r.q_rot, r.k_rot, r.q_text, r.values, r.self_o, r.inv_l
    )
    ky_pre, kyr, vy, text_o, inv_lt, h_one, mixed = r.ky_pre, r.kyr, r.vy, r.text_o, r.inv_lt, r.h_one, r.mixed
    grad_qkv, grad_text, gains, g_attn = r.grad_qkv, r.grad_text, r.gains, r.g_attn
    do_self, do_text, d_self, d_text, dqn, dk, dv, dky, dvy, klive, staged, stage_s = r.work_set
    sums = TpSum(r.partial, r.ffn_sum, r.tp_set[:2], r.tp_set[2:8], r.tp_set[8])
    for fetch in r.fetches:
        fetch.start()
    qgain, kgain, kygain, gate = (heads_ref.at[i : i + 1] for i in range(4))
    engine, text_engine = Idle(), Idle()
    if blocks is not None:
        engine = Scatter(blocks, r.grad, r.out, r.scatter_set, ahead=A_S1)
        text_engine = GatherChain(blocks_t, grad_text, r.all_text, r.gather_set, A_T)
        greet(dp_peers(), tp_peers())
        engine.start()
    else:
        greet([], tp_peers())
    loop(TP_PARTS, sums.stage_one)
    rows, cols = q_rot.shape
    wide = grad_attn.shape[1]
    step_rows = 256
    blocks_here = rows // step_rows
    pairs = cols // PAIR
    gains[...] = jnp.zeros_like(gains)
    dk[...] = jnp.zeros_like(dk)
    dv[...] = jnp.zeros_like(dv)
    dky[...] = jnp.zeros_like(dky)
    dvy[...] = jnp.zeros_like(dvy)

    def halves(value, first_head):
        lane = lax.broadcasted_iota(jnp.int32, (step_rows, PAIR), 1)
        out = jnp.zeros((step_rows, PAIR), F32)
        for head in range(2):
            total = jnp.sum(value * half_mask(step_rows, head, F32), axis=-1, keepdims=True)
            high = total.astype(BF16).astype(F32)
            spot = 2 * (first_head + head)
            out = out + jnp.where(lane == spot, high, jnp.where(lane == spot + 1, total - high, 0.0))
        return out

    def start_rows(i):
        here = block_rows(i, step_rows)
        g = dot_nn(grad_attn[here, :], weights[...])
        other = text_o[here, :].astype(F32)
        gains[3:4, :] += jnp.sum(g * other, axis=0, keepdims=True)
        first = (g * inv_l[here, :]).astype(BF16)
        do_self[here, :] = first
        second = (g * gate[...] * inv_lt[here, :]).astype(BF16)
        do_text[here, :] = second
        dot_self = first.astype(F32) * self_o[here, :].astype(F32)
        dot_text = second.astype(F32) * other
        each = [slice(pair * PAIR, (pair + 1) * PAIR) for pair in range(pairs)]
        d_self[here, :] = sum(halves(dot_self[:, lanes], 2 * pair) for pair, lanes in enumerate(each)).astype(BF16)
        d_text[here, :] = sum(halves(dot_text[:, lanes], 2 * pair) for pair, lanes in enumerate(each)).astype(BF16)
        klive[here, :] = k_rot[here, :] * live_rows(frames, i * step_rows, step_rows, cols).astype(BF16)

    def back(q_ref, k_ref, k_live, v_in, do_ref, d_ref, dk_ref, dv_ref, turned):
        def step(i):
            pair, block = lax.div(i, blocks_here), lax.rem(i, blocks_here)
            here, lanes = block_rows(block, step_rows), pair_lanes(pair)
            keys = k_ref[:, lanes]
            values = v_in[:, lanes]
            lane = lax.broadcasted_iota(jnp.int32, values.shape, 1)
            dq = jnp.zeros((step_rows, PAIR), F32)
            for head in range(2):
                mask = half_mask(step_rows, head, BF16)
                q = q_ref[here, lanes] * mask
                do = do_ref[here, lanes] * mask
                scores = dot_nt(keys, q)
                p = jnp.exp(scores)
                dv_ref[:, lanes] += dot_nn(p.astype(BF16), do)
                spot = 2 * (2 * pair + head)
                minus = jnp.where((lane == spot) | (lane == spot + 1), -1.0, 0.0).astype(BF16)
                left = jnp.concatenate([values, minus], axis=1)
                right = jnp.concatenate([do, d_ref[here, :]], axis=1)
                ds = (p * dot_nt(left, right)).astype(BF16)
                dk_ref[:, lanes] += dot_nn(ds, q)
                key_mask = half_mask(keys.shape[0], head, BF16)
                dq = dq + dot_tn(ds, k_live[:, lanes] * key_mask)
            dq = dq * SCALE
            if turned:
                dqn[here, lanes] += rope_back(dq, cos_ref[here, :], sa_ref[here, :], sb_ref[here, :])
            else:
                dqn[here, lanes] = dq

        return step

    out_fetch.wait()
    paced(blocks_here, start_rows, (engine, 2))
    def norm_back(grad_normed, pre, gain, row):
        inverse = head_inverse(pre, seg_ref[...])
        hat = pre * inverse
        gains[row : row + 1, :] += jnp.sum(grad_normed * hat, axis=0, keepdims=True)
        scaled = grad_normed * gain
        average = segment_sum(scaled * hat, seg_ref[...]) * (1.0 / HEAD)
        return (inverse * (scaled - hat * average)).astype(BF16)

    def end_rows(i):
        here = block_rows(i, step_rows)
        cosines, sine_a, sine_b = thrice(cos_ref[here, :]), thrice(sa_ref[here, :]), thrice(sb_ref[here, :])
        live = live_rows(frames, i * step_rows, step_rows, cols)
        grad_qkv[here, :cols] = norm_back(dqn[here, :], q_pre[here, :], qgain[...], 0)
        dkn = rope_back(dk[here, :] * live, cosines, sine_a, sine_b)
        grad_qkv[here, cols : 2 * cols] = norm_back(dkn, k_pre[here, :], kgain[...], 1)
        grad_qkv[here, 2 * cols : 3 * cols] = (dv[here, :] * live).astype(BF16)
        for k in range(TP_PARTS // blocks_here):
            sums.stage_three(i * (TP_PARTS // blocks_here) + k)

    for fetch in (r.fetch.q_text, r.fetch.kyr, r.fetch.vy):
        fetch.wait()
    text_back = back(q_text, kyr, kyr, vy, do_text, d_text, dky, dvy, False)

    def text_step(i):
        text_back(i)
        pl.when(i < TP_PARTS)(lambda: sums.stage_two(i))

    paced(pairs * blocks_here, text_step, (engine, 3))
    for fetch in (r.fetch.seg, r.fetch.ky_pre, r.fetch.q_rot, r.fetch.values, r.fetch.cos, r.fetch.sa, r.fetch.sb):
        fetch.wait()
    grad_text[:, :cols] = norm_back(dky[...], ky_pre[...], kygain[...], 2)
    grad_text[:, cols:] = dvy[...].astype(BF16)
    text_engine.start()
    self_back = back(q_rot, k_rot, klive, v_ref, do_self, d_self, dk, dv, True)

    half = pairs * blocks_here // 2
    paced(half, self_back, (engine, 6), (text_engine, 2))
    paced(half, lambda i: self_back(i + half), (text_engine, 3))
    for fetch in (r.fetch.q_pre, r.fetch.k_pre, r.fetch.h_one, r.fetch.mixed):
        fetch.wait()
    paced(blocks_here, end_rows, (text_engine, 2))
    tall = wide // LINE

    def copy(m):
        return pltpu.make_async_copy(staged.at[lax.rem(m, 2)], g_attn.at[m], stage_s.at[lax.rem(m, 2)])

    def products(m):
        lanes = pl.ds(pl.multiple_of(m * tall, 128), tall)
        pl.when(m >= 2)(lambda: copy(m - 2).wait())
        first = dot_tn(h_one[:, lanes], grad_qkv[...]).astype(BF16)
        second = dot_tn(grad_attn[:, lanes], mixed[...]).astype(BF16)
        for y in range(2):
            part = slice(y * tall // 2, (y + 1) * tall // 2)
            staged[lax.rem(m, 2), y, :, : 3 * cols] = first[part]
            staged[lax.rem(m, 2), y, :, 3 * cols :] = second[part]
        copy(m).start()

    paced(LINE, products, (text_engine, 4))
    finish_pumps(engine)
    finish_pumps(text_engine)
    text_engine.arrive()
    loop(TP_PARTS, sums.stage_four)
    copy(LINE - 2).wait()
    copy(LINE - 1).wait()
    sums.drain()
    engine.drain()
    text_engine.drain()


def attn_backward(clips, frames, grad_attn, full_attn, heads_table, tables, seg, p, partial, g_last):
    rows, wide = grad_attn.shape
    cols = heads_table.shape[1]
    rows_t = p.kyr.shape[0]
    depth, last_wide = wide // GRID, g_last.shape[-1]
    grid = clips == GRID
    f, b = pltpu.VMEM((rows, cols), F32), pltpu.VMEM((rows, cols), BF16)
    ft = pltpu.VMEM((rows_t, cols), F32)
    slim = pltpu.VMEM((rows, PAIR), BF16)
    n = Named()
    n.ins.update(frames=(frames, IN_SMEM), grad_attn=(grad_attn, IN_VMEM), full=(full_attn, ANY))
    n.ins.update(heads=(heads_table, IN_VMEM), k_rot=(p.k_rot, IN_VMEM), self_o=(p.self_o, IN_VMEM))
    n.ins.update(inv_l=(p.inv_l, IN_VMEM), text_o=(p.text_o, IN_VMEM), inv_lt=(p.inv_lt, IN_VMEM), partial=(partial, ANY))
    n.late.update(q_text=p.q_text, kyr=p.kyr, vy=p.vy, seg=seg, ky_pre=p.ky_pre, q_rot=p.q_rot, values=p.values)
    n.late.update(cos=tables[0], sa=tables[1], sb=tables[2], q_pre=p.q_pre, k_pre=p.k_pre, h_one=p.h_one, mixed=p.mixed)
    n.outs.update(
        grad_qkv=(shaped((rows, 3 * cols), BF16), IN_VMEM),
        grad_text=(shaped((rows_t, 2 * cols), BF16), IN_VMEM),
        gains=(shaped((8, cols), F32), IN_VMEM),
        ffn_sum=(shaped((rows, wide), BF16), IN_VMEM),
        g_attn=(shaped((LINE, 2, depth, 4 * cols), BF16), ANY),
    )
    n.scratch.update(
        work_set=[b, b, slim, slim, f, f, f, ft, ft, b, pltpu.VMEM((2, 2, depth, 4 * cols), BF16), DMA((2,))],
        tp_set=TpSum.scratch(rows, wide) + [DMA((TP_PARTS,))],
        weights=pltpu.VMEM((wide, cols), BF16),
        weights_s=DMA,
    )
    parts = blocks_t = None
    if grid:
        parts = Blocks(depth, last_wide, 96, 256)
        blocks_t = Blocks(rows_t, 2 * cols, 32, 2 * cols)
        n.ins.update(grad=(g_last, ANY))
        n.outs.update(
            out=(shaped((depth, last_wide), F32), IN_VMEM), all_text=(shaped((GRID * rows_t, 2 * cols), BF16), ANY)
        )
        n.scratch.update(scatter_set=Scatter.scratch(parts), gather_set=GatherChain.scratch(blocks_t.count))
    return n.call(functools.partial(attn_back_kernel, n, parts, blocks_t), params(3))


def last_kernel(named, parts, *refs):
    r = named.take(refs)
    frames, grad_qkv, weights, tok, grad_state = r.frames, r.grad_qkv, r.weights, r.tok, r.grad_state
    rows_ref, sums_two, gains, ffn_sum, attn_sum, cot = r.rows, r.sums_two, r.gains, r.ffn_sum, r.attn_sum, r.cot
    result, grad_tokens, vecs = r.result, r.grad_tokens, r.vecs
    partial, grad_n, colsum, outsum, vec = r.work_set
    sums = TpSum(partial, grad_n, r.tp_set[:2], r.tp_set[2:8])
    me = lax.axis_index("dp")
    engine = Idle()
    peers = []
    for fetch in r.fetches:
        fetch.start()
    if parts is not None:
        v_s, v_r = r.sems_set
        text_all, all_text, g_tk, g_tv = r.text_all, r.all_text, r.g_tk, r.g_tv
        peers = dp_peers()
        engine = Scatter(parts, r.grad_a, r.out_a, r.scatter_set, ahead=A_S2)
        greet(peers, tp_peers())
        engine.start()
    else:
        greet([], tp_peers())
    mult_one, tanh_one, _, tanh_two, gain_one, lift_one, gain_two, lift_two = (rows_ref[i : i + 1, :] for i in range(8))
    colsum[...] = jnp.zeros_like(colsum)
    outsum[...] = jnp.zeros_like(outsum)
    wide = tok.shape[1]
    cols = grad_qkv.shape[1] // 3
    step_rows = 256

    def project(which):
        def step(i):
            here = pl.ds(pl.multiple_of(which * sums.half + i * step_rows, 16), step_rows)
            partial[here, :] = dot_nt(grad_qkv[here, :], weights[:, : 3 * cols]).astype(BF16)

        return step

    parts_each = TP_PARTS // (sums.half // step_rows)

    def project_send(i):
        project(1 - sums.core)(i)
        loop(parts_each, lambda k: sums.stage_one(i * parts_each + k))

    paced(sums.half // step_rows, project_send)
    paced(sums.half // step_rows, project(sums.core), (engine, P_1))
    paced(TP_PARTS, sums.stage_two, (engine, P_2))

    def output(i):
        here = block_rows(i, 64)
        live = live_rows(frames, i * 64, 64, wide)
        added = live * ffn_sum[here, :].astype(F32)
        state = tok[here, :].astype(F32) + live * tanh_one * attn_sum[here, :].astype(F32)
        result[here, :] = (state + tanh_two * added).astype(BF16)
        outsum[...] += jnp.sum(added * cot[here, :].astype(F32), axis=0, keepdims=True)

    for fetch in (r.fetch.tok, r.fetch.ffn_sum, r.fetch.attn_sum, r.fetch.cot):
        fetch.wait()
    paced(tok.shape[0] // 64, output, (engine, P_3))
    if parts is not None:
        rows_t = text_all.shape[1]

        def text_products(i):
            here = block_rows(i, rows_t)
            g_tk[...] += dot_tn(text_all[i], all_text[here, :cols])
            g_tv[...] += dot_tn(text_all[i], all_text[here, cols:])

        g_tk[...] = jnp.zeros_like(g_tk)
        g_tv[...] = jnp.zeros_like(g_tv)
        r.fetch.text_all.wait()
        r.fetch.all_text.wait()
        paced(GRID, text_products, (engine, P_4))

    def update(k, which):
        here = sums.spot(k, which)
        x = tok[here, :].astype(F32)
        inverse = lax.rsqrt(jnp.mean(x * x, axis=-1, keepdims=True) + EPS)
        hat = x * inverse
        g = grad_n[here, :].astype(F32)
        scaled = g * mult_one
        back = inverse * (scaled - hat * jnp.mean(scaled * hat, axis=-1, keepdims=True))
        grad_tokens[here, :] = (grad_state[here, :].astype(F32) + back).astype(BF16)
        colsum[...] += jnp.sum(g * hat, axis=0, keepdims=True)

    def three(k):
        sums.stage_three(k)
        update(k, sums.core)

    r.fetch.grad_state.wait()
    paced(TP_PARTS, three, (engine, 4))

    def four(k):
        sums.stage_four(k)
        update(k, 1 - sums.core)

    paced(TP_PARTS, four, (engine, 2))
    pieces = (
        colsum[...] * gain_one,
        sums_two[1:2, :] * (1.0 - tanh_one * tanh_one),
        sums_two[0:1, :] * gain_two,
        outsum[...] * (1.0 - tanh_two * tanh_two),
        colsum[...] * lift_one,
        sums_two[0:1, :] * lift_two,
    )
    for i, piece in enumerate(pieces):
        vec[:, i * wide : (i + 1) * wide] = piece
    for i in range(4):
        vec[:, 6 * wide + i * cols : 6 * wide + (i + 1) * cols] = gains[i : i + 1, :]
    for i, there in enumerate(peers):
        remote(vec, vecs.at[me], v_s.at[i], v_r.at[i], dp=there).start()
    finish_pumps(engine)
    vecs[pl.ds(me if peers else 0, 1)] = vec[...][None]
    for i, there in enumerate(peers):
        here = lax.rem(me + GRID - 1 - i, GRID)
        remote(vec, vecs.at[here], v_s.at[i], v_r.at[i], dp=me).wait_recv()
        remote(vec, vecs.at[me], v_s.at[i], v_r.at[i], dp=there).wait_send()
    sums.drain()
    engine.drain()


def last_backward(clips, frames, tokens, cotangent, p, state, back, qkv_weights):
    rows, wide = tokens.shape
    grid = clips == GRID
    cols = back.gains.shape[1]
    depth, wide_a = back.g_attn.shape[-2:]
    whole = (shaped((rows, wide), BF16), IN_VMEM)
    vec = (1, 6 * wide + 4 * cols)
    n = Named()
    n.ins.update(frames=(frames, IN_SMEM), grad_qkv=(back.grad_qkv, IN_VMEM), weights=(qkv_weights, IN_VMEM))
    n.ins.update(rows=(p.rows, IN_VMEM), sums_two=(state.colsums, IN_VMEM), gains=(back.gains, IN_VMEM))
    n.late.update(tok=tokens, ffn_sum=back.ffn_sum, attn_sum=p.attn_sum, cot=cotangent)
    n.outs.update(result=whole, grad_tokens=whole, vecs=(shaped(((GRID if grid else 1),) + vec, F32), IN_VMEM))
    n.scratch.update(
        work_set=[
            pltpu.VMEM((rows, wide), BF16),
            pltpu.VMEM((rows, wide), BF16),
            pltpu.VMEM((1, wide), F32),
            pltpu.VMEM((1, wide), F32),
            pltpu.VMEM(vec, F32),
        ],
        tp_set=TpSum.scratch(rows, wide),
    )
    parts = None
    if grid:
        parts = Blocks(depth, wide_a, 96, 256)
        g_text = (shaped((p.text_all.shape[-1], cols), F32), IN_VMEM)
        n.ins.update(grad_a=(back.g_attn, ANY))
        n.late.update(text_all=p.text_all, all_text=back.all_text)
        n.outs.update(g_tk=g_text, g_tv=g_text, out_a=(shaped((depth, wide_a), F32), IN_VMEM))
        n.scratch.update(sems_set=[DMA((GRID - 1,))] * 2, scatter_set=Scatter.scratch(parts))
    n.late.update(grad_state=state.grad_state)
    return n.call(functools.partial(last_kernel, n, parts), params(4))


def gather_plain(shard):
    return lax.all_gather(shard, "dp", axis=0, tiled=True)


def scatter_plain(grad):
    return lax.psum_scatter(grad, "dp", scatter_dimension=0, tiled=True).astype(F32)


def first_plain(shard, cond, small, w_ada, text, w_tk, w_tv):
    act = jax.nn.silu(lax.all_to_all(cond[:, 0], "dp", 0, 0, tiled=True)).astype(BF16)
    parts = dot_nn(act, w_ada)
    mods = lax.psum_scatter(parts, "dp", scatter_dimension=0, tiled=True)[0]
    full_text = gather_plain(jnp.concatenate([w_tk, w_tv], axis=1))
    smalls = lax.all_gather(small, "dp", axis=0)[:, 0, :]
    wide = w_ada.shape[1] // 4
    bias, gain = 4 * wide // smalls.shape[0], wide // smalls.shape[0]
    scale_one, gate_one, scale_two, gate_two = jnp.split(mods + smalls[:, :bias].reshape(-1), 4)
    gain_one, gain_two = smalls[:, bias : bias + gain].reshape(-1), smalls[:, bias + gain :].reshape(-1)
    lift_one, lift_two = 1.0 + scale_one, 1.0 + scale_two
    values = (
        gain_one * lift_one,
        jnp.tanh(gate_one),
        gain_two * lift_two,
        jnp.tanh(gate_two),
        gain_one,
        lift_one,
        gain_two,
        lift_two,
    )
    return gather_plain(shard), jnp.stack(values), act.astype(F32), dot_nn(text, full_text)


def unpack_kernel(count, *refs):
    blocks, (attn, vecs, act) = refs[:count], refs[count : count + 3]
    q, k, v, out, gate, up, down, g_ada, bias, g_one, g_two, rest = refs[count + 3 :]
    cols = q.shape[1]
    for i, ref in enumerate((q, k, v, out)):
        ref[...] = attn[:, i * cols : (i + 1) * cols]
    b = 0
    for ref in blocks:
        for at in range(0, ref.shape[1], 3 * UNITS):
            for i, place in enumerate((gate, up, down)):
                place[:, b * UNITS : (b + 1) * UNITS] = ref[:, at + i * UNITS : at + (i + 1) * UNITS]
            b += 1
    total = vecs[0]
    for i in range(1, vecs.shape[0]):
        total = total + vecs[i]
    wide = g_ada.shape[1] // 4
    rest[...] = total[:, 6 * wide :]
    me = lax.axis_index("dp")
    for i in range(vecs.shape[0]):

        @pl.when(me == i)
        def _():
            bias[...] = total[:, i * bias.shape[1] : (i + 1) * bias.shape[1]]
            gain = g_one.shape[1]
            g_one[...] = total[:, 4 * wide + i * gain : 4 * wide + (i + 1) * gain]
            g_two[...] = total[:, 5 * wide + i * gain : 5 * wide + (i + 1) * gain]

    clips = jnp.concatenate([vecs[i][:, : 4 * wide] for i in range(vecs.shape[0])], axis=0)
    turned = act[...].T
    for at in range(0, 4 * wide, 512):
        part = turned[:, 0:1] * clips[0:1, at : at + 512]
        for i in range(1, clips.shape[0]):
            part = part + turned[:, i : i + 1] * clips[i : i + 1, at : at + 512]
        g_ada[:, at : at + 512] = part


def unpack(blocks, attn, vecs, act, units, bias_rows, gain_rows):
    depth, cols = attn.shape[0], attn.shape[1] // 4
    wide = (vecs.shape[2] - 4 * cols) // 6
    shapes = [(depth, cols)] * 4 + [(depth, units)] * 3
    shapes += [(act.shape[1], 4 * wide), (1, bias_rows), (1, gain_rows), (1, gain_rows), (1, 4 * cols)]
    return pl.pallas_call(
        functools.partial(unpack_kernel, len(blocks)),
        out_shape=[shaped(shape, F32) for shape in shapes],
        in_specs=[IN_VMEM] * (len(blocks) + 3),
        out_specs=[IN_VMEM] * len(shapes),
        compiler_params=plain_params(),
    )(*blocks, attn, vecs, act)


def on_device(
    tokens,
    text,
    cond,
    frames,
    w_query,
    w_key,
    w_value,
    w_out,
    w_text_key,
    w_text_value,
    w_gate,
    w_up,
    w_down,
    w_ada,
    ada_bias,
    norm_one,
    norm_two,
    query_gain,
    key_gain,
    text_key_gain,
    cross_gate,
    cotangent,
):
    rows, wide = tokens.shape
    clips = lax.axis_size("dp")
    grid = clips == GRID
    cols, units = w_query.shape[1], w_gate.shape[1]
    heads_here = cols // HEAD
    bias_rows, gain_rows = ada_bias.shape[0], norm_one.shape[0]
    gate_tanh = jnp.tanh(cross_gate.astype(F32))
    vectors = (ada_bias, norm_one, norm_two, query_gain, key_gain, text_key_gain, jnp.repeat(gate_tanh, HEAD))
    cond_rows = cond.astype(F32).reshape(clips, 1, -1)
    packed = pack(w_query, w_key, w_value, w_out.T, w_gate, w_up, w_down.T, vectors)
    attn_shard, *pieces, small, heads_table = packed
    opening = (attn_shard, cond_rows, small, w_ada, text, w_text_key, w_text_value)
    if not grid:
        full_attn, rows_table, act_rows, ty = first_plain(*opening)
        opening = (full_attn, rows_table, ty)
    tables, seg = rope_tables(rows), segment_ones(cols)
    passed = forward(clips, frames, tokens, heads_table, tables, seg, pieces[0], opening)
    full_attn, rows_table = passed.weights, passed.rows
    if grid:
        act_rows, half_one, second = passed.act, passed.full_ffn, pieces[1]
    else:
        half_one, second = gather_plain(pieces[0]), gather_plain(pieces[1])
    p = passed
    fed = ffn(clips, frames, p.h_two, cotangent, p.rows, half_one, second)
    state = state_backward(clips, frames, tokens, p.attn_sum, cotangent, p.rows, p.h_two, half_one, fed)
    back = attn_backward(
        clips, frames, state.grad_attn, full_attn, heads_table, tables, seg, p, state.p_ffn, state.g_last
    )
    last = last_backward(clips, frames, tokens, cotangent, p, state, back, full_attn)
    vecs = last.vecs
    s_blocks = [fed.out, state.out] if grid else [scatter_plain(fed.grads.reshape(wide, -1))]
    if grid:
        s_last, s_attn, s_text_key, s_text_value = back.out, last.out_a, last.g_tk, last.g_tv
    if not grid:
        s_last, s_attn = (scatter_plain(g.reshape(wide, -1)) for g in (state.g_last, back.g_attn))
        s_text = scatter_plain(dot_tn(text, back.grad_text).astype(BF16))
        s_text_key, s_text_value = s_text[:, :cols], s_text[:, cols:]
        vecs = lax.all_gather(vecs[0], "dp", axis=0)
    g_query, g_key, g_value, g_out, g_gate, g_up, g_down, g_ada, g_bias, g_one, g_two, rest = unpack(
        (*s_blocks, s_last), s_attn, vecs, act_rows, units, bias_rows, gain_rows
    )
    rest = rest[0]
    g_cross_gate = jnp.sum(rest[3 * cols :].reshape(heads_here, HEAD), axis=1) * (1.0 - gate_tanh * gate_tanh)
    return (
        last.result,
        last.grad_tokens,
        g_query,
        g_key,
        g_value,
        g_out.T,
        s_text_key,
        s_text_value,
        g_gate,
        g_up,
        g_down.T,
        g_ada,
        g_bias[0],
        g_one[0],
        g_two[0],
        rest[:cols],
        rest[cols : 2 * cols],
        rest[2 * cols : 3 * cols],
        g_cross_gate,
    )


def solution(mesh):
    placed = (
        P("dp", None),
        P("dp", None),
        P("dp", None),
        P("dp"),
        P("dp", "tp"),
        P("dp", "tp"),
        P("dp", "tp"),
        P("tp", "dp"),
        P("dp", "tp"),
        P("dp", "tp"),
        P("dp", "tp"),
        P("dp", "tp"),
        P("tp", "dp"),
        P("dp", None),
        P("dp"),
        P("dp"),
        P("dp"),
        P("tp"),
        P("tp"),
        P("tp"),
        P("tp"),
        P("dp", None),
    )
    return jax.shard_map(
        on_device,
        mesh=mesh,
        in_specs=placed,
        out_specs=(
            P("dp", None),
            P("dp", None),
            P("dp", "tp"),
            P("dp", "tp"),
            P("dp", "tp"),
            P("tp", "dp"),
            P("dp", "tp"),
            P("dp", "tp"),
            P("dp", "tp"),
            P("dp", "tp"),
            P("tp", "dp"),
            P("dp", None),
            P("dp"),
            P("dp"),
            P("dp"),
            P("tp"),
            P("tp"),
            P("tp"),
            P("tp"),
        ),
        check_vma=False,
    )
```

```python
import functools
import types

import jax
import jax.numpy as jnp
import numpy as np
from jax import lax
from jax.experimental import pallas as pl
from jax.experimental.pallas import tpu as pltpu
from jax.sharding import PartitionSpec as P

HEAD = 64
FRAME_TOK = 64
EPS = 1e-06
ROPE_BASE = 10000.0
SCALE = HEAD**-0.5
MESH = pl.DeviceIdType.MESH
VMEM_LIMIT = 60 * 2**20
GRID = 8
LINE = 4
PAIR = 2 * HEAD
TP_PARTS = 8
AHEAD = 2
LAG = 3
P_1 = 1
P_2 = 0
P_3 = 4
P_4 = 4
O_1 = 2
O_2 = 2
O_3 = 1
O_4 = 1
A_A = 3
A_T = 2
A_S1 = 2
A_S0 = 2
A_S2 = 3
A_P = 2
DMA = pltpu.SemaphoreType.DMA
F32 = jnp.float32
BF16 = jnp.bfloat16


def dot_nn(left, right):
    return jnp.dot(left, right, preferred_element_type=F32)


def dot_nt(left, right):
    return lax.dot_general(left, right, (((1,), (1,)), ((), ())), preferred_element_type=F32)


def dot_tn(left, right):
    return lax.dot_general(left, right, (((0,), (0,)), ((), ())), preferred_element_type=F32)


def remote(src, dst, send, recv, **where):
    return pltpu.make_async_remote_copy(
        src_ref=src, dst_ref=dst, send_sem=send, recv_sem=recv, device_id=where, device_id_type=MESH
    )


def greet(dp_peers, tp_peers):
    barrier = pltpu.get_barrier_semaphore()
    for peer in dp_peers:
        pl.semaphore_signal(barrier, inc=1, device_id={"dp": peer}, device_id_type=MESH)
    for peer in tp_peers:
        pl.semaphore_signal(barrier, inc=1, device_id={"tp": peer}, device_id_type=MESH)
    pl.semaphore_wait(barrier, len(dp_peers) + len(tp_peers))


def dp_peers():
    me = lax.axis_index("dp")
    return [lax.rem(me + step, GRID) for step in range(1, GRID)]


def tp_peers():
    me = lax.axis_index("tp")
    return [me + 1 - 2 * lax.rem(me, 2), lax.rem(me + 2, 4)]


def aligned(value, by):
    return value if isinstance(value, int) else pl.multiple_of(value, by)


def loop(count, step):
    def body(i, carry):
        step(i)
        return carry

    lax.fori_loop(0, count, body, 0)


def add_rows(out_ref, first, *others):
    rows, wide = out_ref.shape
    tall = min(rows, 96 if wide <= 384 else 32)
    plain = len(others) == 1 and out_ref.dtype == BF16

    def step(i):
        here = pl.ds(aligned(i * tall, 16), tall)
        total = first[here, :] if plain else first[here, :].astype(F32)
        for other in others:
            total = total + (other[here, :] if plain else other[here, :].astype(F32))
        out_ref[here, :] = total.astype(out_ref.dtype)

    if rows == tall:
        step(0)
    else:
        loop(rows // tall, step)


class Blocks:
    def __init__(self, depth, wide, rows, cols, first=0):
        self.depth, self.wide, self.rows, self.cols, self.first = depth, wide, rows, cols, first
        self.down = depth // rows
        self.count = self.down * (wide // cols)

    def at(self, c):
        if isinstance(c, int):
            return c % self.down * self.rows, self.first + c // self.down * self.cols
        row = aligned(lax.rem(c, self.down) * self.rows, 16)
        col = aligned(self.first + lax.div(c, self.down) * self.cols, 128)
        return row, col

class Gather:
    def __init__(self, blocks, shard, full, sems, ahead=AHEAD):
        self.b, self.shard, self.full, self.ahead = blocks, shard, full, min(ahead, blocks.count)
        self.z_s, self.z_r, self.y_s, self.y_r, self.own_s = sems
        self.me = lax.axis_index("dp")
        self.z, self.y = self.me // 2, lax.rem(self.me, 2)
        self.lines = [lax.rem(self.z + step, LINE) for step in range(1, LINE)]
        self.ticks, self.done = blocks.count, 0

    @staticmethod
    def scratch(count):
        return [DMA((count, 3))] * 2 + [DMA((count, 4))] * 2 + [DMA((count,))]

    def own(self, c):
        row, col = self.b.at(c)
        return self.shard.at[pl.ds(row, self.b.rows), pl.ds(col, self.b.cols)]

    def place(self, c, origin):
        row, col = self.b.at(c)
        start = pl.multiple_of(origin * self.b.depth + row, 16)
        return self.full.at[pl.ds(start, self.b.rows), pl.ds(col, self.b.cols)]

    def along(self, c, i):
        there = 2 * self.lines[i] + self.y
        return remote(self.own(c), self.place(c, self.me), self.z_s.at[c, i], self.z_r.at[c, i], dp=there)

    def came_along(self, c, i):
        line = lax.rem(self.z + LINE - 1 - i, LINE)
        place = self.place(c, 2 * line + self.y)
        return line, remote(place, place, self.z_s.at[c, i], self.z_r.at[c, i], dp=self.me)

    def across(self, c, line, mine=False):
        origin = 2 * line + self.y
        src = self.own(c) if mine else self.place(c, origin)
        other = self.me + 1 - 2 * self.y
        return remote(src, self.place(c, origin), self.y_s.at[c, line], self.y_r.at[c, line], dp=other)

    def came_across(self, c, line):
        place = self.place(c, 2 * line + 1 - self.y)
        return remote(place, place, self.y_s.at[c, line], self.y_r.at[c, line], dp=self.me)

    def local(self, c):
        return pltpu.make_async_copy(self.own(c), self.place(c, self.me), self.own_s.at[c])

    def begin(self, c):
        for i in range(LINE - 1):
            self.along(c, i).start()
        self.across(c, self.z, True).start()
        self.local(c).start()

    def start(self):
        for c in range(self.ahead):
            self.begin(c)

    def pump(self, t):
        pl.when(t + self.ahead < self.b.count)(lambda: self.begin(t + self.ahead))
        for i in range(LINE - 1):
            line, came = self.came_along(t, i)
            came.wait_recv()
            self.across(t, line).start()

    def arrive(self, first=0, count=None):
        def step(i):
            c = first + i
            for line in range(LINE):
                self.came_across(c, line).wait_recv()
            self.local(c).wait()

        loop(self.b.count if count is None else count, step)

    def drain(self):
        def step(c):
            for line in range(LINE):
                self.across(c, line).wait_send()
            for i in range(LINE - 1):
                self.along(c, i).wait_send()

        loop(self.b.count, step)


class GatherChain:
    def __init__(self, blocks, shard, full, sems, ahead=AHEAD):
        self.b, self.shard, self.full, self.ahead = blocks, shard, full, min(ahead, blocks.count)
        self.up_s, self.up_r, self.dn_s, self.dn_r, self.y_s, self.y_r, self.own_s = sems
        self.me = lax.axis_index("dp")
        self.z, self.y = self.me // 2, lax.rem(self.me, 2)
        self.ticks, self.done = blocks.count + LINE - 2, 0

    @staticmethod
    def scratch(count):
        return [DMA((count, 3))] * 4 + [DMA((count, 4))] * 2 + [DMA((count,))]

    def own(self, c):
        row, col = self.b.at(c)
        return self.shard.at[pl.ds(row, self.b.rows), pl.ds(col, self.b.cols)]

    def place(self, c, origin):
        row, col = self.b.at(c)
        start = pl.multiple_of(origin * self.b.depth + row, 16)
        return self.full.at[pl.ds(start, self.b.rows), pl.ds(col, self.b.cols)]

    def up(self, c, hop):
        origin = self.me - 2 * hop
        src = self.own(c) if hop == 0 else self.place(c, origin)
        return remote(src, self.place(c, origin), self.up_s.at[c, hop], self.up_r.at[c, hop], dp=self.me + 2)

    def down(self, c, hop):
        origin = self.me + 2 * hop
        src = self.own(c) if hop == 0 else self.place(c, origin)
        return remote(src, self.place(c, origin), self.dn_s.at[c, hop], self.dn_r.at[c, hop], dp=self.me - 2)

    def across(self, c, line, mine=False):
        origin = 2 * line + self.y
        src = self.own(c) if mine else self.place(c, origin)
        other = self.me + 1 - 2 * self.y
        return remote(src, self.place(c, origin), self.y_s.at[c, line], self.y_r.at[c, line], dp=other)

    def came(self, c, origin, sems):
        return remote(self.place(c, origin), self.place(c, origin), sems, sems, dp=self.me)

    def local(self, c):
        return pltpu.make_async_copy(self.own(c), self.place(c, self.me), self.own_s.at[c])

    def begin(self, c):
        pl.when(self.z < LINE - 1)(lambda: self.up(c, 0).start())
        pl.when(self.z > 0)(lambda: self.down(c, 0).start())
        self.across(c, self.z, True).start()
        self.local(c).start()

    def start(self):
        for c in range(self.ahead):
            self.begin(c)

    def pump(self, t):
        me, z, count = self.me, self.z, self.b.count
        pl.when(t + self.ahead < count)(lambda: self.begin(t + self.ahead))
        for hop in range(LINE - 1):
            c = t - hop
            valid = (c >= 0) & (c < count)

            @pl.when(valid & (z - 1 - hop >= 0))
            def _():
                self.came(c, me - 2 * (hop + 1), self.up_r.at[c, hop]).wait_recv()
                if hop < LINE - 2:
                    pl.when(z < LINE - 1)(lambda: self.up(c, hop + 1).start())
                self.across(c, z - 1 - hop).start()

            @pl.when(valid & (z + 1 + hop <= LINE - 1))
            def _():
                self.came(c, me + 2 * (hop + 1), self.dn_r.at[c, hop]).wait_recv()
                if hop < LINE - 2:
                    pl.when(z > 0)(lambda: self.down(c, hop + 1).start())
                self.across(c, z + 1 + hop).start()

    def arrive(self, first=0, count=None):
        def step(i):
            c = first + i
            for line in range(LINE):
                self.came(c, 2 * line + 1 - self.y, self.y_r.at[c, line]).wait_recv()
            self.local(c).wait()

        loop(self.b.count if count is None else count, step)

    def drain(self):
        z = self.z

        def step(c):
            for line in range(LINE):
                self.across(c, line).wait_send()
            for hop in range(LINE - 1):
                pl.when((z < LINE - 1) & (z - hop >= 0))(lambda: self.up(c, hop).wait_send())
                pl.when((z > 0) & (z + hop <= LINE - 1))(lambda: self.down(c, hop).wait_send())

        loop(self.b.count, step)


class Scatter:
    def __init__(self, blocks, grad, out, refs, inplace=False, ahead=AHEAD):
        self.b, self.grad, self.out, self.inplace = blocks, grad, out, inplace
        self.ahead = min(ahead, blocks.count)
        self.crossed, self.landed = refs[:2]
        self.y_s, self.y_r, self.own_s, self.z_s, self.z_r = refs[2:7]
        self.held = None if inplace else refs[7]
        self.me = lax.axis_index("dp")
        self.z, self.y = self.me // 2, lax.rem(self.me, 2)
        self.lines = [lax.rem(self.z + step, LINE) for step in range(1, LINE)]
        self.ticks, self.done = blocks.count + LAG, 0

    @staticmethod
    def scratch(blocks, inplace=False):
        shape = (blocks.rows, blocks.cols)
        count = blocks.count
        bufs = [pltpu.VMEM((count, lines) + shape, BF16) for lines in (4, 3)]
        held = [] if inplace else [pltpu.VMEM((count, 4) + shape, BF16)]
        return bufs + [DMA((count,))] * 3 + [DMA((count, 3))] * 2 + held

    def part(self, c, row_y):
        row, col = self.b.at(c)
        return self.grad.at[:, row_y, pl.ds(row, self.b.rows), pl.ds(col, self.b.cols)]

    def hold(self, c, line):
        if not self.inplace:
            return self.held.at[c, line]
        row, col = self.b.at(c)
        return self.grad.at[line, self.y, pl.ds(row, self.b.rows), pl.ds(col, self.b.cols)]

    def across(self, c):
        other = self.me + 1 - 2 * self.y
        return remote(self.part(c, 1 - self.y), self.crossed.at[c], self.y_s.at[c], self.y_r.at[c], dp=other)

    def load(self, c):
        return pltpu.make_async_copy(self.part(c, self.y), self.held.at[c], self.own_s.at[c])

    def along(self, c, i):
        line = self.lines[i]
        return remote(
            self.hold(c, line), self.landed.at[c, i], self.z_s.at[c, i], self.z_r.at[c, i], dp=2 * line + self.y
        )

    def begin(self, c):
        self.across(c).start()
        if not self.inplace:
            self.load(c).start()

    def start(self):
        for c in range(self.ahead):
            self.begin(c)

    def fold(self, c):
        self.across(c).wait_recv()
        if not self.inplace:
            self.load(c).wait()
        for i in (1, 0, 2):
            line = self.lines[i]
            add_rows(self.hold(c, line), self.hold(c, line), self.crossed.at[c, line])
            self.along(c, i).start()

    def finish(self, c):
        row, col = self.b.at(c)
        for i in range(LINE - 1):
            self.along(c, i).wait_recv()
        out_col = aligned(col - self.b.first, 128)
        out = self.out.at[pl.ds(row, self.b.rows), pl.ds(out_col, self.b.cols)]
        landed = [self.landed.at[c, i] for i in range(LINE - 1)]
        add_rows(out, self.hold(c, self.z), self.crossed.at[c, self.z], *landed)

    def pump(self, t):
        pl.when(t + self.ahead < self.b.count)(lambda: self.begin(t + self.ahead))
        pl.when(t < self.b.count)(lambda: self.fold(t))
        pl.when(t >= LAG)(lambda: self.finish(t - LAG))

    def drain(self):
        def step(c):
            self.across(c).wait_send()
            for i in range(LINE - 1):
                self.along(c, i).wait_send()

        loop(self.b.count, step)


class Idle:
    ticks = done = 0

    def start(self):
        pass

    def pump(self, t):
        pass

    def arrive(self):
        pass

    def drain(self):
        pass


class TpSum:
    def __init__(self, partial, out, bufs, sems, own_sems=None):
        self.p, self.out = partial, out
        self.crossed, self.other = bufs
        self.c_s, self.c_r, self.x_s, self.x_r, self.o_s, self.o_r = sems
        self.core = lax.rem(lax.axis_index("tp"), 2)
        self.beside, self.far = tp_peers()
        self.half = partial.shape[0] // 2
        self.rows = self.half // TP_PARTS
        self.own_s = own_sems

    @staticmethod
    def scratch(rows, wide):
        return [pltpu.VMEM((rows // 2, wide), BF16)] * 2 + [DMA((TP_PARTS,))] * 6

    def spot(self, k, which):
        return pl.ds(pl.multiple_of(which * self.half + k * self.rows, 16), self.rows)

    def part(self, k):
        return pl.ds(aligned(k * self.rows, 16), self.rows)

    def first(self, k):
        return remote(
            self.p.at[self.spot(k, 1 - self.core)],
            self.crossed.at[self.part(k)],
            self.c_s.at[k],
            self.c_r.at[k],
            tp=self.beside,
        )

    def second(self, k):
        here = self.out.at[self.spot(k, self.core)]
        return remote(here, self.other.at[self.part(k)], self.x_s.at[k], self.x_r.at[k], tp=self.far)

    def third(self, k, which):
        here = self.out.at[self.spot(k, which)]
        return remote(here, here, self.o_s.at[k], self.o_r.at[k], tp=self.beside)

    def load(self, k):
        mine = self.spot(k, self.core)
        return pltpu.make_async_copy(self.p.at[mine], self.out.at[mine], self.own_s.at[k])

    def stage_one(self, k):
        self.first(k).start()
        if self.own_s is not None:
            self.load(k).start()

    def stage_two(self, k):
        self.first(k).wait_recv()
        mine = self.spot(k, self.core)
        held = self.p.at[mine]
        if self.own_s is not None:
            self.load(k).wait()
            held = self.out.at[mine]
        add_rows(self.out.at[mine], held, self.crossed.at[self.part(k)])
        self.second(k).start()

    def stage_three(self, k):
        self.second(k).wait()
        mine = self.out.at[self.spot(k, self.core)]
        add_rows(mine, mine, self.other.at[self.part(k)])
        self.third(k, self.core).start()

    def stage_four(self, k):
        self.third(k, 1 - self.core).wait_recv()

    def sent(self, k):
        self.third(k, self.core).wait_send()

    def drain(self, sent=False):
        def step(k):
            self.first(k).wait_send()
            if not sent:
                self.sent(k)

        loop(TP_PARTS, step)


def params(number):
    return pltpu.CompilerParams(
        collective_id=number, has_side_effects=True, vmem_limit_bytes=VMEM_LIMIT
    )


def plain_params():
    return pltpu.CompilerParams(vmem_limit_bytes=VMEM_LIMIT)


ANY = pl.BlockSpec(memory_space=pl.ANY)
IN_VMEM = pl.BlockSpec(memory_space=pltpu.VMEM)
IN_SMEM = pl.BlockSpec(memory_space=pltpu.SMEM)


def shaped(shape, dtype):
    return jax.ShapeDtypeStruct(shape, dtype)


def segment_sum(value, seg):
    high = value.astype(BF16)
    low = (value - high.astype(F32)).astype(BF16)
    return dot_nn(high, seg) + dot_nn(low, seg)


def head_inverse(value, seg):
    return lax.rsqrt(segment_sum(value * value, seg) * (1.0 / HEAD) + EPS)


def thrice(table):
    return jnp.concatenate([table] * 3, axis=1)


def rope(value, cosines, sine_a, sine_b):
    wide = value.shape[1]
    ahead = pltpu.roll(value, wide - HEAD // 4, 1)
    behind = pltpu.roll(value, HEAD // 4, 1)
    return value * cosines + ahead * sine_a + behind * sine_b


def rope_back(grad, cosines, sine_a, sine_b):
    wide = grad.shape[1]
    ahead = pltpu.roll(grad * sine_b, wide - HEAD // 4, 1)
    behind = pltpu.roll(grad * sine_a, HEAD // 4, 1)
    return grad * cosines + ahead + behind


def rope_tables(row_count):
    lane = np.arange(PAIR)
    within = lane % HEAD
    quarter = HEAD // 4
    which = within // quarter
    freqs = (ROPE_BASE ** (-(within % quarter).astype(np.float32) / np.float32(quarter))).astype(np.float32)
    row = np.arange(row_count)
    frame, place = (row // FRAME_TOK).astype(np.float32), (row % FRAME_TOK).astype(np.float32)
    position = np.where(which[None, :] < 2, frame[:, None], place[:, None])
    angles = (position * freqs[None, :]).astype(np.float32)
    cosines, sines = np.cos(angles), np.sin(angles)
    even = (which % 2 == 0)[None, :]
    return (
        jnp.asarray(cosines.astype(np.float32)),
        jnp.asarray(np.where(even, -sines, 0.0).astype(np.float32)),
        jnp.asarray(np.where(even, 0.0, sines).astype(np.float32)),
    )


def segment_ones(wide):
    head = np.arange(wide) // HEAD
    return jnp.asarray((head[:, None] == head[None, :]).astype(np.float32)).astype(BF16)


def live_rows(frames_ref, start, rows, wide):
    row = start + lax.broadcasted_iota(jnp.int32, (rows, wide), 0)
    return (row < frames_ref[0] * FRAME_TOK).astype(F32)


def half_mask(rows, head, dtype):
    lane = lax.broadcasted_iota(jnp.int32, (rows, PAIR), 1)
    return ((lane < HEAD) if head == 0 else (lane >= HEAD)).astype(dtype)


def pair_lanes(pair, wide=PAIR):
    return pl.ds(pl.multiple_of(pair * wide, PAIR), wide)


def block_rows(block, rows):
    return pl.ds(pl.multiple_of(block * rows, rows), rows)


def paced(count, step, *plans):
    jobs = []
    for engine, pumps in plans:
        pumps = min(pumps, engine.ticks - engine.done)
        if pumps > 0:
            jobs.append((engine, pumps, engine.done))
            engine.done += pumps

    def body(i):
        step(i)
        for engine, pumps, base in jobs:
            if pumps <= count:
                every = count // pumps
                turn = lax.div(i, every)
                now = (lax.rem(i, every) == every - 1) & (turn < pumps)
                pl.when(now)(functools.partial(engine.pump, base + turn))
            else:
                each = -(-pumps // count)
                for j in range(each):
                    pl.when(i * each + j < pumps)(functools.partial(engine.pump, base + i * each + j))

    loop(count, body)


def finish_pumps(engine):
    base = engine.done
    if base < engine.ticks:
        loop(engine.ticks - base, lambda i: engine.pump(base + i))
    engine.done = engine.ticks


class Named:
    def __init__(self):
        self.ins, self.outs, self.scratch, self.late = {}, {}, {}, {}

    def take(self, refs):
        found, at = {}, 0
        for name in (*self.ins, *self.outs):
            found[name] = refs[at]
            at += 1
        for name, item in self.scratch.items():
            many = isinstance(item, list)
            found[name] = refs[at : at + len(item)] if many else refs[at]
            at += len(item) if many else 1
        count = len(self.late)
        copies = []
        for i, name in enumerate(self.late):
            found[name] = refs[at + count + i]
            copies.append(pltpu.make_async_copy(refs[at + i], found[name], refs[at + 2 * count + i]))
        r = types.SimpleNamespace(**found)
        r.fetch = types.SimpleNamespace(**dict(zip(self.late, copies)))
        r.fetches = copies
        return r

    def call(self, kernel, compiler_params):
        flat = []
        for item in self.scratch.values():
            flat += item if isinstance(item, list) else [item]
        late = list(self.late.values())
        flat += [pltpu.VMEM(value.shape, value.dtype) for value in late] + [DMA] * len(late)
        ins, outs = list(self.ins.values()), list(self.outs.values())
        first, many = len(ins) + len(outs), len(late)

        def body(*refs):
            own = refs[: len(ins)] + refs[len(ins) + many : first + many]
            scratch = refs[first + many : len(refs) - 2 * many]
            kernel(*own, *scratch, *refs[len(ins) : len(ins) + many], *refs[len(refs) - 2 * many :])

        results = pl.pallas_call(
            body,
            out_shape=[shape for shape, _ in outs],
            in_specs=[spec for _, spec in ins] + [ANY] * many,
            out_specs=[spec for _, spec in outs],
            scratch_shapes=flat,
            compiler_params=compiler_params,
        )(*[value for value, _ in ins], *late)
        return types.SimpleNamespace(**dict(zip(self.outs, results)))


class Opening:
    def __init__(self, r):
        self.r = r
        self.me, self.tp = lax.axis_index("dp"), lax.axis_index("tp")
        self.peers, (self.beside, self.far) = dp_peers(), tp_peers()
        self.sources = [lax.rem(self.me + GRID - step, GRID) for step in range(1, GRID)]
        self.share = r.text_all.shape[1] // 4
        self.cond, self.small, self.parts, self.slabs, self.quarters = (r.sems_set[2 * i : 2 * i + 2] for i in range(5))
        self.own_s = r.sems_set[10]

    def send(self, sems, i, src, dst, **where):
        return remote(src, dst, sems[0].at[i], sems[1].at[i], **where)

    def quarter(self, which):
        rows = pl.ds(pl.multiple_of(which * self.share, 16), self.share)
        return self.r.text_all.at[:, rows, :]

    def slab(self, there, origin):
        depth = self.r.text_all.shape[2]
        rows = pl.ds(pl.multiple_of(self.tp * self.share, 16), self.share)
        src = self.r.text.at[rows, pl.ds(pl.multiple_of(there * depth, 128), depth)]
        return src, self.r.text_all.at[origin, rows, :]

    def cond_out(self, i):
        there = self.peers[i]
        return self.send(self.cond, i, self.r.cond.at[there], self.r.conds.at[self.me], dp=there)

    def small_out(self, i):
        return self.send(self.small, i, self.r.small, self.r.smalls.at[self.me], dp=self.peers[i])

    def slab_out(self, i):
        return self.send(self.slabs, i, *self.slab(self.peers[i], self.me), dp=self.peers[i])

    def part_out(self, i):
        there = self.peers[i]
        return self.send(self.parts, i, self.r.part.at[there], self.r.parts.at[self.me], dp=there)

    def came(self, sems, i, ref):
        self.send(sems, i, ref, ref, dp=self.me).wait_recv()

    def begin(self):
        r, me = self.r, self.me
        for i in range(GRID - 1):
            self.cond_out(i).start()
            self.small_out(i).start()
        for i in range(GRID - 1):
            self.slab_out(i).start()
        pltpu.make_async_copy(*self.slab(me, me), self.own_s).start()
        r.conds[pl.ds(me, 1)] = r.cond[pl.ds(me, 1)]
        r.smalls[pl.ds(me, 1)] = r.small[...][None]

    def partial_rows(self):
        r, me = self.r, self.me
        for i, here in enumerate(self.sources):
            self.came(self.cond, i, r.conds.at[here])
        cond = jnp.concatenate([r.conds[i] for i in range(GRID)], axis=0)
        act = (cond * (1.0 / (1.0 + jnp.exp(-cond)))).astype(BF16)
        r.act[...] = act.astype(F32)
        width = r.w_ada.shape[1] // 4
        for i in range(4):
            cols = pl.ds(i * width, width)
            product = dot_nn(act, r.w_ada[:, cols])
            for j in range(GRID):
                r.part[j, :, cols] = product[j : j + 1, :]
        for i in range(GRID - 1):
            self.part_out(i).start()
        r.parts[pl.ds(me, 1)] = r.part[pl.ds(me, 1)]

    def spread(self):
        pltpu.make_async_copy(*self.slab(self.me, self.me), self.own_s).wait()
        for i, here in enumerate(self.sources):
            self.came(self.slabs, i, self.slab(here, here)[1])
        mine = self.quarter(self.tp)
        self.send(self.quarters, 0, mine, mine, tp=self.beside).start()
        self.send(self.quarters, 1, mine, mine, tp=self.far).start()

    def modulate(self):
        r = self.r
        for i, here in enumerate(self.sources):
            self.came(self.parts, i, r.parts.at[here])
            self.came(self.small, i, r.smalls.at[here])
        wide = r.rows.shape[1]
        bias = r.small.shape[1] - 2 * (wide // GRID)
        ends = r.small.shape[1]
        smalls = [r.smalls[i] for i in range(GRID)]
        mods = sum(r.parts[i] for i in range(GRID)) + jnp.concatenate([v[:, :bias] for v in smalls], axis=1)
        gain_one = jnp.concatenate([v[:, bias : bias + wide // GRID] for v in smalls], axis=1)
        gain_two = jnp.concatenate([v[:, bias + wide // GRID : ends] for v in smalls], axis=1)
        lift_one, lift_two = 1.0 + mods[:, :wide], 1.0 + mods[:, 2 * wide : 3 * wide]
        tanh_one, tanh_two = jnp.tanh(mods[:, wide : 2 * wide]), jnp.tanh(mods[:, 3 * wide :])
        values = (gain_one * lift_one, tanh_one, gain_two * lift_two, tanh_two, gain_one, lift_one, gain_two, lift_two)
        for i, value in enumerate(values):
            r.rows[i : i + 1, :] = value

    def pass_on(self):
        from_far = self.quarter(lax.rem(self.tp + 2, 4))
        self.send(self.quarters, 1, from_far, from_far, tp=self.far).wait_recv()
        self.send(self.quarters, 2, from_far, from_far, tp=self.beside).start()

    def collect(self):
        near = self.quarter(self.tp + 1 - 2 * lax.rem(self.tp, 2))
        self.send(self.quarters, 0, near, near, tp=self.beside).wait_recv()
        self.send(self.quarters, 2, near, near, tp=self.beside).wait_recv()

    def multiply(self, i):
        r = self.r
        cols = r.w_tk.shape[1]
        rows = r.text_all[i]
        line, y = lax.div(i, 2), lax.rem(i, 2)
        r.products[line, y, :, :cols] = dot_nn(rows, r.w_tk[...]).astype(BF16)
        r.products[line, y, :, cols:] = dot_nn(rows, r.w_tv[...]).astype(BF16)

    def drain(self):
        mine = self.quarter(self.tp)
        self.send(self.quarters, 0, mine, mine, tp=self.beside).wait_send()
        self.send(self.quarters, 1, mine, mine, tp=self.far).wait_send()
        self.send(self.quarters, 2, mine, mine, tp=self.beside).wait_send()
        for i in range(GRID - 1):
            self.cond_out(i).wait_send()
            self.small_out(i).wait_send()
            self.slab_out(i).wait_send()
            self.part_out(i).wait_send()


def pack_kernel(q, k, v, out, gate, up, down, *refs):
    vectors, (attn_ref, one_ref, two_ref, small_ref, heads_ref) = refs[:7], refs[7:]
    cols = q.shape[1]
    at = 0
    for vector in vectors[:3]:
        count = vector.shape[0]
        small_ref[:, at : at + count] = vector[...].astype(F32).reshape(1, count)
        at += count
    heads_ref[...] = jnp.zeros_like(heads_ref)
    for i, vector in enumerate(vectors[3:]):
        heads_ref[i : i + 1, :] = vector[...].astype(F32).reshape(1, cols)
    for i, w in enumerate((q, k, v)):
        attn_ref[:, i * cols : (i + 1) * cols] = w[...]
    attn_ref[:, 3 * cols :] = out[...]
    for b in range(gate.shape[1] // UNITS):
        ref, at = (one_ref, b) if b < ONES else (two_ref, b - ONES)
        here = slice(b * UNITS, (b + 1) * UNITS)
        for i, value in enumerate((gate[:, here], up[:, here], down[:, here])):
            ref[:, (3 * at + i) * UNITS : (3 * at + i + 1) * UNITS] = value


def pack(q, k, v, out, gate, up, down, vectors):
    depth, cols = q.shape
    blocks = gate.shape[1] // UNITS
    widths = (4 * cols, 3 * UNITS * ONES, 3 * UNITS * (blocks - ONES))
    return pl.pallas_call(
        pack_kernel,
        out_shape=[shaped((depth, wide), BF16) for wide in widths]
        + [shaped((1, sum(vector.shape[0] for vector in vectors[:3])), F32), shaped((8, cols), F32)],
        in_specs=[IN_VMEM] * 14,
        out_specs=[IN_VMEM] * 5,
        compiler_params=plain_params(),
    )(q, k, v, out, gate, up, down, *vectors)


def forward_kernel(named, grid, cuts, *refs):
    r = named.take(refs)
    tok, weights, rows_ref, heads_ref = r.tok, r.weights, r.rows, r.heads
    cos_ref, sa_ref, sb_ref, seg_ref = r.cos, r.sa, r.sb, r.seg
    attn_sum, partial, mixed, ty = r.attn_sum, r.partial, r.mixed, r.ty
    sums = TpSum(partial, attn_sum, r.tp_set[:2], r.tp_set[2:8])
    mult, tanh_attn, mult_two = rows_ref.at[0:1], rows_ref.at[1:2], rows_ref.at[2:3]
    qgain, kgain, kygain, gate = (heads_ref.at[i : i + 1] for i in range(4))
    rows, cols = r.q_rot.shape
    step_rows = 256
    blocks_here = rows // step_rows
    pairs = cols // PAIR
    attn_engine = text_engine = engine = Idle()
    for fetch in r.fetches:
        fetch.start()
    if grid:
        opening = Opening(r)
        attn_engine = GatherChain(cuts[0], r.attn_shard, weights, r.attn_set, A_A)
        text_engine = Scatter(cuts[1], r.products, ty, r.text_set, True, ahead=A_P)
        engine = GatherChain(cuts[2], r.ffn_shard, r.full_ffn, r.ffn_set)
        greet(dp_peers(), tp_peers())
        opening.begin()
        attn_engine.start()
        opening.partial_rows()
        paced(1, lambda i: None, (attn_engine, O_1))
        opening.spread()
        paced(1, lambda i: None, (attn_engine, O_2))
        opening.modulate()
        paced(1, lambda i: None, (attn_engine, O_3))
        opening.pass_on()
        paced(1, lambda i: None, (attn_engine, O_4))
        opening.collect()
        r.fetch.w_tk.wait()
        r.fetch.w_tv.wait()
        paced(GRID, opening.multiply, (attn_engine, 2))
        text_engine.start()
        finish_pumps(attn_engine)
        attn_engine.arrive()
        engine.start()
    else:
        greet([], tp_peers())

    def project(i):
        here = block_rows(i, step_rows)
        x = tok[here, :].astype(F32)
        inverse = lax.rsqrt(jnp.mean(x * x, axis=-1, keepdims=True) + EPS)
        h = (x * inverse * mult[...]).astype(BF16)
        r.h_one[here, :] = h
        cosines, sine_a, sine_b = thrice(cos_ref[here, :]), thrice(sa_ref[here, :]), thrice(sb_ref[here, :])
        q = dot_nn(h, weights[:, :cols])
        r.q_pre[here, :] = q
        qn = q * head_inverse(q, seg_ref[...]) * qgain[...]
        r.q_text[here, :] = (qn * SCALE).astype(BF16)
        r.q_rot[here, :] = (rope(qn, cosines, sine_a, sine_b) * SCALE).astype(BF16)
        k = dot_nn(h, weights[:, cols : 2 * cols])
        r.k_pre[here, :] = k
        kn = k * head_inverse(k, seg_ref[...]) * kgain[...]
        r.k_rot[here, :] = rope(kn, cosines, sine_a, sine_b).astype(BF16)
        v = dot_nn(h, weights[:, 2 * cols : 3 * cols]).astype(BF16)
        r.values[here, :] = v
        live = live_rows(r.frames, i * step_rows, step_rows, PAIR).astype(BF16)
        for pair in range(pairs):
            r.vaug[here, 2 * pair * PAIR : (2 * pair + 1) * PAIR] = v[:, pair * PAIR : (pair + 1) * PAIR] * live
            r.vaug[here, (2 * pair + 1) * PAIR : (2 * pair + 2) * PAIR] = live

    def attention(q_ref, k_ref, v_ref, inv_ref):
        def step(i):
            pair, block = lax.div(i, blocks_here), lax.rem(i, blocks_here)
            here, lanes = block_rows(block, step_rows), pair_lanes(pair)
            q = q_ref[here, lanes]
            keys = k_ref[:, lanes]
            values = v_ref[:, pair_lanes(pair, 2 * PAIR)]
            outs = jnp.zeros((step_rows, PAIR), F32)
            total = jnp.zeros((step_rows, PAIR), F32)
            for head in range(2):
                p = jnp.exp(dot_nt(q * half_mask(step_rows, head, BF16), keys)).astype(BF16)
                both = dot_nn(p, values)
                wide_mask = half_mask(step_rows, head, F32)
                outs = outs + both[:, :PAIR] * wide_mask
                total = total + both[:, PAIR:] * wide_mask
            inverse = 1.0 / total
            inv_ref[here, lanes] = inverse
            return here, lanes, outs * inverse

        return step

    self_attention = attention(r.q_rot, r.k_rot, r.vaug, r.inv_l)
    text_attention = attention(r.q_text, r.kyr, r.vyaug, r.inv_lt)

    def attend(i):
        here, lanes, out = self_attention(i)
        r.mixed_self[here, lanes] = out
        r.self_o[here, lanes] = out.astype(BF16)

    def attend_text(i):
        here, lanes, out = text_attention(i)
        r.text_o[here, lanes] = out.astype(BF16)
        mixed[here, lanes] = (r.mixed_self[here, lanes] + gate[:, lanes] * out).astype(BF16)

    half_blocks = blocks_here // 2
    parts_each = TP_PARTS // half_blocks

    def output(which):
        def step(i):
            block = which * half_blocks + i
            for pair in range(pairs):
                attend_text(pair * blocks_here + block)
            here = block_rows(block, step_rows)
            partial[here, :] = dot_nt(mixed[here, :], weights[:, 3 * cols :]).astype(BF16)

        return step

    def output_send(i):
        output(1 - sums.core)(i)
        loop(parts_each, lambda k: sums.stage_one(i * parts_each + k))

    def output_add(i):
        output(sums.core)(i)
        loop(parts_each, lambda k: sums.stage_two(i * parts_each + k))

    for fetch in (r.fetch.tok, r.fetch.cos, r.fetch.sa, r.fetch.sb, r.fetch.seg):
        fetch.wait()
    paced(blocks_here, project, (text_engine, 4), (engine, 2))
    paced(pairs * blocks_here, attend, (text_engine, 4), (engine, 3))
    finish_pumps(text_engine)

    ky = ty[:, :cols]
    r.ky_pre[...] = ky
    r.kyr[...] = (ky * head_inverse(ky, seg_ref[...]) * kygain[...]).astype(BF16)
    vy = ty[:, cols:].astype(BF16)
    r.vy[...] = vy
    for pair in range(pairs):
        r.vyaug[:, 2 * pair * PAIR : (2 * pair + 1) * PAIR] = vy[:, pair * PAIR : (pair + 1) * PAIR]
        r.vyaug[:, (2 * pair + 1) * PAIR : (2 * pair + 2) * PAIR] = jnp.ones((vy.shape[0], PAIR), BF16)
    paced(half_blocks, output_send, (engine, 2))
    paced(half_blocks, output_add, (engine, 2))

    def update(k, which):
        here = sums.spot(k, which)
        live = live_rows(r.frames, which * sums.half + k * sums.rows, sums.rows, tok.shape[1])
        state = tok[here, :].astype(F32) + live * tanh_attn[...] * attn_sum[here, :].astype(F32)
        inverse = lax.rsqrt(jnp.mean(state * state, axis=-1, keepdims=True) + EPS)
        r.h_two[here, :] = (state * inverse * mult_two[...]).astype(BF16)

    def three(k):
        sums.stage_three(k)
        update(k, sums.core)

    paced(TP_PARTS, three, (engine, 4))

    def four(k):
        sums.stage_four(k)
        update(k, 1 - sums.core)

    paced(TP_PARTS, four, (engine, 1))
    finish_pumps(engine)
    engine.arrive()
    sums.drain()
    if grid:
        opening.drain()
    attn_engine.drain()
    text_engine.drain()
    engine.drain()


def forward(clips, frames, tokens, heads_table, tables, seg, ffn_shard, start):
    rows, wide = tokens.shape
    cols = heads_table.shape[1]
    grid = clips == GRID
    depth, ffn_wide = ffn_shard.shape
    n = Named()
    n.ins.update(frames=(frames, IN_SMEM), heads=(heads_table, IN_VMEM))
    cuts = None
    if grid:
        attn_shard, cond, small, w_ada, text, w_tk, w_tv = start
        rows_t, slab = text.shape[0], w_tk.shape[0]
        mods = w_ada.shape[1]
        n.ins.update(attn_shard=(attn_shard, ANY), cond=(cond, IN_VMEM), small=(small, IN_VMEM))
        n.ins.update(w_ada=(w_ada, IN_VMEM), text=(text, ANY))
        n.late.update(w_tk=w_tk, w_tv=w_tv)
        n.ins.update(ffn_shard=(ffn_shard, ANY))
        cuts = (
            Blocks(*attn_shard.shape, 96, 384),
            Blocks(rows_t, 2 * cols, 32, 2 * cols),
            Blocks(depth, ffn_wide, 96, 384),
        )
    else:
        weights, rows_table, ty = start
        rows_t = ty.shape[0]
        n.ins.update(weights=(weights, IN_VMEM), rows=(rows_table, IN_VMEM), ty=(ty, IN_VMEM))
    f, b = (shaped((rows, cols), F32), IN_VMEM), (shaped((rows, cols), BF16), IN_VMEM)
    ft, bt = (shaped((rows_t, cols), F32), IN_VMEM), (shaped((rows_t, cols), BF16), IN_VMEM)
    whole = (shaped((rows, wide), BF16), IN_VMEM)
    n.outs.update(q_pre=f, k_pre=f, q_rot=b, k_rot=b, q_text=b, values=b, self_o=b, inv_l=f, ky_pre=ft, kyr=bt, vy=bt)
    n.outs.update(text_o=b, inv_lt=f, h_one=whole, mixed=b, attn_sum=whole, h_two=whole)
    n.scratch.update(
        vaug=pltpu.VMEM((rows, 2 * cols), BF16),
        vyaug=pltpu.VMEM((rows_t, 2 * cols), BF16),
        partial=pltpu.VMEM((rows, wide), BF16),
        mixed_self=pltpu.VMEM((rows, cols), F32),
        tp_set=TpSum.scratch(rows, wide),
    )
    if grid:
        n.outs.update(
            weights=(shaped((GRID * attn_shard.shape[0], attn_shard.shape[1]), BF16), IN_VMEM),
            rows=(shaped((8, wide), F32), IN_VMEM),
            act=(shaped((GRID, cond.shape[2]), F32), IN_VMEM),
            text_all=(shaped((GRID, rows_t, slab), BF16), IN_VMEM),
            full_ffn=(shaped((GRID * depth, ffn_wide), BF16), ANY),
        )
        n.scratch.update(
            ty=pltpu.VMEM((rows_t, 2 * cols), F32),
            products=pltpu.VMEM((LINE, 2, rows_t, 2 * cols), BF16),
            smalls=pltpu.VMEM((GRID,) + small.shape, F32),
            conds=pltpu.VMEM((GRID, 1, cond.shape[2]), F32),
            part=pltpu.VMEM((GRID, 1, mods), F32),
            parts=pltpu.VMEM((GRID, 1, mods), F32),
            sems_set=[DMA((GRID - 1,))] * 8 + [DMA((3,))] * 2 + [DMA],
            attn_set=GatherChain.scratch(cuts[0].count),
            text_set=Scatter.scratch(cuts[1], True),
            ffn_set=GatherChain.scratch(cuts[2].count),
        )
    n.late.update(tok=tokens, cos=tables[0], sa=tables[1], sb=tables[2], seg=seg)
    out = n.call(functools.partial(forward_kernel, n, grid, cuts), params(1))
    if not grid:
        out.weights, out.rows, out.text_all = weights, rows_table, jnp.zeros((1, 16, 128), BF16)
    return out


UNITS = 256
ONES = 3
SP = ((0, 0), (2, 2), (2, 2), (2, 0))


def ffn_kernel(named, cut, cut_back, *refs):
    r = named.take(refs)
    engine, scatter = Idle(), Idle()
    for fetch in r.fetches:
        fetch.start()
    if cut is not None:
        engine = GatherChain(cut, r.shard, r.w_two, r.gather_set)
        scatter = Scatter(cut_back, r.grads, r.out, r.scatter_set)
        greet(dp_peers(), [])
        engine.start()
    rows, wide = r.h_two.shape
    step_rows = 256
    count = rows // step_rows
    tall = wide // LINE
    tanh_two = r.rows[3:4, :]
    ones, twos = r.w_one.shape[1] // (3 * UNITS), r.w_two.shape[1] // (3 * UNITS)

    def start_rows(i):
        here = block_rows(i, step_rows)
        live = live_rows(r.frames, i * step_rows, step_rows, wide)
        r.grad_ffn[here, :] = (live * tanh_two * r.cot[here, :].astype(F32)).astype(BF16)

    def copy(b):
        place = r.grads.at[:, :, :, pl.ds(b * 3 * UNITS, 3 * UNITS)]
        return pltpu.make_async_copy(r.staged.at[b % 2], place, r.stage_s.at[b % 2])

    def block(b):
        w = r.w_one if b < ones else r.w_two
        first = (b if b < ones else b - ones) * 3 * UNITS
        last = b == ones + twos - 1
        dgu = r.dgu_last if last else r.dgu

        def units(i):
            here = block_rows(i, step_rows)
            both = dot_nn(r.h_two[here, :], w[:, first : first + 2 * UNITS])
            gate, up = both[:, :UNITS], both[:, UNITS:]
            back = dot_nn(r.grad_ffn[here, :], w[:, first + 2 * UNITS : first + 3 * UNITS])
            logistic = 1.0 / (1.0 + jnp.exp(-gate))
            swish = gate * logistic
            r.hid[here, b * UNITS : (b + 1) * UNITS] = (swish * up).astype(BF16)
            d_gate = (back * up * logistic * (1.0 + gate * (1.0 - logistic))).astype(BF16)
            d_both = jnp.concatenate([d_gate, (back * swish).astype(BF16)], axis=1)
            dgu[here, :] = d_both
            added = dot_nt(d_both, w[:, first : first + 2 * UNITS])
            if b == 0:
                r.total[here, :] = added
            elif not last:
                r.total[here, :] += added
            else:
                r.partial[here, :] = (r.total[here, :] + added).astype(BF16)

        def products(m):
            lanes = pl.ds(pl.multiple_of(m * tall, 128), tall)
            downs = dot_tn(r.grad_ffn[:, lanes], r.hid[:, b * UNITS : (b + 1) * UNITS]).astype(BF16)
            ins = dot_tn(r.h_two[:, lanes], dgu[...]).astype(BF16)
            for y in range(2):
                part = slice(y * tall // 2, (y + 1) * tall // 2)
                r.staged[b % 2, m, y, :, : 2 * UNITS] = ins[part]
                r.staged[b % 2, m, y, :, 2 * UNITS :] = downs[part]

        pumps = 1 if b < ones else 2
        paced(count, units, (engine, pumps), (scatter, SP[b][0]))
        if not last:
            if b >= 2 and (b > 2 or cut is None):
                copy(b - 2).wait()
            paced(LINE, products, (engine, pumps), (scatter, SP[b][1]))
            copy(b).start()
        if b == 0 and cut is not None:
            copy(0).wait()
            scatter.start()

    paced(count, start_rows, (engine, 1))
    r.fetch.h_two.wait()
    r.fetch.w_one.wait()
    each = cut.count // twos if cut is not None else 0
    for b in range(ones):
        block(b)
    for b in range(ones, ones + twos):
        if cut is not None:
            need = min(engine.ticks, (b - ones + 1) * each + 2)
            while engine.done < need:
                paced(1, lambda i: None, (engine, 1))
            engine.arrive((b - ones) * each, each)
        block(b)
    copy(ones + twos - 3).wait()
    copy(ones + twos - 2).wait()
    finish_pumps(scatter)
    scatter.drain()
    engine.drain()


def ffn(clips, frames, h_two, cotangent, rows_table, w_one, second):
    rows, wide = h_two.shape
    half_wide = second.shape[1]
    blocks = (w_one.shape[1] + half_wide) // (3 * UNITS)
    grid = clips == GRID
    depth = wide // GRID
    n = Named()
    n.ins.update(frames=(frames, IN_SMEM), cot=(cotangent, IN_VMEM), rows=(rows_table, IN_VMEM))
    n.late.update(h_two=h_two, w_one=w_one)
    whole = (shaped((rows, wide), BF16), IN_VMEM)
    cut = Blocks(depth, half_wide, 96, 384) if grid else None
    cut_back = None
    if grid:
        n.ins.update(shard=(second, ANY))
        cut_back = Blocks(depth, 3 * UNITS, 96, 256)
        n.outs.update(w_two=(shaped((wide, half_wide), BF16), IN_VMEM), out=(shaped((depth, 3 * UNITS), F32), IN_VMEM))
        n.scratch.update(gather_set=GatherChain.scratch(cut.count), scatter_set=Scatter.scratch(cut_back))
    else:
        n.ins.update(w_two=(second, IN_VMEM))
    n.outs.update(partial=whole, grad_ffn=whole, hid=(shaped((rows, blocks * UNITS), BF16), IN_VMEM))
    n.outs.update(dgu_last=(shaped((rows, 2 * UNITS), BF16), IN_VMEM))
    n.outs.update(grads=(shaped((LINE, 2, depth, (blocks - 1) * 3 * UNITS), BF16), ANY))
    n.scratch.update(
        dgu=pltpu.VMEM((rows, 2 * UNITS), BF16),
        total=pltpu.VMEM((rows, wide), F32),
        staged=pltpu.VMEM((2, LINE, 2, depth, 3 * UNITS), BF16),
        stage_s=DMA((2,)),
    )
    out = n.call(functools.partial(ffn_kernel, n, cut, cut_back), params(5) if grid else plain_params())
    if not grid:
        out.w_two = second
    return out


def state_kernel(named, cut, *refs):
    r = named.take(refs)
    sums = TpSum(r.partial, r.grad_attn, r.tp_set[:2], r.tp_set[2:8], r.tp_set[8])
    tanh_attn, mult = r.rows.at[1:2], r.rows.at[2:3]
    engine = Idle()
    if cut is not None:
        engine = Scatter(cut, r.grads, r.out, r.scatter_set, ahead=A_S0)
        greet(dp_peers(), tp_peers())
        engine.start()
    else:
        greet([], tp_peers())
    loop(TP_PARTS, sums.stage_one)
    rows, wide = r.tok.shape
    step_rows = 256
    tall = wide // LINE
    blocks = r.hid.shape[1] // UNITS
    ones = r.w_one.shape[1] // (3 * UNITS)

    def down_copy(b):
        w = r.w_one if b < ones else r.w_two
        first = (b if b < ones else b - ones) * 3 * UNITS + 2 * UNITS
        place = r.down.at[:, pl.ds(b * UNITS, UNITS)]
        return pltpu.make_async_copy(w.at[:, pl.ds(first, UNITS)], place, r.down_s.at[b])

    for fetch in r.fetches:
        fetch.start()
    for b in range(blocks):
        down_copy(b).start()
    r.colsums[...] = jnp.zeros_like(r.colsums)

    def products(m):
        lanes = pl.ds(pl.multiple_of(m * tall, 128), tall)
        downs = dot_tn(r.grad_ffn[:, lanes], r.hid[:, (blocks - 1) * UNITS :]).astype(BF16)
        ins = dot_tn(r.h_two[:, lanes], r.dgu[...]).astype(BF16)
        for y in range(2):
            part = slice(y * tall // 2, (y + 1) * tall // 2)
            r.g_last[m, y, :, : 2 * UNITS] = ins[part]
            r.g_last[m, y, :, 2 * UNITS :] = downs[part]

    def p_copy(i):
        place = r.p_ffn.at[block_rows(i, step_rows)]
        return pltpu.make_async_copy(r.p_staged.at[lax.rem(i, 2)], place, r.p_s.at[lax.rem(i, 2)])

    def p_block(i):
        pl.when(i >= 2)(lambda: p_copy(i - 2).wait())
        r.p_staged[lax.rem(i, 2)] = dot_nt(r.hid[block_rows(i, step_rows), :], r.down[...]).astype(BF16)
        p_copy(i).start()

    def update(k, which):
        here = sums.spot(k, which)
        live = live_rows(r.frames, which * sums.half + k * sums.rows, sums.rows, wide)
        added = r.attn_sum[here, :].astype(F32)
        state = r.tok[here, :].astype(F32) + live * tanh_attn[...] * added
        inverse = lax.rsqrt(jnp.mean(state * state, axis=-1, keepdims=True) + EPS)
        hat = state * inverse
        g = r.grad_attn[here, :].astype(F32)
        scaled = g * mult[...]
        g_hat = g * hat
        back = inverse * (scaled - hat * jnp.mean(scaled * hat, axis=-1, keepdims=True))
        total = r.cot[here, :].astype(F32) + back
        r.grad_state[here, :] = total.astype(BF16)
        live_total = live * total
        r.grad_attn[here, :] = (tanh_attn[...] * live_total).astype(BF16)
        r.colsums[0:1, :] += jnp.sum(g_hat, axis=0, keepdims=True)
        r.colsums[1:2, :] += jnp.sum(live_total * added, axis=0, keepdims=True)

    paced(TP_PARTS, sums.stage_two, (engine, 2))
    for fetch in (r.fetch.h_two, r.fetch.grad_ffn, r.fetch.hid, r.fetch.dgu):
        fetch.wait()
    paced(LINE, products, (engine, 2))
    for b in range(blocks):
        down_copy(b).wait()
    paced(rows // step_rows, p_block, (engine, 2))

    for fetch in (r.fetch.tok, r.fetch.attn_sum, r.fetch.cot):
        fetch.wait()

    def three(k):
        sums.stage_three(k)

        @pl.when(k > 0)
        def _():
            sums.sent(k - 1)
            update(k - 1, sums.core)

    paced(TP_PARTS, three, (engine, 8))
    sums.sent(TP_PARTS - 1)
    update(TP_PARTS - 1, sums.core)

    def four(k):
        sums.stage_four(k)
        update(k, 1 - sums.core)

    paced(TP_PARTS, four, (engine, 2))
    finish_pumps(engine)
    for i in (1, 2):
        p_copy(rows // step_rows - i).wait()
    sums.drain(True)
    engine.drain()


def state_backward(clips, frames, tokens, attn_sum, cotangent, rows_table, h_two, w_one, fed):
    rows, wide = tokens.shape
    grid = clips == GRID
    depth = wide // GRID
    units, scattered = fed.hid.shape[1], fed.grads.shape[-1]
    cut = Blocks(depth, scattered - 3 * UNITS, 96, 256, 3 * UNITS) if grid else None
    n = Named()
    n.ins.update(frames=(frames, IN_SMEM), rows=(rows_table, IN_VMEM), w_one=(w_one, ANY), w_two=(fed.w_two, ANY))
    n.ins.update(partial=(fed.partial, ANY))
    n.late.update(h_two=h_two, grad_ffn=fed.grad_ffn, hid=fed.hid, dgu=fed.dgu_last)
    n.late.update(tok=tokens, attn_sum=attn_sum, cot=cotangent)
    whole = shaped((rows, wide), BF16)
    n.outs.update(grad_attn=(whole, IN_VMEM), grad_state=(whole, IN_VMEM), colsums=(shaped((8, wide), F32), IN_VMEM))
    n.outs.update(g_last=(shaped((LINE, 2, depth, 3 * UNITS), BF16), IN_VMEM), p_ffn=(whole, ANY))
    n.scratch.update(
        down=pltpu.VMEM((wide, units), BF16),
        down_s=DMA((units // UNITS,)),
        p_staged=pltpu.VMEM((2, 256, wide), BF16),
        p_s=DMA((2,)),
        tp_set=TpSum.scratch(rows, wide) + [DMA((TP_PARTS,))],
    )
    if grid:
        n.ins.update(grads=(fed.grads, ANY))
        n.outs.update(out=(shaped((depth, scattered - 3 * UNITS), F32), IN_VMEM))
        n.scratch.update(scatter_set=Scatter.scratch(cut))
    return n.call(functools.partial(state_kernel, n, cut), params(2))


def attn_back_kernel(named, blocks, blocks_t, *refs):
    r = named.take(refs)
    out_cols = r.full.shape[1] * 3 // 4
    out_fetch = pltpu.make_async_copy(r.full.at[:, out_cols:], r.weights, r.weights_s)
    out_fetch.start()
    frames, grad_attn, weights, heads_ref, seg_ref = r.frames, r.grad_attn, r.weights, r.heads, r.seg
    cos_ref, sa_ref, sb_ref = r.cos, r.sa, r.sb
    q_pre, k_pre, q_rot, k_rot, q_text, v_ref, self_o, inv_l = (
        r.q_pre, r.k_pre, r.q_rot, r.k_rot, r.q_text, r.values, r.self_o, r.inv_l
    )
    ky_pre, kyr, vy, text_o, inv_lt, h_one, mixed = r.ky_pre, r.kyr, r.vy, r.text_o, r.inv_lt, r.h_one, r.mixed
    grad_qkv, grad_text, gains, g_attn = r.grad_qkv, r.grad_text, r.gains, r.g_attn
    do_self, do_text, d_self, d_text, dqn, dk, dv, dky, dvy, klive, staged, stage_s = r.work_set
    sums = TpSum(r.partial, r.ffn_sum, r.tp_set[:2], r.tp_set[2:8], r.tp_set[8])
    for fetch in r.fetches:
        fetch.start()
    qgain, kgain, kygain, gate = (heads_ref.at[i : i + 1] for i in range(4))
    engine, text_engine = Idle(), Idle()
    if blocks is not None:
        engine = Scatter(blocks, r.grad, r.out, r.scatter_set, ahead=A_S1)
        text_engine = GatherChain(blocks_t, grad_text, r.all_text, r.gather_set, A_T)
        greet(dp_peers(), tp_peers())
        engine.start()
    else:
        greet([], tp_peers())
    loop(TP_PARTS, sums.stage_one)
    rows, cols = q_rot.shape
    wide = grad_attn.shape[1]
    step_rows = 256
    blocks_here = rows // step_rows
    pairs = cols // PAIR
    gains[...] = jnp.zeros_like(gains)
    dk[...] = jnp.zeros_like(dk)
    dv[...] = jnp.zeros_like(dv)
    dky[...] = jnp.zeros_like(dky)
    dvy[...] = jnp.zeros_like(dvy)

    def halves(value, first_head):
        lane = lax.broadcasted_iota(jnp.int32, (step_rows, PAIR), 1)
        out = jnp.zeros((step_rows, PAIR), F32)
        for head in range(2):
            total = jnp.sum(value * half_mask(step_rows, head, F32), axis=-1, keepdims=True)
            high = total.astype(BF16).astype(F32)
            spot = 2 * (first_head + head)
            out = out + jnp.where(lane == spot, high, jnp.where(lane == spot + 1, total - high, 0.0))
        return out

    def start_rows(i):
        here = block_rows(i, step_rows)
        g = dot_nn(grad_attn[here, :], weights[...])
        other = text_o[here, :].astype(F32)
        gains[3:4, :] += jnp.sum(g * other, axis=0, keepdims=True)
        first = (g * inv_l[here, :]).astype(BF16)
        do_self[here, :] = first
        second = (g * gate[...] * inv_lt[here, :]).astype(BF16)
        do_text[here, :] = second
        dot_self = first.astype(F32) * self_o[here, :].astype(F32)
        dot_text = second.astype(F32) * other
        each = [slice(pair * PAIR, (pair + 1) * PAIR) for pair in range(pairs)]
        d_self[here, :] = sum(halves(dot_self[:, lanes], 2 * pair) for pair, lanes in enumerate(each)).astype(BF16)
        d_text[here, :] = sum(halves(dot_text[:, lanes], 2 * pair) for pair, lanes in enumerate(each)).astype(BF16)
        klive[here, :] = k_rot[here, :] * live_rows(frames, i * step_rows, step_rows, cols).astype(BF16)

    def back(q_ref, k_ref, k_live, v_in, do_ref, d_ref, dk_ref, dv_ref, turned):
        def step(i):
            pair, block = lax.div(i, blocks_here), lax.rem(i, blocks_here)
            here, lanes = block_rows(block, step_rows), pair_lanes(pair)
            keys = k_ref[:, lanes]
            values = v_in[:, lanes]
            lane = lax.broadcasted_iota(jnp.int32, values.shape, 1)
            dq = jnp.zeros((step_rows, PAIR), F32)
            for head in range(2):
                mask = half_mask(step_rows, head, BF16)
                q = q_ref[here, lanes] * mask
                do = do_ref[here, lanes] * mask
                scores = dot_nt(keys, q)
                p = jnp.exp(scores)
                dv_ref[:, lanes] += dot_nn(p.astype(BF16), do)
                spot = 2 * (2 * pair + head)
                minus = jnp.where((lane == spot) | (lane == spot + 1), -1.0, 0.0).astype(BF16)
                left = jnp.concatenate([values, minus], axis=1)
                right = jnp.concatenate([do, d_ref[here, :]], axis=1)
                ds = (p * dot_nt(left, right)).astype(BF16)
                dk_ref[:, lanes] += dot_nn(ds, q)
                key_mask = half_mask(keys.shape[0], head, BF16)
                dq = dq + dot_tn(ds, k_live[:, lanes] * key_mask)
            dq = dq * SCALE
            if turned:
                dqn[here, lanes] += rope_back(dq, cos_ref[here, :], sa_ref[here, :], sb_ref[here, :])
            else:
                dqn[here, lanes] = dq

        return step

    out_fetch.wait()
    paced(blocks_here, start_rows, (engine, 2))
    def norm_back(grad_normed, pre, gain, row):
        inverse = head_inverse(pre, seg_ref[...])
        hat = pre * inverse
        gains[row : row + 1, :] += jnp.sum(grad_normed * hat, axis=0, keepdims=True)
        scaled = grad_normed * gain
        average = segment_sum(scaled * hat, seg_ref[...]) * (1.0 / HEAD)
        return (inverse * (scaled - hat * average)).astype(BF16)

    def end_rows(i):
        here = block_rows(i, step_rows)
        cosines, sine_a, sine_b = thrice(cos_ref[here, :]), thrice(sa_ref[here, :]), thrice(sb_ref[here, :])
        live = live_rows(frames, i * step_rows, step_rows, cols)
        grad_qkv[here, :cols] = norm_back(dqn[here, :], q_pre[here, :], qgain[...], 0)
        dkn = rope_back(dk[here, :] * live, cosines, sine_a, sine_b)
        grad_qkv[here, cols : 2 * cols] = norm_back(dkn, k_pre[here, :], kgain[...], 1)
        grad_qkv[here, 2 * cols : 3 * cols] = (dv[here, :] * live).astype(BF16)
        for k in range(TP_PARTS // blocks_here):
            sums.stage_three(i * (TP_PARTS // blocks_here) + k)

    for fetch in (r.fetch.q_text, r.fetch.kyr, r.fetch.vy):
        fetch.wait()
    text_back = back(q_text, kyr, kyr, vy, do_text, d_text, dky, dvy, False)

    def text_step(i):
        text_back(i)
        pl.when(i < TP_PARTS)(lambda: sums.stage_two(i))

    paced(pairs * blocks_here, text_step, (engine, 3))
    for fetch in (r.fetch.seg, r.fetch.ky_pre, r.fetch.q_rot, r.fetch.values, r.fetch.cos, r.fetch.sa, r.fetch.sb):
        fetch.wait()
    grad_text[:, :cols] = norm_back(dky[...], ky_pre[...], kygain[...], 2)
    grad_text[:, cols:] = dvy[...].astype(BF16)
    text_engine.start()
    self_back = back(q_rot, k_rot, klive, v_ref, do_self, d_self, dk, dv, True)

    half = pairs * blocks_here // 2
    paced(half, self_back, (engine, 6), (text_engine, 2))
    paced(half, lambda i: self_back(i + half), (text_engine, 3))
    for fetch in (r.fetch.q_pre, r.fetch.k_pre, r.fetch.h_one, r.fetch.mixed):
        fetch.wait()
    paced(blocks_here, end_rows, (text_engine, 2))
    tall = wide // LINE

    def copy(m):
        return pltpu.make_async_copy(staged.at[lax.rem(m, 2)], g_attn.at[m], stage_s.at[lax.rem(m, 2)])

    def products(m):
        lanes = pl.ds(pl.multiple_of(m * tall, 128), tall)
        pl.when(m >= 2)(lambda: copy(m - 2).wait())
        first = dot_tn(h_one[:, lanes], grad_qkv[...]).astype(BF16)
        second = dot_tn(grad_attn[:, lanes], mixed[...]).astype(BF16)
        for y in range(2):
            part = slice(y * tall // 2, (y + 1) * tall // 2)
            staged[lax.rem(m, 2), y, :, : 3 * cols] = first[part]
            staged[lax.rem(m, 2), y, :, 3 * cols :] = second[part]
        copy(m).start()

    paced(LINE, products, (text_engine, 4))
    finish_pumps(engine)
    finish_pumps(text_engine)
    text_engine.arrive()
    loop(TP_PARTS, sums.stage_four)
    copy(LINE - 2).wait()
    copy(LINE - 1).wait()
    sums.drain()
    engine.drain()
    text_engine.drain()


def attn_backward(clips, frames, grad_attn, full_attn, heads_table, tables, seg, p, partial, g_last):
    rows, wide = grad_attn.shape
    cols = heads_table.shape[1]
    rows_t = p.kyr.shape[0]
    depth, last_wide = wide // GRID, g_last.shape[-1]
    grid = clips == GRID
    f, b = pltpu.VMEM((rows, cols), F32), pltpu.VMEM((rows, cols), BF16)
    ft = pltpu.VMEM((rows_t, cols), F32)
    slim = pltpu.VMEM((rows, PAIR), BF16)
    n = Named()
    n.ins.update(frames=(frames, IN_SMEM), grad_attn=(grad_attn, IN_VMEM), full=(full_attn, ANY))
    n.ins.update(heads=(heads_table, IN_VMEM), k_rot=(p.k_rot, IN_VMEM), self_o=(p.self_o, IN_VMEM))
    n.ins.update(inv_l=(p.inv_l, IN_VMEM), text_o=(p.text_o, IN_VMEM), inv_lt=(p.inv_lt, IN_VMEM), partial=(partial, ANY))
    n.late.update(q_text=p.q_text, kyr=p.kyr, vy=p.vy, seg=seg, ky_pre=p.ky_pre, q_rot=p.q_rot, values=p.values)
    n.late.update(cos=tables[0], sa=tables[1], sb=tables[2], q_pre=p.q_pre, k_pre=p.k_pre, h_one=p.h_one, mixed=p.mixed)
    n.outs.update(
        grad_qkv=(shaped((rows, 3 * cols), BF16), IN_VMEM),
        grad_text=(shaped((rows_t, 2 * cols), BF16), IN_VMEM),
        gains=(shaped((8, cols), F32), IN_VMEM),
        ffn_sum=(shaped((rows, wide), BF16), IN_VMEM),
        g_attn=(shaped((LINE, 2, depth, 4 * cols), BF16), ANY),
    )
    n.scratch.update(
        work_set=[b, b, slim, slim, f, f, f, ft, ft, b, pltpu.VMEM((2, 2, depth, 4 * cols), BF16), DMA((2,))],
        tp_set=TpSum.scratch(rows, wide) + [DMA((TP_PARTS,))],
        weights=pltpu.VMEM((wide, cols), BF16),
        weights_s=DMA,
    )
    parts = blocks_t = None
    if grid:
        parts = Blocks(depth, last_wide, 96, 256)
        blocks_t = Blocks(rows_t, 2 * cols, 32, 2 * cols)
        n.ins.update(grad=(g_last, ANY))
        n.outs.update(
            out=(shaped((depth, last_wide), F32), IN_VMEM), all_text=(shaped((GRID * rows_t, 2 * cols), BF16), ANY)
        )
        n.scratch.update(scatter_set=Scatter.scratch(parts), gather_set=GatherChain.scratch(blocks_t.count))
    return n.call(functools.partial(attn_back_kernel, n, parts, blocks_t), params(3))


def last_kernel(named, parts, *refs):
    r = named.take(refs)
    frames, grad_qkv, weights, tok, grad_state = r.frames, r.grad_qkv, r.weights, r.tok, r.grad_state
    rows_ref, sums_two, gains, ffn_sum, attn_sum, cot = r.rows, r.sums_two, r.gains, r.ffn_sum, r.attn_sum, r.cot
    result, grad_tokens, vecs = r.result, r.grad_tokens, r.vecs
    partial, grad_n, colsum, outsum, vec = r.work_set
    sums = TpSum(partial, grad_n, r.tp_set[:2], r.tp_set[2:8])
    me = lax.axis_index("dp")
    engine = Idle()
    peers = []
    for fetch in r.fetches:
        fetch.start()
    if parts is not None:
        v_s, v_r = r.sems_set
        text_all, all_text, g_tk, g_tv = r.text_all, r.all_text, r.g_tk, r.g_tv
        peers = dp_peers()
        engine = Scatter(parts, r.grad_a, r.out_a, r.scatter_set, ahead=A_S2)
        greet(peers, tp_peers())
        engine.start()
    else:
        greet([], tp_peers())
    mult_one, tanh_one, _, tanh_two, gain_one, lift_one, gain_two, lift_two = (rows_ref[i : i + 1, :] for i in range(8))
    colsum[...] = jnp.zeros_like(colsum)
    outsum[...] = jnp.zeros_like(outsum)
    wide = tok.shape[1]
    cols = grad_qkv.shape[1] // 3
    step_rows = 256

    def project(which):
        def step(i):
            here = pl.ds(pl.multiple_of(which * sums.half + i * step_rows, 16), step_rows)
            partial[here, :] = dot_nt(grad_qkv[here, :], weights[:, : 3 * cols]).astype(BF16)

        return step

    parts_each = TP_PARTS // (sums.half // step_rows)

    def project_send(i):
        project(1 - sums.core)(i)
        loop(parts_each, lambda k: sums.stage_one(i * parts_each + k))

    paced(sums.half // step_rows, project_send)
    paced(sums.half // step_rows, project(sums.core), (engine, P_1))
    paced(TP_PARTS, sums.stage_two, (engine, P_2))

    def output(i):
        here = block_rows(i, 64)
        live = live_rows(frames, i * 64, 64, wide)
        added = live * ffn_sum[here, :].astype(F32)
        state = tok[here, :].astype(F32) + live * tanh_one * attn_sum[here, :].astype(F32)
        result[here, :] = (state + tanh_two * added).astype(BF16)
        outsum[...] += jnp.sum(added * cot[here, :].astype(F32), axis=0, keepdims=True)

    for fetch in (r.fetch.tok, r.fetch.ffn_sum, r.fetch.attn_sum, r.fetch.cot):
        fetch.wait()
    paced(tok.shape[0] // 64, output, (engine, P_3))
    if parts is not None:
        rows_t = text_all.shape[1]

        def text_products(i):
            here = block_rows(i, rows_t)
            g_tk[...] += dot_tn(text_all[i], all_text[here, :cols])
            g_tv[...] += dot_tn(text_all[i], all_text[here, cols:])

        g_tk[...] = jnp.zeros_like(g_tk)
        g_tv[...] = jnp.zeros_like(g_tv)
        r.fetch.text_all.wait()
        r.fetch.all_text.wait()
        paced(GRID, text_products, (engine, P_4))

    def update(k, which):
        here = sums.spot(k, which)
        x = tok[here, :].astype(F32)
        inverse = lax.rsqrt(jnp.mean(x * x, axis=-1, keepdims=True) + EPS)
        hat = x * inverse
        g = grad_n[here, :].astype(F32)
        scaled = g * mult_one
        back = inverse * (scaled - hat * jnp.mean(scaled * hat, axis=-1, keepdims=True))
        grad_tokens[here, :] = (grad_state[here, :].astype(F32) + back).astype(BF16)
        colsum[...] += jnp.sum(g * hat, axis=0, keepdims=True)

    def three(k):
        sums.stage_three(k)
        update(k, sums.core)

    r.fetch.grad_state.wait()
    paced(TP_PARTS, three, (engine, 4))

    def four(k):
        sums.stage_four(k)
        update(k, 1 - sums.core)

    paced(TP_PARTS, four, (engine, 2))
    pieces = (
        colsum[...] * gain_one,
        sums_two[1:2, :] * (1.0 - tanh_one * tanh_one),
        sums_two[0:1, :] * gain_two,
        outsum[...] * (1.0 - tanh_two * tanh_two),
        colsum[...] * lift_one,
        sums_two[0:1, :] * lift_two,
    )
    for i, piece in enumerate(pieces):
        vec[:, i * wide : (i + 1) * wide] = piece
    for i in range(4):
        vec[:, 6 * wide + i * cols : 6 * wide + (i + 1) * cols] = gains[i : i + 1, :]
    for i, there in enumerate(peers):
        remote(vec, vecs.at[me], v_s.at[i], v_r.at[i], dp=there).start()
    finish_pumps(engine)
    vecs[pl.ds(me if peers else 0, 1)] = vec[...][None]
    for i, there in enumerate(peers):
        here = lax.rem(me + GRID - 1 - i, GRID)
        remote(vec, vecs.at[here], v_s.at[i], v_r.at[i], dp=me).wait_recv()
        remote(vec, vecs.at[me], v_s.at[i], v_r.at[i], dp=there).wait_send()
    sums.drain()
    engine.drain()


def last_backward(clips, frames, tokens, cotangent, p, state, back, qkv_weights):
    rows, wide = tokens.shape
    grid = clips == GRID
    cols = back.gains.shape[1]
    depth, wide_a = back.g_attn.shape[-2:]
    whole = (shaped((rows, wide), BF16), IN_VMEM)
    vec = (1, 6 * wide + 4 * cols)
    n = Named()
    n.ins.update(frames=(frames, IN_SMEM), grad_qkv=(back.grad_qkv, IN_VMEM), weights=(qkv_weights, IN_VMEM))
    n.ins.update(rows=(p.rows, IN_VMEM), sums_two=(state.colsums, IN_VMEM), gains=(back.gains, IN_VMEM))
    n.late.update(tok=tokens, ffn_sum=back.ffn_sum, attn_sum=p.attn_sum, cot=cotangent)
    n.outs.update(result=whole, grad_tokens=whole, vecs=(shaped(((GRID if grid else 1),) + vec, F32), IN_VMEM))
    n.scratch.update(
        work_set=[
            pltpu.VMEM((rows, wide), BF16),
            pltpu.VMEM((rows, wide), BF16),
            pltpu.VMEM((1, wide), F32),
            pltpu.VMEM((1, wide), F32),
            pltpu.VMEM(vec, F32),
        ],
        tp_set=TpSum.scratch(rows, wide),
    )
    parts = None
    if grid:
        parts = Blocks(depth, wide_a, 96, 256)
        g_text = (shaped((p.text_all.shape[-1], cols), F32), IN_VMEM)
        n.ins.update(grad_a=(back.g_attn, ANY))
        n.late.update(text_all=p.text_all, all_text=back.all_text)
        n.outs.update(g_tk=g_text, g_tv=g_text, out_a=(shaped((depth, wide_a), F32), IN_VMEM))
        n.scratch.update(sems_set=[DMA((GRID - 1,))] * 2, scatter_set=Scatter.scratch(parts))
    n.late.update(grad_state=state.grad_state)
    return n.call(functools.partial(last_kernel, n, parts), params(4))


def gather_plain(shard):
    return lax.all_gather(shard, "dp", axis=0, tiled=True)


def scatter_plain(grad):
    return lax.psum_scatter(grad, "dp", scatter_dimension=0, tiled=True).astype(F32)


def first_plain(shard, cond, small, w_ada, text, w_tk, w_tv):
    act = jax.nn.silu(lax.all_to_all(cond[:, 0], "dp", 0, 0, tiled=True)).astype(BF16)
    parts = dot_nn(act, w_ada)
    mods = lax.psum_scatter(parts, "dp", scatter_dimension=0, tiled=True)[0]
    full_text = gather_plain(jnp.concatenate([w_tk, w_tv], axis=1))
    smalls = lax.all_gather(small, "dp", axis=0)[:, 0, :]
    wide = w_ada.shape[1] // 4
    bias, gain = 4 * wide // smalls.shape[0], wide // smalls.shape[0]
    scale_one, gate_one, scale_two, gate_two = jnp.split(mods + smalls[:, :bias].reshape(-1), 4)
    gain_one, gain_two = smalls[:, bias : bias + gain].reshape(-1), smalls[:, bias + gain :].reshape(-1)
    lift_one, lift_two = 1.0 + scale_one, 1.0 + scale_two
    values = (
        gain_one * lift_one,
        jnp.tanh(gate_one),
        gain_two * lift_two,
        jnp.tanh(gate_two),
        gain_one,
        lift_one,
        gain_two,
        lift_two,
    )
    return gather_plain(shard), jnp.stack(values), act.astype(F32), dot_nn(text, full_text)


def unpack_kernel(count, *refs):
    blocks, (attn, vecs, act) = refs[:count], refs[count : count + 3]
    q, k, v, out, gate, up, down, g_ada, bias, g_one, g_two, rest = refs[count + 3 :]
    cols = q.shape[1]
    for i, ref in enumerate((q, k, v, out)):
        ref[...] = attn[:, i * cols : (i + 1) * cols]
    b = 0
    for ref in blocks:
        for at in range(0, ref.shape[1], 3 * UNITS):
            for i, place in enumerate((gate, up, down)):
                place[:, b * UNITS : (b + 1) * UNITS] = ref[:, at + i * UNITS : at + (i + 1) * UNITS]
            b += 1
    total = vecs[0]
    for i in range(1, vecs.shape[0]):
        total = total + vecs[i]
    wide = g_ada.shape[1] // 4
    rest[...] = total[:, 6 * wide :]
    me = lax.axis_index("dp")
    for i in range(vecs.shape[0]):

        @pl.when(me == i)
        def _():
            bias[...] = total[:, i * bias.shape[1] : (i + 1) * bias.shape[1]]
            gain = g_one.shape[1]
            g_one[...] = total[:, 4 * wide + i * gain : 4 * wide + (i + 1) * gain]
            g_two[...] = total[:, 5 * wide + i * gain : 5 * wide + (i + 1) * gain]

    clips = jnp.concatenate([vecs[i][:, : 4 * wide] for i in range(vecs.shape[0])], axis=0)
    turned = act[...].T
    for at in range(0, 4 * wide, 512):
        part = turned[:, 0:1] * clips[0:1, at : at + 512]
        for i in range(1, clips.shape[0]):
            part = part + turned[:, i : i + 1] * clips[i : i + 1, at : at + 512]
        g_ada[:, at : at + 512] = part


def unpack(blocks, attn, vecs, act, units, bias_rows, gain_rows):
    depth, cols = attn.shape[0], attn.shape[1] // 4
    wide = (vecs.shape[2] - 4 * cols) // 6
    shapes = [(depth, cols)] * 4 + [(depth, units)] * 3
    shapes += [(act.shape[1], 4 * wide), (1, bias_rows), (1, gain_rows), (1, gain_rows), (1, 4 * cols)]
    return pl.pallas_call(
        functools.partial(unpack_kernel, len(blocks)),
        out_shape=[shaped(shape, F32) for shape in shapes],
        in_specs=[IN_VMEM] * (len(blocks) + 3),
        out_specs=[IN_VMEM] * len(shapes),
        compiler_params=plain_params(),
    )(*blocks, attn, vecs, act)


def on_device(
    tokens,
    text,
    cond,
    frames,
    w_query,
    w_key,
    w_value,
    w_out,
    w_text_key,
    w_text_value,
    w_gate,
    w_up,
    w_down,
    w_ada,
    ada_bias,
    norm_one,
    norm_two,
    query_gain,
    key_gain,
    text_key_gain,
    cross_gate,
    cotangent,
):
    rows, wide = tokens.shape
    clips = lax.axis_size("dp")
    grid = clips == GRID
    cols, units = w_query.shape[1], w_gate.shape[1]
    heads_here = cols // HEAD
    bias_rows, gain_rows = ada_bias.shape[0], norm_one.shape[0]
    gate_tanh = jnp.tanh(cross_gate.astype(F32))
    vectors = (ada_bias, norm_one, norm_two, query_gain, key_gain, text_key_gain, jnp.repeat(gate_tanh, HEAD))
    cond_rows = cond.astype(F32).reshape(clips, 1, -1)
    packed = pack(w_query, w_key, w_value, w_out.T, w_gate, w_up, w_down.T, vectors)
    attn_shard, *pieces, small, heads_table = packed
    opening = (attn_shard, cond_rows, small, w_ada, text, w_text_key, w_text_value)
    if not grid:
        full_attn, rows_table, act_rows, ty = first_plain(*opening)
        opening = (full_attn, rows_table, ty)
    tables, seg = rope_tables(rows), segment_ones(cols)
    passed = forward(clips, frames, tokens, heads_table, tables, seg, pieces[0], opening)
    full_attn, rows_table = passed.weights, passed.rows
    if grid:
        act_rows, half_one, second = passed.act, passed.full_ffn, pieces[1]
    else:
        half_one, second = gather_plain(pieces[0]), gather_plain(pieces[1])
    p = passed
    fed = ffn(clips, frames, p.h_two, cotangent, p.rows, half_one, second)
    state = state_backward(clips, frames, tokens, p.attn_sum, cotangent, p.rows, p.h_two, half_one, fed)
    back = attn_backward(
        clips, frames, state.grad_attn, full_attn, heads_table, tables, seg, p, state.p_ffn, state.g_last
    )
    last = last_backward(clips, frames, tokens, cotangent, p, state, back, full_attn)
    vecs = last.vecs
    s_blocks = [fed.out, state.out] if grid else [scatter_plain(fed.grads.reshape(wide, -1))]
    if grid:
        s_last, s_attn, s_text_key, s_text_value = back.out, last.out_a, last.g_tk, last.g_tv
    if not grid:
        s_last, s_attn = (scatter_plain(g.reshape(wide, -1)) for g in (state.g_last, back.g_attn))
        s_text = scatter_plain(dot_tn(text, back.grad_text).astype(BF16))
        s_text_key, s_text_value = s_text[:, :cols], s_text[:, cols:]
        vecs = lax.all_gather(vecs[0], "dp", axis=0)
    g_query, g_key, g_value, g_out, g_gate, g_up, g_down, g_ada, g_bias, g_one, g_two, rest = unpack(
        (*s_blocks, s_last), s_attn, vecs, act_rows, units, bias_rows, gain_rows
    )
    rest = rest[0]
    g_cross_gate = jnp.sum(rest[3 * cols :].reshape(heads_here, HEAD), axis=1) * (1.0 - gate_tanh * gate_tanh)
    return (
        last.result,
        last.grad_tokens,
        g_query,
        g_key,
        g_value,
        g_out.T,
        s_text_key,
        s_text_value,
        g_gate,
        g_up,
        g_down.T,
        g_ada,
        g_bias[0],
        g_one[0],
        g_two[0],
        rest[:cols],
        rest[cols : 2 * cols],
        rest[2 * cols : 3 * cols],
        g_cross_gate,
    )


def solution(mesh):
    placed = (
        P("dp", None),
        P("dp", None),
        P("dp", None),
        P("dp"),
        P("dp", "tp"),
        P("dp", "tp"),
        P("dp", "tp"),
        P("tp", "dp"),
        P("dp", "tp"),
        P("dp", "tp"),
        P("dp", "tp"),
        P("dp", "tp"),
        P("tp", "dp"),
        P("dp", None),
        P("dp"),
        P("dp"),
        P("dp"),
        P("tp"),
        P("tp"),
        P("tp"),
        P("tp"),
        P("dp", None),
    )
    return jax.shard_map(
        on_device,
        mesh=mesh,
        in_specs=placed,
        out_specs=(
            P("dp", None),
            P("dp", None),
            P("dp", "tp"),
            P("dp", "tp"),
            P("dp", "tp"),
            P("tp", "dp"),
            P("dp", "tp"),
            P("dp", "tp"),
            P("dp", "tp"),
            P("dp", "tp"),
            P("tp", "dp"),
            P("dp", None),
            P("dp"),
            P("dp"),
            P("dp"),
            P("tp"),
            P("tp"),
            P("tp"),
            P("tp"),
        ),
        check_vma=False,
    )
```
